32 devices in a mesh: fsdp: 8 (over z, core), sp: 4 (over y, x).
Axes of the slice: x: 2, y: 2, z: 4, core: 2. Of those that a mesh axis runs over, the one named last changes fastest.
Arguments:
- layer_input: bfloat16 [8192, 2048], P(('fsdp', 'sp')), may hold values from -6 to 6
- output_grad: bfloat16 [8192, 2048], P(('fsdp', 'sp')), may hold values from -6 to 6
- w_query: bfloat16 [2048, 2048], P(('fsdp', 'sp')), may hold values from -0.125 to 0.125
- w_key: bfloat16 [2048, 2048], P(('fsdp', 'sp')), may hold values from -0.125 to 0.125
- w_value: bfloat16 [2048, 2048], P(('fsdp', 'sp')), may hold values from -0.125 to 0.125
- w_output: bfloat16 [2048, 2048], P(('fsdp', 'sp')), may hold values from -1 to 1
- w_router: bfloat16 [2048, 16], P(('fsdp', 'sp')), may hold values from -0.0625 to 0.0625
- norm_gains: bfloat16 [4, 2048], P(None, ('fsdp', 'sp')), may hold values from 0.5 to 1.5
- w_gate: bfloat16 [16, 2048, 1024], P('fsdp', 'sp'), may hold values from -0.125 to 0.125
- w_up: bfloat16 [16, 2048, 1024], P('fsdp', 'sp'), may hold values from -0.125 to 0.125
- w_down: bfloat16 [16, 1024, 2048], P('fsdp', 'sp'), may hold values from -3 to 3
- expert_routes: int32 [8192, 8], P(('fsdp', 'sp')), may hold values from 0 to 15, all different within a row; in each aligned block of 256 rows (0 to 255, 256 to 511, ...) at most 136 rows name the same one
Outputs:
- layer_out: bfloat16 [8192, 2048], P(('fsdp', 'sp'))
- input_grad: float32 [8192, 2048], P(('fsdp', 'sp'))
- grad_query: float32 [2048, 2048], P(('fsdp', 'sp'))
- grad_key: float32 [2048, 2048], P(('fsdp', 'sp'))
- grad_value: float32 [2048, 2048], P(('fsdp', 'sp'))
- grad_output: float32 [2048, 2048], P(('fsdp', 'sp'))
- grad_router: float32 [2048, 16], P(('fsdp', 'sp'))
- grad_gains: float32 [4, 2048], P(None, ('fsdp', 'sp'))
- grad_gate: float32 [16, 2048, 1024], P('fsdp', 'sp')
- grad_up: float32 [16, 2048, 1024], P('fsdp', 'sp')
- grad_down: float32 [16, 1024, 2048], P('fsdp', 'sp')
The draws below stay inside these ranges and needn't reach their ends.
Inputs may be any that keep to these rules, and one draw needn't show every extreme that they name: `expert_routes`: among the 256 tokens of one device no expert is named more than 136 times, a bound that some block reaches; every token names 8 different experts.
All inputs are finite; a program needn't handle non-finite values.
Results may differ from the reference program's by a relative error of at most 0.02.
Values may be sent and summed in bfloat16 or wider, within the bound.
A program may use at most 320 MiB of HBM per device.

```python
import math
import jax
import jax.numpy as jnp
import numpy as np
from jax import lax

D = 2048
HEADS = 16
HEAD_DIM = 128
FF = 1024
TOP = 8
BLK = 256
TOK_DEV = 256
EXPERTS = 16
SEQ = 1024
TOKENS = 8192
CAP = 136
DEVICES = 32


def shard_levels(stream_key, extent, cuts, smallest, largest):
    def one(position, shards_of):
        heights = jax.random.uniform(jax.random.fold_in(jax.random.fold_in(stream_key, 6), position), (shards_of,), jnp.float32, smallest / len(cuts), largest / len(cuts))
        return jnp.repeat(jnp.exp(heights), extent[position] // shards_of).reshape((-1,) + (1,) * (len(extent) - position - 1))

    gain = one(*cuts[0])
    for cut in cuts[1:]:
        gain = gain * one(*cut)
    return gain


def deal_out(own_key, own, number, rows, count, top, bound, skew):
    ranking = jax.random.permutation(own_key, count)
    heavy_load, usual = load_shares(count, rows * top, bound, skew, True), load_shares(count, rows * top, bound, skew, False)
    places = jnp.arange(count)

    def named(sizes, turn):
        used = int((sizes > 0).sum())
        fixed = max(1, used // 4)
        passed = fixed + (places - fixed + turn * (used - fixed)) % max(1, count - fixed)
        return jnp.zeros((count,), jnp.int32).at[ranking[jnp.where(places < fixed, places, passed)]].set(jnp.asarray(sizes, jnp.int32))

    sizes = jnp.where(number % 4 == 0, named(heavy_load, number // 4), named(usual, number - number // 4 - 1))
    mixed = jax.random.permutation(jax.random.fold_in(own, 3), count)
    source_of, sink = mixed[0:count // 2 * 2:2], mixed[1:count // 2 * 2:2]
    slack = jnp.minimum(sizes[source_of] - 1, bound - sizes[sink]) // 2
    slack = jnp.where((source_of == ranking[0]) | (sink == ranking[0]) | (sizes[sink] == 0), 0, jnp.maximum(slack, 0))
    passed = jax.random.randint(jax.random.fold_in(own, 4), (count // 2,), 0, 1 << 20) % (slack + 1)
    sizes = sizes.at[source_of].add(-passed).at[sink].add(passed)
    items = jnp.searchsorted(jnp.cumsum(sizes), jnp.arange(rows * top), side="right").astype(jnp.int32)
    table = items.reshape(top, rows).T
    table = table[jax.random.permutation(jax.random.fold_in(own, 1), rows)]
    turn = jax.random.randint(jax.random.fold_in(own, 2), (rows, 1), 0, top)
    return jnp.take_along_axis(table, (jnp.arange(top)[None, :] + turn) % top, axis=1)


def load_shares(number_of, total, bound, lean, full):
    portions = [(1 << 20) // math.isqrt(grade ** lean) + 1 for grade in range(1, number_of + 1)]
    largest = bound if full else min(bound, max(-(-total // number_of), total * portions[0] // sum(portions)))
    least = 1 if total - largest >= number_of - 1 else 0
    given, rest = [largest] + [least] * (number_of - 1), total - largest - least * (number_of - 1)
    while rest > 0:
        movable = [i for i in range(1, number_of) if given[i] < largest] or [i for i in range(1, number_of) if given[i] < bound]
        mass, budget = sum([portions[i] for i in movable]), rest
        for i in movable:
            addition = min(bound - given[i], max(1, budget * portions[i] // mass), rest)
            given[i] = given[i] + addition
            rest = rest - addition
    return np.array(given)


def bell_draw(key, extent, scale, bound, shards=(), kind=jnp.bfloat16):
    drawn = scale * jax.random.normal(key, extent, jnp.float32)
    if shards:
        drawn = drawn * shard_levels(key, extent, shards, -0.22, 0.18)
    return jnp.clip(drawn, -bound, bound).astype(kind)


def setup_inputs(seed: int = 0) -> dict:
    key_list = jax.random.split(jax.random.key(seed), 13)
    layer_input = bell_draw(key_list[0], (TOKENS, D), 1.0, 6.0, ((0, 32),))
    output_grad = bell_draw(key_list[1], (TOKENS, D), 1.0, 6.0, ((0, 32),))
    w_query = bell_draw(key_list[2], (D, D), D ** -0.5, 0.125, ((0, 32),))
    w_key = bell_draw(key_list[3], (D, D), D ** -0.5, 0.125, ((0, 32),))
    w_value = bell_draw(key_list[4], (D, D), D ** -0.5, 0.125, ((0, 32),))
    w_output = bell_draw(key_list[5], (D, D), (max(D // 64, 1)) ** -0.5, 1.0, ((0, 32),))
    w_router = bell_draw(key_list[6], (D, EXPERTS), (4 * D) ** -0.5, 0.0625, ((0, 32),))
    norm_gains = jnp.clip(1.0 + 0.1 * jax.random.normal(key_list[7], (4, D), jnp.float32), 0.5, 1.5).astype(jnp.bfloat16)
    w_gate = bell_draw(key_list[8], (EXPERTS, D, FF), D ** -0.5, 0.125, ((0, 8), (1, 4)))
    w_up = bell_draw(key_list[9], (EXPERTS, D, FF), D ** -0.5, 0.125, ((0, 8), (1, 4)))
    w_down = bell_draw(key_list[10], (EXPERTS, FF, D), (max(FF // 256, 1)) ** -0.5, 3.0, ((0, 8), (1, 4)))
    expert_routes_keys = jax.random.split(jax.random.fold_in(key_list[11], 1), TOKENS // TOK_DEV)
    expert_routes_turns = jax.random.permutation(jax.random.fold_in(key_list[11], 3), TOKENS // TOK_DEV)
    expert_routes = jax.vmap(lambda own, number: deal_out(jax.random.fold_in(key_list[11], 2), own, number, TOK_DEV, EXPERTS, TOP, CAP, 1))(expert_routes_keys, expert_routes_turns).reshape((TOKENS, TOP))
    return dict(layer_input=layer_input, output_grad=output_grad, w_query=w_query, w_key=w_key, w_value=w_value, w_output=w_output, w_router=w_router, norm_gains=norm_gains, w_gate=w_gate, w_up=w_up, w_down=w_down, expert_routes=expert_routes)


EPSILON = 1e-05
ROPE_BASE = 10000.0
MASKED = -1000000000.0

@jax.custom_vjp
def low(v):
    return lax.optimization_barrier(v.astype(jnp.bfloat16)).astype(jnp.float32)

@jax.custom_vjp
def low_back(v):
    return v

def low_keep(v):
    return (low(v), None)

def low_pass(kept, grad):
    return (grad,)

def back_keep(v):
    return (v, None)

def back_low(kept, grad):
    return (low(grad),)
low.defvjp(low_keep, low_pass)
low_back.defvjp(back_keep, back_low)

def matmul_high(left, right):
    return jnp.dot(left, right, precision=lax.Precision.HIGHEST, preferred_element_type=jnp.float32)

def rms_norm(values_in, gain_row):
    inverse = lax.rsqrt(lax.optimization_barrier(jnp.mean(values_in * values_in, axis=-1, keepdims=True)) + EPSILON)
    return values_in * inverse * gain_row

def angles(positions):
    freqs = ROPE_BASE ** (-2.0 * jnp.arange(HEAD_DIM // 2, dtype=jnp.float32) / HEAD_DIM)
    turned = positions.astype(jnp.float32)[:, None] * freqs[None, :]
    return (jnp.cos(turned)[:, None, :], jnp.sin(turned)[:, None, :])

def rotate(values_in, cosine_table, sine_table):
    row_count = values_in.shape[0]
    pieces = values_in.reshape(row_count, HEADS, HEAD_DIM)
    front = pieces[:, :, :HEAD_DIM // 2]
    behind = pieces[:, :, HEAD_DIM // 2:]
    joined = jnp.concatenate([front * cosine_table - behind * sine_table, behind * cosine_table + front * sine_table], axis=-1)
    return joined.reshape(row_count, HEADS * HEAD_DIM)

def attend(pieces):
    queries, keys, values = pieces
    q_heads = queries.reshape(SEQ, HEADS, HEAD_DIM)
    k_heads = keys.reshape(SEQ, HEADS, HEAD_DIM)
    v_heads = values.reshape(SEQ, HEADS, HEAD_DIM)
    scores = jnp.einsum('qhd,khd->hqk', q_heads, k_heads, precision=lax.Precision.HIGHEST) * HEAD_DIM ** (-0.5)
    scores = low_back(scores)
    blocks = jnp.arange(SEQ, dtype=jnp.int32) // BLK
    allowed = blocks[None, :] <= blocks[:, None]
    scores = jnp.where(allowed[None, :, :], scores, MASKED)
    row_max = lax.optimization_barrier(jnp.max(scores, axis=-1, keepdims=True))
    exp_rows = jnp.exp(scores - row_max)
    weights = low(exp_rows / lax.optimization_barrier(jnp.sum(exp_rows, axis=-1, keepdims=True)))
    mixed = jnp.einsum('hqk,khd->qhd', weights, v_heads, precision=lax.Precision.HIGHEST)
    return mixed.reshape(SEQ, D)

def reference(layer_input, output_grad, w_query, w_key, w_value, w_output, w_router, norm_gains, w_gate, w_up, w_down, expert_routes):
    flat_routes = expert_routes.reshape(DEVICES, TOK_DEV * TOP)
    onehot = (flat_routes[:, :, None] == jnp.arange(EXPERTS, dtype=jnp.int32)[None, None, :]).astype(jnp.int32)
    slot_index = lax.optimization_barrier(jnp.sum((jnp.cumsum(onehot, axis=1) - onehot) * onehot, axis=2))
    device_ids = jnp.broadcast_to(jnp.arange(DEVICES, dtype=jnp.int32)[:, None], flat_routes.shape)
    pair_ids = jnp.arange(TOKENS * TOP, dtype=jnp.int32).reshape(DEVICES, TOK_DEV * TOP)
    row_table = jnp.full((EXPERTS, DEVICES, CAP), TOKENS, jnp.int32).at[flat_routes, device_ids, slot_index].set(pair_ids // TOP)
    pair_table = jnp.full((EXPERTS, DEVICES, CAP), TOKENS * TOP, jnp.int32).at[flat_routes, device_ids, slot_index].set(pair_ids)
    row_table = row_table.reshape(EXPERTS, DEVICES * CAP)
    pair_table = pair_table.reshape(EXPERTS, DEVICES * CAP)
    cosine_table, sine_table = angles(jnp.arange(TOKENS, dtype=jnp.int32) % SEQ)

    def forward(inputs, query_w, key_w, value_w, output_w, router_w, gains, gate_all, up_all, down_all):
        first_in = low(rms_norm(inputs, gains[0]))
        q_raw = low_back(matmul_high(first_in, query_w))
        k_raw = low_back(matmul_high(first_in, key_w))
        v_raw = low_back(matmul_high(first_in, value_w))
        queries = low(rotate(rms_norm(q_raw, gains[2]), cosine_table, sine_table))
        keys = low(rotate(rms_norm(k_raw, gains[3]), cosine_table, sine_table))
        values = low(v_raw)
        count = TOKENS // SEQ
        attended = lax.map(jax.checkpoint(attend), (queries.reshape(count, SEQ, D), keys.reshape(count, SEQ, D), values.reshape(count, SEQ, D)))
        attended = low(low_back(attended.reshape(TOKENS, D)))
        mid = inputs + low_back(matmul_high(attended, output_w))
        second_in = low(rms_norm(mid, gains[1]))
        logits = matmul_high(second_in, router_w)
        exp_logits = jnp.exp(logits - lax.optimization_barrier(jnp.max(logits, axis=1, keepdims=True)))
        router_probs = exp_logits / lax.optimization_barrier(jnp.sum(exp_logits, axis=1, keepdims=True))
        gates = jnp.take_along_axis(router_probs, expert_routes, axis=1)
        gate_pad = jnp.concatenate([gates.reshape(TOKENS * TOP), jnp.zeros((1,), jnp.float32)])
        second_pad = jnp.concatenate([second_in, jnp.zeros((1, D), jnp.float32)], axis=0)

        def one_expert(pieces):
            gate_w, up_w, down_w, row_ids, pair_rows = pieces
            rows_in = low_back(second_pad[row_ids])
            gate_pre = low_back(matmul_high(rows_in, gate_w))
            up_pre = low_back(matmul_high(rows_in, up_w))
            hidden = low(jax.nn.silu(gate_pre) * up_pre)
            result = low(low_back(matmul_high(hidden, down_w)))
            return result * gate_pad[pair_rows][:, None]
        outputs = lax.map(jax.checkpoint(one_expert), (gate_all, up_all, down_all, row_table, pair_table))
        summed = jnp.zeros((TOKENS + 1, D), jnp.float32).at[row_table.reshape(-1)].add(outputs.reshape(EXPERTS * DEVICES * CAP, D))
        return mid + summed[:TOKENS]
    result, pullback = jax.vjp(forward, layer_input.astype(jnp.float32), w_query.astype(jnp.float32), w_key.astype(jnp.float32), w_value.astype(jnp.float32), w_output.astype(jnp.float32), w_router.astype(jnp.float32), norm_gains.astype(jnp.float32), w_gate.astype(jnp.float32), w_up.astype(jnp.float32), w_down.astype(jnp.float32))
    grads = pullback(output_grad.astype(jnp.float32))
    return (result.astype(jnp.bfloat16), grads[0], grads[1], grads[2], grads[3], grads[4], grads[5], grads[6], grads[7], grads[8], grads[9])
```

```python
import functools

import jax
import jax.numpy as jnp
from jax import lax
from jax.experimental import pallas as pl
from jax.experimental.pallas import tpu as pltpu
from jax.sharding import PartitionSpec as P

D = 2048
HEADS = 16
HEAD_DIM = 128
TOP = 8
EXP_DEV = 2
BLK = 256
TOK_DEV = 256
EPSILON = 1e-05
ROPE_BASE = 10000.0
MASKED = -1000000000.0
SCALE = HEAD_DIM ** (-0.5)
MESH = pl.DeviceIdType.MESH
ANY = pl.BlockSpec(memory_space=pl.ANY)
VMEM = pl.BlockSpec(memory_space=pltpu.VMEM)
VLIM = 56 * 1024 * 1024
F32 = jnp.float32
BF16 = jnp.bfloat16


def remote(src, dst, send_sem, recv_sem, device):
    return pltpu.make_async_remote_copy(
        src_ref=src,
        dst_ref=dst,
        send_sem=send_sem,
        recv_sem=recv_sem,
        device_id=device,
        device_id_type=MESH,
    )


def landed(ref, sem):
    pltpu.make_async_copy(ref, ref, sem).wait()


def signal(sem, device):
    pl.semaphore_signal(sem, inc=1, device_id=device, device_id_type=MESH)


def greet_line(barrier, lines, f, s):
    place, core = f // 2, f % 2
    signal(barrier, (f + 1 - 2 * core, s))

    @pl.when(place > 0)
    def _():
        signal(barrier, (f - 2, s))

    @pl.when(place < lines - 1)
    def _():
        signal(barrier, (f + 2, s))

    return 1 + jnp.where(place > 0, 1, 0) + jnp.where(place < lines - 1, 1, 0)


class LineGather:
    def __init__(self, views, lines, f, s, send, recv):
        self.views, self.lines, self.f, self.s = views, lines, f, s
        self.send, self.recv = send, recv
        self.place, self.core = f // 2, f % 2

    def copy(self, v, block, slot, way):
        device = {
            "right": (self.f + 2, self.s),
            "left": (self.f - 2, self.s),
            "partner": (self.f + 1 - 2 * self.core, self.s),
        }[way]
        index = {"right": 0, "left": 1, "partner": 2}[way]
        ref = self.views[v](block)
        return remote(ref, ref, self.send.at[v, slot, index], self.recv.at[v, block], device)

    def each(self, v, action):
        pass

    def start_own(self, v):
        self.copy(v, self.f, 0, "partner").start()

        @pl.when(self.place < self.lines - 1)
        def _():
            self.copy(v, self.f, 0, "right").start()

        @pl.when(self.place > 0)
        def _():
            self.copy(v, self.f, 0, "left").start()

    def forward(self, v, k):
        place, lines = self.place, self.lines

        @pl.when(place >= k)
        def _():
            block = self.f - 2 * k
            landed(self.views[v](block), self.recv.at[v, block])

            @pl.when(place < lines - 1)
            def _():
                self.copy(v, block, k, "right").start()

            self.copy(v, block, k, "partner").start()

        @pl.when(place + k < lines)
        def _():
            block = self.f + 2 * k
            landed(self.views[v](block), self.recv.at[v, block])

            @pl.when(place > 0)
            def _():
                self.copy(v, block, lines - 1 + k, "left").start()

            self.copy(v, block, lines - 1 + k, "partner").start()

    def finish(self, v):
        place, lines = self.place, self.lines
        for line in range(lines):
            block = 2 * line + 1 - self.core
            landed(self.views[v](block), self.recv.at[v, block])
        self.copy(v, self.f, 0, "partner").wait_send()

        @pl.when(place < lines - 1)
        def _():
            self.copy(v, self.f, 0, "right").wait_send()

        @pl.when(place > 0)
        def _():
            self.copy(v, self.f, 0, "left").wait_send()

        for k in range(1, lines):

            @pl.when(place >= k)
            def _():
                block = self.f - 2 * k

                @pl.when(place < lines - 1)
                def _():
                    self.copy(v, block, k, "right").wait_send()

                self.copy(v, block, k, "partner").wait_send()

            @pl.when(place + k < lines)
            def _():
                block = self.f + 2 * k

                @pl.when(place > 0)
                def _():
                    self.copy(v, block, lines - 1 + k, "left").wait_send()

                self.copy(v, block, lines - 1 + k, "partner").wait_send()


def line_sems(arrays, fsdp):
    lines = fsdp // 2
    return [
        pltpu.SemaphoreType.DMA((arrays, 2 * lines, 3)),
        pltpu.SemaphoreType.DMA((arrays, fsdp)),
    ]


def start_kernel(
    fsdp, sp, x_ref, w_ref, wo_ref, misc_ref, routes_ref,
    x_all, w_all, wo_all, misc_all, routes_all,
    send, recv, xsend, xrecv, psend, precv, wsend, wrecv, msend, mrecv, rsend, rrecv, local,
):
    f, s = lax.axis_index("fsdp"), lax.axis_index("sp")
    count, lines = fsdp * sp, fsdp // 2
    me = f * sp + s
    rows = w_ref.shape[1]
    cols = D // sp
    half = TOK_DEV // 2
    barrier = pltpu.get_barrier_semaphore()

    def greet(i, carry):
        other = lax.rem(me + i, count)
        signal(barrier, (other // sp, lax.rem(other, sp)))
        return carry

    lax.fori_loop(1, count, greet, 0)
    pl.semaphore_wait(barrier, count - 1)

    def w_block(i, s_to):
        return w_ref.at[:, :, pl.ds(pl.multiple_of(s_to * cols, cols), cols)]

    def w_rows(i):
        return w_all.at[:, pl.ds(pl.multiple_of(i * rows, rows), rows), :]

    def w_view(b):
        size = rows * sp
        return w_all.at[:, pl.ds(pl.multiple_of(b * size, size), size), :]

    def wo_view(b):
        return wo_all.at[pl.ds(pl.multiple_of(b * rows, rows), rows), :]

    def x_rows(place, first, size):
        return x_all.at[pl.ds(pl.multiple_of(place * TOK_DEV + first, half), size), :]

    w_own = pltpu.make_async_copy(w_block(me, s), w_rows(me), local.at[0])
    w_own.start()
    w_copies = []
    for k in range(1, sp):
        s_to = s ^ k
        copy = remote(w_block(me, s_to), w_rows(me), psend.at[k], precv.at[k], (f, s_to))
        copy.start()
        w_copies.append(copy)
    target_s, target_f = me // fsdp, lax.rem(me, fsdp)
    stays = jnp.logical_and(target_s == s, target_f == f)
    wo_copy = remote(wo_ref, wo_view(target_f), wsend, wrecv, (target_f, target_s))
    wo_own = pltpu.make_async_copy(wo_ref, wo_view(f), wrecv)

    @pl.when(stays)
    def _():
        wo_own.start()

    @pl.when(jnp.logical_not(stays))
    def _():
        wo_copy.start()

    x_own = pltpu.make_async_copy(x_ref, x_rows(s, 0, TOK_DEV), local.at[1])
    x_own.start()
    x_near = []
    for k in (1, 2):
        copy = remote(x_ref, x_rows(s, 0, TOK_DEV), xsend.at[k - 1], xrecv.at[k - 1], (f, s ^ k))
        copy.start()
        x_near.append(copy)
    misc_own = pltpu.make_async_copy(misc_ref, misc_all.at[me], local.at[2])
    misc_own.start()

    def misc_copy(i):
        other = lax.rem(me + i, count)
        return remote(
            misc_ref, misc_all.at[me], msend.at[i], mrecv.at[me], (other // sp, lax.rem(other, sp))
        )

    def misc_go(i, carry):
        misc_copy(i).start()
        return carry

    lax.fori_loop(1, count, misc_go, 0)

    routes_own = pltpu.make_async_copy(routes_ref, routes_all.at[f], local.at[3])
    routes_own.start()

    def routes_copy(i):
        other = lax.rem(f + i, fsdp)
        return remote(routes_ref, routes_all.at[f], rsend.at[i], rrecv.at[f], (other, s))

    def routes_go(i, carry):
        routes_copy(i).start()
        return carry

    lax.fori_loop(1, fsdp, routes_go, 0)

    w_own.wait()
    for k in range(1, sp):
        landed(w_rows(f * sp + (s ^ k)), precv.at[k])
    line = LineGather([w_view, wo_view], lines, f, s, send, recv)
    line.start_own(0)
    landed(wo_view(f), wrecv)
    line.start_own(1)

    landed(x_rows(s ^ 1, 0, TOK_DEV), xrecv.at[0])
    x_on_a = remote(
        x_rows(s ^ 1, 0, half), x_rows(s ^ 1, 0, half), xsend.at[2], xrecv.at[2], (f, s ^ 2)
    )
    x_on_a.start()
    landed(x_rows(s ^ 2, 0, TOK_DEV), xrecv.at[1])
    x_on_b = remote(
        x_rows(s ^ 2, half, half), x_rows(s ^ 2, half, half), xsend.at[3], xrecv.at[3], (f, s ^ 1)
    )
    x_on_b.start()

    for k in range(1, lines):
        line.forward(0, k)
        line.forward(1, k)
    line.finish(0)
    line.finish(1)
    landed(x_rows(s ^ 3, 0, half), xrecv.at[2])
    landed(x_rows(s ^ 3, half, half), xrecv.at[3])

    def misc_end(i, carry):
        misc_copy(i).wait_send()
        other = lax.rem(me + i, count)
        landed(misc_all.at[other], mrecv.at[other])
        return carry

    lax.fori_loop(1, count, misc_end, 0)

    def routes_end(i, carry):
        routes_copy(i).wait_send()
        other = lax.rem(f + i, fsdp)
        landed(routes_all.at[other], rrecv.at[other])
        return carry

    lax.fori_loop(1, fsdp, routes_end, 0)
    for copy in w_copies + x_near + [x_on_a, x_on_b]:
        copy.wait_send()

    @pl.when(jnp.logical_not(stays))
    def _():
        wo_copy.wait_send()

    x_own.wait()
    misc_own.wait()
    routes_own.wait()


def gather_start(fsdp, sp, x, w, wo, misc, routes):
    count = fsdp * sp
    dma = pltpu.SemaphoreType.DMA
    return pl.pallas_call(
        functools.partial(start_kernel, fsdp, sp),
        out_shape=(
            jax.ShapeDtypeStruct((sp * TOK_DEV, D), BF16),
            jax.ShapeDtypeStruct((3, D, D // sp), BF16),
            jax.ShapeDtypeStruct((D // sp, D), BF16),
            jax.ShapeDtypeStruct((count,) + misc.shape, BF16),
            jax.ShapeDtypeStruct((fsdp,) + routes.shape, jnp.int32),
        ),
        in_specs=[ANY] * 5,
        out_specs=[ANY] * 5,
        scratch_shapes=line_sems(2, fsdp)
        + [
            dma((4,)), dma((4,)), dma((sp,)), dma((sp,)), dma, dma,
            dma((count,)), dma((count,)), dma((fsdp,)), dma((fsdp,)), dma((4,)),
        ],
        compiler_params=pltpu.CompilerParams(collective_id=0, has_side_effects=True),
        name="gather_start",
    )(x, w, wo, misc, routes)


def line_gather_kernel(fsdp, parts, x_ref, out_ref, send, recv, local):
    f, s = lax.axis_index("fsdp"), lax.axis_index("sp")
    lines = fsdp // 2
    rows = x_ref.shape[0]
    size = rows // parts
    barrier = pltpu.get_barrier_semaphore()
    expected = greet_line(barrier, lines, f, s)
    own = pltpu.make_async_copy(x_ref, out_ref.at[pl.ds(pl.multiple_of(f * rows, rows), rows)], local)
    own.start()
    pl.semaphore_wait(barrier, expected)
    own.wait()

    def view(part):
        return lambda b: out_ref.at[pl.ds(pl.multiple_of(b * rows + part * size, size), size)]

    line = LineGather([view(p) for p in range(parts)], lines, f, s, send, recv)
    for p in range(parts):
        line.start_own(p)
    for k in range(1, lines):
        for p in range(parts):
            line.forward(p, k)
    for p in range(parts):
        line.finish(p)


def line_gather(fsdp, x, number, name):
    parts = 2
    return pl.pallas_call(
        functools.partial(line_gather_kernel, fsdp, parts),
        out_shape=jax.ShapeDtypeStruct((fsdp * x.shape[0], x.shape[1]), x.dtype),
        in_specs=[ANY],
        out_specs=ANY,
        scratch_shapes=line_sems(parts, fsdp) + [pltpu.SemaphoreType.DMA],
        compiler_params=pltpu.CompilerParams(collective_id=number, has_side_effects=True),
        name=name,
    )(x)


def add_rows(dst, a, b, rows):
    def step(i, carry):
        at = pl.ds(pl.multiple_of(i * 32, 32), 32)
        dst[at, :] = (a[at, :].astype(F32) + b[at, :].astype(F32)).astype(dst.dtype)
        return carry

    lax.fori_loop(0, rows // 32, step, 0)


def line_reduce_kernel(
    fsdp, p_ref, out_ref, own, paired, from_left, from_right, psend, precv, send, lrecv, rrecv, local
):
    f, s = lax.axis_index("fsdp"), lax.axis_index("sp")
    lines = fsdp // 2
    place, core = f // 2, f % 2
    rows = out_ref.shape[0]
    barrier = pltpu.get_barrier_semaphore()
    expected = greet_line(barrier, lines, f, s)
    order_right = [(n, lines - 1 - n) for n in range(lines)]

    def load(i):
        return pltpu.make_async_copy(p_ref.at[2 * i + core], own.at[i], local.at[i])

    def swap(i):
        return remote(
            p_ref.at[2 * i + 1 - core], paired.at[i], psend.at[i], precv.at[i], (f + 1 - 2 * core, s)
        )

    for n in range(lines):
        load(n).start()
    pl.semaphore_wait(barrier, expected)
    for n in range(lines):
        swap(lines - 1 - n if n % 2 == 0 else n // 2 if False else lines - 1 - n).start()
    for n in range(lines):
        i = lines - 1 - n
        load(i).wait()
        landed(paired.at[i], precv.at[i])
        add_rows(own.at[i], own.at[i], paired.at[i], rows)

    def right(d):
        return remote(own.at[d], from_left.at[d], send.at[d], lrecv.at[d], (f + 2, s))

    def left(d):
        return remote(own.at[d], from_right.at[d], send.at[d], rrecv.at[d], (f - 2, s))

    for n in range(lines - 1):
        d_right = lines - 1 - n

        @pl.when(place < d_right)
        def _():
            @pl.when(place > 0)
            def _():
                landed(from_left.at[d_right], lrecv.at[d_right])
                add_rows(own.at[d_right], own.at[d_right], from_left.at[d_right], rows)

            right(d_right).start()

        d_left = n

        @pl.when(place > d_left)
        def _():
            @pl.when(place < lines - 1)
            def _():
                landed(from_right.at[d_left], rrecv.at[d_left])
                add_rows(own.at[d_left], own.at[d_left], from_right.at[d_left], rows)

            left(d_left).start()

    add_rows(out_ref, own.at[place], own.at[place], rows) if False else None

    def first(i, carry):
        at = pl.ds(pl.multiple_of(i * 32, 32), 32)
        out_ref[at, :] = own[place, at, :].astype(F32)
        return carry

    lax.fori_loop(0, rows // 32, first, 0)

    @pl.when(place > 0)
    def _():
        landed(from_left.at[place], lrecv.at[place])
        add_rows(out_ref, out_ref, from_left.at[place], rows)

    @pl.when(place < lines - 1)
    def _():
        landed(from_right.at[place], rrecv.at[place])
        add_rows(out_ref, out_ref, from_right.at[place], rows)

    for i in range(lines):
        swap(i).wait_send()

        @pl.when(place < i)
        def _():
            right(i).wait_send()

        @pl.when(place > i)
        def _():
            left(i).wait_send()


def line_reduce(fsdp, partial, number, name):
    lines = fsdp // 2
    block = partial.shape[1:]
    dma = pltpu.SemaphoreType.DMA
    return pl.pallas_call(
        functools.partial(line_reduce_kernel, fsdp),
        out_shape=jax.ShapeDtypeStruct(block, F32),
        in_specs=[ANY],
        out_specs=VMEM,
        scratch_shapes=[pltpu.VMEM((lines,) + block, BF16) for _ in range(4)]
        + [dma((lines,)) for _ in range(6)],
        compiler_params=pltpu.CompilerParams(
            collective_id=number, has_side_effects=True, vmem_limit_bytes=VLIM
        ),
        name=name,
    )(partial)


def greet_plane(f, s):
    barrier = pltpu.get_barrier_semaphore()
    for k in (1, 2):
        signal(barrier, (f, s ^ k))
    pl.semaphore_wait(barrier, 2)


def plane_gather_kernel(x_ref, out_ref, send, recv, local):
    f, s = lax.axis_index("fsdp"), lax.axis_index("sp")
    rows = x_ref.shape[0]
    half = rows // 2

    def at(place, first, size):
        return out_ref.at[pl.ds(pl.multiple_of(place * rows + first, half), size), :]

    own = pltpu.make_async_copy(x_ref, at(s, 0, rows), local)
    own.start()
    greet_plane(f, s)
    near = [
        remote(x_ref, at(s, 0, rows), send.at[k - 1], recv.at[k - 1], (f, s ^ k)) for k in (1, 2)
    ]
    for copy in near:
        copy.start()
    landed(at(s ^ 1, 0, rows), recv.at[0])
    on_a = remote(at(s ^ 1, 0, half), at(s ^ 1, 0, half), send.at[2], recv.at[2], (f, s ^ 2))
    on_a.start()
    landed(at(s ^ 2, 0, rows), recv.at[1])
    on_b = remote(at(s ^ 2, half, half), at(s ^ 2, half, half), send.at[3], recv.at[3], (f, s ^ 1))
    on_b.start()
    landed(at(s ^ 3, 0, half), recv.at[2])
    landed(at(s ^ 3, half, half), recv.at[3])
    own.wait()
    for copy in near + [on_a, on_b]:
        copy.wait_send()


def plane_gather(sp, x, number, name):
    dma = pltpu.SemaphoreType.DMA
    return pl.pallas_call(
        plane_gather_kernel,
        out_shape=jax.ShapeDtypeStruct((sp * x.shape[0], x.shape[1]), x.dtype),
        in_specs=[ANY],
        out_specs=ANY,
        scratch_shapes=[dma((4,)), dma((4,)), dma],
        compiler_params=pltpu.CompilerParams(collective_id=number, has_side_effects=True),
        name=name,
    )(x)


def plane_reduce_kernel(p_ref, out_ref, own, got, got_on, send, recv, local):
    f, s = lax.axis_index("fsdp"), lax.axis_index("sp")
    rows = out_ref.shape[0]
    half = rows // 2

    def part(ref, h):
        return ref.at[pl.ds(h * half, half), :]

    loads = []
    for n, d in enumerate((s, s ^ 2, s ^ 1)):
        load = pltpu.make_async_copy(p_ref.at[d], own.at[n], local.at[n])
        load.start()
        loads.append(load)
    greet_plane(f, s)
    hops = []
    for h, k in ((0, 1), (1, 2)):
        far = remote(
            part(p_ref.at[s ^ 3], h), part(got.at[1], h), send.at[h, 0], recv.at[h, 0], (f, s ^ k)
        )
        far.start()
        hops.append(far)
    for h, k in ((0, 1), (1, 2)):
        near = remote(
            part(p_ref.at[s ^ k], h), part(got.at[0], h), send.at[h, 1], recv.at[h, 1], (f, s ^ k)
        )
        near.start()
        hops.append(near)
    for load in loads:
        load.wait()
    for h, k, n in ((0, 1, 1), (1, 2, 2)):
        landed(part(got.at[1], h), recv.at[h, 0])
        add_rows(part(own.at[n], h), part(own.at[n], h), part(got.at[1], h), half)
        on = remote(
            part(own.at[n], h), part(got_on, h), send.at[h, 2], recv.at[h, 2], (f, s ^ (3 - k))
        )
        on.start()
        hops.append(on)
    for h in (0, 1):
        landed(part(got.at[0], h), recv.at[h, 1])
        add_rows(part(out_ref, h), part(own.at[0], h), part(got.at[0], h), half)
    for h in (0, 1):
        landed(part(got_on, h), recv.at[h, 2])
        add_rows(part(out_ref, h), part(out_ref, h), part(got_on, h), half)
    for copy in hops:
        copy.wait_send()


def plane_reduce(sp, partial, number, name):
    block = partial.shape[1:]
    dma = pltpu.SemaphoreType.DMA
    return pl.pallas_call(
        plane_reduce_kernel,
        out_shape=jax.ShapeDtypeStruct(block, F32),
        in_specs=[ANY],
        out_specs=VMEM,
        scratch_shapes=[
            pltpu.VMEM((3,) + block, BF16),
            pltpu.VMEM((2,) + block, BF16),
            pltpu.VMEM(block, BF16),
            dma((2, 3)),
            dma((2, 3)),
            dma((3,)),
        ],
        compiler_params=pltpu.CompilerParams(
            collective_id=number, has_side_effects=True, vmem_limit_bytes=VLIM
        ),
        name=name,
    )(partial)


def plane_sum_kernel(x_ref, out_ref, got, send, recv):
    f, s = lax.axis_index("fsdp"), lax.axis_index("sp")
    barrier = pltpu.get_barrier_semaphore()
    for k in (1, 2, 3):
        signal(barrier, (f, s ^ k))
    pl.semaphore_wait(barrier, 3)
    copies = []
    for k in (1, 2, 3):
        copy = remote(x_ref, got.at[k - 1], send.at[k - 1], recv.at[k - 1], (f, s ^ k))
        copy.start()
        copies.append(copy)
    for copy in copies:
        copy.wait()
    near = x_ref[...] + got[0]
    far = got[1] + got[2]
    out_ref[...] = near + far


def plane_sum(x, number, name):
    dma = pltpu.SemaphoreType.DMA
    return pl.pallas_call(
        plane_sum_kernel,
        out_shape=jax.ShapeDtypeStruct(x.shape, F32),
        in_specs=[VMEM],
        out_specs=VMEM,
        scratch_shapes=[pltpu.VMEM((3,) + x.shape, F32), dma((3,)), dma((3,))],
        compiler_params=pltpu.CompilerParams(collective_id=number, has_side_effects=True),
        name=name,
    )(x)


def end_kernel(
    fsdp, sp, q_ref, o_ref, m_ref, q_out, o_out, m_out,
    qsend, qrecv, osend, orecv, msend, mrecv, local,
):
    f, s = lax.axis_index("fsdp"), lax.axis_index("sp")
    count = fsdp * sp
    me = f * sp + s
    rows = o_ref.shape[0]
    barrier = pltpu.get_barrier_semaphore()

    def greet(i, carry):
        other = lax.rem(me + i, count)
        signal(barrier, (other // sp, lax.rem(other, sp)))
        return carry

    lax.fori_loop(1, count, greet, 0)
    pl.semaphore_wait(barrier, count - 1)

    def q_from(place):
        return q_ref.at[:, pl.ds(pl.multiple_of(place * rows, rows), rows), :]

    q_own = pltpu.make_async_copy(q_from(s), q_out.at[s], local.at[0])
    q_own.start()
    copies = []
    for k in range(1, sp):
        copy = remote(q_from(s ^ k), q_out.at[s], qsend.at[k], qrecv.at[k], (f, s ^ k))
        copy.start()
        copies.append(copy)
    flat = s * fsdp + f
    target_f, target_s = flat // sp, lax.rem(flat, sp)
    stays = jnp.logical_and(target_s == s, target_f == f)
    o_copy = remote(o_ref, o_out, osend, orecv, (target_f, target_s))
    o_own = pltpu.make_async_copy(o_ref, o_out, orecv)

    @pl.when(stays)
    def _():
        o_own.start()

    @pl.when(jnp.logical_not(stays))
    def _():
        o_copy.start()

    m_own = pltpu.make_async_copy(m_ref.at[me], m_out.at[me], local.at[1])
    m_own.start()

    def m_copy(i):
        other = lax.rem(me + i, count)
        return remote(
            m_ref.at[other], m_out.at[me], msend.at[i], mrecv.at[me], (other // sp, lax.rem(other, sp))
        )

    def m_go(i, carry):
        m_copy(i).start()
        return carry

    lax.fori_loop(1, count, m_go, 0)

    def m_end(i, carry):
        m_copy(i).wait_send()
        other = lax.rem(me + i, count)
        landed(m_out.at[other], mrecv.at[other])
        return carry

    lax.fori_loop(1, count, m_end, 0)
    landed(o_out, orecv)

    @pl.when(jnp.logical_not(stays))
    def _():
        o_copy.wait_send()

    for k in range(1, sp):
        landed(q_out.at[s ^ k], qrecv.at[k])
    for copy in copies:
        copy.wait_send()
    q_own.wait()
    m_own.wait()


def exchange_end(fsdp, sp, q, o, m, number):
    count = fsdp * sp
    rows = o.shape[0]
    dma = pltpu.SemaphoreType.DMA
    return pl.pallas_call(
        functools.partial(end_kernel, fsdp, sp),
        out_shape=(
            jax.ShapeDtypeStruct((sp, 3, rows, D // sp), q.dtype),
            jax.ShapeDtypeStruct(o.shape, o.dtype),
            jax.ShapeDtypeStruct(m.shape, m.dtype),
        ),
        in_specs=[ANY] * 3,
        out_specs=[ANY] * 3,
        scratch_shapes=[
            dma((sp,)), dma((sp,)), dma, dma, dma((count,)), dma((count,)), dma((2,)),
        ],
        compiler_params=pltpu.CompilerParams(collective_id=number, has_side_effects=True),
        name="exchange_end",
    )(q, o, m)


def dot_nt(a, b):
    return lax.dot_general(a, b, (((1,), (1,)), ((), ())), preferred_element_type=F32)


def dot_tn(a, b):
    return lax.dot_general(a, b, (((0,), (0,)), ((), ())), preferred_element_type=F32)


def dot_nn(a, b):
    return jnp.dot(a, b, preferred_element_type=F32)


def attend_kernel(q_ref, k_ref, v_ref, o_ref, sum_ref):
    for i in range(q_ref.shape[0] // BLK):
        rows, seen = pl.ds(i * BLK, BLK), pl.ds(0, (i + 1) * BLK)
        scores = dot_nt(q_ref[rows, :], k_ref[seen, :]) * SCALE
        row_max = jnp.max(scores, axis=-1, keepdims=True)
        exp_rows = jnp.exp(scores - row_max)
        row_sum = jnp.sum(exp_rows, axis=-1, keepdims=True)
        probs = (exp_rows / row_sum).astype(BF16)
        o_ref[rows, :] = dot_nn(probs, v_ref[seen, :]).astype(BF16)
        sum_ref[0, rows, :] = row_max + jnp.log(row_sum)


def attend(q, k, v):
    seq, width = q.shape
    heads = width // HEAD_DIM
    spec = pl.BlockSpec((seq, HEAD_DIM), lambda h: (0, h))
    return pl.pallas_call(
        attend_kernel,
        grid=(heads,),
        out_shape=(
            jax.ShapeDtypeStruct((seq, width), BF16),
            jax.ShapeDtypeStruct((heads, seq, 1), F32),
        ),
        in_specs=[spec] * 3,
        out_specs=[spec, pl.BlockSpec((1, seq, 1), lambda h: (h, 0, 0))],
        compiler_params=pltpu.CompilerParams(vmem_limit_bytes=VLIM),
        cost_estimate=pl.CostEstimate(
            flops=4 * seq * seq * width * 5 // 8, bytes_accessed=12 * seq * width,
            transcendentals=heads * seq * seq * 5 // 8,
        ),
        name="attend",
    )(q, k, v)


def attend_back_kernel(q_ref, k_ref, v_ref, g_ref, sum_ref, dq_ref, dk_ref, dv_ref):
    dk_ref[...] = jnp.zeros_like(dk_ref)
    dv_ref[...] = jnp.zeros_like(dv_ref)
    for i in range(q_ref.shape[0] // BLK):
        rows, seen = pl.ds(i * BLK, BLK), pl.ds(0, (i + 1) * BLK)
        q, g, keys = q_ref[rows, :], g_ref[rows, :], k_ref[seen, :]
        scores = dot_nt(q, keys) * SCALE
        probs = jnp.exp(scores - sum_ref[0, rows, :])
        grad_probs = dot_nt(g, v_ref[seen, :])
        row_dot = jnp.sum(probs * grad_probs, axis=-1, keepdims=True)
        grad_scores = (probs * (grad_probs - row_dot)).astype(BF16)
        dq_ref[rows, :] = dot_nn(grad_scores, keys) * SCALE
        dk_ref[seen, :] += dot_tn(grad_scores, q) * SCALE
        dv_ref[seen, :] += dot_tn(probs.astype(BF16), g)


def attend_back(q, k, v, g, log_sum):
    seq, width = q.shape
    heads = width // HEAD_DIM
    spec = pl.BlockSpec((seq, HEAD_DIM), lambda h: (0, h))
    return pl.pallas_call(
        attend_back_kernel,
        grid=(heads,),
        out_shape=tuple(jax.ShapeDtypeStruct((seq, width), F32) for _ in range(3)),
        in_specs=[spec] * 4 + [pl.BlockSpec((1, seq, 1), lambda h: (h, 0, 0))],
        out_specs=[spec] * 3,
        compiler_params=pltpu.CompilerParams(vmem_limit_bytes=VLIM),
        cost_estimate=pl.CostEstimate(
            flops=10 * seq * seq * width * 5 // 8, bytes_accessed=20 * seq * width,
            transcendentals=heads * seq * seq * 5 // 8,
        ),
        name="attend_back",
    )(q, k, v, g, log_sum)


def rms_parts(values_in):
    inverse = lax.rsqrt(jnp.mean(values_in * values_in, axis=-1, keepdims=True) + EPSILON)
    return (values_in * inverse, inverse)


def rms_back(grad_out, normed, inverse, gain_row):
    scaled = grad_out * gain_row
    grad_in = inverse * (scaled - normed * jnp.mean(scaled * normed, axis=-1, keepdims=True))
    return (grad_in, jnp.sum(grad_out * normed, axis=0))


def angles(positions):
    freqs = ROPE_BASE ** (-2.0 * jnp.arange(HEAD_DIM // 2, dtype=F32) / HEAD_DIM)
    turned = positions.astype(F32)[:, None] * freqs[None, :]
    return (jnp.cos(turned)[:, None, :], jnp.sin(turned)[:, None, :])


def rotate(values_in, cosine_table, sine_table):
    row_count, width = values_in.shape
    pieces = values_in.reshape(row_count, width // HEAD_DIM, HEAD_DIM)
    front = pieces[:, :, : HEAD_DIM // 2]
    behind = pieces[:, :, HEAD_DIM // 2 :]
    joined = jnp.concatenate(
        [front * cosine_table - behind * sine_table, behind * cosine_table + front * sine_table],
        axis=-1,
    )
    return joined.reshape(row_count, width)


def two_row_sums(first, second, number, name):
    seq = first.shape[0]
    packed = jnp.concatenate([first, second], axis=0).reshape(2 * seq // 128, 128)
    total = plane_sum(packed, number, name).reshape(2, seq, 1)
    return total[0], total[1]


def spread(x, fsdp):
    f = lax.axis_index("fsdp")
    lines = fsdp // 2
    pieces = [x]
    for k in range(1, lines):
        pieces.append(lax.ppermute(x, "fsdp", [(i, i ^ (2 * k)) for i in range(fsdp)]))
    own = jnp.stack(pieces)
    other = lax.ppermute(own, "fsdp", [(i, i ^ 1) for i in range(fsdp)])
    place, core = f // 2, f % 2
    both = jnp.where(core == 0, jnp.stack([own, other], axis=1), jnp.stack([other, own], axis=1))
    order = jnp.arange(lines, dtype=jnp.int32) ^ place
    return both[order].reshape((fsdp * x.shape[0],) + x.shape[1:])


def gather_back(partial, fsdp):
    f = lax.axis_index("fsdp")
    lines = fsdp // 2
    place, core = f // 2, f % 2
    pairs = partial.reshape((lines, 2) + partial.shape[1:])
    keep = lax.dynamic_index_in_dim(pairs, core, axis=1, keepdims=False)
    give = lax.dynamic_index_in_dim(pairs, 1 - core, axis=1, keepdims=False)
    got = lax.ppermute(give, "fsdp", [(i, i ^ 1) for i in range(fsdp)])
    both = (keep.astype(F32) + got.astype(F32)).astype(BF16)
    total = lax.dynamic_index_in_dim(both, place, axis=0, keepdims=False).astype(F32)
    for k in range(1, lines):
        piece = lax.dynamic_index_in_dim(both, place ^ k, axis=0, keepdims=False)
        moved = lax.ppermute(piece, "fsdp", [(i, i ^ (2 * k)) for i in range(fsdp)])
        total = total + moved.astype(F32)
    return total


def body(
    layer_input, output_grad, w_query, w_key, w_value, w_output, w_router, norm_gains,
    w_gate, w_up, w_down, expert_routes,
):
    fsdp, sp = lax.axis_size("fsdp"), lax.axis_size("sp")
    f, s = lax.axis_index("fsdp"), lax.axis_index("sp")
    count = fsdp * sp
    experts = EXP_DEV * fsdp
    capacity = TOK_DEV * TOP // experts * 17 // 16
    slots = -(-capacity // 16) * 16
    seq = TOK_DEV * sp
    cols = D // sp
    rows = D // count
    tokens = fsdp * TOK_DEV

    expert_set = (
        lax.all_gather(w_gate, "sp", axis=1, tiled=True),
        lax.all_gather(w_up, "sp", axis=1, tiled=True),
        lax.all_gather(w_down, "sp", axis=1, tiled=True),
    )
    grad_tok = spread(output_grad, fsdp)

    router_size = rows * experts
    misc = jnp.concatenate([w_router.reshape(router_size), norm_gains.reshape(4 * rows)])
    misc_rows = -(-misc.shape[0] // 2048) * 16
    misc = jnp.pad(misc, (0, misc_rows * 128 - misc.shape[0])).reshape(misc_rows, 128)
    routes = expert_routes.reshape(TOK_DEV * TOP // 128, 128)
    x_all, w_all, wo_s, misc_all, routes_all = gather_start(
        fsdp, sp, layer_input, jnp.stack([w_query, w_key, w_value]), w_output, misc, routes
    )
    misc_all = misc_all.reshape(count, misc_rows * 128)
    router_w = misc_all[:, :router_size].reshape(D, experts)
    gains_w = misc_all[:, router_size : router_size + 4 * rows].reshape(count, 4, rows)
    gains32 = gains_w.transpose(1, 0, 2).reshape(4, D).astype(F32)
    gains_own = lax.dynamic_slice_in_dim(gains32, s * cols, cols, axis=1)
    routes_tok = routes_all.reshape(tokens, TOP)

    normed_a, _ = rms_parts(x_all.astype(F32))
    first_in = (normed_a * gains32[0]).astype(BF16)
    q_raw = dot_nn(first_in, w_all[0])
    k_raw = dot_nn(first_in, w_all[1])
    values = dot_nn(first_in, w_all[2]).astype(BF16)
    q_square, k_square = two_row_sums(
        jnp.sum(q_raw * q_raw, axis=-1, keepdims=True),
        jnp.sum(k_raw * k_raw, axis=-1, keepdims=True),
        1,
        "norm_sums",
    )
    q_inverse = lax.rsqrt(q_square / D + EPSILON)
    k_inverse = lax.rsqrt(k_square / D + EPSILON)
    q_normed, k_normed = q_raw * q_inverse, k_raw * k_inverse
    cosine_table, sine_table = angles(jnp.arange(seq, dtype=jnp.int32))
    queries = rotate(q_normed * gains_own[2], cosine_table, sine_table).astype(BF16)
    keys = rotate(k_normed * gains_own[3], cosine_table, sine_table).astype(BF16)
    attended, log_sum = attend(queries, keys, values)
    branch = dot_nn(attended, wo_s).astype(BF16).reshape(sp, TOK_DEV, D)
    inputs = layer_input.astype(F32)
    mid = inputs + plane_reduce(sp, branch, 2, "branch_sum")
    normed_m, inverse_m = rms_parts(mid)
    second_in = (normed_m * gains32[1]).astype(BF16)

    second_tok = line_gather(fsdp, second_in, 3, "token_gather")
    logits = dot_nn(second_tok, router_w)
    exp_logits = jnp.exp(logits - jnp.max(logits, axis=1, keepdims=True))
    router_probs = exp_logits / jnp.sum(exp_logits, axis=1, keepdims=True)
    own_ids = f * EXP_DEV + jnp.arange(EXP_DEV, dtype=jnp.int32)
    chosen = jnp.any(routes_tok[:, :, None] == own_ids[None, None, :], axis=1)
    columns = jnp.arange(experts, dtype=jnp.int32)[:, None] == own_ids[None, :]
    gate_tok = jnp.sum(
        jnp.where(columns[None, :, :], router_probs[:, :, None], 0.0), axis=1
    )
    chosen_block = chosen.reshape(fsdp, TOK_DEV, EXP_DEV)
    before = jnp.arange(TOK_DEV)[:, None] > jnp.arange(TOK_DEV)[None, :]
    place = jnp.einsum(
        "ut,fte->fue", before.astype(BF16), chosen_block.astype(BF16), preferred_element_type=F32
    ).astype(jnp.int32)
    slot_ids = jnp.arange(slots, dtype=jnp.int32)
    picks = (
        (place.transpose(0, 2, 1)[:, :, None, :] == slot_ids[None, None, :, None])
        & chosen_block.transpose(0, 2, 1)[:, :, None, :]
    )
    picks_low = picks.astype(BF16)
    gate_block = gate_tok.reshape(fsdp, TOK_DEV, EXP_DEV).transpose(0, 2, 1)
    slot_gates = jnp.sum(jnp.where(picks, gate_block[:, :, None, :], 0.0), axis=3)
    slot_gates = slot_gates.transpose(1, 0, 2).reshape(EXP_DEV, fsdp * slots, 1)
    total = fsdp * slots

    def take(rows_in):
        return (
            jnp.einsum(
                "fect,ftd->efcd", picks_low, rows_in.reshape(fsdp, TOK_DEV, D),
                preferred_element_type=F32,
            )
            .astype(BF16)
            .reshape(EXP_DEV, total, D)
        )

    received = take(second_tok)
    grad_rows_in = take(grad_tok)
    gate_full, up_full, down_full = expert_set
    gate_pre = jnp.einsum("erd,edf->erf", received, gate_full, preferred_element_type=F32)
    up_pre = jnp.einsum("erd,edf->erf", received, up_full, preferred_element_type=F32)
    sigmoid_g = jax.nn.sigmoid(gate_pre)
    silu_g = gate_pre * sigmoid_g
    hidden = (silu_g * up_pre).astype(BF16)
    grad_expert = (slot_gates * grad_rows_in.astype(F32)).astype(BF16)
    grad_hidden = jnp.einsum("erd,efd->erf", grad_expert, down_full, preferred_element_type=F32)
    grad_gate_pre = (grad_hidden * up_pre * sigmoid_g * (1.0 + gate_pre * (1.0 - sigmoid_g))).astype(
        BF16
    )
    grad_up_pre = (grad_hidden * silu_g).astype(BF16)

    def shed(grad):
        return lax.psum_scatter(grad.astype(BF16), "sp", scatter_dimension=1, tiled=True).astype(F32)

    grad_down = shed(jnp.einsum("erf,erd->efd", hidden, grad_expert, preferred_element_type=F32))
    grad_gate = shed(jnp.einsum("erd,erf->edf", received, grad_gate_pre, preferred_element_type=F32))
    grad_up = shed(jnp.einsum("erd,erf->edf", received, grad_up_pre, preferred_element_type=F32))

    expert_out = jnp.einsum("erf,efd->erd", hidden, down_full, preferred_element_type=F32).astype(BF16)
    slot_dots = jnp.sum(expert_out.astype(F32) * grad_rows_in.astype(F32), axis=2)
    slot_dots = slot_dots.reshape(EXP_DEV, fsdp, 1, slots).transpose(1, 0, 3, 2)
    gate_grads = jnp.sum(jnp.where(picks, slot_dots, 0.0), axis=2)
    gate_grads = gate_grads.transpose(0, 2, 1).reshape(tokens, EXP_DEV)
    choice_grad = jnp.sum(jnp.where(columns[None, :, :], gate_grads[:, None, :], 0.0), axis=2)
    grad_logits = router_probs * (
        choice_grad - jnp.sum(router_probs * choice_grad, axis=1, keepdims=True)
    )
    logits_high = grad_logits.astype(BF16)
    logits_low = (grad_logits - logits_high.astype(F32)).astype(BF16)
    logits_two = jnp.concatenate([logits_high, logits_low], axis=1)
    router_two = jnp.einsum("td,te->de", second_tok, logits_two, preferred_element_type=F32)
    grad_router = router_two[:, :experts] + router_two[:, experts:]

    grad_rows = jnp.einsum("erf,edf->erd", grad_gate_pre, gate_full, preferred_element_type=F32)
    grad_rows = (
        grad_rows + jnp.einsum("erf,edf->erd", grad_up_pre, up_full, preferred_element_type=F32)
    ).astype(BF16)
    second_part = jnp.einsum(
        "fect,efcd->ftd", picks_low, grad_rows.reshape(EXP_DEV, fsdp, slots, D),
        preferred_element_type=F32,
    )
    second_part = second_part + jnp.einsum(
        "te,de->td", logits_two, jnp.concatenate([router_w, router_w], axis=1),
        preferred_element_type=F32,
    ).reshape(fsdp, TOK_DEV, D)
    grad_second = line_reduce(fsdp, second_part.astype(BF16), 4, "token_grads")

    out_part = jnp.zeros((fsdp, TOK_DEV, D), F32)
    for e in range(EXP_DEV):
        back = jnp.einsum(
            "fct,fcd->ftd", picks_low[:, e], expert_out[e].reshape(fsdp, slots, D),
            preferred_element_type=F32,
        )
        out_part = out_part + back * gate_block[:, e, :, None]
    layer_out = (mid + gather_back(out_part.astype(BF16), fsdp)).astype(BF16)

    grad_final = output_grad.astype(F32)
    grad_mid_norm, gain_m = rms_back(grad_second, normed_m, inverse_m, gains32[1])
    grad_mid = grad_final + grad_mid_norm
    grad_branch = plane_gather(sp, grad_mid.astype(BF16), 5, "branch_grads")
    grad_attended = dot_nt(grad_branch, wo_s).astype(BF16)
    grad_w_output = dot_tn(attended, grad_branch)
    grad_queries, grad_keys, grad_values = attend_back(queries, keys, values, grad_attended, log_sum)
    grad_q_normed = rotate(grad_queries, cosine_table, -sine_table)
    grad_k_normed = rotate(grad_keys, cosine_table, -sine_table)
    q_scaled, k_scaled = grad_q_normed * gains_own[2], grad_k_normed * gains_own[3]
    q_mean, k_mean = two_row_sums(
        jnp.sum(q_scaled * q_normed, axis=-1, keepdims=True),
        jnp.sum(k_scaled * k_normed, axis=-1, keepdims=True),
        6,
        "norm_grad_sums",
    )
    grad_q_low = (q_inverse * (q_scaled - q_normed * (q_mean / D))).astype(BF16)
    grad_k_low = (k_inverse * (k_scaled - k_normed * (k_mean / D))).astype(BF16)
    grad_v_low = grad_values.astype(BF16)
    gain_q = jnp.sum(grad_q_normed * q_normed, axis=0)
    gain_k = jnp.sum(grad_k_normed * k_normed, axis=0)
    grad_first = dot_nt(grad_q_low, w_all[0]) + dot_nt(grad_k_low, w_all[1])
    grad_first = (grad_first + dot_nt(grad_v_low, w_all[2])).astype(BF16)
    grad_first = plane_reduce(sp, grad_first.reshape(sp, TOK_DEV, D), 7, "input_grads")
    normed_own, inverse_own = rms_parts(inputs)
    grad_in_norm, gain_a = rms_back(grad_first, normed_own, inverse_own, gains32[0])
    input_grad = grad_mid + grad_in_norm

    parts = [
        dot_tn(first_in, low).astype(BF16).reshape(fsdp, D // fsdp, cols)
        for low in (grad_q_low, grad_k_low, grad_v_low)
    ]
    output_part = grad_w_output.astype(BF16).reshape(fsdp, rows, sp, cols).transpose(0, 2, 1, 3)
    parts.append(output_part.reshape(fsdp, sp * rows, cols))
    summed = line_reduce(fsdp, jnp.concatenate(parts, axis=1), 8, "weight_grads")
    height = D // fsdp
    qkv = summed[: 3 * height].reshape(3, height, cols)
    out_rows = summed[3 * height :].reshape(sp, rows, cols).transpose(1, 0, 2).reshape(rows, D)
    wide = jnp.zeros((2, D), F32)
    wide = lax.dynamic_update_slice(wide, jnp.stack([gain_q, gain_k]), (0, s * cols))
    gain_rows = jnp.concatenate([jnp.stack([gain_a, gain_m]), wide], axis=0)
    small = jnp.concatenate(
        [
            grad_router.reshape(count, router_size),
            gain_rows.reshape(4, count, rows).transpose(1, 0, 2).reshape(count, 4 * rows),
        ],
        axis=1,
    )
    small = jnp.pad(small, ((0, 0), (0, misc_rows * 128 - small.shape[1])))
    qkv_own, grad_output, small_all = exchange_end(
        fsdp, sp, qkv, out_rows, small.reshape(count, misc_rows, 128), 9
    )
    qkv_own = qkv_own.transpose(1, 2, 0, 3).reshape(3, rows, D)
    small_sum = jnp.sum(small_all, axis=0).reshape(misc_rows * 128)
    grad_router_own = small_sum[:router_size].reshape(rows, experts)
    grad_gains = small_sum[router_size : router_size + 4 * rows].reshape(4, rows)
    return (
        layer_out, input_grad, qkv_own[0], qkv_own[1], qkv_own[2], grad_output,
        grad_router_own, grad_gains, grad_gate, grad_up, grad_down,
    )


def solution(mesh):
    both, split = P(("fsdp", "sp"), None), P("fsdp", "sp", None)
    gains = P(None, ("fsdp", "sp"))
    return jax.shard_map(
        body,
        mesh=mesh,
        in_specs=(both,) * 7 + (gains,) + (split,) * 3 + (both,),
        out_specs=(both,) * 7 + (gains,) + (split,) * 3,
        check_vma=False,
    )
```

```python
import functools

import jax
import jax.numpy as jnp
from jax import lax
from jax.experimental import pallas as pl
from jax.experimental.pallas import tpu as pltpu
from jax.sharding import PartitionSpec as P

D = 2048
HEADS = 16
HEAD_DIM = 128
TOP = 8
EXP_DEV = 2
BLK = 256
TOK_DEV = 256
EPSILON = 1e-05
ROPE_BASE = 10000.0
MASKED = -1000000000.0
SCALE = HEAD_DIM ** (-0.5)
MESH = pl.DeviceIdType.MESH
ANY = pl.BlockSpec(memory_space=pl.ANY)
VMEM = pl.BlockSpec(memory_space=pltpu.VMEM)
VLIM = 60 * 1024 * 1024
F32 = jnp.float32
BF16 = jnp.bfloat16


def remote(src, dst, send_sem, recv_sem, device):
    return pltpu.make_async_remote_copy(
        src_ref=src,
        dst_ref=dst,
        send_sem=send_sem,
        recv_sem=recv_sem,
        device_id=device,
        device_id_type=MESH,
    )


def landed(ref, sem):
    pltpu.make_async_copy(ref, ref, sem).wait()


def signal(sem, device):
    pl.semaphore_signal(sem, inc=1, device_id=device, device_id_type=MESH)


def greet_line(barrier, lines, f, s):
    place, core = f // 2, f % 2
    signal(barrier, (f + 1 - 2 * core, s))

    @pl.when(place > 0)
    def _():
        signal(barrier, (f - 2, s))

    @pl.when(place < lines - 1)
    def _():
        signal(barrier, (f + 2, s))

    return 1 + jnp.where(place > 0, 1, 0) + jnp.where(place < lines - 1, 1, 0)


class LineGather:
    def __init__(self, views, owns, lines, f, s, send, recv):
        self.views, self.owns, self.lines, self.f, self.s = views, owns, lines, f, s
        self.send, self.recv = send, recv
        self.place, self.core = f // 2, f % 2

    def copy(self, v, block, slot, way):
        device = {
            "right": (self.f + 2, self.s),
            "left": (self.f - 2, self.s),
            "partner": (self.f + 1 - 2 * self.core, self.s),
        }[way]
        index = {"right": 0, "left": 1, "partner": 2}[way]
        ref = self.views[v](block)
        own = self.owns[v] if slot == 0 and self.owns[v] is not None else ref
        return remote(own, ref, self.send.at[v, slot, index], self.recv.at[v, block], device)

    def start_own(self, v):
        @pl.when(self.place < self.lines - 1)
        def _():
            self.copy(v, self.f, 0, "right").start()

        @pl.when(self.place > 0)
        def _():
            self.copy(v, self.f, 0, "left").start()

        self.copy(v, self.f, 0, "partner").start()

    def forward(self, v, k):
        place, lines = self.place, self.lines

        @pl.when(place >= k)
        def _():
            block = self.f - 2 * k
            landed(self.views[v](block), self.recv.at[v, block])

            @pl.when(place < lines - 1)
            def _():
                self.copy(v, block, k, "right").start()

            self.copy(v, block, k, "partner").start()

        @pl.when(place + k < lines)
        def _():
            block = self.f + 2 * k
            landed(self.views[v](block), self.recv.at[v, block])

            @pl.when(place > 0)
            def _():
                self.copy(v, block, lines - 1 + k, "left").start()

            self.copy(v, block, lines - 1 + k, "partner").start()

    def finish(self, v):
        place, lines = self.place, self.lines
        for line in range(lines):
            block = 2 * line + 1 - self.core
            landed(self.views[v](block), self.recv.at[v, block])
        self.copy(v, self.f, 0, "partner").wait_send()

        @pl.when(place < lines - 1)
        def _():
            self.copy(v, self.f, 0, "right").wait_send()

        @pl.when(place > 0)
        def _():
            self.copy(v, self.f, 0, "left").wait_send()

        for k in range(1, lines):

            @pl.when(place >= k)
            def _():
                block = self.f - 2 * k

                @pl.when(place < lines - 1)
                def _():
                    self.copy(v, block, k, "right").wait_send()

                self.copy(v, block, k, "partner").wait_send()

            @pl.when(place + k < lines)
            def _():
                block = self.f + 2 * k

                @pl.when(place > 0)
                def _():
                    self.copy(v, block, lines - 1 + k, "left").wait_send()

                self.copy(v, block, lines - 1 + k, "partner").wait_send()


def line_sems(arrays, fsdp):
    lines = fsdp // 2
    return [
        pltpu.SemaphoreType.DMA((arrays, 2 * lines, 3)),
        pltpu.SemaphoreType.DMA((arrays, fsdp)),
    ]


def add_rows(dst, a, b, rows):
    def step(i, carry):
        at = pl.ds(pl.multiple_of(i * 32, 32), 32)
        dst[at, :] = a[at, :].astype(dst.dtype) + b[at, :].astype(dst.dtype)
        return carry

    lax.fori_loop(0, rows // 32, step, 0)


class LineReduce:
    def __init__(self, p_ref, scratch, lines, f, s):
        self.p_ref, self.lines, self.f, self.s = p_ref, lines, f, s
        self.own, self.paired, self.got, self.last = scratch[:4]
        self.psend, self.precv, self.send, self.recv, self.final, self.local = scratch[4:]
        self.place, self.core = f // 2, f % 2
        self.rows = p_ref.shape[1]
        self.order = []
        for n in range(lines):
            for d in (lines - 1 - n, n):
                if d not in self.order:
                    self.order.append(d)

    @staticmethod
    def scratch(fsdp, block):
        lines = fsdp // 2
        dma = pltpu.SemaphoreType.DMA
        return [
            pltpu.VMEM((lines,) + block, BF16),
            pltpu.VMEM((lines,) + block, BF16),
            pltpu.VMEM((lines,) + block, BF16),
            pltpu.VMEM(block, BF16),
            dma((lines,)), dma((lines,)), dma((lines,)), dma((lines,)), dma, dma((lines,)),
        ]

    def load(self, i):
        return pltpu.make_async_copy(self.p_ref.at[2 * i + self.core], self.own.at[i], self.local.at[i])

    def swap(self, i):
        return remote(
            self.p_ref.at[2 * i + 1 - self.core], self.paired.at[i], self.psend.at[i],
            self.precv.at[i], (self.f + 1 - 2 * self.core, self.s),
        )

    def right(self, d, last):
        dst = self.last if last else self.got.at[d]
        sem = self.final if last else self.recv.at[d]
        return remote(self.own.at[d], dst, self.send.at[d], sem, (self.f + 2, self.s))

    def left(self, d):
        return remote(
            self.own.at[d], self.got.at[d], self.send.at[d], self.recv.at[d], (self.f - 2, self.s)
        )

    def start(self):
        for i in self.order:
            self.swap(i).start()
        for i in self.order:
            self.load(i).start()
        for i in self.order:
            self.load(i).wait()
            landed(self.paired.at[i], self.precv.at[i])
            add_rows(self.own.at[i], self.own.at[i], self.paired.at[i], self.rows)

    def step(self, t):
        place, lines = self.place, self.lines
        d = lines - 1 - t + place

        @pl.when(t >= place)
        def _():
            @pl.when(place > 0)
            def _():
                landed(self.got.at[d], self.recv.at[d])
                add_rows(self.own.at[d], self.own.at[d], self.got.at[d], self.rows)

            @pl.when(d == place + 1)
            def _():
                self.right(d, True).start()

            @pl.when(d != place + 1)
            def _():
                self.right(d, False).start()

        e = t - (lines - 1 - place)

        @pl.when(e >= 0)
        def _():
            @pl.when(place < lines - 1)
            def _():
                landed(self.got.at[e], self.recv.at[e])
                add_rows(self.own.at[e], self.own.at[e], self.got.at[e], self.rows)

            self.left(e).start()

    def finish(self, out_ref):
        place, lines, rows = self.place, self.lines, self.rows

        def first(i, carry):
            at = pl.ds(pl.multiple_of(i * 32, 32), 32)
            out_ref[at, :] = self.own[place, at, :].astype(F32)
            return carry

        lax.fori_loop(0, rows // 32, first, 0)

        @pl.when(place > 0)
        def _():
            landed(self.last, self.final)
            add_rows(out_ref, out_ref, self.last, rows)

        @pl.when(place < lines - 1)
        def _():
            landed(self.got.at[place], self.recv.at[place])
            add_rows(out_ref, out_ref, self.got.at[place], rows)

        for i in range(lines):
            self.swap(i).wait_send()

            @pl.when(place < i)
            def _():
                self.right(i, False).wait_send()

            @pl.when(place > i)
            def _():
                self.left(i).wait_send()


class PlaneGather:
    def __init__(self, own, out, f, s, send, recv):
        self.own, self.out, self.f, self.s, self.send, self.recv = own, out, f, s, send, recv
        self.rows = own.shape[0]
        self.half = self.rows // 2

    def at(self, place, first, size):
        return self.out.at[pl.ds(pl.multiple_of(place * self.rows + first, self.half), size), :]

    def near(self, k):
        return remote(
            self.own, self.at(self.s, 0, self.rows), self.send.at[k - 1], self.recv.at[k - 1],
            (self.f, self.s ^ k),
        )

    def on(self, k):
        ref = self.at(self.s ^ k, (k - 1) * self.half, self.half)
        return remote(ref, ref, self.send.at[k + 1], self.recv.at[k + 1], (self.f, self.s ^ (3 - k)))

    def start(self):
        self.near(1).start()
        self.near(2).start()

    def forward(self):
        for k in (1, 2):
            landed(self.at(self.s ^ k, 0, self.rows), self.recv.at[k - 1])
            self.on(k).start()

    def finish(self):
        landed(self.at(self.s ^ 3, 0, self.half), self.recv.at[2])
        landed(self.at(self.s ^ 3, self.half, self.half), self.recv.at[3])
        for k in (1, 2):
            self.near(k).wait_send()
            self.on(k).wait_send()


class PlaneReduce:
    WAYS = ((0, 1, 1), (1, 2, 2))

    def __init__(self, p_ref, out_ref, scratch, f, s):
        self.p_ref, self.out_ref, self.f, self.s = p_ref, out_ref, f, s
        self.own, self.got, self.got_on, self.send, self.recv, self.local = scratch
        self.half = p_ref.shape[1] // 2

    @staticmethod
    def scratch(block):
        dma = pltpu.SemaphoreType.DMA
        return [
            pltpu.VMEM((3,) + block, BF16), pltpu.VMEM((2,) + block, BF16),
            pltpu.VMEM(block, BF16), dma((2, 3)), dma((2, 3)), dma((3,)),
        ]

    def part(self, ref, h):
        return ref.at[pl.ds(h * self.half, self.half), :]

    def load(self, n):
        d = (self.s, self.s ^ 2, self.s ^ 1)[n]
        return pltpu.make_async_copy(self.p_ref.at[d], self.own.at[n], self.local.at[n])

    def hop(self, h, k, far):
        d = self.s ^ 3 if far else self.s ^ k
        n = 0 if far else 1
        return remote(
            self.part(self.p_ref.at[d], h), self.part(self.got.at[1 - n], h), self.send.at[h, n],
            self.recv.at[h, n], (self.f, self.s ^ k),
        )

    def on(self, h, k, n):
        return remote(
            self.part(self.own.at[n], h), self.part(self.got_on, h), self.send.at[h, 2],
            self.recv.at[h, 2], (self.f, self.s ^ (3 - k)),
        )

    def start(self):
        for far in (True, False):
            for h, k, _ in self.WAYS:
                self.hop(h, k, far).start()
        for n in range(3):
            self.load(n).start()

    def forward(self):
        for n in range(3):
            self.load(n).wait()
        for h, k, n in self.WAYS:
            mine = self.part(self.own.at[n], h)
            landed(self.part(self.got.at[1], h), self.recv.at[h, 0])
            add_rows(mine, mine, self.part(self.got.at[1], h), self.half)
            self.on(h, k, n).start()

    def finish(self):
        for h in (0, 1):
            landed(self.part(self.got.at[0], h), self.recv.at[h, 1])
            add_rows(
                self.part(self.out_ref, h), self.part(self.own.at[0], h), self.part(self.got.at[0], h),
                self.half,
            )
        for h in (0, 1):
            landed(self.part(self.got_on, h), self.recv.at[h, 2])
            out = self.part(self.out_ref, h)
            add_rows(out, out, self.part(self.got_on, h), self.half)
        for h, k, n in self.WAYS:
            self.hop(h, k, True).wait_send()
            self.hop(h, k, False).wait_send()
            self.on(h, k, n).wait_send()


def greet_plane(barrier, f, s):
    for k in (1, 2):
        signal(barrier, (f, s ^ k))
    return 2


def rows_view(ref, rows):
    return lambda b: ref.at[pl.ds(pl.multiple_of(b * rows, rows), rows), :]


def block_view(ref):
    return lambda b: ref.at[b]


def comm_params(number):
    return pltpu.CompilerParams(
        collective_id=number, has_side_effects=True, vmem_limit_bytes=VLIM
    )


def start_kernel(
    fsdp, sp, x_ref, w_ref, wo_ref, g_ref, misc_ref, routes_ref,
    x_all, w_all, wo_all, g_all, misc_all, routes_all,
    send, recv, xsend, xrecv, psend, precv, wsend, wrecv, msend, mrecv, rsend, rrecv, local,
):
    f, s = lax.axis_index("fsdp"), lax.axis_index("sp")
    count, lines = fsdp * sp, fsdp // 2
    me = f * sp + s
    rows = w_ref.shape[1]
    cols = D // sp
    barrier = pltpu.get_barrier_semaphore()

    def greet(i, carry):
        other = lax.rem(me + i, count)
        signal(barrier, (other // sp, lax.rem(other, sp)))
        return carry

    def w_block(s_to):
        return w_ref.at[:, :, pl.ds(pl.multiple_of(s_to * cols, cols), cols)]

    def w_rows(i):
        return w_all.at[:, pl.ds(pl.multiple_of(i * rows, rows), rows), :]

    def w_view(b):
        size = rows * sp
        return w_all.at[:, pl.ds(pl.multiple_of(b * size, size), size), :]

    wo_view = rows_view(wo_all, rows)
    x_view = rows_view(x_all, TOK_DEV)
    owns = [
        pltpu.make_async_copy(w_block(s), w_rows(me), local.at[0]),
        pltpu.make_async_copy(x_ref, x_view(s), local.at[1]),
        pltpu.make_async_copy(misc_ref, misc_all.at[me], local.at[2]),
        pltpu.make_async_copy(routes_ref, routes_all.at[f], local.at[3]),
        pltpu.make_async_copy(g_ref, g_all.at[f], local.at[4]),
    ]
    for copy in owns:
        copy.start()
    lax.fori_loop(1, count, greet, 0)
    pl.semaphore_wait(barrier, count - 1)

    line = LineGather([w_view, wo_view, block_view(g_all)], [None, None, g_ref], lines, f, s, send, recv)
    line.start_own(2)
    w_copies = []
    for k in (3, 1, 2):
        s_to = s ^ k
        copy = remote(w_block(s_to), w_rows(me), psend.at[k], precv.at[k], (f, s_to))
        copy.start()
        w_copies.append(copy)
    target_s, target_f = me // fsdp, lax.rem(me, fsdp)
    stays = jnp.logical_and(target_s == s, target_f == f)
    wo_copy = remote(wo_ref, wo_view(target_f), wsend, wrecv, (target_f, target_s))
    wo_own = pltpu.make_async_copy(wo_ref, wo_view(f), wrecv)

    @pl.when(stays)
    def _():
        wo_own.start()

    @pl.when(jnp.logical_not(stays))
    def _():
        wo_copy.start()

    def misc_copy(i):
        other = lax.rem(me + i, count)
        return remote(
            misc_ref, misc_all.at[me], msend.at[i], mrecv.at[me], (other // sp, lax.rem(other, sp))
        )

    def misc_go(i, carry):
        misc_copy(i).start()
        return carry

    lax.fori_loop(1, count, misc_go, 0)

    def routes_copy(i):
        other = lax.rem(f + i, fsdp)
        return remote(routes_ref, routes_all.at[f], rsend.at[i], rrecv.at[f], (other, s))

    def routes_go(i, carry):
        routes_copy(i).start()
        return carry

    lax.fori_loop(1, fsdp, routes_go, 0)

    owns[0].wait()
    for k in range(1, sp):
        landed(w_rows(f * sp + (s ^ k)), precv.at[k])
    line.start_own(0)
    tokens = PlaneGather(x_ref, x_all, f, s, xsend, xrecv)
    tokens.start()
    landed(wo_view(f), wrecv)
    line.start_own(1)
    for k in range(1, lines):
        for v in (2, 0, 1):
            line.forward(v, k)
        if k == min(2, lines - 1):
            tokens.forward()
    for v in range(3):
        line.finish(v)
    tokens.finish()

    def misc_end(i, carry):
        misc_copy(i).wait_send()
        other = lax.rem(me + i, count)
        landed(misc_all.at[other], mrecv.at[other])
        return carry

    lax.fori_loop(1, count, misc_end, 0)

    def routes_end(i, carry):
        routes_copy(i).wait_send()
        other = lax.rem(f + i, fsdp)
        landed(routes_all.at[other], rrecv.at[other])
        return carry

    lax.fori_loop(1, fsdp, routes_end, 0)
    for copy in w_copies:
        copy.wait_send()

    @pl.when(jnp.logical_not(stays))
    def _():
        wo_copy.wait_send()

    for copy in owns[1:]:
        copy.wait()


def gather_start(fsdp, sp, x, w, wo, g, misc, routes):
    count = fsdp * sp
    dma = pltpu.SemaphoreType.DMA
    return pl.pallas_call(
        functools.partial(start_kernel, fsdp, sp),
        out_shape=(
            jax.ShapeDtypeStruct((sp * TOK_DEV, D), BF16),
            jax.ShapeDtypeStruct((3, D, D // sp), BF16),
            jax.ShapeDtypeStruct((D // sp, D), BF16),
            jax.ShapeDtypeStruct((fsdp,) + g.shape, BF16),
            jax.ShapeDtypeStruct((count,) + misc.shape, BF16),
            jax.ShapeDtypeStruct((fsdp,) + routes.shape, jnp.int32),
        ),
        in_specs=[VMEM] * 6,
        out_specs=[ANY] * 6,
        scratch_shapes=line_sems(3, fsdp)
        + [
            dma((4,)), dma((4,)), dma((sp,)), dma((sp,)), dma, dma,
            dma((count,)), dma((count,)), dma((fsdp,)), dma((fsdp,)), dma((5,)),
        ],
        compiler_params=comm_params(0),
        name="gather_start",
    )(x, w, wo, g, misc, routes)


def branch_kernel(fsdp, p_ref, g_ref, out_ref, g_all, *scratch):
    f, s = lax.axis_index("fsdp"), lax.axis_index("sp")
    lines = fsdp // 2
    barrier = pltpu.get_barrier_semaphore()
    expected = greet_line(barrier, lines, f, s) + greet_plane(barrier, f, s)
    send, recv, own_sem = scratch[-3:]
    own = pltpu.make_async_copy(g_ref, g_all.at[f], own_sem)
    own.start()
    pl.semaphore_wait(barrier, expected)
    plane = PlaneReduce(p_ref, out_ref, scratch[:-3], f, s)
    line = LineGather([block_view(g_all)], [g_ref], lines, f, s, send, recv)
    plane.start()
    line.start_own(0)
    for k in range(1, lines):
        line.forward(0, k)
        if k == min(2, lines - 1):
            plane.forward()
    plane.finish()
    line.finish(0)
    own.wait()


def branch_sum(fsdp, partial, g):
    block = partial.shape[1:]
    return pl.pallas_call(
        functools.partial(branch_kernel, fsdp),
        out_shape=(jax.ShapeDtypeStruct(block, F32), jax.ShapeDtypeStruct((fsdp,) + g.shape, BF16)),
        in_specs=[ANY, VMEM],
        out_specs=[VMEM, ANY],
        scratch_shapes=PlaneReduce.scratch(block) + line_sems(1, fsdp) + [pltpu.SemaphoreType.DMA],
        compiler_params=comm_params(2),
        name="branch_sum",
    )(partial, g)


def token_kernel(
    fsdp, x_ref, g_first, g_second, picks, w_ref, out_ref, taken_ref, back_ref,
    g_buf, w_buf, taken, back, send, recv, local, loads, stores, back_sem,
):
    f, s = lax.axis_index("fsdp"), lax.axis_index("sp")
    lines = fsdp // 2
    parts = 2
    size = TOK_DEV // parts
    early, later = g_first.shape[1], g_second.shape[1]
    slots = picks.shape[1] // EXP_DEV
    ff = w_ref.shape[1]
    barrier = pltpu.get_barrier_semaphore()
    expected = greet_line(barrier, lines, f, s)
    own = pltpu.make_async_copy(x_ref, out_ref.at[f], local)
    own.start()
    reads = [
        pltpu.make_async_copy(g_first, g_buf.at[:, pl.ds(0, early), :], loads.at[0]),
        pltpu.make_async_copy(g_second, g_buf.at[:, pl.ds(early, later), :], loads.at[1]),
        pltpu.make_async_copy(w_ref, w_buf, loads.at[2]),
    ]
    for copy in reads:
        copy.start()
    pl.semaphore_wait(barrier, expected)

    def view(part):
        return lambda b: out_ref.at[b, pl.ds(part * size, size), :]

    owns = [x_ref.at[pl.ds(p * size, size), :] for p in range(parts)]
    line = LineGather([view(p) for p in range(parts)], owns, lines, f, s, send, recv)
    for p in range(parts):
        line.start_own(p)

    def take_all():
        reads[0].wait()
        reads[1].wait()

        def block(b, carry):
            for n in range(D // 512):
                at = pl.ds(n * 512, 512)
                got = dot_nn(picks[b], g_buf[b, :, at]).astype(BF16)
                for e in range(EXP_DEV):
                    to = pl.ds(pl.multiple_of(b * slots, 16), slots)
                    taken[e, to, at] = got[e * slots : (e + 1) * slots]
            return carry

        lax.fori_loop(0, fsdp, block, 0)
        for e in range(EXP_DEV):
            pltpu.make_async_copy(taken.at[e], taken_ref.at[e], stores.at[e]).start()

    def back_copy(e, j, slot):
        at = pl.ds(pl.multiple_of(j * FT, FT), FT)
        return pltpu.make_async_copy(back.at[slot], back_ref.at[e, :, at], back_sem.at[slot])

    def back_of(e):
        if e == 0:
            reads[2].wait()
        for j in range(ff // FT):
            slot = j % 2
            if e > 0 or j > 1:
                back_copy(e, j, slot).wait()
            back[slot] = dot_nt(taken[e], w_buf[e, pl.ds(j * FT, FT), :])
            back_copy(e, j, slot).start()

    work = [take_all] + [functools.partial(back_of, e) for e in range(EXP_DEV)]
    for k in range(1, lines):
        if k - 1 < len(work):
            work[k - 1]()
        for p in range(parts):
            line.forward(p, k)
    for unit in work[lines - 1 :]:
        unit()
    for p in range(parts):
        line.finish(p)
    own.wait()
    for slot in range(2):
        back_copy(0, slot, slot).wait()
    for e in range(EXP_DEV):
        pltpu.make_async_copy(taken.at[e], taken_ref.at[e], stores.at[e]).wait()


def token_gather(fsdp, x, g_first, g_second, picks, w_down):
    slots = picks.shape[1] // EXP_DEV
    total = fsdp * slots
    ff = w_down.shape[1]
    dma = pltpu.SemaphoreType.DMA
    return pl.pallas_call(
        functools.partial(token_kernel, fsdp),
        out_shape=(
            jax.ShapeDtypeStruct((fsdp, TOK_DEV, D), BF16),
            jax.ShapeDtypeStruct((EXP_DEV, total, D), BF16),
            jax.ShapeDtypeStruct((EXP_DEV, total, ff), F32),
        ),
        in_specs=[VMEM, ANY, ANY, VMEM, ANY],
        out_specs=[ANY, ANY, ANY],
        scratch_shapes=[
            pltpu.VMEM((fsdp, TOK_DEV, D), BF16),
            pltpu.VMEM((EXP_DEV, ff, D), BF16),
            pltpu.VMEM((EXP_DEV, total, D), BF16),
            pltpu.VMEM((2, total, FT), F32),
        ]
        + line_sems(2, fsdp)
        + [dma, dma((3,)), dma((EXP_DEV,)), dma((2,))],
        compiler_params=comm_params(3),
        name="token_gather",
    )(x, g_first, g_second, picks, w_down)


def token_back_kernel(
    fsdp, p_ref, gated_ref, w_ref, turned, x_ref, gg_ref, gu_ref,
    out_ref, part_ref, wg_ref, wu_ref,
    wide, narrow, w_buf, tile, grad_tile, loads, tile_sem, grad_sem, *scratch,
):
    f, s = lax.axis_index("fsdp"), lax.axis_index("sp")
    lines = fsdp // 2
    slots = turned.shape[3]
    height = grad_tile.shape[1]
    barrier = pltpu.get_barrier_semaphore()
    expected = greet_line(barrier, lines, f, s)
    reads = [
        pltpu.make_async_copy(gated_ref, narrow, loads.at[0]),
        pltpu.make_async_copy(w_ref, w_buf, loads.at[1]),
        pltpu.make_async_copy(x_ref, wide, loads.at[2]),
        pltpu.make_async_copy(gg_ref.at[0], narrow.at[0], loads.at[3]),
        pltpu.make_async_copy(gu_ref.at[0], narrow.at[1], loads.at[4]),
        pltpu.make_async_copy(gg_ref.at[1], narrow.at[0], loads.at[3]),
        pltpu.make_async_copy(gu_ref.at[1], narrow.at[1], loads.at[4]),
    ]
    reads[0].start()
    reads[1].start()
    pl.semaphore_wait(barrier, expected)
    line = LineReduce(p_ref, scratch, lines, f, s)
    line.start()

    def down_of(e):
        if e == 0:
            reads[0].wait()
            reads[1].wait()

        def columns(n, carry):
            at = pl.ds(pl.multiple_of(n * 512, 512), 512)
            wide[e, :, at] = dot_nn(narrow[e], w_buf[e, :, at]).astype(BF16)
            return carry

        lax.fori_loop(0, D // 512, columns, 0)

    def tile_copy(b, slot):
        return pltpu.make_async_copy(tile.at[slot], part_ref.at[b], tile_sem.at[slot])

    def sum_all():
        reads[3].start()
        reads[4].start()

        def pair(i, carry):
            for slot in range(2):
                b = 2 * i + slot

                @pl.when(i > 0)
                def _():
                    tile_copy(b, slot).wait()

                for n in range(D // 512):
                    at = pl.ds(n * 512, 512)
                    summed = jnp.zeros((TOK_DEV, 512), F32)
                    for e in range(EXP_DEV):
                        rows = wide[e, pl.ds(pl.multiple_of(b * slots, 16), slots), at]
                        summed += dot_nn(turned[b, e], rows)
                    tile[slot, :, at] = summed.astype(BF16)
                tile_copy(b, slot).start()
            return carry

        lax.fori_loop(0, fsdp // 2, pair, 0)
        reads[2].start()

    def grad_copy(to, e, i, slot):
        at = pl.ds(pl.multiple_of(i * height, height), height)
        return pltpu.make_async_copy(grad_tile.at[slot], to.at[e, at, :], grad_sem.at[slot])

    def grad_of(e, n, to, first):
        if n == 0 and e == 0:
            reads[2].wait()
            reads[3].wait()
            reads[4].wait()
        if n == 0 and e == 1:
            reads[5].wait()
            reads[6].wait()

        def pair(i, carry):
            for slot in range(2):
                part = 2 * i + slot

                def before():
                    grad_copy(to, e, part, slot).wait()

                if first:
                    pl.when(i > 0)(before)
                else:
                    before()
                at = pl.ds(pl.multiple_of(part * height, height), height)
                grad_tile[slot] = dot_tn(wide[e, :, at], narrow[n]).astype(BF16)
                grad_copy(to, e, part, slot).start()
            return carry

        lax.fori_loop(0, D // height // 2, pair, 0)
        if n == 1 and e == 0:
            reads[5].start()
            reads[6].start()

    work = [functools.partial(down_of, e) for e in range(EXP_DEV)] + [sum_all]
    for e in range(EXP_DEV):
        for n, to in ((0, wg_ref), (1, wu_ref)):
            work.append(functools.partial(grad_of, e, n, to, e == 0 and n == 0))
    done = 0
    for t in range(lines - 1):
        line.step(t)
        until = (t + 1) * len(work) // (lines - 1)
        for unit in work[done:until]:
            unit()
        done = until
    line.finish(out_ref)
    for slot in range(2):
        tile_copy(slot, slot).wait()
        grad_copy(wg_ref, 0, slot, slot).wait()


def token_back(fsdp, partial, gated, w_down, turned, received, grad_gate_pre, grad_up_pre):
    block = partial.shape[1:]
    total, ff = gated.shape[1:]
    height = 256
    dma = pltpu.SemaphoreType.DMA
    weight = jax.ShapeDtypeStruct((EXP_DEV, D, ff), BF16)
    return pl.pallas_call(
        functools.partial(token_back_kernel, fsdp),
        out_shape=(
            jax.ShapeDtypeStruct(block, F32),
            jax.ShapeDtypeStruct(partial.shape, BF16),
            weight,
            weight,
        ),
        in_specs=[ANY, ANY, ANY, VMEM, ANY, ANY, ANY],
        out_specs=[VMEM, ANY, ANY, ANY],
        scratch_shapes=[
            pltpu.VMEM((EXP_DEV, total, D), BF16),
            pltpu.VMEM((EXP_DEV, total, ff), BF16),
            pltpu.VMEM((EXP_DEV, ff, D), BF16),
            pltpu.VMEM((2,) + block, BF16),
            pltpu.VMEM((2, height, ff), BF16),
            dma((5,)),
            dma((2,)),
            dma((2,)),
        ]
        + LineReduce.scratch(fsdp, block),
        compiler_params=comm_params(4),
        name="token_back",
    )(partial, gated, w_down, turned, received, grad_gate_pre, grad_up_pre)


def branch_back_kernel(fsdp, x_ref, p_ref, all_ref, out_ref, xsend, xrecv, own_sem, *scratch):
    f, s = lax.axis_index("fsdp"), lax.axis_index("sp")
    lines = fsdp // 2
    barrier = pltpu.get_barrier_semaphore()
    expected = greet_line(barrier, lines, f, s) + greet_plane(barrier, f, s)
    plane = PlaneGather(x_ref, all_ref, f, s, xsend, xrecv)
    own = pltpu.make_async_copy(x_ref, plane.at(s, 0, x_ref.shape[0]), own_sem)
    own.start()
    pl.semaphore_wait(barrier, expected)
    plane.start()
    line = LineReduce(p_ref, scratch, lines, f, s)
    line.start()
    for t in range(lines - 1):
        line.step(t)
        if t == min(1, lines - 2):
            plane.forward()
    plane.finish()
    line.finish(out_ref)
    own.wait()


def branch_back(fsdp, sp, x, partial):
    block = partial.shape[1:]
    dma = pltpu.SemaphoreType.DMA
    return pl.pallas_call(
        functools.partial(branch_back_kernel, fsdp),
        out_shape=(
            jax.ShapeDtypeStruct((sp * x.shape[0], x.shape[1]), BF16),
            jax.ShapeDtypeStruct(block, F32),
        ),
        in_specs=[VMEM, ANY],
        out_specs=[ANY, VMEM],
        scratch_shapes=[dma((4,)), dma((4,)), dma] + LineReduce.scratch(fsdp, block),
        compiler_params=comm_params(5),
        name="branch_back",
    )(x, partial)


def line_reduce_kernel(fsdp, p_ref, out_ref, *scratch):
    f, s = lax.axis_index("fsdp"), lax.axis_index("sp")
    lines = fsdp // 2
    barrier = pltpu.get_barrier_semaphore()
    expected = greet_line(barrier, lines, f, s)
    pl.semaphore_wait(barrier, expected)
    line = LineReduce(p_ref, scratch, lines, f, s)
    line.start()
    for t in range(lines - 1):
        line.step(t)
    line.finish(out_ref)


def line_reduce(fsdp, partial, number, name):
    block = partial.shape[1:]
    return pl.pallas_call(
        functools.partial(line_reduce_kernel, fsdp),
        out_shape=jax.ShapeDtypeStruct(block, F32),
        in_specs=[ANY],
        out_specs=VMEM,
        scratch_shapes=LineReduce.scratch(fsdp, block),
        compiler_params=comm_params(number),
        name=name,
    )(partial)


def plane_sum_kernel(x_ref, out_ref, got, send, recv):
    f, s = lax.axis_index("fsdp"), lax.axis_index("sp")
    barrier = pltpu.get_barrier_semaphore()
    for k in (1, 2, 3):
        signal(barrier, (f, s ^ k))
    pl.semaphore_wait(barrier, 3)
    copies = []
    for k in (1, 2, 3):
        copy = remote(x_ref, got.at[k - 1], send.at[k - 1], recv.at[k - 1], (f, s ^ k))
        copy.start()
        copies.append(copy)
    for copy in copies:
        copy.wait()
    near = x_ref[...] + got[0]
    far = got[1] + got[2]
    out_ref[...] = near + far


def plane_sum(x, number, name):
    dma = pltpu.SemaphoreType.DMA
    return pl.pallas_call(
        plane_sum_kernel,
        out_shape=jax.ShapeDtypeStruct(x.shape, F32),
        in_specs=[VMEM],
        out_specs=VMEM,
        scratch_shapes=[pltpu.VMEM((3,) + x.shape, F32), dma((3,)), dma((3,))],
        compiler_params=pltpu.CompilerParams(collective_id=number, has_side_effects=True),
        name=name,
    )(x)


def end_kernel(
    fsdp, sp, q_ref, o_ref, m_ref, q_out, o_out, m_out,
    qsend, qrecv, osend, orecv, msend, mrecv, local,
):
    f, s = lax.axis_index("fsdp"), lax.axis_index("sp")
    count = fsdp * sp
    me = f * sp + s
    rows = o_ref.shape[0]
    barrier = pltpu.get_barrier_semaphore()

    def greet(i, carry):
        other = lax.rem(me + i, count)
        signal(barrier, (other // sp, lax.rem(other, sp)))
        return carry

    lax.fori_loop(1, count, greet, 0)
    pl.semaphore_wait(barrier, count - 1)

    def q_from(place):
        return q_ref.at[:, pl.ds(pl.multiple_of(place * rows, rows), rows), :]

    q_own = pltpu.make_async_copy(q_from(s), q_out.at[s], local.at[0])
    q_own.start()
    copies = []
    for k in range(1, sp):
        copy = remote(q_from(s ^ k), q_out.at[s], qsend.at[k], qrecv.at[k], (f, s ^ k))
        copy.start()
        copies.append(copy)
    flat = s * fsdp + f
    target_f, target_s = flat // sp, lax.rem(flat, sp)
    stays = jnp.logical_and(target_s == s, target_f == f)
    o_copy = remote(o_ref, o_out, osend, orecv, (target_f, target_s))
    o_own = pltpu.make_async_copy(o_ref, o_out, orecv)

    @pl.when(stays)
    def _():
        o_own.start()

    @pl.when(jnp.logical_not(stays))
    def _():
        o_copy.start()

    m_own = pltpu.make_async_copy(m_ref.at[me], m_out.at[me], local.at[1])
    m_own.start()

    def m_copy(i):
        other = lax.rem(me + i, count)
        return remote(
            m_ref.at[other], m_out.at[me], msend.at[i], mrecv.at[me], (other // sp, lax.rem(other, sp))
        )

    def m_go(i, carry):
        m_copy(i).start()
        return carry

    lax.fori_loop(1, count, m_go, 0)

    def m_end(i, carry):
        m_copy(i).wait_send()
        other = lax.rem(me + i, count)
        landed(m_out.at[other], mrecv.at[other])
        return carry

    lax.fori_loop(1, count, m_end, 0)
    landed(o_out, orecv)

    @pl.when(jnp.logical_not(stays))
    def _():
        o_copy.wait_send()

    for k in range(1, sp):
        landed(q_out.at[s ^ k], qrecv.at[k])
    for copy in copies:
        copy.wait_send()
    q_own.wait()
    m_own.wait()


def exchange_end(fsdp, sp, q, o, m, number):
    count = fsdp * sp
    rows = o.shape[0]
    dma = pltpu.SemaphoreType.DMA
    return pl.pallas_call(
        functools.partial(end_kernel, fsdp, sp),
        out_shape=(
            jax.ShapeDtypeStruct((sp, 3, rows, D // sp), q.dtype),
            jax.ShapeDtypeStruct(o.shape, o.dtype),
            jax.ShapeDtypeStruct(m.shape, m.dtype),
        ),
        in_specs=[ANY] * 3,
        out_specs=[ANY] * 3,
        scratch_shapes=[
            dma((sp,)), dma((sp,)), dma, dma, dma((count,)), dma((count,)), dma((2,)),
        ],
        compiler_params=pltpu.CompilerParams(collective_id=number, has_side_effects=True),
        name="exchange_end",
    )(q, o, m)


def dot_nt(a, b):
    return lax.dot_general(a, b, (((1,), (1,)), ((), ())), preferred_element_type=F32)


def dot_tn(a, b):
    return lax.dot_general(a, b, (((0,), (0,)), ((), ())), preferred_element_type=F32)


def dot_nn(a, b):
    return jnp.dot(a, b, preferred_element_type=F32)


def whole(shape):
    return pl.BlockSpec(shape, lambda *_: (0,) * len(shape))


def turn(v, cosine, sine):
    return v * cosine + pltpu.roll(v, HEAD_DIM // 2, 1) * sine


def project_kernel(x_ref, gain, w_ref, first_out, q_out, k_out, v_out, q_square, k_square):
    x = x_ref[...].astype(F32)
    inverse = lax.rsqrt(jnp.mean(x * x, axis=-1, keepdims=True) + EPSILON)
    first = (x * inverse * gain[0:1, :]).astype(BF16)
    first_out[...] = first
    q = dot_nn(first, w_ref[0])
    q_out[...] = q
    q_square[...] = jnp.sum(q * q, axis=-1, keepdims=True)
    k = dot_nn(first, w_ref[1])
    k_out[...] = k
    k_square[...] = jnp.sum(k * k, axis=-1, keepdims=True)
    v_out[...] = dot_nn(first, w_ref[2]).astype(BF16)


def project(x, gains, w):
    seq, cols = x.shape[0], w.shape[2]

    def block(width):
        return pl.BlockSpec((TOK_DEV, width), lambda i: (i, 0))

    return pl.pallas_call(
        project_kernel,
        grid=(seq // TOK_DEV,),
        out_shape=(
            jax.ShapeDtypeStruct((seq, D), BF16),
            jax.ShapeDtypeStruct((seq, cols), F32),
            jax.ShapeDtypeStruct((seq, cols), F32),
            jax.ShapeDtypeStruct((seq, cols), BF16),
            jax.ShapeDtypeStruct((seq, 1), F32),
            jax.ShapeDtypeStruct((seq, 1), F32),
        ),
        in_specs=[block(D), whole(gains.shape), whole(w.shape)],
        out_specs=[block(D), block(cols), block(cols), block(cols), block(1), block(1)],
        compiler_params=pltpu.CompilerParams(vmem_limit_bytes=VLIM),
        name="project",
    )(x, gains, w)


def attend_kernel(
    q_raw, k_raw, v_ref, q_inv, k_inv, gain, cosine, sine, o_ref, sum_ref, q_ref, k_ref
):
    c, d = cosine[...], sine[...]
    q_ref[...] = turn(q_raw[...] * q_inv[...] * gain[2:3, :], c, d).astype(BF16)
    k_ref[...] = turn(k_raw[...] * k_inv[...] * gain[3:4, :], c, d).astype(BF16)
    for i in range(q_ref.shape[0] // BLK):
        rows, seen = pl.ds(i * BLK, BLK), pl.ds(0, (i + 1) * BLK)
        scores = dot_nt(q_ref[rows, :], k_ref[seen, :]) * SCALE
        row_max = jnp.max(scores, axis=-1, keepdims=True)
        exp_rows = jnp.exp(scores - row_max)
        row_sum = jnp.sum(exp_rows, axis=-1, keepdims=True)
        probs = (exp_rows / row_sum).astype(BF16)
        o_ref[rows, :] = dot_nn(probs, v_ref[seen, :]).astype(BF16)
        sum_ref[0, rows, :] = row_max + jnp.log(row_sum)


def attend(q_raw, k_raw, v, q_inv, k_inv, gains, cosine, sine):
    seq, width = v.shape
    heads = width // HEAD_DIM
    spec = pl.BlockSpec((seq, HEAD_DIM), lambda h: (0, h))
    return pl.pallas_call(
        attend_kernel,
        grid=(heads,),
        out_shape=(
            jax.ShapeDtypeStruct((seq, width), BF16),
            jax.ShapeDtypeStruct((heads, seq, 1), F32),
            jax.ShapeDtypeStruct((seq, width), BF16),
            jax.ShapeDtypeStruct((seq, width), BF16),
        ),
        in_specs=[
            spec, spec, spec, whole((seq, 1)), whole((seq, 1)),
            pl.BlockSpec((4, HEAD_DIM), lambda h: (0, h)),
            whole((seq, HEAD_DIM)), whole((seq, HEAD_DIM)),
        ],
        out_specs=[spec, pl.BlockSpec((1, seq, 1), lambda h: (h, 0, 0)), spec, spec],
        compiler_params=pltpu.CompilerParams(vmem_limit_bytes=VLIM),
        name="attend",
    )(q_raw, k_raw, v, q_inv, k_inv, gains, cosine, sine)


def attend_back_kernel(
    q_ref, k_ref, v_ref, g_ref, sum_ref, q_raw, k_raw, q_inv, k_inv, gain, cosine, sine,
    q_scaled, k_scaled, dv_out, q_dots, k_dots, gains_out, dk_ref, dv_ref,
):
    head = pl.program_id(0)

    @pl.when(head == 0)
    def _():
        q_dots[...] = jnp.zeros_like(q_dots)
        k_dots[...] = jnp.zeros_like(k_dots)

    dk_ref[...] = jnp.zeros_like(dk_ref)
    dv_ref[...] = jnp.zeros_like(dv_ref)
    gain_q, gain_k = gain[2:3, :], gain[3:4, :]
    gain_sum = jnp.zeros((1, HEAD_DIM), F32)
    for i in range(q_ref.shape[0] // BLK):
        rows, seen = pl.ds(i * BLK, BLK), pl.ds(0, (i + 1) * BLK)
        q, g, keys = q_ref[rows, :], g_ref[rows, :], k_ref[seen, :]
        scores = dot_nt(q, keys) * SCALE
        probs = jnp.exp(scores - sum_ref[0, rows, :])
        grad_probs = dot_nt(g, v_ref[seen, :])
        row_dot = jnp.sum(probs * grad_probs, axis=-1, keepdims=True)
        grad_scores = (probs * (grad_probs - row_dot)).astype(BF16)
        dk_ref[seen, :] += dot_tn(grad_scores, q)
        dv_ref[seen, :] += dot_tn(probs.astype(BF16), g)
        grad_y = turn(dot_nn(grad_scores, keys) * SCALE, cosine[rows, :], -sine[rows, :])
        normed = q_raw[rows, :] * q_inv[rows, :]
        scaled = grad_y * gain_q
        q_scaled[rows, :] = scaled
        q_dots[rows, :] += jnp.sum(scaled * normed, axis=-1, keepdims=True)
        gain_sum += jnp.sum(grad_y * normed, axis=0, keepdims=True)
    grad_y = turn(dk_ref[...] * SCALE, cosine[...], -sine[...])
    normed = k_raw[...] * k_inv[...]
    scaled = grad_y * gain_k
    k_scaled[...] = scaled
    k_dots[...] += jnp.sum(scaled * normed, axis=-1, keepdims=True)
    gains_out[0:1, :] = gain_sum
    gains_out[1:2, :] = jnp.sum(grad_y * normed, axis=0, keepdims=True)
    dv_out[...] = dv_ref[...].astype(BF16)


def attend_back(q, k, v, g, log_sum, q_raw, k_raw, q_inv, k_inv, gains, cosine, sine):
    seq, width = q.shape
    heads = width // HEAD_DIM
    spec = pl.BlockSpec((seq, HEAD_DIM), lambda h: (0, h))
    column, table = whole((seq, 1)), whole((seq, HEAD_DIM))
    return pl.pallas_call(
        attend_back_kernel,
        grid=(heads,),
        out_shape=(
            jax.ShapeDtypeStruct((seq, width), F32),
            jax.ShapeDtypeStruct((seq, width), F32),
            jax.ShapeDtypeStruct((seq, width), BF16),
            jax.ShapeDtypeStruct((seq, 1), F32),
            jax.ShapeDtypeStruct((seq, 1), F32),
            jax.ShapeDtypeStruct((2, width), F32),
        ),
        in_specs=[spec] * 4
        + [pl.BlockSpec((1, seq, 1), lambda h: (h, 0, 0)), spec, spec, column, column]
        + [pl.BlockSpec((4, HEAD_DIM), lambda h: (0, h)), table, table],
        out_specs=[spec] * 3 + [column, column, pl.BlockSpec((2, HEAD_DIM), lambda h: (0, h))],
        scratch_shapes=[pltpu.VMEM((seq, HEAD_DIM), F32)] * 2,
        compiler_params=pltpu.CompilerParams(vmem_limit_bytes=VLIM),
        name="attend_back",
    )(q, k, v, g, log_sum, q_raw, k_raw, q_inv, k_inv, gains, cosine, sine)


def two_parts(x, axis):
    high = x.astype(BF16)
    return jnp.concatenate([high, (x - high.astype(F32)).astype(BF16)], axis=axis)


def blocks_of(shape):
    return pl.BlockSpec((1,) + shape, lambda b: (b,) + (0,) * len(shape))


def slots_of(slots, width):
    return pl.BlockSpec((EXP_DEV, slots, width), lambda b: (0, b, 0))


def route_kernel(picks, rows_in, router, columns, out, probs_out, gates_out):
    slots = out.shape[1]
    for n in range(D // 512):
        at = pl.ds(n * 512, 512)
        got = dot_nn(picks[0], rows_in[0, :, at]).astype(BF16)
        for e in range(EXP_DEV):
            out[e, :, at] = got[e * slots : (e + 1) * slots]
    logits = dot_nt(rows_in[0], router[...])
    exp_logits = jnp.exp(logits - jnp.max(logits, axis=1, keepdims=True))
    probs = exp_logits / jnp.sum(exp_logits, axis=1, keepdims=True)
    probs_out[0] = probs
    both = two_parts(probs, 1)
    for e in range(EXP_DEV):
        moved = dot_nn(picks[0, e * slots : (e + 1) * slots, :], both)
        mask = columns[e : e + 1, :]
        gates_out[e] = jnp.sum(moved * jnp.concatenate([mask, mask], axis=1), axis=1, keepdims=True)


def route(picks, tokens, router_t, columns):
    blocks = tokens.shape[0]
    slots = picks.shape[1] // EXP_DEV
    total = blocks * slots
    experts = router_t.shape[0]
    return pl.pallas_call(
        route_kernel,
        grid=(blocks,),
        out_shape=(
            jax.ShapeDtypeStruct((EXP_DEV, total, D), BF16),
            jax.ShapeDtypeStruct((blocks, TOK_DEV, experts), F32),
            jax.ShapeDtypeStruct((EXP_DEV, total, 1), F32),
        ),
        in_specs=[
            blocks_of(picks.shape[1:]), blocks_of((TOK_DEV, D)), whole(router_t.shape),
            whole(columns.shape),
        ],
        out_specs=[slots_of(slots, D), blocks_of((TOK_DEV, experts)), slots_of(slots, 1)],
        compiler_params=pltpu.CompilerParams(vmem_limit_bytes=VLIM),
        name="route",
    )(picks, tokens, router_t, columns)


FT = 256


def active_kernel(x_ref, g_ref, w_ref, u_ref, gates, gated, grad_gate, grad_up, dots):
    @pl.when(pl.program_id(1) == 0)
    def _():
        dots[...] = jnp.zeros_like(dots)

    gate_pre = dot_nn(x_ref[0], g_ref[0])
    up_pre = dot_nn(x_ref[0], w_ref[0])
    sig = jax.nn.sigmoid(gate_pre)
    silu = gate_pre * sig
    hidden = silu * up_pre
    back = u_ref[0]
    gate = gates[0]
    dots[0] += jnp.sum(hidden * back, axis=1, keepdims=True)
    gated[0] = (hidden * gate).astype(BF16)
    back = back * gate
    grad_gate[0] = (back * up_pre * (sig * (1.0 + gate_pre * (1.0 - sig)))).astype(BF16)
    grad_up[0] = (back * silu).astype(BF16)


def active(x, w_gate, w_up, u, gates):
    _, total, _ = x.shape
    ff = w_up.shape[2]
    tile = pl.BlockSpec((1, total, FT), lambda e, j: (e, 0, j))
    weight = pl.BlockSpec((1, D, FT), lambda e, j: (e, 0, j))
    column = pl.BlockSpec((1, total, 1), lambda e, j: (e, 0, 0))
    low = jax.ShapeDtypeStruct((EXP_DEV, total, ff), BF16)
    return pl.pallas_call(
        active_kernel,
        grid=(EXP_DEV, ff // FT),
        out_shape=(low, low, low, jax.ShapeDtypeStruct((EXP_DEV, total, 1), F32)),
        in_specs=[
            pl.BlockSpec((1, total, D), lambda e, j: (e, 0, 0)), weight, weight, tile, column,
        ],
        out_specs=[tile, tile, tile, column],
        compiler_params=pltpu.CompilerParams(vmem_limit_bytes=VLIM),
        name="active",
    )(x, w_gate, w_up, u, gates)


def rows_back_kernel(a_ref, b_ref, g_ref, w_ref, out):
    out[0] = (dot_nt(a_ref[0], g_ref[0]) + dot_nt(b_ref[0], w_ref[0])).astype(BF16)


def rows_back(grad_gate_pre, grad_up_pre, w_gate, w_up):
    _, total, ff = grad_up_pre.shape
    size = 512
    row = pl.BlockSpec((1, total, ff), lambda e, j: (e, 0, 0))
    weight = pl.BlockSpec((1, size, ff), lambda e, j: (e, j, 0))
    return pl.pallas_call(
        rows_back_kernel,
        grid=(EXP_DEV, D // size),
        out_shape=jax.ShapeDtypeStruct((EXP_DEV, total, D), BF16),
        in_specs=[row, row, weight, weight],
        out_specs=pl.BlockSpec((1, total, size), lambda e, j: (e, 0, j)),
        compiler_params=pltpu.CompilerParams(vmem_limit_bytes=VLIM),
        name="rows_back",
    )(grad_gate_pre, grad_up_pre, w_gate, w_up)


def combine_kernel(turned, rows_ref, tokens, probs, dots, router, columns, out, router_out):
    @pl.when(pl.program_id(0) == 0)
    def _():
        router_out[...] = jnp.zeros_like(router_out)

    choice = jnp.zeros(probs.shape[1:], F32)
    for e in range(EXP_DEV):
        moved = dot_nn(turned[0, e], dots[e])
        choice += jnp.sum(moved, axis=1, keepdims=True) * columns[e : e + 1, :]
    p = probs[0]
    grad_logits = p * (choice - jnp.sum(p * choice, axis=1, keepdims=True))
    both = two_parts(grad_logits, 1)
    for n in range(D // 512):
        at = pl.ds(n * 512, 512)
        total = dot_nn(both, router[:, at])
        for e in range(EXP_DEV):
            total += dot_nn(turned[0, e], rows_ref[e, :, at])
        out[0, :, at] = total.astype(BF16)
    router_out[...] += dot_tn(both, tokens[0])


def combine(turned, grad_rows, tokens, probs, dots, router_two, columns):
    blocks = tokens.shape[0]
    slots = turned.shape[3]
    return pl.pallas_call(
        combine_kernel,
        grid=(blocks,),
        out_shape=(
            jax.ShapeDtypeStruct((blocks, TOK_DEV, D), BF16),
            jax.ShapeDtypeStruct((router_two.shape[0], D), F32),
        ),
        in_specs=[
            blocks_of(turned.shape[1:]), slots_of(slots, D), blocks_of((TOK_DEV, D)),
            blocks_of(probs.shape[1:]), slots_of(slots, 128), whole(router_two.shape),
            whole(columns.shape),
        ],
        out_specs=[blocks_of((TOK_DEV, D)), whole((router_two.shape[0], D))],
        compiler_params=pltpu.CompilerParams(vmem_limit_bytes=VLIM),
        name="combine",
    )(turned, grad_rows, tokens, probs, dots, router_two, columns)


def rms_parts(values_in):
    inverse = lax.rsqrt(jnp.mean(values_in * values_in, axis=-1, keepdims=True) + EPSILON)
    return (values_in * inverse, inverse)


def rms_back(grad_out, normed, inverse, gain_row):
    scaled = grad_out * gain_row
    grad_in = inverse * (scaled - normed * jnp.mean(scaled * normed, axis=-1, keepdims=True))
    return (grad_in, jnp.sum(grad_out * normed, axis=0))


def angles(positions):
    freqs = ROPE_BASE ** (-2.0 * jnp.arange(HEAD_DIM // 2, dtype=F32) / HEAD_DIM)
    turned = positions.astype(F32)[:, None] * freqs[None, :]
    cosine, sine = jnp.cos(turned), jnp.sin(turned)
    return (jnp.concatenate([cosine, cosine], axis=1), jnp.concatenate([-sine, sine], axis=1))


def two_row_sums(first, second, number, name):
    seq = first.shape[0]
    packed = jnp.concatenate([first, second], axis=0).reshape(2 * seq // 128, 128)
    total = plane_sum(packed, number, name).reshape(2, seq, 1)
    return total[0], total[1]


def plane_back(partial, s, sp):
    total = lax.dynamic_index_in_dim(partial, s, axis=0, keepdims=False).astype(F32)
    for k in (3, 1, 2):
        piece = lax.dynamic_index_in_dim(partial, s ^ k, axis=0, keepdims=False)
        total = total + lax.ppermute(piece, "sp", [(i, i ^ k) for i in range(sp)]).astype(F32)
    return total


def body(
    layer_input, output_grad, w_query, w_key, w_value, w_output, w_router, norm_gains,
    w_gate, w_up, w_down, expert_routes,
):
    fsdp, sp = lax.axis_size("fsdp"), lax.axis_size("sp")
    f, s = lax.axis_index("fsdp"), lax.axis_index("sp")
    count = fsdp * sp
    experts = EXP_DEV * fsdp
    capacity = TOK_DEV * TOP // experts * 17 // 16
    slots = -(-capacity // 16) * 16
    seq = TOK_DEV * sp
    cols = D // sp
    rows = D // count

    down_full = lax.all_gather(w_down, "sp", axis=1, tiled=True)
    gate_full = lax.all_gather(w_gate, "sp", axis=1, tiled=True)
    up_full = lax.all_gather(w_up, "sp", axis=1, tiled=True)

    router_size = rows * experts
    misc = jnp.concatenate([w_router.reshape(router_size), norm_gains.reshape(4 * rows)])
    misc_rows = -(-misc.shape[0] // 2048) * 16
    misc = jnp.pad(misc, (0, misc_rows * 128 - misc.shape[0])).reshape(misc_rows, 128)
    routes = expert_routes.reshape(TOK_DEV * TOP // 128, 128)
    early = TOK_DEV // 4
    x_all, w_all, wo_s, grad_first_half, misc_all, routes_all = gather_start(
        fsdp, sp, layer_input, jnp.stack([w_query, w_key, w_value]), w_output, output_grad[:early],
        misc, routes,
    )
    misc_all = misc_all.reshape(count, misc_rows * 128)
    router_w = misc_all[:, :router_size].reshape(D, experts)
    router_t = router_w.T
    gains_w = misc_all[:, router_size : router_size + 4 * rows].reshape(count, 4, rows)
    gains32 = gains_w.transpose(1, 0, 2).reshape(4, D).astype(F32)
    gains_own = lax.dynamic_slice_in_dim(gains32, s * cols, cols, axis=1)

    routes_block = routes_all.reshape(fsdp, TOK_DEV, TOP)
    own_ids = f * EXP_DEV + jnp.arange(EXP_DEV, dtype=jnp.int32)
    chosen = jnp.any(routes_block[:, :, :, None] == own_ids, axis=2)
    before = jnp.arange(TOK_DEV)[:, None] > jnp.arange(TOK_DEV)[None, :]
    place = jnp.einsum(
        "ut,fte->feu", before.astype(BF16), chosen.astype(BF16), preferred_element_type=F32
    ).astype(jnp.int32)
    slot_ids = jnp.arange(slots, dtype=jnp.int32)
    picks = (
        (place[:, :, None, :] == slot_ids[:, None]) & chosen.transpose(0, 2, 1)[:, :, None, :]
    ).astype(BF16).reshape(fsdp, EXP_DEV * slots, TOK_DEV)
    turned = (
        (place[:, :, :, None] == slot_ids) & chosen.transpose(0, 2, 1)[:, :, :, None]
    ).astype(BF16)
    columns = (jnp.arange(experts, dtype=jnp.int32)[None, :] == own_ids[:, None]).astype(F32)

    first_in, q_raw, k_raw, values, q_square, k_square = project(x_all, gains32, w_all)
    q_square, k_square = two_row_sums(q_square, k_square, 1, "norm_sums")
    q_inverse = lax.rsqrt(q_square / D + EPSILON)
    k_inverse = lax.rsqrt(k_square / D + EPSILON)
    cosine, sine = angles(jnp.arange(seq, dtype=jnp.int32))
    attended, log_sum, queries, keys = attend(
        q_raw, k_raw, values, q_inverse, k_inverse, gains_own, cosine, sine
    )
    branch = dot_nn(attended, wo_s).astype(BF16).reshape(sp, TOK_DEV, D)
    inputs = layer_input.astype(F32)
    branch, grad_second_half = branch_sum(fsdp, branch, output_grad[early:])
    mid = inputs + branch
    normed_m, inverse_m = rms_parts(mid)
    second_in = (normed_m * gains32[1]).astype(BF16)

    tokens, grad_taken, unscaled = token_gather(
        fsdp, second_in, grad_first_half, grad_second_half, picks, down_full
    )
    received, probs, slot_gates = route(picks, tokens, router_t, columns)
    gated, grad_gate_pre, grad_up_pre, slot_dots = active(
        received, gate_full, up_full, unscaled, slot_gates
    )
    dots_two = jnp.pad(two_parts(slot_dots, 2), ((0, 0), (0, 0), (0, 126)))
    grad_rows = rows_back(grad_gate_pre, grad_up_pre, gate_full, up_full)
    second_part, router_two = combine(
        turned, grad_rows, tokens, probs, dots_two, jnp.concatenate([router_t, router_t], axis=0),
        columns,
    )
    grad_router = (router_two[:experts] + router_two[experts:]).T

    def shed(grad):
        return lax.psum_scatter(grad, "sp", scatter_dimension=1, tiled=True).astype(F32)

    down_part = jnp.einsum("erf,erd->efd", gated, grad_taken, preferred_element_type=F32).astype(BF16)
    grad_down = shed(down_part)
    grad_second, out_part, gate_part, up_part = token_back(
        fsdp, second_part, gated, down_full, turned, received, grad_gate_pre, grad_up_pre
    )
    grad_gate, grad_up = shed(gate_part), shed(up_part)

    grad_final = output_grad.astype(F32)
    grad_mid_norm, gain_m = rms_back(grad_second, normed_m, inverse_m, gains32[1])
    grad_mid = grad_final + grad_mid_norm
    grad_branch, out_sum = branch_back(fsdp, sp, grad_mid.astype(BF16), out_part)
    layer_out = (mid + out_sum).astype(BF16)
    grad_attended = dot_nt(grad_branch, wo_s).astype(BF16)
    grad_w_output = dot_tn(attended, grad_branch).astype(BF16)
    q_scaled, k_scaled, grad_v_low, q_dots, k_dots, gain_qk = attend_back(
        queries, keys, values, grad_attended, log_sum, q_raw, k_raw, q_inverse, k_inverse,
        gains_own, cosine, sine,
    )
    q_mean, k_mean = two_row_sums(q_dots, k_dots, 6, "norm_grad_sums")
    grad_q_low = (q_inverse * (q_scaled - q_raw * (q_inverse * (q_mean / D)))).astype(BF16)
    grad_k_low = (k_inverse * (k_scaled - k_raw * (k_inverse * (k_mean / D)))).astype(BF16)
    grad_first = dot_nt(grad_q_low, w_all[0]) + dot_nt(grad_k_low, w_all[1])
    grad_first = (grad_first + dot_nt(grad_v_low, w_all[2])).astype(BF16)
    grad_first, grad_q_low, grad_k_low, grad_v_low, grad_w_output = lax.optimization_barrier(
        (grad_first, grad_q_low, grad_k_low, grad_v_low, grad_w_output)
    )
    grad_first = plane_back(grad_first.reshape(sp, TOK_DEV, D), s, sp)
    normed_own, inverse_own = rms_parts(inputs)
    grad_in_norm, gain_a = rms_back(grad_first, normed_own, inverse_own, gains32[0])
    input_grad = grad_mid + grad_in_norm

    parts = [
        dot_tn(first_in, low).astype(BF16).reshape(fsdp, D // fsdp, cols)
        for low in (grad_q_low, grad_k_low, grad_v_low)
    ]
    output_part = grad_w_output.reshape(fsdp, rows, sp, cols).transpose(0, 2, 1, 3)
    parts.append(output_part.reshape(fsdp, sp * rows, cols))
    summed = line_reduce(fsdp, jnp.concatenate(parts, axis=1), 8, "weight_grads")
    summed, grad_gate, grad_up, grad_down = lax.optimization_barrier(
        (summed, grad_gate, grad_up, grad_down)
    )
    summed = summed.astype(BF16)
    height = D // fsdp
    qkv = summed[: 3 * height].reshape(3, height, cols)
    out_rows = summed[3 * height :].reshape(sp, rows, cols).transpose(1, 0, 2).reshape(rows, D)
    wide = jnp.zeros((2, D), F32)
    wide = lax.dynamic_update_slice(wide, gain_qk, (0, s * cols))
    gain_rows = jnp.concatenate([jnp.stack([gain_a, gain_m]), wide], axis=0)
    small = jnp.concatenate(
        [
            grad_router.reshape(count, router_size),
            gain_rows.reshape(4, count, rows).transpose(1, 0, 2).reshape(count, 4 * rows),
        ],
        axis=1,
    )
    small = jnp.pad(small, ((0, 0), (0, misc_rows * 128 - small.shape[1])))
    qkv_own, grad_output, small_all = exchange_end(
        fsdp, sp, qkv, out_rows, small.reshape(count, misc_rows, 128), 9
    )
    qkv_own = qkv_own.transpose(1, 2, 0, 3).reshape(3, rows, D).astype(F32)
    grad_output = grad_output.astype(F32)
    small_sum = jnp.sum(small_all, axis=0).reshape(misc_rows * 128)
    grad_router_own = small_sum[:router_size].reshape(rows, experts)
    grad_gains = small_sum[router_size : router_size + 4 * rows].reshape(4, rows)
    return (
        layer_out, input_grad, qkv_own[0], qkv_own[1], qkv_own[2], grad_output,
        grad_router_own, grad_gains, grad_gate, grad_up, grad_down,
    )


def solution(mesh):
    both, split = P(("fsdp", "sp"), None), P("fsdp", "sp", None)
    gains = P(None, ("fsdp", "sp"))
    return jax.shard_map(
        body,
        mesh=mesh,
        in_specs=(both,) * 7 + (gains,) + (split,) * 3 + (both,),
        out_specs=(both,) * 7 + (gains,) + (split,) * 3,
        check_vma=False,
    )
```

```python
import functools

import jax
import jax.numpy as jnp
import numpy as np
from jax import lax
from jax.experimental import pallas as pl
from jax.experimental.pallas import tpu as pltpu
from jax.sharding import PartitionSpec as P

D = 2048
HEADS = 16
HEAD_DIM = 128
TOP = 8
EXP_DEV = 2
BLK = 256
TOK_DEV = 256
EPSILON = 1e-05
ROPE_BASE = 10000.0
MASKED = -1000000000.0
SCALE = HEAD_DIM ** (-0.5)
MESH = pl.DeviceIdType.MESH
ANY = pl.BlockSpec(memory_space=pl.ANY)
VMEM = pl.BlockSpec(memory_space=pltpu.VMEM)
VLIM = 60 * 1024 * 1024
F32 = jnp.float32
BF16 = jnp.bfloat16


def remote(src, dst, send_sem, recv_sem, device):
    return pltpu.make_async_remote_copy(
        src_ref=src,
        dst_ref=dst,
        send_sem=send_sem,
        recv_sem=recv_sem,
        device_id=device,
        device_id_type=MESH,
    )


def landed(ref, sem):
    pltpu.make_async_copy(ref, ref, sem).wait()


def signal(sem, device):
    pl.semaphore_signal(sem, inc=1, device_id=device, device_id_type=MESH)


def greet_line(barrier, lines, f, s):
    place, core = f // 2, f % 2
    signal(barrier, (f + 1 - 2 * core, s))

    @pl.when(place > 0)
    def _():
        signal(barrier, (f - 2, s))

    @pl.when(place < lines - 1)
    def _():
        signal(barrier, (f + 2, s))

    return 1 + jnp.where(place > 0, 1, 0) + jnp.where(place < lines - 1, 1, 0)


class LineGather:
    def __init__(self, views, owns, lines, f, s, send, recv):
        self.views, self.owns, self.lines, self.f, self.s = views, owns, lines, f, s
        self.send, self.recv = send, recv
        self.place, self.core = f // 2, f % 2

    def copy(self, v, block, slot, way):
        device = {
            "right": (self.f + 2, self.s),
            "left": (self.f - 2, self.s),
            "partner": (self.f + 1 - 2 * self.core, self.s),
        }[way]
        index = {"right": 0, "left": 1, "partner": 2}[way]
        ref = self.views[v](block)
        own = self.owns[v] if slot == 0 and self.owns[v] is not None else ref
        return remote(own, ref, self.send.at[v, slot, index], self.recv.at[v, block], device)

    def start_own(self, v):
        @pl.when(self.place < self.lines - 1)
        def _():
            self.copy(v, self.f, 0, "right").start()

        @pl.when(self.place > 0)
        def _():
            self.copy(v, self.f, 0, "left").start()

        self.copy(v, self.f, 0, "partner").start()

    def forward(self, v, k):
        place, lines = self.place, self.lines

        @pl.when(place >= k)
        def _():
            block = self.f - 2 * k
            landed(self.views[v](block), self.recv.at[v, block])

            @pl.when(place < lines - 1)
            def _():
                self.copy(v, block, k, "right").start()

            self.copy(v, block, k, "partner").start()

        @pl.when(place + k < lines)
        def _():
            block = self.f + 2 * k
            landed(self.views[v](block), self.recv.at[v, block])

            @pl.when(place > 0)
            def _():
                self.copy(v, block, lines - 1 + k, "left").start()

            self.copy(v, block, lines - 1 + k, "partner").start()

    def finish(self, v):
        place, lines = self.place, self.lines
        for line in range(lines):
            block = 2 * line + 1 - self.core
            landed(self.views[v](block), self.recv.at[v, block])
        self.copy(v, self.f, 0, "partner").wait_send()

        @pl.when(place < lines - 1)
        def _():
            self.copy(v, self.f, 0, "right").wait_send()

        @pl.when(place > 0)
        def _():
            self.copy(v, self.f, 0, "left").wait_send()

        for k in range(1, lines):

            @pl.when(place >= k)
            def _():
                block = self.f - 2 * k

                @pl.when(place < lines - 1)
                def _():
                    self.copy(v, block, k, "right").wait_send()

                self.copy(v, block, k, "partner").wait_send()

            @pl.when(place + k < lines)
            def _():
                block = self.f + 2 * k

                @pl.when(place > 0)
                def _():
                    self.copy(v, block, lines - 1 + k, "left").wait_send()

                self.copy(v, block, lines - 1 + k, "partner").wait_send()


def line_sems(arrays, fsdp):
    lines = fsdp // 2
    return [
        pltpu.SemaphoreType.DMA((arrays, 2 * lines, 3)),
        pltpu.SemaphoreType.DMA((arrays, fsdp)),
    ]


def add_rows(dst, a, b, rows):
    def step(i, carry):
        at = pl.ds(pl.multiple_of(i * 32, 32), 32)
        dst[at, :] = a[at, :].astype(dst.dtype) + b[at, :].astype(dst.dtype)
        return carry

    lax.fori_loop(0, rows // 32, step, 0)


class LineReduce:
    def __init__(self, p_ref, scratch, lines, f, s):
        self.p_ref, self.lines, self.f, self.s = p_ref, lines, f, s
        self.own, self.paired, self.got, self.last = scratch[:4]
        self.psend, self.precv, self.send, self.recv, self.final, self.local = scratch[4:]
        self.place, self.core = f // 2, f % 2
        self.rows = p_ref.shape[1]
        self.order = []
        for n in range(lines):
            for d in (lines - 1 - n, n):
                if d not in self.order:
                    self.order.append(d)

    @staticmethod
    def scratch(fsdp, block):
        lines = fsdp // 2
        dma = pltpu.SemaphoreType.DMA
        return [
            pltpu.VMEM((lines,) + block, BF16),
            pltpu.VMEM((lines,) + block, BF16),
            pltpu.VMEM((lines,) + block, BF16),
            pltpu.VMEM(block, BF16),
            dma((lines,)), dma((lines,)), dma((lines,)), dma((lines,)), dma, dma((lines,)),
        ]

    def load(self, i):
        return pltpu.make_async_copy(self.p_ref.at[2 * i + self.core], self.own.at[i], self.local.at[i])

    def swap(self, i):
        return remote(
            self.p_ref.at[2 * i + 1 - self.core], self.paired.at[i], self.psend.at[i],
            self.precv.at[i], (self.f + 1 - 2 * self.core, self.s),
        )

    def right(self, d, last):
        dst = self.last if last else self.got.at[d]
        sem = self.final if last else self.recv.at[d]
        return remote(self.own.at[d], dst, self.send.at[d], sem, (self.f + 2, self.s))

    def left(self, d):
        return remote(
            self.own.at[d], self.got.at[d], self.send.at[d], self.recv.at[d], (self.f - 2, self.s)
        )

    def start(self):
        for i in self.order:
            self.swap(i).start()
        for i in self.order:
            self.load(i).start()
        self.added = 0
        self.add_pairs(2)

    def add_pairs(self, until):
        for i in self.order[self.added : until]:
            self.load(i).wait()
            landed(self.paired.at[i], self.precv.at[i])
            add_rows(self.own.at[i], self.own.at[i], self.paired.at[i], self.rows)
        self.added = max(self.added, until)

    def step(self, t):
        place, lines = self.place, self.lines
        d = lines - 1 - t + place

        @pl.when(t >= place)
        def _():
            @pl.when(place > 0)
            def _():
                landed(self.got.at[d], self.recv.at[d])
                add_rows(self.own.at[d], self.own.at[d], self.got.at[d], self.rows)

            @pl.when(d == place + 1)
            def _():
                self.right(d, True).start()

            @pl.when(d != place + 1)
            def _():
                self.right(d, False).start()

        e = t - (lines - 1 - place)

        @pl.when(e >= 0)
        def _():
            @pl.when(place < lines - 1)
            def _():
                landed(self.got.at[e], self.recv.at[e])
                add_rows(self.own.at[e], self.own.at[e], self.got.at[e], self.rows)

            self.left(e).start()

        self.add_pairs(2 * t + 4)

    def finish(self, out_ref):
        place, lines, rows = self.place, self.lines, self.rows

        def first(i, carry):
            at = pl.ds(pl.multiple_of(i * 32, 32), 32)
            out_ref[at, :] = self.own[place, at, :].astype(F32)
            return carry

        lax.fori_loop(0, rows // 32, first, 0)

        @pl.when(place > 0)
        def _():
            landed(self.last, self.final)
            add_rows(out_ref, out_ref, self.last, rows)

        @pl.when(place < lines - 1)
        def _():
            landed(self.got.at[place], self.recv.at[place])
            add_rows(out_ref, out_ref, self.got.at[place], rows)

        for i in range(lines):
            self.swap(i).wait_send()

            @pl.when(place < i)
            def _():
                self.right(i, False).wait_send()

            @pl.when(place > i)
            def _():
                self.left(i).wait_send()


class PlaneGather:
    def __init__(self, own, out, f, s, send, recv):
        self.own, self.out, self.f, self.s, self.send, self.recv = own, out, f, s, send, recv
        self.rows = own.shape[0]
        self.half = self.rows // 2

    def at(self, place, first, size):
        return self.out.at[pl.ds(pl.multiple_of(place * self.rows + first, self.half), size), :]

    def near(self, k):
        return remote(
            self.own, self.at(self.s, 0, self.rows), self.send.at[k - 1], self.recv.at[k - 1],
            (self.f, self.s ^ k),
        )

    def on(self, k):
        ref = self.at(self.s ^ k, (k - 1) * self.half, self.half)
        return remote(ref, ref, self.send.at[k + 1], self.recv.at[k + 1], (self.f, self.s ^ (3 - k)))

    def start(self):
        self.near(1).start()
        self.near(2).start()

    def forward(self):
        for k in (1, 2):
            landed(self.at(self.s ^ k, 0, self.rows), self.recv.at[k - 1])
            self.on(k).start()

    def finish(self):
        landed(self.at(self.s ^ 3, 0, self.half), self.recv.at[2])
        landed(self.at(self.s ^ 3, self.half, self.half), self.recv.at[3])
        for k in (1, 2):
            self.near(k).wait_send()
            self.on(k).wait_send()


class AnyGather:
    def __init__(self, own, out, f, s, sp, send, recv):
        self.own, self.out, self.f, self.s, self.sp = own, out, f, s, sp
        self.send, self.recv = send, recv
        self.rows = own.shape[0]

    def at(self, place, first, size):
        return self.out.at[pl.ds(pl.multiple_of(place * self.rows + first, size), size), :]

    def copy(self, k):
        dst = self.at(self.s, 0, self.rows)
        return remote(self.own, dst, self.send.at[k], self.recv.at[k], (self.f, self.s ^ k))

    def start(self):
        for k in range(1, self.sp):
            self.copy(k).start()

    def forward(self):
        pass

    def finish(self):
        for k in range(1, self.sp):
            landed(self.at(self.s ^ k, 0, self.rows), self.recv.at[k])
            self.copy(k).wait_send()


class AnyReduce:
    def __init__(self, p_ref, out_ref, scratch, f, s, sp):
        self.p_ref, self.out_ref, self.f, self.s, self.sp = p_ref, out_ref, f, s, sp
        self.own, self.got, self.send, self.recv, self.local = scratch

    @staticmethod
    def scratch(block, sp):
        dma = pltpu.SemaphoreType.DMA
        return [
            pltpu.VMEM(block, BF16), pltpu.VMEM((sp,) + block, BF16), dma((sp,)), dma((sp,)), dma,
        ]

    def copy(self, k):
        d = self.s ^ k
        return remote(
            self.p_ref.at[d], self.got.at[k], self.send.at[k], self.recv.at[k], (self.f, d)
        )

    def load(self):
        return pltpu.make_async_copy(self.p_ref.at[self.s], self.own, self.local)

    def start(self):
        for k in range(1, self.sp):
            self.copy(k).start()
        self.load().start()

    def forward(self):
        self.load().wait()

    def finish(self):
        rows = self.own.shape[0]
        for k in range(1, self.sp):
            landed(self.got.at[k], self.recv.at[k])
            add_rows(self.out_ref, self.own if k == 1 else self.out_ref, self.got.at[k], rows)
        for k in range(1, self.sp):
            self.copy(k).wait_send()


def plane_gather_of(own, out, f, s, sp, send, recv):
    if sp == 4:
        return PlaneGather(own, out, f, s, send, recv)
    return AnyGather(own, out, f, s, sp, send, recv)


def plane_reduce_of(p_ref, out_ref, scratch, f, s, sp):
    if sp == 4:
        return PlaneReduce(p_ref, out_ref, scratch, f, s)
    return AnyReduce(p_ref, out_ref, scratch, f, s, sp)


def plane_scratch(block, sp):
    return PlaneReduce.scratch(block) if sp == 4 else AnyReduce.scratch(block, sp)


class PlaneReduce:
    WAYS = ((0, 1, 1), (1, 2, 2))

    def __init__(self, p_ref, out_ref, scratch, f, s):
        self.p_ref, self.out_ref, self.f, self.s = p_ref, out_ref, f, s
        self.own, self.got, self.got_on, self.send, self.recv, self.local = scratch
        self.half = p_ref.shape[1] // 2

    @staticmethod
    def scratch(block):
        dma = pltpu.SemaphoreType.DMA
        return [
            pltpu.VMEM((3,) + block, BF16), pltpu.VMEM((2,) + block, BF16),
            pltpu.VMEM(block, BF16), dma((2, 3)), dma((2, 3)), dma((3,)),
        ]

    def part(self, ref, h):
        return ref.at[pl.ds(h * self.half, self.half), :]

    def load(self, n):
        d = (self.s, self.s ^ 2, self.s ^ 1)[n]
        return pltpu.make_async_copy(self.p_ref.at[d], self.own.at[n], self.local.at[n])

    def hop(self, h, k, far):
        d = self.s ^ 3 if far else self.s ^ k
        n = 0 if far else 1
        return remote(
            self.part(self.p_ref.at[d], h), self.part(self.got.at[1 - n], h), self.send.at[h, n],
            self.recv.at[h, n], (self.f, self.s ^ k),
        )

    def on(self, h, k, n):
        return remote(
            self.part(self.own.at[n], h), self.part(self.got_on, h), self.send.at[h, 2],
            self.recv.at[h, 2], (self.f, self.s ^ (3 - k)),
        )

    def start(self):
        for far in (True, False):
            for h, k, _ in self.WAYS:
                self.hop(h, k, far).start()
        for n in range(3):
            self.load(n).start()

    def forward(self):
        for n in range(3):
            self.load(n).wait()
        for h, k, n in self.WAYS:
            mine = self.part(self.own.at[n], h)
            landed(self.part(self.got.at[1], h), self.recv.at[h, 0])
            add_rows(mine, mine, self.part(self.got.at[1], h), self.half)
            self.on(h, k, n).start()

    def finish(self):
        for h in (0, 1):
            landed(self.part(self.got.at[0], h), self.recv.at[h, 1])
            add_rows(
                self.part(self.out_ref, h), self.part(self.own.at[0], h), self.part(self.got.at[0], h),
                self.half,
            )
        for h in (0, 1):
            landed(self.part(self.got_on, h), self.recv.at[h, 2])
            out = self.part(self.out_ref, h)
            add_rows(out, out, self.part(self.got_on, h), self.half)
        for h, k, n in self.WAYS:
            self.hop(h, k, True).wait_send()
            self.hop(h, k, False).wait_send()
            self.on(h, k, n).wait_send()


def greet_plane(barrier, f, s, sp):
    ways = (1, 2) if sp == 4 else range(1, sp)
    for k in ways:
        signal(barrier, (f, s ^ k))
    return len(ways)


def greet_all(barrier, me, count, sp):
    def greet(i, carry):
        other = lax.rem(me + i, count)
        signal(barrier, (other // sp, lax.rem(other, sp)))
        return carry

    lax.fori_loop(1, count, greet, 0)


def rows_view(ref, rows):
    return lambda b: ref.at[pl.ds(pl.multiple_of(b * rows, rows), rows), :]


def block_view(ref):
    return lambda b: ref.at[b]


def comm_params(number):
    return pltpu.CompilerParams(
        collective_id=number, has_side_effects=True, vmem_limit_bytes=VLIM
    )


def start_kernel(
    fsdp, sp, x_ref, w_ref, wo_ref, g_ref, misc_ref, routes_ref,
    x_all, w_all, wo_all, g_all, misc_all, routes_all,
    send, recv, xsend, xrecv, psend, precv, wsend, wrecv, msend, mrecv, rsend, rrecv, local,
):
    f, s = lax.axis_index("fsdp"), lax.axis_index("sp")
    count, lines = fsdp * sp, fsdp // 2
    me = f * sp + s
    rows = w_ref.shape[1]
    cols = D // sp
    barrier = pltpu.get_barrier_semaphore()

    def w_block(s_to):
        return w_ref.at[:, :, pl.ds(pl.multiple_of(s_to * cols, cols), cols)]

    def w_rows(i):
        return w_all.at[:, pl.ds(pl.multiple_of(i * rows, rows), rows), :]

    def w_view(b):
        size = rows * sp
        return w_all.at[:, pl.ds(pl.multiple_of(b * size, size), size), :]

    wo_view = rows_view(wo_all, rows)
    x_view = rows_view(x_all, TOK_DEV)
    owns = [
        pltpu.make_async_copy(w_block(s), w_rows(me), local.at[0]),
        pltpu.make_async_copy(x_ref, x_view(s), local.at[1]),
        pltpu.make_async_copy(misc_ref, misc_all.at[me], local.at[2]),
        pltpu.make_async_copy(routes_ref, routes_all.at[f], local.at[3]),
        pltpu.make_async_copy(g_ref, g_all.at[f], local.at[4]),
    ]
    for copy in owns:
        copy.start()
    greet_all(barrier, me, count, sp)
    pl.semaphore_wait(barrier, count - 1)

    line = LineGather([w_view, wo_view, block_view(g_all)], [None, None, g_ref], lines, f, s, send, recv)
    line.start_own(2)
    w_copies = []
    for k in range(sp - 1, 0, -1):
        s_to = s ^ k
        copy = remote(w_block(s_to), w_rows(me), psend.at[k], precv.at[k], (f, s_to))
        copy.start()
        w_copies.append(copy)
    target_s, target_f = me // fsdp, lax.rem(me, fsdp)
    stays = jnp.logical_and(target_s == s, target_f == f)
    wo_copy = remote(wo_ref, wo_view(target_f), wsend, wrecv, (target_f, target_s))
    wo_own = pltpu.make_async_copy(wo_ref, wo_view(f), wrecv)

    @pl.when(stays)
    def _():
        wo_own.start()

    @pl.when(jnp.logical_not(stays))
    def _():
        wo_copy.start()

    def misc_copy(i):
        other = lax.rem(me + i, count)
        return remote(
            misc_ref, misc_all.at[me], msend.at[i], mrecv.at[me], (other // sp, lax.rem(other, sp))
        )

    def misc_go(i, carry):
        misc_copy(i).start()
        return carry

    lax.fori_loop(1, count, misc_go, 0)

    def routes_copy(i):
        other = lax.rem(f + i, fsdp)
        return remote(routes_ref, routes_all.at[f], rsend.at[i], rrecv.at[f], (other, s))

    def routes_go(i, carry):
        routes_copy(i).start()
        return carry

    lax.fori_loop(1, fsdp, routes_go, 0)

    owns[0].wait()
    for k in range(1, sp):
        landed(w_rows(f * sp + (s ^ k)), precv.at[k])
    line.start_own(0)
    tokens = plane_gather_of(x_ref, x_all, f, s, sp, xsend, xrecv)
    tokens.start()
    landed(wo_view(f), wrecv)
    line.start_own(1)
    for k in range(1, lines):
        for v in (2, 0, 1):
            line.forward(v, k)
        if k == min(2, lines - 1):
            tokens.forward()
    for v in range(3):
        line.finish(v)
    tokens.finish()

    def misc_end(i, carry):
        misc_copy(i).wait_send()
        other = lax.rem(me + i, count)
        landed(misc_all.at[other], mrecv.at[other])
        return carry

    lax.fori_loop(1, count, misc_end, 0)

    def routes_end(i, carry):
        routes_copy(i).wait_send()
        other = lax.rem(f + i, fsdp)
        landed(routes_all.at[other], rrecv.at[other])
        return carry

    lax.fori_loop(1, fsdp, routes_end, 0)
    for copy in w_copies:
        copy.wait_send()

    @pl.when(jnp.logical_not(stays))
    def _():
        wo_copy.wait_send()

    for copy in owns[1:]:
        copy.wait()


def gather_start(fsdp, sp, x, w, wo, g, misc, routes):
    count = fsdp * sp
    dma = pltpu.SemaphoreType.DMA
    return pl.pallas_call(
        functools.partial(start_kernel, fsdp, sp),
        out_shape=(
            jax.ShapeDtypeStruct((sp * TOK_DEV, D), BF16),
            jax.ShapeDtypeStruct((3, D, D // sp), BF16),
            jax.ShapeDtypeStruct((D // sp, D), BF16),
            jax.ShapeDtypeStruct((fsdp,) + g.shape, BF16),
            jax.ShapeDtypeStruct((count,) + misc.shape, BF16),
            jax.ShapeDtypeStruct((fsdp,) + routes.shape, jnp.int32),
        ),
        in_specs=[VMEM] * 6,
        out_specs=[ANY] * 6,
        scratch_shapes=line_sems(3, fsdp)
        + [
            dma((sp,)), dma((sp,)), dma((sp,)), dma((sp,)), dma, dma,
            dma((count,)), dma((count,)), dma((fsdp,)), dma((fsdp,)), dma((5,)),
        ],
        compiler_params=comm_params(0),
        name="gather_start",
    )(x, w, wo, g, misc, routes)


def branch_kernel(fsdp, sp, p_ref, g_ref, out_ref, g_all, *scratch):
    f, s = lax.axis_index("fsdp"), lax.axis_index("sp")
    lines = fsdp // 2
    barrier = pltpu.get_barrier_semaphore()
    expected = greet_line(barrier, lines, f, s) + greet_plane(barrier, f, s, sp)
    send, recv, own_sem = scratch[-3:]
    own = pltpu.make_async_copy(g_ref, g_all.at[f], own_sem)
    own.start()
    pl.semaphore_wait(barrier, expected)
    plane = plane_reduce_of(p_ref, out_ref, scratch[:-3], f, s, sp)
    line = LineGather([block_view(g_all)], [g_ref], lines, f, s, send, recv)
    plane.start()
    line.start_own(0)
    for k in range(1, lines):
        line.forward(0, k)
        if k == min(2, lines - 1):
            plane.forward()
    plane.finish()
    line.finish(0)
    own.wait()


def branch_sum(fsdp, partial, g):
    sp, block = partial.shape[0], partial.shape[1:]
    return pl.pallas_call(
        functools.partial(branch_kernel, fsdp, sp),
        out_shape=(jax.ShapeDtypeStruct(block, F32), jax.ShapeDtypeStruct((fsdp,) + g.shape, BF16)),
        in_specs=[ANY, VMEM],
        out_specs=[VMEM, ANY],
        scratch_shapes=plane_scratch(block, sp) + line_sems(1, fsdp) + [pltpu.SemaphoreType.DMA],
        compiler_params=comm_params(2),
        name="branch_sum",
    )(partial, g)


def token_kernel(
    fsdp, x_ref, g_first, g_second, picks, w_ref, out_ref, taken_ref, back_ref,
    g_buf, w_buf, taken, back, send, recv, local, loads, stores, back_sem,
):
    f, s = lax.axis_index("fsdp"), lax.axis_index("sp")
    lines = fsdp // 2
    parts = 2
    size = TOK_DEV // parts
    early, later = g_first.shape[1], g_second.shape[1]
    slots = picks.shape[1] // EXP_DEV
    ff = w_ref.shape[1]
    barrier = pltpu.get_barrier_semaphore()
    expected = greet_line(barrier, lines, f, s)
    own = pltpu.make_async_copy(x_ref, out_ref.at[f], local)
    own.start()
    reads = [
        pltpu.make_async_copy(g_first, g_buf.at[:, pl.ds(0, early), :], loads.at[0]),
        pltpu.make_async_copy(g_second, g_buf.at[:, pl.ds(early, later), :], loads.at[1]),
        pltpu.make_async_copy(w_ref, w_buf, loads.at[2]),
    ]
    for copy in reads:
        copy.start()
    pl.semaphore_wait(barrier, expected)

    def view(part):
        return lambda b: out_ref.at[b, pl.ds(part * size, size), :]

    owns = [x_ref.at[pl.ds(p * size, size), :] for p in range(parts)]
    line = LineGather([view(p) for p in range(parts)], owns, lines, f, s, send, recv)
    for p in range(parts):
        line.start_own(p)

    def take_all():
        reads[0].wait()
        reads[1].wait()

        def block(b, carry):
            for n in range(D // 512):
                at = pl.ds(n * 512, 512)
                got = dot_nn(picks[b], g_buf[b, :, at]).astype(BF16)
                for e in range(EXP_DEV):
                    to = pl.ds(pl.multiple_of(b * slots, 16), slots)
                    taken[e, to, at] = got[e * slots : (e + 1) * slots]
            return carry

        lax.fori_loop(0, fsdp, block, 0)
        for e in range(EXP_DEV):
            pltpu.make_async_copy(taken.at[e], taken_ref.at[e], stores.at[e]).start()

    def back_copy(e, j, slot):
        at = pl.ds(pl.multiple_of(j * FT, FT), FT)
        return pltpu.make_async_copy(back.at[slot], back_ref.at[e, :, at], back_sem.at[slot])

    def back_of(e):
        if e == 0:
            reads[2].wait()
        for j in range(ff // FT):
            slot = j % 2
            if e > 0 or j > 1:
                back_copy(e, j, slot).wait()
            back[slot] = dot_nt(taken[e], w_buf[e, pl.ds(j * FT, FT), :])
            back_copy(e, j, slot).start()

    work = [take_all] + [functools.partial(back_of, e) for e in range(EXP_DEV)]
    for k in range(1, lines):
        if k - 1 < len(work):
            work[k - 1]()
        for p in range(parts):
            line.forward(p, k)
    for unit in work[lines - 1 :]:
        unit()
    for p in range(parts):
        line.finish(p)
    own.wait()
    for slot in range(2):
        back_copy(0, slot, slot).wait()
    for e in range(EXP_DEV):
        pltpu.make_async_copy(taken.at[e], taken_ref.at[e], stores.at[e]).wait()


def token_gather(fsdp, x, g_first, g_second, picks, w_down):
    slots = picks.shape[1] // EXP_DEV
    total = fsdp * slots
    ff = w_down.shape[1]
    dma = pltpu.SemaphoreType.DMA
    return pl.pallas_call(
        functools.partial(token_kernel, fsdp),
        out_shape=(
            jax.ShapeDtypeStruct((fsdp, TOK_DEV, D), BF16),
            jax.ShapeDtypeStruct((EXP_DEV, total, D), BF16),
            jax.ShapeDtypeStruct((EXP_DEV, total, ff), F32),
        ),
        in_specs=[VMEM, ANY, ANY, VMEM, ANY],
        out_specs=[ANY, ANY, ANY],
        scratch_shapes=[
            pltpu.VMEM((fsdp, TOK_DEV, D), BF16),
            pltpu.VMEM((EXP_DEV, ff, D), BF16),
            pltpu.VMEM((EXP_DEV, total, D), BF16),
            pltpu.VMEM((2, total, FT), F32),
        ]
        + line_sems(2, fsdp)
        + [dma, dma((3,)), dma((EXP_DEV,)), dma((2,))],
        compiler_params=comm_params(3),
        name="token_gather",
    )(x, g_first, g_second, picks, w_down)


def token_back_kernel(
    fsdp, p_ref, gated_ref, w_ref, turned, x_ref, gg_ref, gu_ref,
    out_ref, part_ref, wg_ref, wu_ref,
    wide, narrow, w_buf, tile, grad_tile, loads, tile_sem, grad_sem, *scratch,
):
    f, s = lax.axis_index("fsdp"), lax.axis_index("sp")
    lines = fsdp // 2
    slots = turned.shape[3]
    height = grad_tile.shape[1]
    barrier = pltpu.get_barrier_semaphore()
    expected = greet_line(barrier, lines, f, s)
    reads = [
        pltpu.make_async_copy(gated_ref, narrow, loads.at[0]),
        pltpu.make_async_copy(w_ref, w_buf, loads.at[1]),
        pltpu.make_async_copy(x_ref, wide, loads.at[2]),
        pltpu.make_async_copy(gg_ref.at[0], narrow.at[0], loads.at[3]),
        pltpu.make_async_copy(gu_ref.at[0], narrow.at[1], loads.at[4]),
        pltpu.make_async_copy(gg_ref.at[1], narrow.at[0], loads.at[3]),
        pltpu.make_async_copy(gu_ref.at[1], narrow.at[1], loads.at[4]),
    ]
    reads[0].start()
    reads[1].start()
    pl.semaphore_wait(barrier, expected)
    line = LineReduce(p_ref, scratch, lines, f, s)
    line.start()

    def down_of(e):
        if e == 0:
            reads[0].wait()
            reads[1].wait()

        def columns(n, carry):
            at = pl.ds(pl.multiple_of(n * 512, 512), 512)
            wide[e, :, at] = dot_nn(narrow[e], w_buf[e, :, at]).astype(BF16)
            return carry

        lax.fori_loop(0, D // 512, columns, 0)

    def tile_copy(b, slot):
        return pltpu.make_async_copy(tile.at[slot], part_ref.at[b], tile_sem.at[slot])

    def sum_all():
        reads[3].start()
        reads[4].start()

        def pair(i, carry):
            for slot in range(2):
                b = 2 * i + slot

                @pl.when(i > 0)
                def _():
                    tile_copy(b, slot).wait()

                for n in range(D // 512):
                    at = pl.ds(n * 512, 512)
                    summed = jnp.zeros((TOK_DEV, 512), F32)
                    for e in range(EXP_DEV):
                        rows = wide[e, pl.ds(pl.multiple_of(b * slots, 16), slots), at]
                        summed += dot_nn(turned[b, e], rows)
                    tile[slot, :, at] = summed.astype(BF16)
                tile_copy(b, slot).start()
            return carry

        lax.fori_loop(0, fsdp // 2, pair, 0)
        reads[2].start()

    def grad_copy(to, e, i, slot):
        at = pl.ds(pl.multiple_of(i * height, height), height)
        return pltpu.make_async_copy(grad_tile.at[slot], to.at[e, at, :], grad_sem.at[slot])

    def grad_of(e, n, to, first):
        if n == 0 and e == 0:
            reads[2].wait()
            reads[3].wait()
            reads[4].wait()
        if n == 0 and e == 1:
            reads[5].wait()
            reads[6].wait()

        def pair(i, carry):
            for slot in range(2):
                part = 2 * i + slot

                def before():
                    grad_copy(to, e, part, slot).wait()

                if first:
                    pl.when(i > 0)(before)
                else:
                    before()
                at = pl.ds(pl.multiple_of(part * height, height), height)
                grad_tile[slot] = dot_tn(wide[e, :, at], narrow[n]).astype(BF16)
                grad_copy(to, e, part, slot).start()
            return carry

        lax.fori_loop(0, D // height // 2, pair, 0)
        if n == 1 and e == 0:
            reads[5].start()
            reads[6].start()

    work = [functools.partial(down_of, e) for e in range(EXP_DEV)] + [sum_all]
    for e in range(EXP_DEV):
        for n, to in ((0, wg_ref), (1, wu_ref)):
            work.append(functools.partial(grad_of, e, n, to, e == 0 and n == 0))
    done = 0
    for t in range(lines - 1):
        line.step(t)
        until = (t + 1) * len(work) // (lines - 1)
        for unit in work[done:until]:
            unit()
        done = until
    line.finish(out_ref)
    for slot in range(2):
        tile_copy(slot, slot).wait()
        grad_copy(wg_ref, 0, slot, slot).wait()


def token_back(fsdp, partial, gated, w_down, turned, received, grad_gate_pre, grad_up_pre):
    block = partial.shape[1:]
    total, ff = gated.shape[1:]
    height = 256
    dma = pltpu.SemaphoreType.DMA
    weight = jax.ShapeDtypeStruct((EXP_DEV, D, ff), BF16)
    return pl.pallas_call(
        functools.partial(token_back_kernel, fsdp),
        out_shape=(
            jax.ShapeDtypeStruct(block, F32),
            jax.ShapeDtypeStruct(partial.shape, BF16),
            weight,
            weight,
        ),
        in_specs=[ANY, ANY, ANY, VMEM, ANY, ANY, ANY],
        out_specs=[VMEM, ANY, ANY, ANY],
        scratch_shapes=[
            pltpu.VMEM((EXP_DEV, total, D), BF16),
            pltpu.VMEM((EXP_DEV, total, ff), BF16),
            pltpu.VMEM((EXP_DEV, ff, D), BF16),
            pltpu.VMEM((2,) + block, BF16),
            pltpu.VMEM((2, height, ff), BF16),
            dma((5,)),
            dma((2,)),
            dma((2,)),
        ]
        + LineReduce.scratch(fsdp, block),
        compiler_params=comm_params(4),
        name="token_back",
    )(partial, gated, w_down, turned, received, grad_gate_pre, grad_up_pre)


class PlaneSum:
    def __init__(self, scratch, f, s, sp):
        self.own, self.got, self.send, self.recv = scratch
        self.f, self.s, self.sp = f, s, sp

    @staticmethod
    def scratch(seq, sp):
        dma = pltpu.SemaphoreType.DMA
        return [
            pltpu.VMEM((8, seq), F32), pltpu.VMEM((sp, 8, seq), F32), dma((sp,)), dma((sp,)),
        ]

    def greet(self, barrier):
        for k in range(1, self.sp):
            signal(barrier, (self.f, self.s ^ k))
        return self.sp - 1

    def copy(self, k):
        return remote(
            self.own, self.got.at[k], self.send.at[k], self.recv.at[k], (self.f, self.s ^ k)
        )

    def start(self, x_ref):
        self.own[...] = x_ref[...].T[:8]
        for k in range(1, self.sp):
            self.copy(k).start()

    def finish(self, out_ref):
        for k in range(1, self.sp):
            self.copy(k).wait()
        terms = [self.own[...]] + [self.got[k] for k in range(1, self.sp)]
        while len(terms) > 1:
            terms = [terms[i] + terms[i + 1] for i in range(0, len(terms), 2)]
        seq = out_ref.shape[0]
        out_ref[...] = jnp.concatenate([terms[0], jnp.zeros((120, seq), F32)], axis=0).T


def plane_sum_kernel(sp, x_ref, out_ref, *scratch):
    f, s = lax.axis_index("fsdp"), lax.axis_index("sp")
    total = PlaneSum(scratch, f, s, sp)
    barrier = pltpu.get_barrier_semaphore()
    pl.semaphore_wait(barrier, total.greet(barrier))
    total.start(x_ref)
    total.finish(out_ref)


def plane_sum(sp, x, number, name):
    seq = x.shape[0]
    return pl.pallas_call(
        functools.partial(plane_sum_kernel, sp),
        out_shape=jax.ShapeDtypeStruct(x.shape, F32),
        in_specs=[VMEM],
        out_specs=VMEM,
        scratch_shapes=PlaneSum.scratch(seq, sp),
        compiler_params=comm_params(number),
        name=name,
    )(x)


def end_kernel(
    fsdp, sp, p_ref, b_ref, x_ref, mid_ref, gain, gains_in, router_ref,
    grad_out, qkv_0, qkv_1, qkv_2, o_out, small_out,
    back, summed, low, o_low, gain_sum, pay, small,
    qsend, qrecv, osend, orecv, msend, mrecv, local, *scratch,
):
    f, s = lax.axis_index("fsdp"), lax.axis_index("sp")
    count, lines = fsdp * sp, fsdp // 2
    me = f * sp + s
    rows, cols = o_low.shape[0], D // sp
    height = D // fsdp
    barrier = pltpu.get_barrier_semaphore()
    greet_all(barrier, me, count, sp)
    pl.semaphore_wait(barrier, count - 1)
    plane_parts = 6 if sp == 4 else 5
    plane = plane_reduce_of(b_ref, back, scratch[:plane_parts], f, s, sp)
    line = LineReduce(p_ref, scratch[plane_parts:], lines, f, s)
    plane.start()
    line.start()

    def input_grads():
        gain_sum[...] = jnp.zeros_like(gain_sum)

        def chunk(i, carry):
            at = pl.ds(pl.multiple_of(i * 32, 32), 32)
            x = x_ref[at, :].astype(F32)
            inverse = lax.rsqrt(jnp.mean(x * x, axis=-1, keepdims=True) + EPSILON)
            normed = x * inverse
            grad_y = back[at, :]
            scaled = grad_y * gain[0:1, :]
            mean = jnp.mean(scaled * normed, axis=-1, keepdims=True)
            grad_out[at, :] = mid_ref[at, :] + inverse * (scaled - normed * mean)
            gain_sum[0:1, :] += jnp.sum(grad_y * normed, axis=0, keepdims=True)
            return carry

        lax.fori_loop(0, TOK_DEV // 32, chunk, 0)
        gain_sum[...] += gains_in[...]

        def fill(i, carry):
            at = pl.ds(pl.multiple_of(i * rows // 128 * 128, 128), 128)
            pay[i, 0:8, :] = router_ref[i]
            pay[i, 8:16, :] = gain_sum[:, at]
            return carry

        lax.fori_loop(0, count, fill, 0)

    def m_copy(i):
        other = lax.rem(me + i, count)
        return remote(
            pay.at[other], small.at[me], msend.at[i], mrecv.at[me], (other // sp, lax.rem(other, sp))
        )

    def m_go(i, carry):
        m_copy(i).start()
        return carry

    for t in range(lines - 1):
        line.step(t)
        if t == min(1, lines - 2):
            plane.forward()
    plane.finish()
    input_grads()
    lax.fori_loop(1, count, m_go, 0)
    line.finish(summed)

    def cast(i, carry):
        at = pl.ds(pl.multiple_of(i * 32, 32), 32)
        low[at, :] = summed[at, :].astype(BF16)
        return carry

    lax.fori_loop(0, summed.shape[0] // 32, cast, 0)
    for c in range(sp):
        first = 3 * height + c * rows
        o_low[:, c * cols : (c + 1) * cols] = low[first : first + rows, :]

    def q_from(i, place):
        return low.at[pl.ds(pl.multiple_of(i * height + place * rows, rows), rows), :]

    def q_to(i, place):
        return (qkv_0, qkv_1, qkv_2)[i].at[:, pl.ds(pl.multiple_of(place * cols, cols), cols)]

    def q_copy(i, k):
        return remote(q_from(i, s ^ k), q_to(i, s), qsend.at[k, i], qrecv.at[k, i], (f, s ^ k))

    def q_own(i):
        return pltpu.make_async_copy(q_from(i, s), q_to(i, s), local.at[i])

    for k in range(sp - 1, 0, -1):
        for i in range(3):
            q_copy(i, k).start()
    flat = s * fsdp + f
    target_f, target_s = flat // sp, lax.rem(flat, sp)
    stays = jnp.logical_and(target_s == s, target_f == f)
    o_copy = remote(o_low, o_out, osend, orecv, (target_f, target_s))
    o_own = pltpu.make_async_copy(o_low, o_out, orecv)

    @pl.when(stays)
    def _():
        o_own.start()

    @pl.when(jnp.logical_not(stays))
    def _():
        o_copy.start()

    for i in range(3):
        q_own(i).start()

    def m_end(i, carry):
        m_copy(i).wait_send()
        other = lax.rem(me + i, count)
        landed(small.at[other], mrecv.at[other])
        return carry + small[other]

    small_out[...] = lax.fori_loop(1, count, m_end, pay[me])
    for k in range(1, sp):
        for i in range(3):
            landed(q_to(i, s ^ k), qrecv.at[k, i])
            q_copy(i, k).wait_send()
    landed(o_out, orecv)

    @pl.when(jnp.logical_not(stays))
    def _():
        o_copy.wait_send()

    for i in range(3):
        q_own(i).wait()


def end_exchange(fsdp, sp, partial, back, x, grad_mid, gains, gains_in, router, number):
    count = fsdp * sp
    block = partial.shape[1:]
    rows = D // count
    dma = pltpu.SemaphoreType.DMA
    return pl.pallas_call(
        functools.partial(end_kernel, fsdp, sp),
        out_shape=(
            jax.ShapeDtypeStruct((TOK_DEV, D), F32),
            jax.ShapeDtypeStruct((rows, D), BF16),
            jax.ShapeDtypeStruct((rows, D), BF16),
            jax.ShapeDtypeStruct((rows, D), BF16),
            jax.ShapeDtypeStruct((rows, D), BF16),
            jax.ShapeDtypeStruct((16, 128), F32),
        ),
        in_specs=[ANY, ANY, VMEM, VMEM, VMEM, VMEM, VMEM],
        out_specs=[VMEM, ANY, ANY, ANY, ANY, VMEM],
        scratch_shapes=[
            pltpu.VMEM((TOK_DEV, D), F32),
            pltpu.VMEM(block, F32),
            pltpu.VMEM(block, BF16),
            pltpu.VMEM((rows, D), BF16),
            pltpu.VMEM((8, D), F32),
            pltpu.VMEM((count, 16, 128), F32),
            pltpu.VMEM((count, 16, 128), F32),
            dma((sp, 3)), dma((sp, 3)), dma, dma, dma((count,)), dma((count,)), dma((3,)),
        ]
        + plane_scratch((TOK_DEV, D), sp)
        + LineReduce.scratch(fsdp, block),
        compiler_params=comm_params(number),
        name="end_exchange",
    )(partial, back, x, grad_mid, gains, gains_in, router)


def dot_nt(a, b):
    return lax.dot_general(a, b, (((1,), (1,)), ((), ())), preferred_element_type=F32)


def dot_tn(a, b):
    return lax.dot_general(a, b, (((0,), (0,)), ((), ())), preferred_element_type=F32)


def dot_nn(a, b):
    return jnp.dot(a, b, preferred_element_type=F32)


def whole(shape):
    return pl.BlockSpec(shape, lambda *_: (0,) * len(shape))


def lanes(first, second):
    lane = lax.broadcasted_iota(jnp.int32, (first.shape[0], 128), 1)
    return jnp.where(lane == 0, first, jnp.where(lane == 1, second, 0.0))


def inverse_of(sums, lane):
    return lax.rsqrt(sums[:, lane : lane + 1] / D + EPSILON)


def turn(v, table, sign=1.0):
    half = HEAD_DIM // 2
    front = lax.broadcasted_iota(jnp.int32, table.shape, 1) < half
    turned = pltpu.roll(table, half, 1)
    cosine = jnp.where(front, table, turned)
    sine = jnp.where(front, -turned, table)
    return v * cosine + pltpu.roll(v, half, 1) * (sine * sign)


def turn_back(v, table):
    return turn(v, table, -1.0)


def project_kernel(x_ref, gain, w_ref, first_out, q_out, k_out, v_out, squares):
    x = x_ref[...].astype(F32)
    inverse = lax.rsqrt(jnp.mean(x * x, axis=-1, keepdims=True) + EPSILON)
    first = (x * inverse * gain[0:1, :]).astype(BF16)
    first_out[...] = first
    q = dot_nn(first, w_ref[0])
    q_out[...] = q
    k = dot_nn(first, w_ref[1])
    k_out[...] = k
    squares[...] = lanes(
        jnp.sum(q * q, axis=-1, keepdims=True), jnp.sum(k * k, axis=-1, keepdims=True)
    )
    v_out[...] = dot_nn(first, w_ref[2]).astype(BF16)


def project(x, gains, w):
    seq, cols = x.shape[0], w.shape[2]

    def block(width):
        return pl.BlockSpec((TOK_DEV, width), lambda i: (i, 0))

    return pl.pallas_call(
        project_kernel,
        grid=(seq // TOK_DEV,),
        out_shape=(
            jax.ShapeDtypeStruct((seq, D), BF16),
            jax.ShapeDtypeStruct((seq, cols), F32),
            jax.ShapeDtypeStruct((seq, cols), F32),
            jax.ShapeDtypeStruct((seq, cols), BF16),
            jax.ShapeDtypeStruct((seq, 128), F32),
        ),
        in_specs=[block(D), whole(gains.shape), whole(w.shape)],
        out_specs=[block(D), block(cols), block(cols), block(cols), block(128)],
        compiler_params=pltpu.CompilerParams(vmem_limit_bytes=VLIM),
        name="project",
    )(x, gains, w)


def attend_kernel(
    q_raw, k_raw, v_ref, squares, gain, table, o_ref, sum_ref, q_ref, k_ref
):
    head = pl.program_id(0)

    @pl.when(head == 0)
    def _():
        sum_ref[...] = squares[...]

    q_inv, k_inv = inverse_of(squares, 0), inverse_of(squares, 1)
    q_ref[...] = turn(q_raw[...] * q_inv * gain[2:3, :], table[...]).astype(BF16)
    k_ref[...] = turn(k_raw[...] * k_inv * gain[3:4, :], table[...]).astype(BF16)
    for i in range(q_ref.shape[0] // BLK):
        rows, seen = pl.ds(i * BLK, BLK), pl.ds(0, (i + 1) * BLK)
        scores = dot_nt(q_ref[rows, :], k_ref[seen, :]) * SCALE
        row_max = jnp.max(scores, axis=-1, keepdims=True)
        exp_rows = jnp.exp(scores - row_max)
        row_sum = jnp.sum(exp_rows, axis=-1, keepdims=True)
        probs = (exp_rows / row_sum).astype(BF16)
        o_ref[rows, :] = dot_nn(probs, v_ref[seen, :]).astype(BF16)
        lane = lax.broadcasted_iota(jnp.int32, (BLK, 128), 1)
        sum_ref[rows, :] += jnp.where(lane == head + 2, row_max + jnp.log(row_sum), 0.0)


def attend(q_raw, k_raw, v, squares, gains, table):
    seq, width = v.shape
    heads = width // HEAD_DIM
    spec = pl.BlockSpec((seq, HEAD_DIM), lambda h: (0, h))
    return pl.pallas_call(
        attend_kernel,
        grid=(heads,),
        out_shape=(
            jax.ShapeDtypeStruct((seq, width), BF16),
            jax.ShapeDtypeStruct((seq, 128), F32),
            jax.ShapeDtypeStruct((seq, width), BF16),
            jax.ShapeDtypeStruct((seq, width), BF16),
        ),
        in_specs=[
            spec, spec, spec, whole((seq, 128)),
            pl.BlockSpec((4, HEAD_DIM), lambda h: (0, h)),
            whole((seq, HEAD_DIM)),
        ],
        out_specs=[spec, whole((seq, 128)), spec, spec],
        compiler_params=pltpu.CompilerParams(vmem_limit_bytes=VLIM),
        name="attend",
    )(q_raw, k_raw, v, squares, gains, table)


def attend_back_head(
    h, q_ref, k_ref, v_ref, sums, q_raw, k_raw, gain, table,
    q_scaled, k_scaled, dv_out, dots, gains_out, dv_ref,
):
    head = slice(h * HEAD_DIM, (h + 1) * HEAD_DIM)
    k_scaled[:, head] = jnp.zeros(k_raw[:, head].shape, F32)
    dv_ref[...] = jnp.zeros_like(dv_ref)
    gain_q, gain_k = gain[2:3, head], gain[3:4, head]
    gain_sum = jnp.zeros((1, HEAD_DIM), F32)
    size = BLK if q_ref.shape[0] <= 4 * BLK else BLK // 2
    for i in range(q_ref.shape[0] // size):
        rows, seen = pl.ds(i * size, size), pl.ds(0, (i * size // BLK + 1) * BLK)
        q, g, keys = q_ref[rows, head], dv_out[rows, head], k_ref[seen, head]
        scores = dot_nt(q, keys) * SCALE
        probs = jnp.exp(scores - sums[rows, h + 2 : h + 3])
        grad_probs = dot_nt(g, v_ref[seen, head])
        row_dot = jnp.sum(probs * grad_probs, axis=-1, keepdims=True)
        grad_scores = (probs * (grad_probs - row_dot)).astype(BF16)
        k_scaled[seen, head] += dot_tn(grad_scores, q)
        dv_ref[seen, :] += dot_tn(probs.astype(BF16), g)
        grad_y = turn_back(dot_nn(grad_scores, keys) * SCALE, table[rows, :])
        normed = q_raw[rows, head] * inverse_of(sums.at[rows, :], 0)
        scaled = grad_y * gain_q
        q_scaled[rows, head] = scaled
        dots[rows, :] += lanes(jnp.sum(scaled * normed, axis=-1, keepdims=True), 0.0)
        gain_sum += jnp.sum(grad_y * normed, axis=0, keepdims=True)
    grad_y = turn_back(k_scaled[:, head] * SCALE, table[...])
    normed = k_raw[:, head] * inverse_of(sums, 1)
    scaled = grad_y * gain_k
    k_scaled[:, head] = scaled
    k_dots = jnp.sum(scaled * normed, axis=-1, keepdims=True)
    dots[...] += lanes(jnp.zeros_like(k_dots), k_dots)
    gains_out[0:1, head] = gain_sum
    gains_out[1:2, head] = jnp.sum(grad_y * normed, axis=0, keepdims=True)
    dv_out[:, head] = dv_ref[...].astype(BF16)


def branch_back_kernel(
    fsdp, sp, x_ref, p_ref, wo_ref, q_ref, k_ref, v_ref, sums, q_raw, k_raw, gain, table,
    all_ref, out_ref, q_scaled, k_scaled, dv_out, dots, gains_out,
    g_all, dv_ref, xsend, xrecv, own_sem, all_sem, *scratch,
):
    f, s = lax.axis_index("fsdp"), lax.axis_index("sp")
    lines = fsdp // 2
    barrier = pltpu.get_barrier_semaphore()
    sums_over = PlaneSum(scratch[:4], f, s, sp)
    expected = greet_line(barrier, lines, f, s) + sums_over.greet(barrier)
    plane = plane_gather_of(x_ref, g_all, f, s, sp, xsend, xrecv)
    own = pltpu.make_async_copy(x_ref, plane.at(s, 0, x_ref.shape[0]), own_sem)
    own.start()
    pl.semaphore_wait(barrier, expected)
    plane.start()
    line = LineReduce(p_ref, scratch[4:], lines, f, s)
    line.start()
    dots[...] = jnp.zeros_like(dots)
    out_all = pltpu.make_async_copy(g_all, all_ref, all_sem)
    for t in range(lines - 1):
        line.step(t)
        if t == min(1, lines - 2):
            plane.forward()
    plane.finish()
    own.wait()
    out_all.start()

    def block(i, carry):
        at = pl.ds(pl.multiple_of(i * TOK_DEV, TOK_DEV), TOK_DEV)
        dv_out[at, :] = dot_nt(g_all[at, :], wo_ref[...]).astype(BF16)
        return carry

    lax.fori_loop(0, sp, block, 0)
    for h in range(q_ref.shape[1] // HEAD_DIM):
        attend_back_head(
            h, q_ref, k_ref, v_ref, sums, q_raw, k_raw, gain, table,
            q_scaled, k_scaled, dv_out, dots, gains_out, dv_ref,
        )
    sums_over.start(dots)
    line.finish(out_ref)
    sums_over.finish(dots)
    out_all.wait()


def branch_back(fsdp, sp, x, partial, wo, q, k, v, sums, q_raw, k_raw, gains, table):
    block = partial.shape[1:]
    seq, width = q.shape
    dma = pltpu.SemaphoreType.DMA
    return pl.pallas_call(
        functools.partial(branch_back_kernel, fsdp, sp),
        out_shape=(
            jax.ShapeDtypeStruct((seq, D), BF16),
            jax.ShapeDtypeStruct(block, F32),
            jax.ShapeDtypeStruct((seq, width), F32),
            jax.ShapeDtypeStruct((seq, width), F32),
            jax.ShapeDtypeStruct((seq, width), BF16),
            jax.ShapeDtypeStruct((seq, 128), F32),
            jax.ShapeDtypeStruct((2, width), F32),
        ),
        in_specs=[VMEM, ANY] + [VMEM] * 9,
        out_specs=[ANY] + [VMEM] * 6,
        scratch_shapes=[
            pltpu.VMEM((seq, D), BF16), pltpu.VMEM((seq, HEAD_DIM), F32), dma((sp,)), dma((sp,)), dma, dma,
        ]
        + PlaneSum.scratch(seq, sp)
        + LineReduce.scratch(fsdp, block),
        compiler_params=comm_params(5),
        name="branch_back",
    )(x, partial, wo, q, k, v, sums, q_raw, k_raw, gains, table)


def held(shape):
    return pl.BlockSpec(
        shape, lambda *_: (0,) * len(shape), pipeline_mode=pl.Buffered(buffer_count=1)
    )


def weight_kernel(
    q_scaled, k_scaled, q_raw, k_raw, squares, dots, dv_ref, first, attended, g_ref, w_ref,
    out, back, low, square,
):
    f = pl.program_id(0)
    height = first.shape[1]
    rows = out.shape[1] - 3 * height
    cols = out.shape[2]
    sp = D // cols

    @pl.when(f == 0)
    def _():
        for n, scaled, raw in ((0, q_scaled, q_raw), (1, k_scaled, k_raw)):
            inverse = inverse_of(squares, n)
            mean = dots[:, n : n + 1] / D
            low[:, n * cols : (n + 1) * cols] = (
                inverse * (scaled[...] - raw[...] * (inverse * mean))
            ).astype(BF16)
        low[:, 2 * cols :] = dv_ref[...]
        for c in range(sp):
            at = slice(c * cols, (c + 1) * cols)
            square[:, at] = dot_tn(attended[...], g_ref[:, at]).astype(BF16)

    grads = dot_tn(first[...], low[...]).astype(BF16)
    for n in range(3):
        out[0, n * height : (n + 1) * height, :] = grads[:, n * cols : (n + 1) * cols]
    each = rows // sp
    from_rows = pl.ds(pl.multiple_of(f * each, each), each)
    for c in range(sp):
        at = 3 * height + c * each
        out[0, at : at + each, :] = square[from_rows, c * cols : (c + 1) * cols]
    total = dot_nt(low[:, :cols], w_ref[0]) + dot_nt(low[:, cols : 2 * cols], w_ref[1])
    back[...] = (total + dot_nt(low[:, 2 * cols :], w_ref[2])).astype(BF16)


def weight_parts(fsdp, q_scaled, k_scaled, q_raw, k_raw, squares, dots, dv, first, attended, g, w):
    seq, cols = dv.shape
    height = D // fsdp
    each = cols // fsdp
    return pl.pallas_call(
        weight_kernel,
        grid=(fsdp,),
        out_shape=(
            jax.ShapeDtypeStruct((fsdp, 3 * height + D // cols * each, cols), BF16),
            jax.ShapeDtypeStruct((seq, D), BF16),
        ),
        in_specs=[held((seq, cols))] * 4
        + [held((seq, 128))] * 2
        + [
            held((seq, cols)),
            pl.BlockSpec((seq, height), lambda f: (0, f)),
            held((seq, cols)),
            held((seq, D)),
            pl.BlockSpec((3, height, cols), lambda f: (0, f, 0)),
        ],
        out_specs=[
            pl.BlockSpec((1, 3 * height + D // cols * each, cols), lambda f: (f, 0, 0)),
            pl.BlockSpec((seq, height), lambda f: (0, f)),
        ],
        scratch_shapes=[pltpu.VMEM((seq, 3 * cols), BF16), pltpu.VMEM((cols, D), BF16)],
        compiler_params=pltpu.CompilerParams(vmem_limit_bytes=VLIM),
        name="weight_parts",
    )(q_scaled, k_scaled, q_raw, k_raw, squares, dots, dv, first, attended, g, w)


def two_parts(x, axis):
    high = x.astype(BF16)
    return jnp.concatenate([high, (x - high.astype(F32)).astype(BF16)], axis=axis)


def blocks_of(shape):
    return pl.BlockSpec((1,) + shape, lambda b: (b,) + (0,) * len(shape))


def slots_of(slots, width):
    return pl.BlockSpec((EXP_DEV, slots, width), lambda b: (0, b, 0))


def route_kernel(picks, rows_in, router, columns, out, probs_out, gates_out):
    slots = out.shape[1]
    for n in range(D // 512):
        at = pl.ds(n * 512, 512)
        got = dot_nn(picks[0], rows_in[0, :, at]).astype(BF16)
        for e in range(EXP_DEV):
            out[e, :, at] = got[e * slots : (e + 1) * slots]
    logits = dot_nt(rows_in[0], router[...])
    exp_logits = jnp.exp(logits - jnp.max(logits, axis=1, keepdims=True))
    probs = exp_logits / jnp.sum(exp_logits, axis=1, keepdims=True)
    probs_out[0] = probs
    both = two_parts(probs, 1)
    for e in range(EXP_DEV):
        moved = dot_nn(picks[0, e * slots : (e + 1) * slots, :], both)
        mask = columns[e : e + 1, :]
        gates_out[e] = jnp.sum(moved * jnp.concatenate([mask, mask], axis=1), axis=1, keepdims=True)


def route(picks, tokens, router_t, columns):
    blocks = tokens.shape[0]
    slots = picks.shape[1] // EXP_DEV
    total = blocks * slots
    experts = router_t.shape[0]
    return pl.pallas_call(
        route_kernel,
        grid=(blocks,),
        out_shape=(
            jax.ShapeDtypeStruct((EXP_DEV, total, D), BF16),
            jax.ShapeDtypeStruct((blocks, TOK_DEV, experts), F32),
            jax.ShapeDtypeStruct((EXP_DEV, total, 1), F32),
        ),
        in_specs=[
            blocks_of(picks.shape[1:]), blocks_of((TOK_DEV, D)), whole(router_t.shape),
            whole(columns.shape),
        ],
        out_specs=[slots_of(slots, D), blocks_of((TOK_DEV, experts)), slots_of(slots, 1)],
        compiler_params=pltpu.CompilerParams(vmem_limit_bytes=VLIM),
        name="route",
    )(picks, tokens, router_t, columns)


FT = 256


def active_kernel(x_ref, g_ref, w_ref, u_ref, gates, gated, grad_gate, grad_up, dots):
    @pl.when(pl.program_id(1) == 0)
    def _():
        dots[...] = jnp.zeros_like(dots)

    total = x_ref.shape[1]
    chunk = total // 4
    for first in range(0, total, chunk):
        at = slice(first, first + chunk)
        gate_pre = dot_nn(x_ref[0, at, :], g_ref[0])
        up_pre = dot_nn(x_ref[0, at, :], w_ref[0])
        sig = jax.nn.sigmoid(gate_pre)
        silu = gate_pre * sig
        hidden = silu * up_pre
        back = u_ref[0, at, :]
        gate = gates[0, at, :]
        dots[0, at, :] += jnp.sum(hidden * back, axis=1, keepdims=True)
        gated[0, at, :] = (hidden * gate).astype(BF16)
        back = back * gate
        grad_gate[0, at, :] = (back * up_pre * (sig * (1.0 + gate_pre * (1.0 - sig)))).astype(BF16)
        grad_up[0, at, :] = (back * silu).astype(BF16)


def active(x, w_gate, w_up, u, gates):
    _, total, _ = x.shape
    ff = w_up.shape[2]
    wide = 2 * FT
    tile = pl.BlockSpec((1, total, wide), lambda e, j: (e, 0, j))
    weight = pl.BlockSpec((1, D, wide), lambda e, j: (e, 0, j))
    column = pl.BlockSpec((1, total, 1), lambda e, j: (e, 0, 0))
    low = jax.ShapeDtypeStruct((EXP_DEV, total, ff), BF16)
    return pl.pallas_call(
        active_kernel,
        grid=(EXP_DEV, ff // wide),
        out_shape=(low, low, low, jax.ShapeDtypeStruct((EXP_DEV, total, 1), F32)),
        in_specs=[
            pl.BlockSpec((1, total, D), lambda e, j: (e, 0, 0)), weight, weight, tile, column,
        ],
        out_specs=[tile, tile, tile, column],
        compiler_params=pltpu.CompilerParams(vmem_limit_bytes=VLIM),
        name="active",
    )(x, w_gate, w_up, u, gates)


def down_grad_kernel(a_ref, g_ref, out):
    out[0] = dot_tn(a_ref[0], g_ref[0]).astype(BF16)


def down_grad(gated, g):
    _, total, ff = gated.shape
    size = D // 2
    return pl.pallas_call(
        down_grad_kernel,
        grid=(EXP_DEV, D // size),
        out_shape=jax.ShapeDtypeStruct((EXP_DEV, ff, D), BF16),
        in_specs=[
            pl.BlockSpec((1, total, ff), lambda e, j: (e, 0, 0)),
            pl.BlockSpec((1, total, size), lambda e, j: (e, 0, j)),
        ],
        out_specs=pl.BlockSpec((1, ff, size), lambda e, j: (e, 0, j)),
        compiler_params=pltpu.CompilerParams(vmem_limit_bytes=VLIM),
        name="down_grad",
    )(gated, g)


def rows_back_kernel(a_ref, b_ref, g_ref, w_ref, out):
    out[0] = (dot_nt(a_ref[0], g_ref[0]) + dot_nt(b_ref[0], w_ref[0])).astype(BF16)


def rows_back(grad_gate_pre, grad_up_pre, w_gate, w_up):
    _, total, ff = grad_up_pre.shape
    size = 512
    row = pl.BlockSpec((1, total, ff), lambda e, j: (e, 0, 0))
    weight = pl.BlockSpec((1, size, ff), lambda e, j: (e, j, 0))
    return pl.pallas_call(
        rows_back_kernel,
        grid=(EXP_DEV, D // size),
        out_shape=jax.ShapeDtypeStruct((EXP_DEV, total, D), BF16),
        in_specs=[row, row, weight, weight],
        out_specs=pl.BlockSpec((1, total, size), lambda e, j: (e, 0, j)),
        compiler_params=pltpu.CompilerParams(vmem_limit_bytes=VLIM),
        name="rows_back",
    )(grad_gate_pre, grad_up_pre, w_gate, w_up)


def combine_kernel(turned, rows_ref, tokens, probs, dots, router, columns, out, router_out):
    @pl.when(pl.program_id(0) == 0)
    def _():
        router_out[...] = jnp.zeros_like(router_out)

    choice = jnp.zeros(probs.shape[1:], F32)
    for e in range(EXP_DEV):
        moved = dot_nn(turned[0, e], dots[e])
        choice += jnp.sum(moved, axis=1, keepdims=True) * columns[e : e + 1, :]
    p = probs[0]
    grad_logits = p * (choice - jnp.sum(p * choice, axis=1, keepdims=True))
    both = two_parts(grad_logits, 1)
    for n in range(D // 512):
        at = pl.ds(n * 512, 512)
        total = dot_nn(both, router[:, at])
        for e in range(EXP_DEV):
            total += dot_nn(turned[0, e], rows_ref[e, :, at])
        out[0, :, at] = total.astype(BF16)
    router_out[...] += dot_tn(both, tokens[0])


def combine(turned, grad_rows, tokens, probs, dots, router_two, columns):
    blocks = tokens.shape[0]
    slots = turned.shape[3]
    return pl.pallas_call(
        combine_kernel,
        grid=(blocks,),
        out_shape=(
            jax.ShapeDtypeStruct((blocks, TOK_DEV, D), BF16),
            jax.ShapeDtypeStruct((router_two.shape[0], D), F32),
        ),
        in_specs=[
            blocks_of(turned.shape[1:]), slots_of(slots, D), blocks_of((TOK_DEV, D)),
            blocks_of(probs.shape[1:]), slots_of(slots, 128), whole(router_two.shape),
            whole(columns.shape),
        ],
        out_specs=[blocks_of((TOK_DEV, D)), whole((router_two.shape[0], D))],
        compiler_params=pltpu.CompilerParams(vmem_limit_bytes=VLIM),
        name="combine",
    )(turned, grad_rows, tokens, probs, dots, router_two, columns)


def rms_parts(values_in):
    inverse = lax.rsqrt(jnp.mean(values_in * values_in, axis=-1, keepdims=True) + EPSILON)
    return (values_in * inverse, inverse)


def rms_back(grad_out, normed, inverse, gain_row):
    scaled = grad_out * gain_row
    grad_in = inverse * (scaled - normed * jnp.mean(scaled * normed, axis=-1, keepdims=True))
    return (grad_in, jnp.sum(grad_out * normed, axis=0))


def angles(seq):
    freqs = np.float32(ROPE_BASE) ** (-2.0 * np.arange(HEAD_DIM // 2, dtype=np.float32) / HEAD_DIM)
    turned = np.arange(seq, dtype=np.float32)[:, None] * freqs[None, :].astype(np.float32)
    return jnp.asarray(np.concatenate([np.cos(turned), np.sin(turned)], axis=1), F32)


def body(
    layer_input, output_grad, w_query, w_key, w_value, w_output, w_router, norm_gains,
    w_gate, w_up, w_down, expert_routes,
):
    fsdp, sp = lax.axis_size("fsdp"), lax.axis_size("sp")
    f, s = lax.axis_index("fsdp"), lax.axis_index("sp")
    count = fsdp * sp
    experts = EXP_DEV * fsdp
    capacity = TOK_DEV * TOP // experts * 17 // 16
    slots = -(-capacity // 16) * 16
    seq = TOK_DEV * sp
    cols = D // sp
    rows = D // count

    down_full = lax.all_gather(w_down, "sp", axis=1, tiled=True)
    gate_full = lax.all_gather(w_gate, "sp", axis=1, tiled=True)
    up_full = lax.all_gather(w_up, "sp", axis=1, tiled=True)

    router_size = rows * experts
    misc = jnp.concatenate([w_router.reshape(router_size), norm_gains.reshape(4 * rows)])
    misc_rows = -(-misc.shape[0] // 2048) * 16
    misc = jnp.pad(misc, (0, misc_rows * 128 - misc.shape[0])).reshape(misc_rows, 128)
    routes = expert_routes.reshape(TOK_DEV * TOP // 128, 128)
    early = TOK_DEV // 4
    x_all, w_all, wo_s, grad_first_half, misc_all, routes_all = gather_start(
        fsdp, sp, layer_input, jnp.stack([w_query, w_key, w_value]), w_output, output_grad[:early],
        misc, routes,
    )
    misc_all = misc_all.reshape(count, misc_rows * 128)
    router_w = misc_all[:, :router_size].reshape(D, experts)
    router_t = router_w.T
    gains_w = misc_all[:, router_size : router_size + 4 * rows].reshape(count, 4, rows)
    gains32 = gains_w.transpose(1, 0, 2).reshape(4, D).astype(F32)
    gains_own = lax.dynamic_slice_in_dim(gains32, s * cols, cols, axis=1)

    routes_block = routes_all.reshape(fsdp, TOK_DEV, TOP)
    own_ids = f * EXP_DEV + jnp.arange(EXP_DEV, dtype=jnp.int32)
    chosen = jnp.any(routes_block[:, :, :, None] == own_ids, axis=2)
    before = jnp.arange(TOK_DEV)[:, None] > jnp.arange(TOK_DEV)[None, :]
    place = jnp.einsum(
        "ut,fte->feu", before.astype(BF16), chosen.astype(BF16), preferred_element_type=F32
    ).astype(jnp.int32)
    slot_ids = jnp.arange(slots, dtype=jnp.int32)
    picks = (
        (place[:, :, None, :] == slot_ids[:, None]) & chosen.transpose(0, 2, 1)[:, :, None, :]
    ).astype(BF16).reshape(fsdp, EXP_DEV * slots, TOK_DEV)
    turned = (
        (place[:, :, :, None] == slot_ids) & chosen.transpose(0, 2, 1)[:, :, :, None]
    ).astype(BF16)
    columns = (jnp.arange(experts, dtype=jnp.int32)[None, :] == own_ids[:, None]).astype(F32)

    first_in, q_raw, k_raw, values, squares = project(x_all, gains32, w_all)
    squares = plane_sum(sp, squares, 1, "norm_sums")
    table = angles(seq)
    attended, sums, queries, keys = attend(
        q_raw, k_raw, values, squares, gains_own, table
    )
    branch = dot_nn(attended, wo_s).astype(BF16).reshape(sp, TOK_DEV, D)
    inputs = layer_input.astype(F32)
    branch, grad_second_half = branch_sum(fsdp, branch, output_grad[early:])
    mid = inputs + branch
    normed_m, inverse_m = rms_parts(mid)
    second_in = (normed_m * gains32[1]).astype(BF16)

    tokens, grad_taken, unscaled = token_gather(
        fsdp, second_in, grad_first_half, grad_second_half, picks, down_full
    )
    received, probs, slot_gates = route(picks, tokens, router_t, columns)
    gated, grad_gate_pre, grad_up_pre, slot_dots = active(
        received, gate_full, up_full, unscaled, slot_gates
    )
    dots_two = jnp.pad(two_parts(slot_dots, 2), ((0, 0), (0, 0), (0, 126)))
    grad_rows = rows_back(grad_gate_pre, grad_up_pre, gate_full, up_full)
    second_part, router_two = combine(
        turned, grad_rows, tokens, probs, dots_two, jnp.concatenate([router_t, router_t], axis=0),
        columns,
    )
    grad_router = (router_two[:experts] + router_two[experts:]).T

    def shed(grad):
        return lax.psum_scatter(grad, "sp", scatter_dimension=1, tiled=True).astype(F32)

    grad_down = shed(down_grad(gated, grad_taken))
    grad_second, out_part, gate_part, up_part = token_back(
        fsdp, second_part, gated, down_full, turned, received, grad_gate_pre, grad_up_pre
    )
    grad_gate, grad_up = shed(gate_part), shed(up_part)

    grad_final = output_grad.astype(F32)
    grad_mid_norm, gain_m = rms_back(grad_second, normed_m, inverse_m, gains32[1])
    grad_mid = grad_final + grad_mid_norm
    grad_branch, out_sum, q_scaled, k_scaled, grad_values, dots, gain_qk = branch_back(
        fsdp, sp, grad_mid.astype(BF16), out_part, wo_s, queries, keys, values, sums, q_raw, k_raw,
        gains_own, table,
    )
    layer_out = (mid + out_sum).astype(BF16)
    weight_part, first_part = weight_parts(
        fsdp, q_scaled, k_scaled, q_raw, k_raw, squares, dots, grad_values, first_in, attended,
        grad_branch, w_all,
    )

    gain_rows = lax.dynamic_update_slice(jnp.zeros((8, D), F32), gain_qk, (2, s * cols))
    gain_rows = gain_rows.at[1].set(gain_m)
    router_part = grad_router.reshape(count, router_size)
    router_part = jnp.pad(router_part, ((0, 0), (0, 1024 - router_size))).reshape(count, 8, 128)
    input_grad, *weight_grads, small = end_exchange(
        fsdp, sp, weight_part, first_part.reshape(sp, TOK_DEV, D), layer_input, grad_mid, gains32,
        gain_rows, router_part, 8,
    )
    weight_grads = [grad.astype(F32) for grad in weight_grads]
    grad_router_own = small[:8].reshape(1024)[:router_size].reshape(rows, experts)
    first_lane = (f * sp + s) * rows % 128
    grad_gains = lax.dynamic_slice(small[8:12], (0, first_lane), (4, rows))
    return (
        layer_out, input_grad, *weight_grads,
        grad_router_own, grad_gains, grad_gate, grad_up, grad_down,
    )


def solution(mesh):
    both, split = P(("fsdp", "sp"), None), P("fsdp", "sp", None)
    gains = P(None, ("fsdp", "sp"))
    return jax.shard_map(
        body,
        mesh=mesh,
        in_specs=(both,) * 7 + (gains,) + (split,) * 3 + (both,),
        out_specs=(both,) * 7 + (gains,) + (split,) * 3,
        check_vma=False,
    )
```

```python
import functools

import jax
import jax.numpy as jnp
import numpy as np
from jax import lax
from jax.experimental import pallas as pl
from jax.experimental.pallas import tpu as pltpu
from jax.sharding import PartitionSpec as P

D = 2048
HEADS = 16
HEAD_DIM = 128
TOP = 8
EXP_DEV = 2
BLK = 256
TOK_DEV = 256
EPSILON = 1e-05
ROPE_BASE = 10000.0
MASKED = -1000000000.0
SCALE = HEAD_DIM ** (-0.5)
MESH = pl.DeviceIdType.MESH
ANY = pl.BlockSpec(memory_space=pl.ANY)
VMEM = pl.BlockSpec(memory_space=pltpu.VMEM)
VLIM = 60 * 1024 * 1024
F32 = jnp.float32
BF16 = jnp.bfloat16


def remote(src, dst, send_sem, recv_sem, device):
    return pltpu.make_async_remote_copy(
        src_ref=src,
        dst_ref=dst,
        send_sem=send_sem,
        recv_sem=recv_sem,
        device_id=device,
        device_id_type=MESH,
    )


def landed(ref, sem):
    pltpu.make_async_copy(ref, ref, sem).wait()


def signal(sem, device):
    pl.semaphore_signal(sem, inc=1, device_id=device, device_id_type=MESH)


def greet_line(barrier, lines, f, s):
    place, core = f // 2, f % 2
    signal(barrier, (f + 1 - 2 * core, s))

    @pl.when(place > 0)
    def _():
        signal(barrier, (f - 2, s))

    @pl.when(place < lines - 1)
    def _():
        signal(barrier, (f + 2, s))

    return 1 + jnp.where(place > 0, 1, 0) + jnp.where(place < lines - 1, 1, 0)


class LineGather:
    def __init__(self, views, owns, lines, f, s, send, recv):
        self.views, self.owns, self.lines, self.f, self.s = views, owns, lines, f, s
        self.send, self.recv = send, recv
        self.place, self.core = f // 2, f % 2

    def copy(self, v, block, slot, way):
        device = {
            "right": (self.f + 2, self.s),
            "left": (self.f - 2, self.s),
            "partner": (self.f + 1 - 2 * self.core, self.s),
        }[way]
        index = {"right": 0, "left": 1, "partner": 2}[way]
        ref = self.views[v](block)
        own = self.owns[v] if slot == 0 and self.owns[v] is not None else ref
        return remote(own, ref, self.send.at[v, slot, index], self.recv.at[v, block], device)

    def start_own(self, v):
        @pl.when(self.place < self.lines - 1)
        def _():
            self.copy(v, self.f, 0, "right").start()

        @pl.when(self.place > 0)
        def _():
            self.copy(v, self.f, 0, "left").start()

        self.copy(v, self.f, 0, "partner").start()

    def forward(self, v, k):
        place, lines = self.place, self.lines

        @pl.when(place >= k)
        def _():
            block = self.f - 2 * k
            landed(self.views[v](block), self.recv.at[v, block])

            @pl.when(place < lines - 1)
            def _():
                self.copy(v, block, k, "right").start()

            self.copy(v, block, k, "partner").start()

        @pl.when(place + k < lines)
        def _():
            block = self.f + 2 * k
            landed(self.views[v](block), self.recv.at[v, block])

            @pl.when(place > 0)
            def _():
                self.copy(v, block, lines - 1 + k, "left").start()

            self.copy(v, block, lines - 1 + k, "partner").start()

    def finish(self, v):
        place, lines = self.place, self.lines
        for line in range(lines):
            block = 2 * line + 1 - self.core
            landed(self.views[v](block), self.recv.at[v, block])
        self.copy(v, self.f, 0, "partner").wait_send()

        @pl.when(place < lines - 1)
        def _():
            self.copy(v, self.f, 0, "right").wait_send()

        @pl.when(place > 0)
        def _():
            self.copy(v, self.f, 0, "left").wait_send()

        for k in range(1, lines):

            @pl.when(place >= k)
            def _():
                block = self.f - 2 * k

                @pl.when(place < lines - 1)
                def _():
                    self.copy(v, block, k, "right").wait_send()

                self.copy(v, block, k, "partner").wait_send()

            @pl.when(place + k < lines)
            def _():
                block = self.f + 2 * k

                @pl.when(place > 0)
                def _():
                    self.copy(v, block, lines - 1 + k, "left").wait_send()

                self.copy(v, block, lines - 1 + k, "partner").wait_send()


def line_sems(arrays, fsdp):
    lines = fsdp // 2
    return [
        pltpu.SemaphoreType.DMA((arrays, 2 * lines, 3)),
        pltpu.SemaphoreType.DMA((arrays, fsdp)),
    ]


def add_rows(dst, a, b, rows):
    def step(i, carry):
        at = pl.ds(pl.multiple_of(i * 32, 32), 32)
        dst[at, :] = a[at, :].astype(dst.dtype) + b[at, :].astype(dst.dtype)
        return carry

    lax.fori_loop(0, rows // 32, step, 0)


class LineReduce:
    def __init__(self, p_ref, scratch, lines, f, s):
        self.p_ref, self.lines, self.f, self.s = p_ref, lines, f, s
        self.own, self.paired, self.got, self.last = scratch[:4]
        self.psend, self.precv, self.send, self.recv, self.final, self.local = scratch[4:]
        self.place, self.core = f // 2, f % 2
        self.rows = p_ref.shape[1]
        self.order = []
        for n in range(lines):
            for d in (lines - 1 - n, n):
                if d not in self.order:
                    self.order.append(d)

    @staticmethod
    def scratch(fsdp, block):
        lines = fsdp // 2
        dma = pltpu.SemaphoreType.DMA
        return [
            pltpu.VMEM((lines,) + block, BF16),
            pltpu.VMEM((lines,) + block, BF16),
            pltpu.VMEM((lines,) + block, BF16),
            pltpu.VMEM(block, BF16),
            dma((lines,)), dma((lines,)), dma((lines,)), dma((lines,)), dma, dma((lines,)),
        ]

    def load(self, i):
        return pltpu.make_async_copy(self.p_ref.at[2 * i + self.core], self.own.at[i], self.local.at[i])

    def swap(self, i):
        return remote(
            self.p_ref.at[2 * i + 1 - self.core], self.paired.at[i], self.psend.at[i],
            self.precv.at[i], (self.f + 1 - 2 * self.core, self.s),
        )

    def right(self, d, last):
        dst = self.last if last else self.got.at[d]
        sem = self.final if last else self.recv.at[d]
        return remote(self.own.at[d], dst, self.send.at[d], sem, (self.f + 2, self.s))

    def left(self, d):
        return remote(
            self.own.at[d], self.got.at[d], self.send.at[d], self.recv.at[d], (self.f - 2, self.s)
        )

    def start(self):
        for i in self.order[:2]:
            self.swap(i).start()
        for i in self.order:
            self.load(i).start()
        self.added = 0
        self.add_pairs(2)

    def add_pairs(self, until):
        for i in self.order[self.added : until]:
            self.load(i).wait()
            landed(self.paired.at[i], self.precv.at[i])
            add_rows(self.own.at[i], self.own.at[i], self.paired.at[i], self.rows)
        self.added = max(self.added, until)

    def step(self, t):
        place, lines = self.place, self.lines
        d = lines - 1 - t + place

        @pl.when(t >= place)
        def _():
            @pl.when(place > 0)
            def _():
                landed(self.got.at[d], self.recv.at[d])
                add_rows(self.own.at[d], self.own.at[d], self.got.at[d], self.rows)

            @pl.when(d == place + 1)
            def _():
                self.right(d, True).start()

            @pl.when(d != place + 1)
            def _():
                self.right(d, False).start()

        e = t - (lines - 1 - place)

        @pl.when(e >= 0)
        def _():
            @pl.when(place < lines - 1)
            def _():
                landed(self.got.at[e], self.recv.at[e])
                add_rows(self.own.at[e], self.own.at[e], self.got.at[e], self.rows)

            self.left(e).start()

        if t == 0:
            for i in self.order[2:]:
                self.swap(i).start()
        self.add_pairs(2 * t + 4)

    def finish(self, out_ref):
        place, lines, rows = self.place, self.lines, self.rows

        def total(*extra):
            def step(i, carry):
                at = pl.ds(pl.multiple_of(i * 32, 32), 32)
                value = self.own[place, at, :].astype(F32)
                for ref in extra:
                    value += ref[at, :].astype(F32)
                out_ref[at, :] = value.astype(out_ref.dtype)
                return carry

            lax.fori_loop(0, rows // 32, step, 0)

        @pl.when(place > 0)
        def _():
            landed(self.last, self.final)

        @pl.when(place < lines - 1)
        def _():
            landed(self.got.at[place], self.recv.at[place])

        @pl.when(place == 0)
        def _():
            total(self.got.at[place])

        @pl.when(place == lines - 1)
        def _():
            total(self.last)

        @pl.when(jnp.logical_and(place > 0, place < lines - 1))
        def _():
            total(self.last, self.got.at[place])

        for i in range(lines):
            self.swap(i).wait_send()

            @pl.when(place < i)
            def _():
                self.right(i, False).wait_send()

            @pl.when(place > i)
            def _():
                self.left(i).wait_send()


class PlaneGather:
    def __init__(self, own, out, f, s, send, recv):
        self.own, self.out, self.f, self.s, self.send, self.recv = own, out, f, s, send, recv
        self.rows = own.shape[0]
        self.half = self.rows // 2

    def at(self, place, first, size):
        return self.out.at[pl.ds(pl.multiple_of(place * self.rows + first, self.half), size), :]

    def near(self, k):
        return remote(
            self.own, self.at(self.s, 0, self.rows), self.send.at[k - 1], self.recv.at[k - 1],
            (self.f, self.s ^ k),
        )

    def on(self, k):
        ref = self.at(self.s ^ k, (k - 1) * self.half, self.half)
        return remote(ref, ref, self.send.at[k + 1], self.recv.at[k + 1], (self.f, self.s ^ (3 - k)))

    def start(self):
        self.near(1).start()
        self.near(2).start()

    def forward(self):
        for k in (1, 2):
            landed(self.at(self.s ^ k, 0, self.rows), self.recv.at[k - 1])
            self.on(k).start()

    def finish(self):
        landed(self.at(self.s ^ 3, 0, self.half), self.recv.at[2])
        landed(self.at(self.s ^ 3, self.half, self.half), self.recv.at[3])
        for k in (1, 2):
            self.near(k).wait_send()
            self.on(k).wait_send()


class AnyGather:
    def __init__(self, own, out, f, s, sp, send, recv):
        self.own, self.out, self.f, self.s, self.sp = own, out, f, s, sp
        self.send, self.recv = send, recv
        self.rows = own.shape[0]

    def at(self, place, first, size):
        return self.out.at[pl.ds(pl.multiple_of(place * self.rows + first, size), size), :]

    def copy(self, k):
        dst = self.at(self.s, 0, self.rows)
        return remote(self.own, dst, self.send.at[k], self.recv.at[k], (self.f, self.s ^ k))

    def start(self):
        for k in range(1, self.sp):
            self.copy(k).start()

    def forward(self):
        pass

    def finish(self):
        for k in range(1, self.sp):
            landed(self.at(self.s ^ k, 0, self.rows), self.recv.at[k])
            self.copy(k).wait_send()


class AnyReduce:
    def __init__(self, p_ref, out_ref, scratch, f, s, sp):
        self.p_ref, self.out_ref, self.f, self.s, self.sp = p_ref, out_ref, f, s, sp
        self.own, self.got, self.send, self.recv, self.local = scratch

    @staticmethod
    def scratch(block, sp):
        dma = pltpu.SemaphoreType.DMA
        return [
            pltpu.VMEM(block, BF16), pltpu.VMEM((sp,) + block, BF16), dma((sp,)), dma((sp,)), dma,
        ]

    def copy(self, k):
        d = self.s ^ k
        return remote(
            self.p_ref.at[d], self.got.at[k], self.send.at[k], self.recv.at[k], (self.f, d)
        )

    def load(self):
        return pltpu.make_async_copy(self.p_ref.at[self.s], self.own, self.local)

    def start(self):
        for k in range(1, self.sp):
            self.copy(k).start()
        self.load().start()

    def forward(self):
        self.load().wait()

    def finish(self):
        rows = self.own.shape[0]
        for k in range(1, self.sp):
            landed(self.got.at[k], self.recv.at[k])
            add_rows(self.out_ref, self.own if k == 1 else self.out_ref, self.got.at[k], rows)
        for k in range(1, self.sp):
            self.copy(k).wait_send()


def plane_gather_of(own, out, f, s, sp, send, recv):
    if sp == 4:
        return PlaneGather(own, out, f, s, send, recv)
    return AnyGather(own, out, f, s, sp, send, recv)


def plane_reduce_of(p_ref, out_ref, scratch, f, s, sp):
    if sp == 4:
        return PlaneReduce(p_ref, out_ref, scratch, f, s)
    return AnyReduce(p_ref, out_ref, scratch, f, s, sp)


def plane_scratch(block, sp):
    return PlaneReduce.scratch(block) if sp == 4 else AnyReduce.scratch(block, sp)


class PlaneReduce:
    WAYS = ((0, 1, 1), (1, 2, 2))

    def __init__(self, p_ref, out_ref, scratch, f, s):
        self.p_ref, self.out_ref, self.f, self.s = p_ref, out_ref, f, s
        self.own, self.got, self.got_on, self.send, self.recv, self.local = scratch
        self.half = p_ref.shape[1] // 2

    @staticmethod
    def scratch(block):
        dma = pltpu.SemaphoreType.DMA
        return [
            pltpu.VMEM((3,) + block, BF16), pltpu.VMEM((2,) + block, BF16),
            pltpu.VMEM(block, BF16), dma((2, 3)), dma((2, 3)), dma((3,)),
        ]

    def part(self, ref, h):
        return ref.at[pl.ds(h * self.half, self.half), :]

    def load(self, n):
        d = (self.s, self.s ^ 2, self.s ^ 1)[n]
        return pltpu.make_async_copy(self.p_ref.at[d], self.own.at[n], self.local.at[n])

    def hop(self, h, k, far):
        d = self.s ^ 3 if far else self.s ^ k
        n = 0 if far else 1
        return remote(
            self.part(self.p_ref.at[d], h), self.part(self.got.at[1 - n], h), self.send.at[h, n],
            self.recv.at[h, n], (self.f, self.s ^ k),
        )

    def on(self, h, k, n):
        return remote(
            self.part(self.own.at[n], h), self.part(self.got_on, h), self.send.at[h, 2],
            self.recv.at[h, 2], (self.f, self.s ^ (3 - k)),
        )

    def start(self):
        for far in (True, False):
            for h, k, _ in self.WAYS:
                self.hop(h, k, far).start()
        for n in range(3):
            self.load(n).start()

    def forward(self):
        for n in range(3):
            self.load(n).wait()
        for h, k, n in self.WAYS:
            mine = self.part(self.own.at[n], h)
            landed(self.part(self.got.at[1], h), self.recv.at[h, 0])
            add_rows(mine, mine, self.part(self.got.at[1], h), self.half)
            self.on(h, k, n).start()

    def finish(self):
        for h in (0, 1):
            landed(self.part(self.got.at[0], h), self.recv.at[h, 1])
            add_rows(
                self.part(self.out_ref, h), self.part(self.own.at[0], h), self.part(self.got.at[0], h),
                self.half,
            )
        for h in (0, 1):
            landed(self.part(self.got_on, h), self.recv.at[h, 2])
            out = self.part(self.out_ref, h)
            add_rows(out, out, self.part(self.got_on, h), self.half)
        for h, k, n in self.WAYS:
            self.hop(h, k, True).wait_send()
            self.hop(h, k, False).wait_send()
            self.on(h, k, n).wait_send()


def greet_plane(barrier, f, s, sp):
    ways = (1, 2) if sp == 4 else range(1, sp)
    for k in ways:
        signal(barrier, (f, s ^ k))
    return len(ways)


def greet_all(barrier, me, count, sp):
    def greet(i, carry):
        other = lax.rem(me + i, count)
        signal(barrier, (other // sp, lax.rem(other, sp)))
        return carry

    lax.fori_loop(1, count, greet, 0)


def rows_view(ref, rows):
    return lambda b: ref.at[pl.ds(pl.multiple_of(b * rows, rows), rows), :]


def block_view(ref):
    return lambda b: ref.at[b]


def comm_params(number):
    return pltpu.CompilerParams(
        collective_id=number, has_side_effects=True, vmem_limit_bytes=VLIM
    )


def start_kernel(
    fsdp, sp, x_ref, w_ref, wo_ref, g_ref, misc_ref, routes_ref,
    x_all, w_all, wo_all, g_all, misc_all, routes_all,
    send, recv, xsend, xrecv, psend, precv, wsend, wrecv, msend, mrecv, rsend, rrecv, local,
):
    f, s = lax.axis_index("fsdp"), lax.axis_index("sp")
    count, lines = fsdp * sp, fsdp // 2
    me = f * sp + s
    rows = w_ref.shape[1]
    cols = D // sp
    barrier = pltpu.get_barrier_semaphore()

    def w_block(s_to):
        return w_ref.at[:, :, pl.ds(pl.multiple_of(s_to * cols, cols), cols)]

    def w_rows(i):
        return w_all.at[:, pl.ds(pl.multiple_of(i * rows, rows), rows), :]

    def w_view(b):
        size = rows * sp
        return w_all.at[:, pl.ds(pl.multiple_of(b * size, size), size), :]

    wo_view = rows_view(wo_all, rows)
    x_view = rows_view(x_all, TOK_DEV)
    owns = [
        pltpu.make_async_copy(w_block(s), w_rows(me), local.at[0]),
        pltpu.make_async_copy(x_ref, x_view(s), local.at[1]),
        pltpu.make_async_copy(misc_ref, misc_all.at[me], local.at[2]),
        pltpu.make_async_copy(routes_ref, routes_all.at[f], local.at[3]),
        pltpu.make_async_copy(g_ref, g_all.at[f], local.at[4]),
    ]
    for copy in owns:
        copy.start()
    greet_all(barrier, me, count, sp)
    pl.semaphore_wait(barrier, count - 1)

    line = LineGather([w_view, wo_view, block_view(g_all)], [None, None, g_ref], lines, f, s, send, recv)
    line.start_own(2)
    w_copies = []
    for k in range(sp - 1, 0, -1):
        s_to = s ^ k
        copy = remote(w_block(s_to), w_rows(me), psend.at[k], precv.at[k], (f, s_to))
        copy.start()
        w_copies.append(copy)
    target_s, target_f = me // fsdp, lax.rem(me, fsdp)
    stays = jnp.logical_and(target_s == s, target_f == f)
    wo_copy = remote(wo_ref, wo_view(target_f), wsend, wrecv, (target_f, target_s))
    wo_own = pltpu.make_async_copy(wo_ref, wo_view(f), wrecv)

    @pl.when(stays)
    def _():
        wo_own.start()

    @pl.when(jnp.logical_not(stays))
    def _():
        wo_copy.start()

    def misc_copy(i):
        other = lax.rem(me + i, count)
        return remote(
            misc_ref, misc_all.at[me], msend.at[i], mrecv.at[me], (other // sp, lax.rem(other, sp))
        )

    def misc_go(i, carry):
        misc_copy(i).start()
        return carry

    lax.fori_loop(1, count, misc_go, 0)

    def routes_copy(i):
        other = lax.rem(f + i, fsdp)
        return remote(routes_ref, routes_all.at[f], rsend.at[i], rrecv.at[f], (other, s))

    def routes_go(i, carry):
        routes_copy(i).start()
        return carry

    lax.fori_loop(1, fsdp, routes_go, 0)

    owns[0].wait()
    for k in range(1, sp):
        landed(w_rows(f * sp + (s ^ k)), precv.at[k])
    line.start_own(0)
    tokens = plane_gather_of(x_ref, x_all, f, s, sp, xsend, xrecv)
    tokens.start()
    landed(wo_view(f), wrecv)
    line.start_own(1)
    for k in range(1, lines):
        for v in (2, 0, 1):
            line.forward(v, k)
        if k == min(2, lines - 1):
            tokens.forward()
    for v in range(3):
        line.finish(v)
    tokens.finish()

    def misc_end(i, carry):
        misc_copy(i).wait_send()
        other = lax.rem(me + i, count)
        landed(misc_all.at[other], mrecv.at[other])
        return carry

    lax.fori_loop(1, count, misc_end, 0)

    def routes_end(i, carry):
        routes_copy(i).wait_send()
        other = lax.rem(f + i, fsdp)
        landed(routes_all.at[other], rrecv.at[other])
        return carry

    lax.fori_loop(1, fsdp, routes_end, 0)
    for copy in w_copies:
        copy.wait_send()

    @pl.when(jnp.logical_not(stays))
    def _():
        wo_copy.wait_send()

    for copy in owns[1:]:
        copy.wait()


def gather_start(fsdp, sp, x, w, wo, g, misc, routes):
    count = fsdp * sp
    dma = pltpu.SemaphoreType.DMA
    return pl.pallas_call(
        functools.partial(start_kernel, fsdp, sp),
        out_shape=(
            jax.ShapeDtypeStruct((sp * TOK_DEV, D), BF16),
            jax.ShapeDtypeStruct((3, D, D // sp), BF16),
            jax.ShapeDtypeStruct((D // sp, D), BF16),
            jax.ShapeDtypeStruct((fsdp,) + g.shape, BF16),
            jax.ShapeDtypeStruct((count,) + misc.shape, BF16),
            jax.ShapeDtypeStruct((fsdp,) + routes.shape, jnp.int32),
        ),
        in_specs=[VMEM] * 6,
        out_specs=[ANY] * 6,
        scratch_shapes=line_sems(3, fsdp)
        + [
            dma((sp,)), dma((sp,)), dma((sp,)), dma((sp,)), dma, dma,
            dma((count,)), dma((count,)), dma((fsdp,)), dma((fsdp,)), dma((5,)),
        ],
        compiler_params=comm_params(0),
        name="gather_start",
    )(x, w, wo, g, misc, routes)


def branch_kernel(fsdp, sp, p_ref, g_ref, x_ref, gain, out_ref, second_ref, g_all, *scratch):
    f, s = lax.axis_index("fsdp"), lax.axis_index("sp")
    lines = fsdp // 2
    barrier = pltpu.get_barrier_semaphore()
    expected = greet_line(barrier, lines, f, s) + greet_plane(barrier, f, s, sp)
    send, recv, own_sem = scratch[-3:]
    own = pltpu.make_async_copy(g_ref, g_all.at[f], own_sem)
    own.start()
    pl.semaphore_wait(barrier, expected)
    plane = plane_reduce_of(p_ref, out_ref, scratch[:-3], f, s, sp)
    line = LineGather([block_view(g_all)], [g_ref], lines, f, s, send, recv)
    plane.start()
    line.start_own(0)
    for k in range(1, lines):
        line.forward(0, k)
        if k == min(2, lines - 1):
            plane.forward()
    plane.finish()

    def norm(i, carry):
        at = pl.ds(pl.multiple_of(i * 32, 32), 32)
        mid = x_ref[at, :].astype(F32) + out_ref[at, :]
        out_ref[at, :] = mid
        inverse = lax.rsqrt(jnp.mean(mid * mid, axis=-1, keepdims=True) + EPSILON)
        second_ref[at, :] = (mid * inverse * gain[1:2, :]).astype(BF16)
        return carry

    lax.fori_loop(0, TOK_DEV // 32, norm, 0)
    line.finish(0)
    own.wait()


def branch_sum(fsdp, partial, g, x, gains):
    sp, block = partial.shape[0], partial.shape[1:]
    return pl.pallas_call(
        functools.partial(branch_kernel, fsdp, sp),
        out_shape=(
            jax.ShapeDtypeStruct(block, F32),
            jax.ShapeDtypeStruct(block, BF16),
            jax.ShapeDtypeStruct((fsdp,) + g.shape, BF16),
        ),
        in_specs=[ANY, VMEM, VMEM, VMEM],
        out_specs=[VMEM, VMEM, ANY],
        scratch_shapes=plane_scratch(block, sp) + line_sems(1, fsdp) + [pltpu.SemaphoreType.DMA],
        compiler_params=comm_params(2),
        name="branch_sum",
    )(partial, g, x, gains)


def token_kernel(
    fsdp, x_ref, g_first, g_second, picks, w_ref, out_ref, taken_ref, back_ref,
    g_buf, w_buf, taken, back, send, recv, local, loads, stores, back_sem,
):
    f, s = lax.axis_index("fsdp"), lax.axis_index("sp")
    lines = fsdp // 2
    parts = 2
    size = TOK_DEV // parts
    early, later = g_first.shape[1], g_second.shape[1]
    slots = picks.shape[1] // EXP_DEV
    ff = w_ref.shape[1]
    barrier = pltpu.get_barrier_semaphore()
    expected = greet_line(barrier, lines, f, s)
    own = pltpu.make_async_copy(x_ref, out_ref.at[f], local)
    own.start()
    reads = [
        pltpu.make_async_copy(g_first, g_buf.at[:, pl.ds(0, early), :], loads.at[0]),
        pltpu.make_async_copy(g_second, g_buf.at[:, pl.ds(early, later), :], loads.at[1]),
        pltpu.make_async_copy(w_ref, w_buf, loads.at[2]),
    ]
    for copy in reads:
        copy.start()
    pl.semaphore_wait(barrier, expected)

    def view(part):
        return lambda b: out_ref.at[b, pl.ds(part * size, size), :]

    owns = [x_ref.at[pl.ds(p * size, size), :] for p in range(parts)]
    line = LineGather([view(p) for p in range(parts)], owns, lines, f, s, send, recv)
    for p in range(parts):
        line.start_own(p)

    def take_all():
        reads[0].wait()
        reads[1].wait()

        def block(b, carry):
            for n in range(D // 512):
                at = pl.ds(n * 512, 512)
                got = dot_nn(picks[b], g_buf[b, :, at]).astype(BF16)
                for e in range(EXP_DEV):
                    to = pl.ds(pl.multiple_of(b * slots, 16), slots)
                    taken[e, to, at] = got[e * slots : (e + 1) * slots]
            return carry

        lax.fori_loop(0, fsdp, block, 0)
        for e in range(EXP_DEV):
            pltpu.make_async_copy(taken.at[e], taken_ref.at[e], stores.at[e]).start()

    def back_copy(e, j, slot):
        at = pl.ds(pl.multiple_of(j * FT, FT), FT)
        return pltpu.make_async_copy(back.at[slot], back_ref.at[e, :, at], back_sem.at[slot])

    def back_of(e):
        if e == 0:
            reads[2].wait()
        for j in range(ff // FT):
            slot = j % 2
            if e > 0 or j > 1:
                back_copy(e, j, slot).wait()
            back[slot] = dot_nt(taken[e], w_buf[e, pl.ds(j * FT, FT), :])
            back_copy(e, j, slot).start()

    work = [take_all] + [functools.partial(back_of, e) for e in range(EXP_DEV)]
    for k in range(1, lines):
        if k - 1 < len(work):
            work[k - 1]()
        for p in range(parts):
            line.forward(p, k)
    for unit in work[lines - 1 :]:
        unit()
    for p in range(parts):
        line.finish(p)
    own.wait()
    for slot in range(2):
        back_copy(0, slot, slot).wait()
    for e in range(EXP_DEV):
        pltpu.make_async_copy(taken.at[e], taken_ref.at[e], stores.at[e]).wait()


def token_gather(fsdp, x, g_first, g_second, picks, w_down):
    slots = picks.shape[1] // EXP_DEV
    total = fsdp * slots
    ff = w_down.shape[1]
    dma = pltpu.SemaphoreType.DMA
    return pl.pallas_call(
        functools.partial(token_kernel, fsdp),
        out_shape=(
            jax.ShapeDtypeStruct((fsdp, TOK_DEV, D), BF16),
            jax.ShapeDtypeStruct((EXP_DEV, total, D), BF16),
            jax.ShapeDtypeStruct((EXP_DEV, total, ff), F32),
        ),
        in_specs=[VMEM, ANY, ANY, VMEM, ANY],
        out_specs=[ANY, ANY, ANY],
        scratch_shapes=[
            pltpu.VMEM((fsdp, TOK_DEV, D), BF16),
            pltpu.VMEM((EXP_DEV, ff, D), BF16),
            pltpu.VMEM((EXP_DEV, total, D), BF16),
            pltpu.VMEM((2, total, FT), F32),
        ]
        + line_sems(2, fsdp)
        + [dma, dma((3,)), dma((EXP_DEV,)), dma((2,))],
        compiler_params=comm_params(3),
        name="token_gather",
    )(x, g_first, g_second, picks, w_down)


def token_back_kernel(
    fsdp, p_ref, gated_ref, w_ref, turned, x_ref, gu_ref, mid_ref, g_ref, gain,
    out_ref, low_ref, gain_out, part_ref, wu_ref, wide, narrow, w_buf, tile, grad_tile, loads, tile_sem, grad_sem, *scratch,
):
    f, s = lax.axis_index("fsdp"), lax.axis_index("sp")
    lines = fsdp // 2
    slots = turned.shape[3]
    height = grad_tile.shape[1]
    barrier = pltpu.get_barrier_semaphore()
    expected = greet_line(barrier, lines, f, s)
    reads = [
        pltpu.make_async_copy(gated_ref, narrow, loads.at[0]),
        pltpu.make_async_copy(w_ref.at[0], w_buf, loads.at[1]),
        pltpu.make_async_copy(x_ref, wide, loads.at[2]),
        pltpu.make_async_copy(gu_ref, narrow, loads.at[3]),
        pltpu.make_async_copy(w_ref.at[1], w_buf, loads.at[1]),
    ]
    reads[0].start()
    reads[1].start()
    pl.semaphore_wait(barrier, expected)
    line = LineReduce(p_ref, scratch, lines, f, s)
    line.start()

    def down_of(e):
        if e == 0:
            reads[0].wait()
            reads[1].wait()
        else:
            reads[4].wait()

        def columns(n, carry):
            at = pl.ds(pl.multiple_of(n * 512, 512), 512)
            wide[e, :, at] = dot_nn(narrow[e], w_buf[:, at]).astype(BF16)
            return carry

        lax.fori_loop(0, D // 512, columns, 0)
        if e == 0:
            reads[4].start()

    def tile_copy(b, slot):
        return pltpu.make_async_copy(tile.at[slot], part_ref.at[b], tile_sem.at[slot])

    def sum_all():
        reads[3].start()

        def pair(i, carry):
            for slot in range(2):
                b = 2 * i + slot

                @pl.when(i > 0)
                def _():
                    tile_copy(b, slot).wait()

                for n in range(D // 512):
                    at = pl.ds(n * 512, 512)
                    summed = jnp.zeros((TOK_DEV, 512), F32)
                    for e in range(EXP_DEV):
                        rows = wide[e, pl.ds(pl.multiple_of(b * slots, 16), slots), at]
                        summed += dot_nn(turned[b, e], rows)
                    tile[slot, :, at] = summed.astype(BF16)
                tile_copy(b, slot).start()
            return carry

        lax.fori_loop(0, fsdp // 2, pair, 0)
        reads[2].start()

    def grad_copy(e, i, slot):
        at = pl.ds(pl.multiple_of(i * height, height), height)
        return pltpu.make_async_copy(grad_tile.at[slot], wu_ref.at[e, at, :], grad_sem.at[slot])

    def grad_of(e):
        if e == 0:
            reads[2].wait()
            reads[3].wait()

        def pair(i, carry):
            for slot in range(2):
                part = 2 * i + slot

                def before():
                    grad_copy(e, part, slot).wait()

                if e == 0:
                    pl.when(i > 0)(before)
                else:
                    before()
                at = pl.ds(pl.multiple_of(part * height, height), height)
                grad_tile[slot] = dot_tn(wide[e, :, at], narrow[e]).astype(BF16)
                grad_copy(e, part, slot).start()
            return carry

        lax.fori_loop(0, D // height // 2, pair, 0)

    work = [functools.partial(down_of, e) for e in range(EXP_DEV)] + [sum_all]
    work += [functools.partial(grad_of, e) for e in range(EXP_DEV)]
    done = 0
    for t in range(lines - 1):
        line.step(t)
        until = (t + 1) * len(work) // (lines - 1)
        for unit in work[done:until]:
            unit()
        done = until
    line.finish(out_ref)
    gain_out[...] = jnp.zeros_like(gain_out)

    def norm_back(i, carry):
        at = pl.ds(pl.multiple_of(i * 32, 32), 32)
        mid = mid_ref[at, :]
        inverse = lax.rsqrt(jnp.mean(mid * mid, axis=-1, keepdims=True) + EPSILON)
        normed = mid * inverse
        grad_y = out_ref[at, :]
        scaled = grad_y * gain[1:2, :]
        mean = jnp.mean(scaled * normed, axis=-1, keepdims=True)
        grad = g_ref[at, :].astype(F32) + inverse * (scaled - normed * mean)
        out_ref[at, :] = grad
        low_ref[at, :] = grad.astype(BF16)
        gain_out[1:2, :] += jnp.sum(grad_y * normed, axis=0, keepdims=True)
        return carry

    lax.fori_loop(0, TOK_DEV // 32, norm_back, 0)
    for slot in range(2):
        tile_copy(slot, slot).wait()
        grad_copy(0, slot, slot).wait()


def token_back(fsdp, partial, gated, w_down, turned, received, grad_up_pre, mid, g, gains):
    block = partial.shape[1:]
    total, ff = gated.shape[1:]
    height = 256
    dma = pltpu.SemaphoreType.DMA
    return pl.pallas_call(
        functools.partial(token_back_kernel, fsdp),
        out_shape=(
            jax.ShapeDtypeStruct(block, F32),
            jax.ShapeDtypeStruct(block, BF16),
            jax.ShapeDtypeStruct((8, D), F32),
            jax.ShapeDtypeStruct(partial.shape, BF16),
            jax.ShapeDtypeStruct((EXP_DEV, D, ff), BF16),
        ),
        in_specs=[ANY, ANY, ANY, VMEM, ANY, ANY, VMEM, VMEM, VMEM],
        out_specs=[VMEM, VMEM, VMEM, ANY, ANY],
        scratch_shapes=[
            pltpu.VMEM((EXP_DEV, total, D), BF16),
            pltpu.VMEM((EXP_DEV, total, ff), BF16),
            pltpu.VMEM((ff, D), BF16),
            pltpu.VMEM((2,) + block, BF16),
            pltpu.VMEM((2, height, ff), BF16),
            dma((4,)),
            dma((2,)),
            dma((2,)),
        ]
        + LineReduce.scratch(fsdp, block),
        compiler_params=comm_params(4),
        name="token_back",
    )(partial, gated, w_down, turned, received, grad_up_pre, mid, g, gains)


class PlaneSum:
    def __init__(self, scratch, f, s, sp):
        self.own, self.got, self.send, self.recv = scratch
        self.f, self.s, self.sp = f, s, sp

    @staticmethod
    def scratch(seq, sp):
        dma = pltpu.SemaphoreType.DMA
        return [
            pltpu.VMEM((8, seq), F32), pltpu.VMEM((sp, 8, seq), F32), dma((sp,)), dma((sp,)),
        ]

    def greet(self, barrier):
        for k in range(1, self.sp):
            signal(barrier, (self.f, self.s ^ k))
        return self.sp - 1

    def copy(self, k):
        return remote(
            self.own, self.got.at[k], self.send.at[k], self.recv.at[k], (self.f, self.s ^ k)
        )

    def start(self, x_ref):
        self.own[...] = x_ref[...].T[:8]
        for k in range(1, self.sp):
            self.copy(k).start()

    def finish(self, out_ref):
        for k in range(1, self.sp):
            self.copy(k).wait()
        terms = [self.own[...]] + [self.got[k] for k in range(1, self.sp)]
        while len(terms) > 1:
            terms = [terms[i] + terms[i + 1] for i in range(0, len(terms), 2)]
        seq = out_ref.shape[0]
        out_ref[...] = jnp.concatenate([terms[0], jnp.zeros((120, seq), F32)], axis=0).T


def end_kernel(
    fsdp, sp, p_ref, low_ref, w_ref, x_ref, mid_ref, gain, gains_in, router_ref,
    grad_out, qkv_0, qkv_1, qkv_2, o_out, small_out,
    first, low_in, w_buf, back, low, o_low, gain_sum, pay, small, loads,
    qsend, qrecv, osend, orecv, msend, mrecv, local, *scratch,
):
    f, s = lax.axis_index("fsdp"), lax.axis_index("sp")
    count, lines = fsdp * sp, fsdp // 2
    me = f * sp + s
    rows, cols = o_low.shape[0], D // sp
    height = D // fsdp
    barrier = pltpu.get_barrier_semaphore()
    greet_all(barrier, me, count, sp)
    reads = [
        pltpu.make_async_copy(low_ref, low_in, loads.at[0]),
        pltpu.make_async_copy(w_ref, w_buf, loads.at[1]),
    ]
    for copy in reads:
        copy.start()
    pl.semaphore_wait(barrier, count - 1)
    plane_parts = 6 if sp == 4 else 5
    plane = plane_reduce_of(first, back, scratch[:plane_parts], f, s, sp)
    line = LineReduce(p_ref, scratch[plane_parts:], lines, f, s)
    line.start()

    def first_grads():
        for copy in reads:
            copy.wait()

        def columns(n, carry):
            at = pl.ds(pl.multiple_of(n * 256, 256), 256)
            for d in range(sp):
                rows_at = slice(d * TOK_DEV, (d + 1) * TOK_DEV)
                total = dot_nt(low_in[rows_at, :cols], w_buf[0, at, :])
                total += dot_nt(low_in[rows_at, cols : 2 * cols], w_buf[1, at, :])
                total += dot_nt(low_in[rows_at, 2 * cols :], w_buf[2, at, :])
                first[d, :, at] = total.astype(BF16)
            return carry

        lax.fori_loop(0, D // 256, columns, 0)

    def input_grads():
        gain_sum[...] = jnp.zeros_like(gain_sum)

        def chunk(i, carry):
            at = pl.ds(pl.multiple_of(i * 32, 32), 32)
            x = x_ref[at, :].astype(F32)
            inverse = lax.rsqrt(jnp.mean(x * x, axis=-1, keepdims=True) + EPSILON)
            normed = x * inverse
            grad_y = back[at, :]
            scaled = grad_y * gain[0:1, :]
            mean = jnp.mean(scaled * normed, axis=-1, keepdims=True)
            grad_out[at, :] = mid_ref[at, :] + inverse * (scaled - normed * mean)
            gain_sum[0:1, :] += jnp.sum(grad_y * normed, axis=0, keepdims=True)
            return carry

        lax.fori_loop(0, TOK_DEV // 32, chunk, 0)
        gain_sum[...] += gains_in[...]

        def fill(i, carry):
            at = pl.ds(pl.multiple_of(i * rows // 128 * 128, 128), 128)
            pay[i, 0:8, :] = router_ref[i]
            pay[i, 8:16, :] = gain_sum[:, at]
            return carry

        lax.fori_loop(0, count, fill, 0)

    def m_copy(i):
        other = lax.rem(me + i, count)
        return remote(
            pay.at[other], small.at[me], msend.at[i], mrecv.at[me], (other // sp, lax.rem(other, sp))
        )

    def m_go(i, carry):
        m_copy(i).start()
        return carry

    for t in range(lines - 1):
        line.step(t)
        if t == 0:
            first_grads()
            plane.start()
    plane.forward()
    plane.finish()
    input_grads()
    lax.fori_loop(1, count, m_go, 0)
    line.finish(low)
    for c in range(sp):
        top = 3 * height + c * rows
        o_low[:, c * cols : (c + 1) * cols] = low[top : top + rows, :]

    def q_from(i, place):
        return low.at[pl.ds(pl.multiple_of(i * height + place * rows, rows), rows), :]

    def q_to(i, place):
        return (qkv_0, qkv_1, qkv_2)[i].at[:, pl.ds(pl.multiple_of(place * cols, cols), cols)]

    def q_copy(i, k):
        return remote(q_from(i, s ^ k), q_to(i, s), qsend.at[k, i], qrecv.at[k, i], (f, s ^ k))

    def q_own(i):
        return pltpu.make_async_copy(q_from(i, s), q_to(i, s), local.at[i])

    for k in range(sp - 1, 0, -1):
        for i in range(3):
            q_copy(i, k).start()
    flat = s * fsdp + f
    target_f, target_s = flat // sp, lax.rem(flat, sp)
    stays = jnp.logical_and(target_s == s, target_f == f)
    o_copy = remote(o_low, o_out, osend, orecv, (target_f, target_s))
    o_own = pltpu.make_async_copy(o_low, o_out, orecv)

    @pl.when(stays)
    def _():
        o_own.start()

    @pl.when(jnp.logical_not(stays))
    def _():
        o_copy.start()

    for i in range(3):
        q_own(i).start()

    def m_end(i, carry):
        m_copy(i).wait_send()
        other = lax.rem(me + i, count)
        landed(small.at[other], mrecv.at[other])
        return carry + small[other]

    small_out[...] = lax.fori_loop(1, count, m_end, pay[me])
    for k in range(1, sp):
        for i in range(3):
            landed(q_to(i, s ^ k), qrecv.at[k, i])
            q_copy(i, k).wait_send()
    landed(o_out, orecv)

    @pl.when(jnp.logical_not(stays))
    def _():
        o_copy.wait_send()

    for i in range(3):
        q_own(i).wait()


def end_exchange(fsdp, sp, partial, low, w, x, grad_mid, gains, gains_in, router, number):
    count = fsdp * sp
    block = partial.shape[1:]
    rows = D // count
    dma = pltpu.SemaphoreType.DMA
    return pl.pallas_call(
        functools.partial(end_kernel, fsdp, sp),
        out_shape=(
            jax.ShapeDtypeStruct((TOK_DEV, D), F32),
            jax.ShapeDtypeStruct((rows, D), BF16),
            jax.ShapeDtypeStruct((rows, D), BF16),
            jax.ShapeDtypeStruct((rows, D), BF16),
            jax.ShapeDtypeStruct((rows, D), BF16),
            jax.ShapeDtypeStruct((16, 128), F32),
        ),
        in_specs=[ANY, ANY, ANY, VMEM, VMEM, VMEM, VMEM, VMEM],
        out_specs=[VMEM, ANY, ANY, ANY, ANY, VMEM],
        scratch_shapes=[
            pltpu.VMEM((sp, TOK_DEV, D), BF16),
            pltpu.VMEM(low.shape, BF16),
            pltpu.VMEM(w.shape, BF16),
            pltpu.VMEM((TOK_DEV, D), F32),
            pltpu.VMEM(block, BF16),
            pltpu.VMEM((rows, D), BF16),
            pltpu.VMEM((8, D), F32),
            pltpu.VMEM((count, 16, 128), F32),
            pltpu.VMEM((count, 16, 128), F32),
            dma((2,)),
            dma((sp, 3)), dma((sp, 3)), dma, dma, dma((count,)), dma((count,)), dma((3,)),
        ]
        + plane_scratch((TOK_DEV, D), sp)
        + LineReduce.scratch(fsdp, block),
        compiler_params=comm_params(number),
        name="end_exchange",
    )(partial, low, w, x, grad_mid, gains, gains_in, router)


def dot_nt(a, b):
    return lax.dot_general(a, b, (((1,), (1,)), ((), ())), preferred_element_type=F32)


def dot_tn(a, b):
    return lax.dot_general(a, b, (((0,), (0,)), ((), ())), preferred_element_type=F32)


def dot_nn(a, b):
    return jnp.dot(a, b, preferred_element_type=F32)


def whole(shape):
    return pl.BlockSpec(shape, lambda *_: (0,) * len(shape))


def lanes(first, second):
    lane = lax.broadcasted_iota(jnp.int32, (first.shape[0], 128), 1)
    return jnp.where(lane == 0, first, jnp.where(lane == 1, second, 0.0))


def inverse_of(sums, lane):
    return lax.rsqrt(sums[:, lane : lane + 1] / D + EPSILON)


def turn(v, table, sign=1.0):
    half = HEAD_DIM // 2
    front = lax.broadcasted_iota(jnp.int32, table.shape, 1) < half
    turned = pltpu.roll(table, half, 1)
    cosine = jnp.where(front, table, turned)
    sine = jnp.where(front, -turned, table)
    return v * cosine + pltpu.roll(v, half, 1) * (sine * sign)


def turn_back(v, table):
    return turn(v, table, -1.0)


def project_kernel(sp, x_ref, gain, w_ref, first_out, q_out, k_out, v_out, sums_out, squares, *scratch):
    step = pl.program_id(0)
    total = PlaneSum(scratch, lax.axis_index("fsdp"), lax.axis_index("sp"), sp)
    barrier = pltpu.get_barrier_semaphore()

    @pl.when(step == 0)
    def _():
        total.greet(barrier)

    x = x_ref[...].astype(F32)
    inverse = lax.rsqrt(jnp.mean(x * x, axis=-1, keepdims=True) + EPSILON)
    first = (x * inverse * gain[0:1, :]).astype(BF16)
    first_out[...] = first
    q = dot_nn(first, w_ref[0])
    q_out[...] = q
    k = dot_nn(first, w_ref[1])
    k_out[...] = k
    at = pl.ds(pl.multiple_of(step * TOK_DEV, TOK_DEV), TOK_DEV)
    squares[at, :] = lanes(
        jnp.sum(q * q, axis=-1, keepdims=True), jnp.sum(k * k, axis=-1, keepdims=True)
    )
    last = step == pl.num_programs(0) - 1

    @pl.when(last)
    def _():
        pl.semaphore_wait(barrier, sp - 1)
        total.start(squares)

    v_out[...] = dot_nn(first, w_ref[2]).astype(BF16)

    @pl.when(last)
    def _():
        total.finish(sums_out)


def project(sp, x, gains, w):
    seq, cols = x.shape[0], w.shape[2]

    def block(width):
        return pl.BlockSpec((TOK_DEV, width), lambda i: (i, 0))

    return pl.pallas_call(
        functools.partial(project_kernel, sp),
        grid=(seq // TOK_DEV,),
        out_shape=(
            jax.ShapeDtypeStruct((seq, D), BF16),
            jax.ShapeDtypeStruct((seq, cols), F32),
            jax.ShapeDtypeStruct((seq, cols), F32),
            jax.ShapeDtypeStruct((seq, cols), BF16),
            jax.ShapeDtypeStruct((seq, 128), F32),
        ),
        in_specs=[block(D), whole(gains.shape), whole(w.shape)],
        out_specs=[block(D), block(cols), block(cols), block(cols), whole((seq, 128))],
        scratch_shapes=[pltpu.VMEM((seq, 128), F32)] + PlaneSum.scratch(seq, sp),
        compiler_params=comm_params(1),
        name="project",
    )(x, gains, w)


def attend_kernel(
    q_raw, k_raw, v_ref, squares, gain, table, o_ref, sum_ref, q_ref, k_ref
):
    head = pl.program_id(0)

    @pl.when(head == 0)
    def _():
        sum_ref[...] = squares[...]

    q_inv, k_inv = inverse_of(squares, 0), inverse_of(squares, 1)
    q_ref[...] = turn(q_raw[...] * q_inv * gain[2:3, :], table[...]).astype(BF16)
    k_ref[...] = turn(k_raw[...] * k_inv * gain[3:4, :], table[...]).astype(BF16)
    for i in range(q_ref.shape[0] // BLK):
        rows, seen = pl.ds(i * BLK, BLK), pl.ds(0, (i + 1) * BLK)
        scores = dot_nt(q_ref[rows, :], k_ref[seen, :]) * SCALE
        row_max = jnp.max(scores, axis=-1, keepdims=True)
        exp_rows = jnp.exp(scores - row_max)
        row_sum = jnp.sum(exp_rows, axis=-1, keepdims=True)
        probs = (exp_rows / row_sum).astype(BF16)
        o_ref[rows, :] = dot_nn(probs, v_ref[seen, :]).astype(BF16)
        lane = lax.broadcasted_iota(jnp.int32, (BLK, 128), 1)
        sum_ref[rows, :] += jnp.where(lane == head + 2, row_max + jnp.log(row_sum), 0.0)


def attend(q_raw, k_raw, v, squares, gains, table):
    seq, width = v.shape
    heads = width // HEAD_DIM
    spec = pl.BlockSpec((seq, HEAD_DIM), lambda h: (0, h))
    return pl.pallas_call(
        attend_kernel,
        grid=(heads,),
        out_shape=(
            jax.ShapeDtypeStruct((seq, width), BF16),
            jax.ShapeDtypeStruct((seq, 128), F32),
            jax.ShapeDtypeStruct((seq, width), BF16),
            jax.ShapeDtypeStruct((seq, width), BF16),
        ),
        in_specs=[
            spec, spec, spec, whole((seq, 128)),
            pl.BlockSpec((4, HEAD_DIM), lambda h: (0, h)),
            whole((seq, HEAD_DIM)),
        ],
        out_specs=[spec, whole((seq, 128)), spec, spec],
        compiler_params=pltpu.CompilerParams(vmem_limit_bytes=VLIM),
        name="attend",
    )(q_raw, k_raw, v, squares, gains, table)


def attend_back_head(
    h, q_ref, k_ref, v_ref, sums, q_raw, k_raw, gain, table,
    q_scaled, k_scaled, dv_out, dots, gains_out, dv_ref,
):
    head = slice(h * HEAD_DIM, (h + 1) * HEAD_DIM)
    k_scaled[:, head] = jnp.zeros(k_raw[:, head].shape, F32)
    dv_ref[...] = jnp.zeros_like(dv_ref)
    gain_q, gain_k = gain[2:3, head], gain[3:4, head]
    gain_sum = jnp.zeros((1, HEAD_DIM), F32)
    size = BLK if q_ref.shape[0] <= 4 * BLK else BLK // 2
    for i in range(q_ref.shape[0] // size):
        rows, seen = pl.ds(i * size, size), pl.ds(0, (i * size // BLK + 1) * BLK)
        q, g, keys = q_ref[rows, head], dv_out[rows, head], k_ref[seen, head]
        scores = dot_nt(q, keys) * SCALE
        probs = jnp.exp(scores - sums[rows, h + 2 : h + 3])
        grad_probs = dot_nt(g, v_ref[seen, head])
        row_dot = jnp.sum(probs * grad_probs, axis=-1, keepdims=True)
        grad_scores = (probs * (grad_probs - row_dot)).astype(BF16)
        k_scaled[seen, head] += dot_tn(grad_scores, q)
        dv_ref[seen, :] += dot_tn(probs.astype(BF16), g)
        grad_y = turn_back(dot_nn(grad_scores, keys) * SCALE, table[rows, :])
        normed = q_raw[rows, head] * inverse_of(sums.at[rows, :], 0)
        scaled = grad_y * gain_q
        q_scaled[rows, head] = scaled
        dots[rows, :] += lanes(jnp.sum(scaled * normed, axis=-1, keepdims=True), 0.0)
        gain_sum += jnp.sum(grad_y * normed, axis=0, keepdims=True)
    grad_y = turn_back(k_scaled[:, head] * SCALE, table[...])
    normed = k_raw[:, head] * inverse_of(sums, 1)
    scaled = grad_y * gain_k
    k_scaled[:, head] = scaled
    k_dots = jnp.sum(scaled * normed, axis=-1, keepdims=True)
    dots[...] += lanes(jnp.zeros_like(k_dots), k_dots)
    gains_out[0:1, head] = gain_sum
    gains_out[1:2, head] = jnp.sum(grad_y * normed, axis=0, keepdims=True)
    dv_out[:, head] = dv_ref[...].astype(BF16)


def branch_back_kernel(
    fsdp, sp, x_ref, p_ref, wo_ref, q_ref, k_ref, v_ref, sums, q_raw, k_raw, gain, table,
    all_ref, out_ref, q_scaled, k_scaled, dv_out, dots, gains_out,
    g_all, dv_ref, xsend, xrecv, own_sem, all_sem, *scratch,
):
    f, s = lax.axis_index("fsdp"), lax.axis_index("sp")
    lines = fsdp // 2
    barrier = pltpu.get_barrier_semaphore()
    sums_over = PlaneSum(scratch[:4], f, s, sp)
    expected = greet_line(barrier, lines, f, s) + sums_over.greet(barrier)
    plane = plane_gather_of(x_ref, g_all, f, s, sp, xsend, xrecv)
    own = pltpu.make_async_copy(x_ref, plane.at(s, 0, x_ref.shape[0]), own_sem)
    own.start()
    pl.semaphore_wait(barrier, expected)
    plane.start()
    line = LineReduce(p_ref, scratch[4:], lines, f, s)
    line.start()
    dots[...] = jnp.zeros_like(dots)
    out_all = pltpu.make_async_copy(g_all, all_ref, all_sem)
    for t in range(lines - 1):
        line.step(t)
        if t == min(1, lines - 2):
            plane.forward()
    plane.finish()
    own.wait()
    out_all.start()

    def block(i, carry):
        at = pl.ds(pl.multiple_of(i * TOK_DEV, TOK_DEV), TOK_DEV)
        dv_out[at, :] = dot_nt(g_all[at, :], wo_ref[...]).astype(BF16)
        return carry

    lax.fori_loop(0, sp, block, 0)
    for h in range(q_ref.shape[1] // HEAD_DIM):
        attend_back_head(
            h, q_ref, k_ref, v_ref, sums, q_raw, k_raw, gain, table,
            q_scaled, k_scaled, dv_out, dots, gains_out, dv_ref,
        )
    sums_over.start(dots)
    line.finish(out_ref)
    sums_over.finish(dots)
    out_all.wait()


def branch_back(fsdp, sp, x, partial, wo, q, k, v, sums, q_raw, k_raw, gains, table):
    block = partial.shape[1:]
    seq, width = q.shape
    dma = pltpu.SemaphoreType.DMA
    return pl.pallas_call(
        functools.partial(branch_back_kernel, fsdp, sp),
        out_shape=(
            jax.ShapeDtypeStruct((seq, D), BF16),
            jax.ShapeDtypeStruct(block, F32),
            jax.ShapeDtypeStruct((seq, width), F32),
            jax.ShapeDtypeStruct((seq, width), F32),
            jax.ShapeDtypeStruct((seq, width), BF16),
            jax.ShapeDtypeStruct((seq, 128), F32),
            jax.ShapeDtypeStruct((2, width), F32),
        ),
        in_specs=[VMEM, ANY] + [VMEM] * 9,
        out_specs=[ANY] + [VMEM] * 6,
        scratch_shapes=[
            pltpu.VMEM((seq, D), BF16), pltpu.VMEM((seq, HEAD_DIM), F32), dma((sp,)), dma((sp,)), dma, dma,
        ]
        + PlaneSum.scratch(seq, sp)
        + LineReduce.scratch(fsdp, block),
        compiler_params=comm_params(5),
        name="branch_back",
    )(x, partial, wo, q, k, v, sums, q_raw, k_raw, gains, table)


def held(shape):
    return pl.BlockSpec(
        shape, lambda *_: (0,) * len(shape), pipeline_mode=pl.Buffered(buffer_count=1)
    )


def weight_kernel(
    q_scaled, k_scaled, q_raw, k_raw, squares, dots, dv_ref, first, attended, g_ref, out, low, square
):
    f = pl.program_id(0)
    height = first.shape[1]
    rows = out.shape[1] - 3 * height
    cols = out.shape[2]
    sp = D // cols

    @pl.when(f == 0)
    def _():
        for n, scaled, raw in ((0, q_scaled, q_raw), (1, k_scaled, k_raw)):
            inverse = inverse_of(squares, n)
            mean = dots[:, n : n + 1] / D
            low[:, n * cols : (n + 1) * cols] = (
                inverse * (scaled[...] - raw[...] * (inverse * mean))
            ).astype(BF16)
        low[:, 2 * cols :] = dv_ref[...]
        for c in range(sp):
            at = slice(c * cols, (c + 1) * cols)
            square[:, at] = dot_tn(attended[...], g_ref[:, at]).astype(BF16)

    grads = dot_tn(first[...], low[...]).astype(BF16)
    for n in range(3):
        out[0, n * height : (n + 1) * height, :] = grads[:, n * cols : (n + 1) * cols]
    each = rows // sp
    from_rows = pl.ds(pl.multiple_of(f * each, each), each)
    for c in range(sp):
        at = 3 * height + c * each
        out[0, at : at + each, :] = square[from_rows, c * cols : (c + 1) * cols]


def weight_parts(fsdp, q_scaled, k_scaled, q_raw, k_raw, squares, dots, dv, first, attended, g):
    seq, cols = dv.shape
    height = D // fsdp
    each = cols // fsdp
    return pl.pallas_call(
        weight_kernel,
        grid=(fsdp,),
        out_shape=(
            jax.ShapeDtypeStruct((fsdp, 3 * height + D // cols * each, cols), BF16),
            jax.ShapeDtypeStruct((seq, 3 * cols), BF16),
        ),
        in_specs=[held((seq, cols))] * 4
        + [held((seq, 128))] * 2
        + [
            held((seq, cols)),
            pl.BlockSpec((seq, height), lambda f: (0, f)),
            held((seq, cols)),
            held((seq, D)),
        ],
        out_specs=[
            pl.BlockSpec((1, 3 * height + D // cols * each, cols), lambda f: (f, 0, 0)),
            whole((seq, 3 * cols)),
        ],
        scratch_shapes=[pltpu.VMEM((cols, D), BF16)],
        compiler_params=pltpu.CompilerParams(vmem_limit_bytes=VLIM),
        name="weight_parts",
    )(q_scaled, k_scaled, q_raw, k_raw, squares, dots, dv, first, attended, g)


def two_parts(x, axis):
    high = x.astype(BF16)
    return jnp.concatenate([high, (x - high.astype(F32)).astype(BF16)], axis=axis)


def blocks_of(shape):
    return pl.BlockSpec((1,) + shape, lambda b: (b,) + (0,) * len(shape))


def slots_of(slots, width):
    return pl.BlockSpec((EXP_DEV, slots, width), lambda b: (0, b, 0))


def route_kernel(picks, rows_in, router, columns, out, probs_out, gates_out):
    slots = out.shape[1]
    for n in range(D // 512):
        at = pl.ds(n * 512, 512)
        got = dot_nn(picks[0], rows_in[0, :, at]).astype(BF16)
        for e in range(EXP_DEV):
            out[e, :, at] = got[e * slots : (e + 1) * slots]
    logits = dot_nt(rows_in[0], router[...])
    exp_logits = jnp.exp(logits - jnp.max(logits, axis=1, keepdims=True))
    probs = exp_logits / jnp.sum(exp_logits, axis=1, keepdims=True)
    probs_out[0] = probs
    both = two_parts(probs, 1)
    for e in range(EXP_DEV):
        moved = dot_nn(picks[0, e * slots : (e + 1) * slots, :], both)
        mask = columns[e : e + 1, :]
        gates_out[e] = jnp.sum(moved * jnp.concatenate([mask, mask], axis=1), axis=1, keepdims=True)


def route(picks, tokens, router_t, columns):
    blocks = tokens.shape[0]
    slots = picks.shape[1] // EXP_DEV
    total = blocks * slots
    experts = router_t.shape[0]
    return pl.pallas_call(
        route_kernel,
        grid=(blocks,),
        out_shape=(
            jax.ShapeDtypeStruct((EXP_DEV, total, D), BF16),
            jax.ShapeDtypeStruct((blocks, TOK_DEV, experts), F32),
            jax.ShapeDtypeStruct((EXP_DEV, total, 1), F32),
        ),
        in_specs=[
            blocks_of(picks.shape[1:]), blocks_of((TOK_DEV, D)), whole(router_t.shape),
            whole(columns.shape),
        ],
        out_specs=[slots_of(slots, D), blocks_of((TOK_DEV, experts)), slots_of(slots, 1)],
        compiler_params=pltpu.CompilerParams(vmem_limit_bytes=VLIM),
        name="route",
    )(picks, tokens, router_t, columns)


FT = 256


def active_kernel(x_ref, g_ref, w_ref, u_ref, gates, gated, grad_gate, grad_up, dots):
    @pl.when(pl.program_id(1) == 0)
    def _():
        dots[...] = jnp.zeros_like(dots)

    total = x_ref.shape[1]
    chunk = total // 4
    for first in range(0, total, chunk):
        at = slice(first, first + chunk)
        gate_pre = dot_nn(x_ref[0, at, :], g_ref[0])
        up_pre = dot_nn(x_ref[0, at, :], w_ref[0])
        sig = jax.nn.sigmoid(gate_pre)
        silu = gate_pre * sig
        hidden = silu * up_pre
        back = u_ref[0, at, :]
        gate = gates[0, at, :]
        dots[0, at, :] += jnp.sum(hidden * back, axis=1, keepdims=True)
        gated[0, at, :] = (hidden * gate).astype(BF16)
        back = back * gate
        grad_gate[0, at, :] = (back * up_pre * (sig * (1.0 + gate_pre * (1.0 - sig)))).astype(BF16)
        grad_up[0, at, :] = (back * silu).astype(BF16)


def active(x, w_gate, w_up, u, gates):
    _, total, _ = x.shape
    ff = w_up.shape[2]
    wide = 2 * FT
    tile = pl.BlockSpec((1, total, wide), lambda e, j: (e, 0, j))
    weight = pl.BlockSpec((1, D, wide), lambda e, j: (e, 0, j))
    column = pl.BlockSpec((1, total, 1), lambda e, j: (e, 0, 0))
    low = jax.ShapeDtypeStruct((EXP_DEV, total, ff), BF16)
    return pl.pallas_call(
        active_kernel,
        grid=(EXP_DEV, ff // wide),
        out_shape=(low, low, low, jax.ShapeDtypeStruct((EXP_DEV, total, 1), F32)),
        in_specs=[
            pl.BlockSpec((1, total, D), lambda e, j: (e, 0, 0)), weight, weight, tile, column,
        ],
        out_specs=[tile, tile, tile, column],
        compiler_params=pltpu.CompilerParams(vmem_limit_bytes=VLIM),
        name="active",
    )(x, w_gate, w_up, u, gates)


def weight_grad_kernel(a_ref, b_ref, out):
    out[0] = dot_tn(a_ref[0], b_ref[0]).astype(BF16)


def weight_grad(a, b, name):
    _, total, height = a.shape
    width = b.shape[2]
    size = 1024
    return pl.pallas_call(
        weight_grad_kernel,
        grid=(EXP_DEV, height // size, width // size),
        out_shape=jax.ShapeDtypeStruct((EXP_DEV, height, width), BF16),
        in_specs=[
            pl.BlockSpec((1, total, size), lambda e, i, j: (e, 0, i)),
            pl.BlockSpec((1, total, size), lambda e, i, j: (e, 0, j)),
        ],
        out_specs=pl.BlockSpec((1, size, size), lambda e, i, j: (e, i, j)),
        compiler_params=pltpu.CompilerParams(vmem_limit_bytes=VLIM),
        name=name,
    )(a, b)


def rows_back_kernel(a_ref, b_ref, g_ref, w_ref, out):
    out[0] = (dot_nt(a_ref[0], g_ref[0]) + dot_nt(b_ref[0], w_ref[0])).astype(BF16)


def rows_back(grad_gate_pre, grad_up_pre, w_gate, w_up):
    _, total, ff = grad_up_pre.shape
    size = 512
    row = pl.BlockSpec((1, total, ff), lambda e, j: (e, 0, 0))
    weight = pl.BlockSpec((1, size, ff), lambda e, j: (e, j, 0))
    return pl.pallas_call(
        rows_back_kernel,
        grid=(EXP_DEV, D // size),
        out_shape=jax.ShapeDtypeStruct((EXP_DEV, total, D), BF16),
        in_specs=[row, row, weight, weight],
        out_specs=pl.BlockSpec((1, total, size), lambda e, j: (e, 0, j)),
        compiler_params=pltpu.CompilerParams(vmem_limit_bytes=VLIM),
        name="rows_back",
    )(grad_gate_pre, grad_up_pre, w_gate, w_up)


def combine_kernel(turned, rows_ref, tokens, probs, dots, router, columns, out, router_out):
    @pl.when(pl.program_id(0) == 0)
    def _():
        router_out[...] = jnp.zeros_like(router_out)

    choice = jnp.zeros(probs.shape[1:], F32)
    for e in range(EXP_DEV):
        moved = dot_nn(turned[0, e], dots[e])
        choice += jnp.sum(moved, axis=1, keepdims=True) * columns[e : e + 1, :]
    p = probs[0]
    grad_logits = p * (choice - jnp.sum(p * choice, axis=1, keepdims=True))
    both = two_parts(grad_logits, 1)
    for n in range(D // 512):
        at = pl.ds(n * 512, 512)
        total = dot_nn(both, router[:, at])
        for e in range(EXP_DEV):
            total += dot_nn(turned[0, e], rows_ref[e, :, at])
        out[0, :, at] = total.astype(BF16)
    router_out[...] += dot_tn(both, tokens[0])


def combine(turned, grad_rows, tokens, probs, dots, router_two, columns):
    blocks = tokens.shape[0]
    slots = turned.shape[3]
    return pl.pallas_call(
        combine_kernel,
        grid=(blocks,),
        out_shape=(
            jax.ShapeDtypeStruct((blocks, TOK_DEV, D), BF16),
            jax.ShapeDtypeStruct((router_two.shape[0], D), F32),
        ),
        in_specs=[
            blocks_of(turned.shape[1:]), slots_of(slots, D), blocks_of((TOK_DEV, D)),
            blocks_of(probs.shape[1:]), slots_of(slots, 128), whole(router_two.shape),
            whole(columns.shape),
        ],
        out_specs=[blocks_of((TOK_DEV, D)), whole((router_two.shape[0], D))],
        compiler_params=pltpu.CompilerParams(vmem_limit_bytes=VLIM),
        name="combine",
    )(turned, grad_rows, tokens, probs, dots, router_two, columns)


def widen_kernel(*refs):
    count = len(refs) // 2
    for low, out in zip(refs[:count], refs[count:]):
        out[...] = low[...].astype(F32)


def widen(arrays):
    flat = [x.reshape(-1, x.shape[-1]) for x in arrays]
    steps = 4
    specs = [
        whole(x.shape)
        if x.shape[0] % (16 * steps)
        else pl.BlockSpec((x.shape[0] // steps, x.shape[1]), lambda i: (i, 0))
        for x in flat
    ]
    wide = pl.pallas_call(
        widen_kernel,
        grid=(steps,),
        out_shape=tuple(jax.ShapeDtypeStruct(x.shape, F32) for x in flat),
        in_specs=specs,
        out_specs=specs,
        compiler_params=pltpu.CompilerParams(vmem_limit_bytes=VLIM),
        name="widen",
    )(*flat)
    return [x.reshape(like.shape) for x, like in zip(wide, arrays)]


def angles(seq):
    freqs = np.float32(ROPE_BASE) ** (-2.0 * np.arange(HEAD_DIM // 2, dtype=np.float32) / HEAD_DIM)
    turned = np.arange(seq, dtype=np.float32)[:, None] * freqs[None, :].astype(np.float32)
    return jnp.asarray(np.concatenate([np.cos(turned), np.sin(turned)], axis=1), F32)


def body(
    layer_input, output_grad, w_query, w_key, w_value, w_output, w_router, norm_gains,
    w_gate, w_up, w_down, expert_routes,
):
    fsdp, sp = lax.axis_size("fsdp"), lax.axis_size("sp")
    f, s = lax.axis_index("fsdp"), lax.axis_index("sp")
    count = fsdp * sp
    experts = EXP_DEV * fsdp
    capacity = TOK_DEV * TOP // experts * 17 // 16
    slots = -(-capacity // 16) * 16
    seq = TOK_DEV * sp
    cols = D // sp
    rows = D // count

    down_full = lax.all_gather(w_down, "sp", axis=1, tiled=True)
    gate_full = lax.all_gather(w_gate, "sp", axis=1, tiled=True)
    up_full = lax.all_gather(w_up, "sp", axis=1, tiled=True)

    router_size = rows * experts
    misc = jnp.concatenate([w_router.reshape(router_size), norm_gains.reshape(4 * rows)])
    misc_rows = -(-misc.shape[0] // 2048) * 16
    misc = jnp.pad(misc, (0, misc_rows * 128 - misc.shape[0])).reshape(misc_rows, 128)
    routes = expert_routes.reshape(TOK_DEV * TOP // 128, 128)
    early = TOK_DEV // 8
    x_all, w_all, wo_s, grad_first_half, misc_all, routes_all = gather_start(
        fsdp, sp, layer_input, jnp.stack([w_query, w_key, w_value]), w_output, output_grad[:early],
        misc, routes,
    )
    misc_all = misc_all.reshape(count, misc_rows * 128)
    router_w = misc_all[:, :router_size].reshape(D, experts)
    router_t = router_w.T
    gains_w = misc_all[:, router_size : router_size + 4 * rows].reshape(count, 4, rows)
    gains32 = gains_w.transpose(1, 0, 2).reshape(4, D).astype(F32)
    gains_own = lax.dynamic_slice_in_dim(gains32, s * cols, cols, axis=1)

    routes_block = routes_all.reshape(fsdp, TOK_DEV, TOP)
    own_ids = f * EXP_DEV + jnp.arange(EXP_DEV, dtype=jnp.int32)
    chosen = jnp.any(routes_block[:, :, :, None] == own_ids, axis=2)
    before = jnp.arange(TOK_DEV)[:, None] > jnp.arange(TOK_DEV)[None, :]
    place = jnp.einsum(
        "ut,fte->feu", before.astype(BF16), chosen.astype(BF16), preferred_element_type=F32
    ).astype(jnp.int32)
    slot_ids = jnp.arange(slots, dtype=jnp.int32)
    picks = (
        (place[:, :, None, :] == slot_ids[:, None]) & chosen.transpose(0, 2, 1)[:, :, None, :]
    ).astype(BF16).reshape(fsdp, EXP_DEV * slots, TOK_DEV)
    turned = (
        (place[:, :, :, None] == slot_ids) & chosen.transpose(0, 2, 1)[:, :, :, None]
    ).astype(BF16)
    columns = (jnp.arange(experts, dtype=jnp.int32)[None, :] == own_ids[:, None]).astype(F32)

    first_in, q_raw, k_raw, values, squares = project(sp, x_all, gains32, w_all)
    table = angles(seq)
    attended, sums, queries, keys = attend(
        q_raw, k_raw, values, squares, gains_own, table
    )
    branch = dot_nn(attended, wo_s).astype(BF16).reshape(sp, TOK_DEV, D)
    mid, second_in, grad_second_half = branch_sum(
        fsdp, branch, output_grad[early:], layer_input, gains32
    )

    tokens, grad_taken, unscaled = token_gather(
        fsdp, second_in, grad_first_half, grad_second_half, picks, down_full
    )
    received, probs, slot_gates = route(picks, tokens, router_t, columns)
    gated, grad_gate_pre, grad_up_pre, slot_dots = active(
        received, gate_full, up_full, unscaled, slot_gates
    )
    dots_two = jnp.pad(two_parts(slot_dots, 2), ((0, 0), (0, 0), (0, 126)))
    grad_rows = rows_back(grad_gate_pre, grad_up_pre, gate_full, up_full)
    second_part, router_two = combine(
        turned, grad_rows, tokens, probs, dots_two, jnp.concatenate([router_t, router_t], axis=0),
        columns,
    )
    grad_router = (router_two[:experts] + router_two[experts:]).T

    def shed(grad):
        return lax.psum_scatter(grad, "sp", scatter_dimension=1, tiled=True)

    grad_down = shed(weight_grad(gated, grad_taken, "down_grad"))
    grad_gate = shed(weight_grad(received, grad_gate_pre, "gate_grad"))
    grad_mid, grad_mid_low, gain_rows, out_part, up_part = token_back(
        fsdp, second_part, gated, down_full, turned, received, grad_up_pre, mid, output_grad, gains32
    )
    grad_up = shed(up_part)

    grad_branch, out_sum, q_scaled, k_scaled, grad_values, dots, gain_qk = branch_back(
        fsdp, sp, grad_mid_low, out_part, wo_s, queries, keys, values, sums, q_raw, k_raw,
        gains_own, table,
    )
    layer_out = (mid + out_sum).astype(BF16)
    weight_part, grads_low = weight_parts(
        fsdp, q_scaled, k_scaled, q_raw, k_raw, squares, dots, grad_values, first_in, attended, grad_branch
    )

    gain_rows = lax.dynamic_update_slice(gain_rows, gain_qk, (2, s * cols))
    router_part = grad_router.reshape(count, router_size)
    router_part = jnp.pad(router_part, ((0, 0), (0, 1024 - router_size))).reshape(count, 8, 128)
    input_grad, *weight_grads, small = end_exchange(
        fsdp, sp, weight_part, grads_low, w_all, layer_input, grad_mid, gains32, gain_rows, router_part, 8
    )
    *weight_grads, grad_gate, grad_up, grad_down = widen(
        [*weight_grads, grad_gate, grad_up, grad_down]
    )
    grad_router_own = small[:8].reshape(1024)[:router_size].reshape(rows, experts)
    first_lane = (f * sp + s) * rows % 128
    grad_gains = lax.dynamic_slice(small[8:12], (0, first_lane), (4, rows))
    return (
        layer_out, input_grad, *weight_grads,
        grad_router_own, grad_gains, grad_gate, grad_up, grad_down,
    )


def solution(mesh):
    both, split = P(("fsdp", "sp"), None), P("fsdp", "sp", None)
    gains = P(None, ("fsdp", "sp"))
    return jax.shard_map(
        body,
        mesh=mesh,
        in_specs=(both,) * 7 + (gains,) + (split,) * 3 + (both,),
        out_specs=(both,) * 7 + (gains,) + (split,) * 3,
        check_vma=False,
    )
```

```python
import functools

import jax
import jax.numpy as jnp
import numpy as np
from jax import lax
from jax.experimental import pallas as pl
from jax.experimental.pallas import tpu as pltpu
from jax.sharding import PartitionSpec as P

D = 2048
HEADS = 16
HEAD_DIM = 128
TOP = 8
EXP_DEV = 2
BLK = 256
TOK_DEV = 256
EPSILON = 1e-05
ROPE_BASE = 10000.0
MASKED = -1000000000.0
SCALE = HEAD_DIM ** (-0.5)
MESH = pl.DeviceIdType.MESH
ANY = pl.BlockSpec(memory_space=pl.ANY)
VMEM = pl.BlockSpec(memory_space=pltpu.VMEM)
VLIM = 60 * 1024 * 1024
F32 = jnp.float32
BF16 = jnp.bfloat16


def remote(src, dst, send_sem, recv_sem, device):
    return pltpu.make_async_remote_copy(
        src_ref=src,
        dst_ref=dst,
        send_sem=send_sem,
        recv_sem=recv_sem,
        device_id=device,
        device_id_type=MESH,
    )


def landed(ref, sem):
    pltpu.make_async_copy(ref, ref, sem).wait()


def signal(sem, device):
    pl.semaphore_signal(sem, inc=1, device_id=device, device_id_type=MESH)


def greet_line(barrier, lines, f, s):
    place, core = f // 2, f % 2
    signal(barrier, (f + 1 - 2 * core, s))

    @pl.when(place > 0)
    def _():
        signal(barrier, (f - 2, s))

    @pl.when(place < lines - 1)
    def _():
        signal(barrier, (f + 2, s))

    return 1 + jnp.where(place > 0, 1, 0) + jnp.where(place < lines - 1, 1, 0)


class LineGather:
    def __init__(self, views, owns, lines, f, s, send, recv):
        self.views, self.owns, self.lines, self.f, self.s = views, owns, lines, f, s
        self.send, self.recv = send, recv
        self.place, self.core = f // 2, f % 2

    def copy(self, v, block, slot, way):
        device = {
            "right": (self.f + 2, self.s),
            "left": (self.f - 2, self.s),
            "partner": (self.f + 1 - 2 * self.core, self.s),
        }[way]
        index = {"right": 0, "left": 1, "partner": 2}[way]
        ref = self.views[v](block)
        own = self.owns[v] if slot == 0 and self.owns[v] is not None else ref
        return remote(own, ref, self.send.at[v, slot, index], self.recv.at[v, block], device)

    def start_own(self, v):
        @pl.when(self.place < self.lines - 1)
        def _():
            self.copy(v, self.f, 0, "right").start()

        @pl.when(self.place > 0)
        def _():
            self.copy(v, self.f, 0, "left").start()

        self.copy(v, self.f, 0, "partner").start()

    def forward(self, v, k):
        place, lines = self.place, self.lines

        @pl.when(place >= k)
        def _():
            block = self.f - 2 * k
            landed(self.views[v](block), self.recv.at[v, block])

            @pl.when(place < lines - 1)
            def _():
                self.copy(v, block, k, "right").start()

            self.copy(v, block, k, "partner").start()

        @pl.when(place + k < lines)
        def _():
            block = self.f + 2 * k
            landed(self.views[v](block), self.recv.at[v, block])

            @pl.when(place > 0)
            def _():
                self.copy(v, block, lines - 1 + k, "left").start()

            self.copy(v, block, lines - 1 + k, "partner").start()

    def finish(self, v):
        place, lines = self.place, self.lines
        for line in range(lines):
            block = 2 * line + 1 - self.core
            landed(self.views[v](block), self.recv.at[v, block])
        self.copy(v, self.f, 0, "partner").wait_send()

        @pl.when(place < lines - 1)
        def _():
            self.copy(v, self.f, 0, "right").wait_send()

        @pl.when(place > 0)
        def _():
            self.copy(v, self.f, 0, "left").wait_send()

        for k in range(1, lines):

            @pl.when(place >= k)
            def _():
                block = self.f - 2 * k

                @pl.when(place < lines - 1)
                def _():
                    self.copy(v, block, k, "right").wait_send()

                self.copy(v, block, k, "partner").wait_send()

            @pl.when(place + k < lines)
            def _():
                block = self.f + 2 * k

                @pl.when(place > 0)
                def _():
                    self.copy(v, block, lines - 1 + k, "left").wait_send()

                self.copy(v, block, lines - 1 + k, "partner").wait_send()


def line_sems(arrays, fsdp):
    lines = fsdp // 2
    return [
        pltpu.SemaphoreType.DMA((arrays, 2 * lines, 3)),
        pltpu.SemaphoreType.DMA((arrays, fsdp)),
    ]


def add_rows(dst, a, b, rows):
    def step(i, carry):
        at = pl.ds(pl.multiple_of(i * 32, 32), 32)
        dst[at, :] = a[at, :].astype(dst.dtype) + b[at, :].astype(dst.dtype)
        return carry

    lax.fori_loop(0, rows // 32, step, 0)


class LineReduce:
    def __init__(self, p_ref, scratch, lines, f, s):
        self.p_ref, self.lines, self.f, self.s = p_ref, lines, f, s
        self.own, self.paired, self.got, self.last = scratch[:4]
        self.psend, self.precv, self.send, self.recv, self.final, self.local = scratch[4:]
        self.place, self.core = f // 2, f % 2
        self.rows = p_ref.shape[1]
        self.order = []
        for n in range(lines):
            for d in (lines - 1 - n, n):
                if d not in self.order:
                    self.order.append(d)

    @staticmethod
    def scratch(fsdp, block):
        lines = fsdp // 2
        dma = pltpu.SemaphoreType.DMA
        return [
            pltpu.VMEM((lines,) + block, BF16),
            pltpu.VMEM((lines,) + block, BF16),
            pltpu.VMEM((lines,) + block, BF16),
            pltpu.VMEM(block, BF16),
            dma((lines,)), dma((lines,)), dma((lines,)), dma((lines,)), dma, dma((lines,)),
        ]

    def load(self, i):
        return pltpu.make_async_copy(self.p_ref.at[2 * i + self.core], self.own.at[i], self.local.at[i])

    def swap(self, i):
        return remote(
            self.p_ref.at[2 * i + 1 - self.core], self.paired.at[i], self.psend.at[i],
            self.precv.at[i], (self.f + 1 - 2 * self.core, self.s),
        )

    def right(self, d, last):
        dst = self.last if last else self.got.at[d]
        sem = self.final if last else self.recv.at[d]
        return remote(self.own.at[d], dst, self.send.at[d], sem, (self.f + 2, self.s))

    def left(self, d):
        return remote(
            self.own.at[d], self.got.at[d], self.send.at[d], self.recv.at[d], (self.f - 2, self.s)
        )

    def start(self):
        for i in self.order[:2]:
            self.swap(i).start()
        for i in self.order:
            self.load(i).start()
        self.added = 0
        self.add_pairs(2)

    def add_pairs(self, until):
        for i in self.order[self.added : until]:
            self.load(i).wait()
            landed(self.paired.at[i], self.precv.at[i])
            add_rows(self.own.at[i], self.own.at[i], self.paired.at[i], self.rows)
        self.added = max(self.added, until)

    def step(self, t):
        place, lines = self.place, self.lines
        d = lines - 1 - t + place

        @pl.when(t >= place)
        def _():
            @pl.when(place > 0)
            def _():
                landed(self.got.at[d], self.recv.at[d])
                add_rows(self.own.at[d], self.own.at[d], self.got.at[d], self.rows)

            @pl.when(d == place + 1)
            def _():
                self.right(d, True).start()

            @pl.when(d != place + 1)
            def _():
                self.right(d, False).start()

        e = t - (lines - 1 - place)

        @pl.when(e >= 0)
        def _():
            @pl.when(place < lines - 1)
            def _():
                landed(self.got.at[e], self.recv.at[e])
                add_rows(self.own.at[e], self.own.at[e], self.got.at[e], self.rows)

            self.left(e).start()

        if t == 0:
            for i in self.order[2:]:
                self.swap(i).start()
        self.add_pairs(2 * t + 4)

    def finish(self, out_ref):
        place, lines, rows = self.place, self.lines, self.rows

        def total(*extra):
            def step(i, carry):
                at = pl.ds(pl.multiple_of(i * 32, 32), 32)
                value = self.own[place, at, :].astype(F32)
                for ref in extra:
                    value += ref[at, :].astype(F32)
                out_ref[at, :] = value.astype(out_ref.dtype)
                return carry

            lax.fori_loop(0, rows // 32, step, 0)

        @pl.when(place > 0)
        def _():
            landed(self.last, self.final)

        @pl.when(place < lines - 1)
        def _():
            landed(self.got.at[place], self.recv.at[place])

        @pl.when(place == 0)
        def _():
            total(self.got.at[place])

        @pl.when(place == lines - 1)
        def _():
            total(self.last)

        @pl.when(jnp.logical_and(place > 0, place < lines - 1))
        def _():
            total(self.last, self.got.at[place])

        for i in range(lines):
            self.swap(i).wait_send()

            @pl.when(place < i)
            def _():
                self.right(i, False).wait_send()

            @pl.when(place > i)
            def _():
                self.left(i).wait_send()


class PlaneGather:
    def __init__(self, own, out, f, s, send, recv):
        self.own, self.out, self.f, self.s, self.send, self.recv = own, out, f, s, send, recv
        self.rows = own.shape[0]
        self.half = self.rows // 2

    def at(self, place, first, size):
        return self.out.at[pl.ds(pl.multiple_of(place * self.rows + first, self.half), size), :]

    def near(self, k):
        return remote(
            self.own, self.at(self.s, 0, self.rows), self.send.at[k - 1], self.recv.at[k - 1],
            (self.f, self.s ^ k),
        )

    def on(self, k):
        ref = self.at(self.s ^ k, (k - 1) * self.half, self.half)
        return remote(ref, ref, self.send.at[k + 1], self.recv.at[k + 1], (self.f, self.s ^ (3 - k)))

    def start(self):
        self.near(1).start()
        self.near(2).start()

    def forward(self):
        for k in (1, 2):
            landed(self.at(self.s ^ k, 0, self.rows), self.recv.at[k - 1])
            self.on(k).start()

    def finish(self):
        landed(self.at(self.s ^ 3, 0, self.half), self.recv.at[2])
        landed(self.at(self.s ^ 3, self.half, self.half), self.recv.at[3])
        for k in (1, 2):
            self.near(k).wait_send()
            self.on(k).wait_send()


class AnyGather:
    def __init__(self, own, out, f, s, sp, send, recv):
        self.own, self.out, self.f, self.s, self.sp = own, out, f, s, sp
        self.send, self.recv = send, recv
        self.rows = own.shape[0]

    def at(self, place, first, size):
        return self.out.at[pl.ds(pl.multiple_of(place * self.rows + first, size), size), :]

    def copy(self, k):
        dst = self.at(self.s, 0, self.rows)
        return remote(self.own, dst, self.send.at[k], self.recv.at[k], (self.f, self.s ^ k))

    def start(self):
        for k in range(1, self.sp):
            self.copy(k).start()

    def forward(self):
        pass

    def finish(self):
        for k in range(1, self.sp):
            landed(self.at(self.s ^ k, 0, self.rows), self.recv.at[k])
            self.copy(k).wait_send()


class AnyReduce:
    def __init__(self, p_ref, out_ref, scratch, f, s, sp):
        self.p_ref, self.out_ref, self.f, self.s, self.sp = p_ref, out_ref, f, s, sp
        self.own, self.got, self.send, self.recv, self.local = scratch

    @staticmethod
    def scratch(block, sp):
        dma = pltpu.SemaphoreType.DMA
        return [
            pltpu.VMEM(block, BF16), pltpu.VMEM((sp,) + block, BF16), dma((sp,)), dma((sp,)), dma,
        ]

    def copy(self, k):
        d = self.s ^ k
        return remote(
            self.p_ref.at[d], self.got.at[k], self.send.at[k], self.recv.at[k], (self.f, d)
        )

    def load(self):
        return pltpu.make_async_copy(self.p_ref.at[self.s], self.own, self.local)

    def start(self, make=lambda d: None):
        for k in range(self.sp - 1, 0, -1):
            make(self.s ^ k)
            self.copy(k).start()
        make(self.s)
        self.load().start()

    def forward(self):
        self.load().wait()

    def finish(self):
        rows = self.own.shape[0]
        for k in range(1, self.sp):
            landed(self.got.at[k], self.recv.at[k])
            add_rows(self.out_ref, self.own if k == 1 else self.out_ref, self.got.at[k], rows)
        for k in range(1, self.sp):
            self.copy(k).wait_send()


def plane_gather_of(own, out, f, s, sp, send, recv):
    if sp == 4:
        return PlaneGather(own, out, f, s, send, recv)
    return AnyGather(own, out, f, s, sp, send, recv)


def plane_reduce_of(p_ref, out_ref, scratch, f, s, sp):
    if sp == 4:
        return PlaneReduce(p_ref, out_ref, scratch, f, s)
    return AnyReduce(p_ref, out_ref, scratch, f, s, sp)


def plane_scratch(block, sp):
    return PlaneReduce.scratch(block) if sp == 4 else AnyReduce.scratch(block, sp)


class PlaneReduce:
    WAYS = ((0, 1, 1), (1, 2, 2))

    def __init__(self, p_ref, out_ref, scratch, f, s):
        self.p_ref, self.out_ref, self.f, self.s = p_ref, out_ref, f, s
        self.own, self.got, self.got_on, self.send, self.recv, self.local = scratch
        self.half = p_ref.shape[1] // 2

    @staticmethod
    def scratch(block):
        dma = pltpu.SemaphoreType.DMA
        return [
            pltpu.VMEM((3,) + block, BF16), pltpu.VMEM((2,) + block, BF16),
            pltpu.VMEM(block, BF16), dma((2, 3)), dma((2, 3)), dma((3,)),
        ]

    def part(self, ref, h):
        return ref.at[pl.ds(h * self.half, self.half), :]

    def load(self, n):
        d = (self.s, self.s ^ 2, self.s ^ 1)[n]
        return pltpu.make_async_copy(self.p_ref.at[d], self.own.at[n], self.local.at[n])

    def hop(self, h, k, far):
        d = self.s ^ 3 if far else self.s ^ k
        n = 0 if far else 1
        return remote(
            self.part(self.p_ref.at[d], h), self.part(self.got.at[1 - n], h), self.send.at[h, n],
            self.recv.at[h, n], (self.f, self.s ^ k),
        )

    def on(self, h, k, n):
        return remote(
            self.part(self.own.at[n], h), self.part(self.got_on, h), self.send.at[h, 2],
            self.recv.at[h, 2], (self.f, self.s ^ (3 - k)),
        )

    def start(self, make=lambda d: None):
        make(self.s ^ 3)
        for h, k, _ in self.WAYS:
            self.hop(h, k, True).start()
        make(self.s ^ 1)
        make(self.s ^ 2)
        for h, k, _ in self.WAYS:
            self.hop(h, k, False).start()
        make(self.s)
        for n in range(3):
            self.load(n).start()

    def forward(self):
        for n in range(3):
            self.load(n).wait()
        for h, k, n in self.WAYS:
            mine = self.part(self.own.at[n], h)
            landed(self.part(self.got.at[1], h), self.recv.at[h, 0])
            add_rows(mine, mine, self.part(self.got.at[1], h), self.half)
            self.on(h, k, n).start()

    def finish(self):
        for h in (0, 1):
            landed(self.part(self.got.at[0], h), self.recv.at[h, 1])
            add_rows(
                self.part(self.out_ref, h), self.part(self.own.at[0], h), self.part(self.got.at[0], h),
                self.half,
            )
        for h in (0, 1):
            landed(self.part(self.got_on, h), self.recv.at[h, 2])
            out = self.part(self.out_ref, h)
            add_rows(out, out, self.part(self.got_on, h), self.half)
        for h, k, n in self.WAYS:
            self.hop(h, k, True).wait_send()
            self.hop(h, k, False).wait_send()
            self.on(h, k, n).wait_send()


def greet_plane(barrier, f, s, sp):
    ways = (1, 2) if sp == 4 else range(1, sp)
    for k in ways:
        signal(barrier, (f, s ^ k))
    return len(ways)


def greet_all(barrier, me, count, sp):
    def greet(i, carry):
        other = lax.rem(me + i, count)
        signal(barrier, (other // sp, lax.rem(other, sp)))
        return carry

    lax.fori_loop(1, count, greet, 0)


def rows_view(ref, rows):
    return lambda b: ref.at[pl.ds(pl.multiple_of(b * rows, rows), rows), :]


def block_view(ref):
    return lambda b: ref.at[b]


def comm_params(number):
    return pltpu.CompilerParams(
        collective_id=number, has_side_effects=True, vmem_limit_bytes=VLIM
    )


def row_target(i, rows, sp):
    parts = HEAD_DIM // rows
    head, part = i // parts, lax.rem(i, parts)
    return head // sp * parts + part, lax.rem(head, sp)


def row_owner(f, s, rows, sp):
    parts = HEAD_DIM // rows
    return (f // parts * sp + s) * parts + lax.rem(f, parts)


def start_kernel(
    fsdp, sp, x_ref, w_ref, wo_ref, g_ref, misc_ref, routes_ref,
    x_all, w_all, wo_all, g_all, misc_all, routes_all,
    send, recv, xsend, xrecv, psend, precv, wsend, wrecv, msend, mrecv, rsend, rrecv, local, wlocal,
):
    f, s = lax.axis_index("fsdp"), lax.axis_index("sp")
    count, lines = fsdp * sp, fsdp // 2
    me = f * sp + s
    rows = w_ref.shape[1]
    heads = D // sp // HEAD_DIM
    barrier = pltpu.get_barrier_semaphore()

    def w_block(s_to, g):
        at = pl.multiple_of((g * sp + s_to) * HEAD_DIM, HEAD_DIM)
        return w_ref.at[:, :, pl.ds(at, HEAD_DIM)]

    def w_rows(i, g):
        at = pl.ds(pl.multiple_of(i * rows, rows), rows)
        return w_all.at[:, at, pl.ds(g * HEAD_DIM, HEAD_DIM)]

    def w_view(b):
        size = rows * sp
        return w_all.at[:, pl.ds(pl.multiple_of(b * size, size), size), :]

    wo_view = rows_view(wo_all, rows)
    x_view = rows_view(x_all, TOK_DEV)
    w_owns = [
        pltpu.make_async_copy(w_block(s, g), w_rows(me, g), wlocal.at[g]) for g in range(heads)
    ]
    owns = [
        pltpu.make_async_copy(x_ref, x_view(s), local.at[0]),
        pltpu.make_async_copy(misc_ref, misc_all.at[me], local.at[1]),
        pltpu.make_async_copy(routes_ref, routes_all.at[f], local.at[2]),
        pltpu.make_async_copy(g_ref, g_all.at[f], local.at[3]),
    ]
    for copy in w_owns + owns:
        copy.start()
    greet_all(barrier, me, count, sp)
    pl.semaphore_wait(barrier, count - 1)

    line = LineGather([w_view, wo_view, block_view(g_all)], [None, None, g_ref], lines, f, s, send, recv)
    line.start_own(2)
    w_copies = []
    for k in range(sp - 1, 0, -1):
        s_to = s ^ k
        for g in range(heads):
            copy = remote(
                w_block(s_to, g), w_rows(me, g), psend.at[k, g], precv.at[k, g], (f, s_to)
            )
            copy.start()
            w_copies.append(copy)
    target_f, target_s = row_target(me, rows, sp)
    stays = jnp.logical_and(target_s == s, target_f == f)
    wo_copy = remote(wo_ref, wo_view(target_f), wsend, wrecv, (target_f, target_s))
    wo_own = pltpu.make_async_copy(wo_ref, wo_view(f), wrecv)

    @pl.when(stays)
    def _():
        wo_own.start()

    @pl.when(jnp.logical_not(stays))
    def _():
        wo_copy.start()

    def misc_copy(i):
        other = lax.rem(me + i, count)
        return remote(
            misc_ref, misc_all.at[me], msend.at[i], mrecv.at[me], (other // sp, lax.rem(other, sp))
        )

    def misc_go(i, carry):
        misc_copy(i).start()
        return carry

    lax.fori_loop(1, count, misc_go, 0)

    def routes_copy(i):
        other = lax.rem(f + i, fsdp)
        return remote(routes_ref, routes_all.at[f], rsend.at[i], rrecv.at[f], (other, s))

    def routes_go(i, carry):
        routes_copy(i).start()
        return carry

    lax.fori_loop(1, fsdp, routes_go, 0)

    for copy in w_owns:
        copy.wait()
    for k in range(1, sp):
        for g in range(heads):
            landed(w_rows(f * sp + (s ^ k), g), precv.at[k, g])
    line.start_own(0)
    tokens = plane_gather_of(x_ref, x_all, f, s, sp, xsend, xrecv)
    tokens.start()
    landed(wo_view(f), wrecv)
    line.start_own(1)
    for k in range(1, lines):
        for v in (2, 0, 1):
            line.forward(v, k)
        if k == min(2, lines - 1):
            tokens.forward()
    for v in range(3):
        line.finish(v)
    tokens.finish()

    def misc_end(i, carry):
        misc_copy(i).wait_send()
        other = lax.rem(me + i, count)
        landed(misc_all.at[other], mrecv.at[other])
        return carry

    lax.fori_loop(1, count, misc_end, 0)

    def routes_end(i, carry):
        routes_copy(i).wait_send()
        other = lax.rem(f + i, fsdp)
        landed(routes_all.at[other], rrecv.at[other])
        return carry

    lax.fori_loop(1, fsdp, routes_end, 0)
    for copy in w_copies:
        copy.wait_send()

    @pl.when(jnp.logical_not(stays))
    def _():
        wo_copy.wait_send()

    for copy in owns:
        copy.wait()


def gather_start(fsdp, sp, x, w, wo, g, misc, routes):
    count = fsdp * sp
    heads = D // sp // HEAD_DIM
    dma = pltpu.SemaphoreType.DMA
    return pl.pallas_call(
        functools.partial(start_kernel, fsdp, sp),
        out_shape=(
            jax.ShapeDtypeStruct((sp * TOK_DEV, D), BF16),
            jax.ShapeDtypeStruct((3, D, D // sp), BF16),
            jax.ShapeDtypeStruct((D // sp, D), BF16),
            jax.ShapeDtypeStruct((fsdp,) + g.shape, BF16),
            jax.ShapeDtypeStruct((count,) + misc.shape, BF16),
            jax.ShapeDtypeStruct((fsdp,) + routes.shape, jnp.int32),
        ),
        in_specs=[VMEM] * 6,
        out_specs=[ANY] * 6,
        scratch_shapes=line_sems(3, fsdp)
        + [
            dma((sp,)), dma((sp,)), dma((sp, heads)), dma((sp, heads)), dma, dma,
            dma((count,)), dma((count,)), dma((fsdp,)), dma((fsdp,)), dma((4,)), dma((heads,)),
        ],
        compiler_params=comm_params(0),
        name="gather_start",
    )(x, w, wo, g, misc, routes)


def branch_kernel(
    fsdp, sp, a_ref, w_ref, g_ref, x_ref, gain, out_ref, second_ref, g_all, terms, *scratch
):
    f, s = lax.axis_index("fsdp"), lax.axis_index("sp")
    lines = fsdp // 2
    barrier = pltpu.get_barrier_semaphore()
    expected = greet_line(barrier, lines, f, s) + greet_plane(barrier, f, s, sp)
    send, recv, own_sem = scratch[-3:]
    own = pltpu.make_async_copy(g_ref, g_all.at[f], own_sem)
    own.start()
    pl.semaphore_wait(barrier, expected)
    plane = plane_reduce_of(terms, out_ref, scratch[:-3], f, s, sp)
    line = LineGather([block_view(g_all)], [g_ref], lines, f, s, send, recv)
    line.start_own(0)

    def branch_of(d):
        rows = pl.ds(pl.multiple_of(d * TOK_DEV, TOK_DEV), TOK_DEV)
        for n in range(D // 512):
            at = pl.ds(n * 512, 512)
            terms[d, :, at] = dot_nn(a_ref[rows, :], w_ref[:, at]).astype(BF16)

    plane.start(branch_of)
    for k in range(1, lines):
        line.forward(0, k)
        if k == min(2, lines - 1):
            plane.forward()
    plane.finish()

    def norm(i, carry):
        at = pl.ds(pl.multiple_of(i * 32, 32), 32)
        mid = x_ref[at, :].astype(F32) + out_ref[at, :]
        out_ref[at, :] = mid
        inverse = lax.rsqrt(jnp.mean(mid * mid, axis=-1, keepdims=True) + EPSILON)
        second_ref[at, :] = (mid * inverse * gain[1:2, :]).astype(BF16)
        return carry

    lax.fori_loop(0, TOK_DEV // 32, norm, 0)
    line.finish(0)
    own.wait()


def branch_sum(fsdp, attended, w, g, x, gains):
    sp, block = attended.shape[0] // TOK_DEV, x.shape
    return pl.pallas_call(
        functools.partial(branch_kernel, fsdp, sp),
        out_shape=(
            jax.ShapeDtypeStruct(block, F32),
            jax.ShapeDtypeStruct(block, BF16),
            jax.ShapeDtypeStruct((fsdp,) + g.shape, BF16),
        ),
        in_specs=[VMEM] * 5,
        out_specs=[VMEM, VMEM, ANY],
        scratch_shapes=[pltpu.VMEM((sp,) + block, BF16)]
        + plane_scratch(block, sp) + line_sems(1, fsdp) + [pltpu.SemaphoreType.DMA],
        compiler_params=comm_params(2),
        name="branch_sum",
    )(attended, w, g, x, gains)


def token_kernel(
    fsdp, x_ref, g_first, g_second, picks, w_ref, out_ref, taken_ref, back_ref,
    g_buf, w_buf, taken, back, send, recv, local, loads, stores, back_sem,
):
    f, s = lax.axis_index("fsdp"), lax.axis_index("sp")
    lines = fsdp // 2
    parts = 2
    size = TOK_DEV // parts
    early, later = g_first.shape[1], g_second.shape[1]
    slots = picks.shape[1] // EXP_DEV
    ff = w_ref.shape[1]
    barrier = pltpu.get_barrier_semaphore()
    expected = greet_line(barrier, lines, f, s)
    own = pltpu.make_async_copy(x_ref, out_ref.at[f], local)
    own.start()
    reads = [
        pltpu.make_async_copy(g_first, g_buf.at[:, pl.ds(0, early), :], loads.at[0]),
        pltpu.make_async_copy(g_second, g_buf.at[:, pl.ds(early, later), :], loads.at[1]),
        pltpu.make_async_copy(w_ref, w_buf, loads.at[2]),
    ]
    for copy in reads:
        copy.start()
    pl.semaphore_wait(barrier, expected)

    def view(part):
        return lambda b: out_ref.at[b, pl.ds(part * size, size), :]

    owns = [x_ref.at[pl.ds(p * size, size), :] for p in range(parts)]
    line = LineGather([view(p) for p in range(parts)], owns, lines, f, s, send, recv)
    for p in range(parts):
        line.start_own(p)

    def take_all():
        reads[0].wait()
        reads[1].wait()

        def block(b, carry):
            for n in range(D // 512):
                at = pl.ds(n * 512, 512)
                got = dot_nn(picks[b], g_buf[b, :, at]).astype(BF16)
                for e in range(EXP_DEV):
                    to = pl.ds(pl.multiple_of(b * slots, 16), slots)
                    taken[e, to, at] = got[e * slots : (e + 1) * slots]
            return carry

        lax.fori_loop(0, fsdp, block, 0)
        for e in range(EXP_DEV):
            pltpu.make_async_copy(taken.at[e], taken_ref.at[e], stores.at[e]).start()

    def back_copy(e, j, slot):
        at = pl.ds(pl.multiple_of(j * FT, FT), FT)
        return pltpu.make_async_copy(back.at[slot], back_ref.at[e, :, at], back_sem.at[slot])

    def back_of(e):
        if e == 0:
            reads[2].wait()
        for j in range(ff // FT):
            slot = j % 2
            if e > 0 or j > 1:
                back_copy(e, j, slot).wait()
            back[slot] = dot_nt(taken[e], w_buf[e, pl.ds(j * FT, FT), :])
            back_copy(e, j, slot).start()

    work = [take_all] + [functools.partial(back_of, e) for e in range(EXP_DEV)]
    for k in range(1, lines):
        if k - 1 < len(work):
            work[k - 1]()
        for p in range(parts):
            line.forward(p, k)
    for unit in work[lines - 1 :]:
        unit()
    for p in range(parts):
        line.finish(p)
    own.wait()
    for slot in range(2):
        back_copy(0, slot, slot).wait()
    for e in range(EXP_DEV):
        pltpu.make_async_copy(taken.at[e], taken_ref.at[e], stores.at[e]).wait()


def token_gather(fsdp, x, g_first, g_second, picks, w_down):
    slots = picks.shape[1] // EXP_DEV
    total = fsdp * slots
    ff = w_down.shape[1]
    dma = pltpu.SemaphoreType.DMA
    return pl.pallas_call(
        functools.partial(token_kernel, fsdp),
        out_shape=(
            jax.ShapeDtypeStruct((fsdp, TOK_DEV, D), BF16),
            jax.ShapeDtypeStruct((EXP_DEV, total, D), BF16),
            jax.ShapeDtypeStruct((EXP_DEV, total, ff), F32),
        ),
        in_specs=[VMEM, ANY, ANY, VMEM, ANY],
        out_specs=[ANY, ANY, ANY],
        scratch_shapes=[
            pltpu.VMEM((fsdp, TOK_DEV, D), BF16),
            pltpu.VMEM((EXP_DEV, ff, D), BF16),
            pltpu.VMEM((EXP_DEV, total, D), BF16),
            pltpu.VMEM((2, total, FT), F32),
        ]
        + line_sems(2, fsdp)
        + [dma, dma((3,)), dma((EXP_DEV,)), dma((2,))],
        compiler_params=comm_params(3),
        name="token_gather",
    )(x, g_first, g_second, picks, w_down)


def token_back_kernel(
    fsdp, p_ref, gated_ref, w_ref, turned, x_ref, gu_ref, mid_ref, g_ref, gain,
    out_ref, low_ref, gain_out, part_ref, wu_ref, wide, narrow, w_buf, tile, grad_tile, loads, tile_sem, grad_sem, *scratch,
):
    f, s = lax.axis_index("fsdp"), lax.axis_index("sp")
    lines = fsdp // 2
    slots = turned.shape[3]
    height = grad_tile.shape[1]
    barrier = pltpu.get_barrier_semaphore()
    expected = greet_line(barrier, lines, f, s)
    reads = [
        pltpu.make_async_copy(gated_ref, narrow, loads.at[0]),
        pltpu.make_async_copy(w_ref.at[0], w_buf, loads.at[1]),
        pltpu.make_async_copy(x_ref, wide, loads.at[2]),
        pltpu.make_async_copy(gu_ref, narrow, loads.at[3]),
        pltpu.make_async_copy(w_ref.at[1], w_buf, loads.at[1]),
    ]
    reads[0].start()
    reads[1].start()
    pl.semaphore_wait(barrier, expected)
    line = LineReduce(p_ref, scratch, lines, f, s)
    line.start()

    def down_of(e):
        if e == 0:
            reads[0].wait()
            reads[1].wait()
        else:
            reads[4].wait()

        def columns(n, carry):
            at = pl.ds(pl.multiple_of(n * 512, 512), 512)
            wide[e, :, at] = dot_nn(narrow[e], w_buf[:, at]).astype(BF16)
            return carry

        lax.fori_loop(0, D // 512, columns, 0)
        if e == 0:
            reads[4].start()

    def tile_copy(b, slot):
        return pltpu.make_async_copy(tile.at[slot], part_ref.at[b], tile_sem.at[slot])

    def sum_all():
        reads[3].start()

        def pair(i, carry):
            for slot in range(2):
                b = 2 * i + slot

                @pl.when(i > 0)
                def _():
                    tile_copy(b, slot).wait()

                for n in range(D // 512):
                    at = pl.ds(n * 512, 512)
                    summed = jnp.zeros((TOK_DEV, 512), F32)
                    for e in range(EXP_DEV):
                        rows = wide[e, pl.ds(pl.multiple_of(b * slots, 16), slots), at]
                        summed += dot_nn(turned[b, e], rows)
                    tile[slot, :, at] = summed.astype(BF16)
                tile_copy(b, slot).start()
            return carry

        lax.fori_loop(0, fsdp // 2, pair, 0)
        reads[2].start()

    def grad_copy(e, i, slot):
        at = pl.ds(pl.multiple_of(i * height, height), height)
        return pltpu.make_async_copy(grad_tile.at[slot], wu_ref.at[e, at, :], grad_sem.at[slot])

    def grad_of(e):
        if e == 0:
            reads[2].wait()
            reads[3].wait()

        def pair(i, carry):
            for slot in range(2):
                part = 2 * i + slot

                def before():
                    grad_copy(e, part, slot).wait()

                if e == 0:
                    pl.when(i > 0)(before)
                else:
                    before()
                at = pl.ds(pl.multiple_of(part * height, height), height)
                grad_tile[slot] = dot_tn(wide[e, :, at], narrow[e]).astype(BF16)
                grad_copy(e, part, slot).start()
            return carry

        lax.fori_loop(0, D // height // 2, pair, 0)

    work = [functools.partial(down_of, e) for e in range(EXP_DEV)] + [sum_all]
    work += [functools.partial(grad_of, e) for e in range(EXP_DEV)]
    done = 0
    for t in range(lines - 1):
        line.step(t)
        until = (t + 1) * len(work) // (lines - 1)
        for unit in work[done:until]:
            unit()
        done = until
    line.finish(out_ref)
    gain_out[...] = jnp.zeros_like(gain_out)

    def norm_back(i, carry):
        at = pl.ds(pl.multiple_of(i * 32, 32), 32)
        mid = mid_ref[at, :]
        inverse = lax.rsqrt(jnp.mean(mid * mid, axis=-1, keepdims=True) + EPSILON)
        normed = mid * inverse
        grad_y = out_ref[at, :]
        scaled = grad_y * gain[1:2, :]
        mean = jnp.mean(scaled * normed, axis=-1, keepdims=True)
        grad = g_ref[at, :].astype(F32) + inverse * (scaled - normed * mean)
        out_ref[at, :] = grad
        low_ref[at, :] = grad.astype(BF16)
        gain_out[1:2, :] += jnp.sum(grad_y * normed, axis=0, keepdims=True)
        return carry

    lax.fori_loop(0, TOK_DEV // 32, norm_back, 0)
    for slot in range(2):
        tile_copy(slot, slot).wait()
        grad_copy(0, slot, slot).wait()


def token_back(fsdp, partial, gated, w_down, turned, received, grad_up_pre, mid, g, gains):
    block = partial.shape[1:]
    total, ff = gated.shape[1:]
    height = 256
    dma = pltpu.SemaphoreType.DMA
    return pl.pallas_call(
        functools.partial(token_back_kernel, fsdp),
        out_shape=(
            jax.ShapeDtypeStruct(block, F32),
            jax.ShapeDtypeStruct(block, BF16),
            jax.ShapeDtypeStruct((8, D), F32),
            jax.ShapeDtypeStruct(partial.shape, BF16),
            jax.ShapeDtypeStruct((EXP_DEV, D, ff), BF16),
        ),
        in_specs=[ANY, ANY, ANY, VMEM, ANY, ANY, VMEM, VMEM, VMEM],
        out_specs=[VMEM, VMEM, VMEM, ANY, ANY],
        scratch_shapes=[
            pltpu.VMEM((EXP_DEV, total, D), BF16),
            pltpu.VMEM((EXP_DEV, total, ff), BF16),
            pltpu.VMEM((ff, D), BF16),
            pltpu.VMEM((2,) + block, BF16),
            pltpu.VMEM((2, height, ff), BF16),
            dma((4,)),
            dma((2,)),
            dma((2,)),
        ]
        + LineReduce.scratch(fsdp, block),
        compiler_params=comm_params(4),
        name="token_back",
    )(partial, gated, w_down, turned, received, grad_up_pre, mid, g, gains)


class PlaneSum:
    def __init__(self, scratch, f, s, sp):
        self.own, self.got, self.send, self.recv = scratch
        self.f, self.s, self.sp = f, s, sp

    @staticmethod
    def scratch(seq, sp):
        dma = pltpu.SemaphoreType.DMA
        return [
            pltpu.VMEM((8, seq), F32), pltpu.VMEM((sp, 8, seq), F32), dma((sp,)), dma((sp,)),
        ]

    def greet(self, barrier):
        for k in range(1, self.sp):
            signal(barrier, (self.f, self.s ^ k))
        return self.sp - 1

    def copy(self, k):
        return remote(
            self.own, self.got.at[k], self.send.at[k], self.recv.at[k], (self.f, self.s ^ k)
        )

    def start(self, x_ref):
        self.own[...] = x_ref[...].T[:8]
        for k in range(1, self.sp):
            self.copy(k).start()

    def finish(self, out_ref):
        for k in range(1, self.sp):
            self.copy(k).wait()
        terms = [self.own[...]] + [self.got[k] for k in range(1, self.sp)]
        while len(terms) > 1:
            terms = [terms[i] + terms[i + 1] for i in range(0, len(terms), 2)]
        seq = out_ref.shape[0]
        out_ref[...] = jnp.concatenate([terms[0], jnp.zeros((120, seq), F32)], axis=0).T


def end_kernel(
    fsdp, sp, p_ref, low_ref, w_ref, x_ref, mid_ref, gain, gains_in, router_ref,
    grad_out, qkv_0, qkv_1, qkv_2, o_out, small_out,
    first, low_in, w_buf, back, low, o_low, gain_sum, pay, small, loads,
    qsend, qrecv, osend, orecv, msend, mrecv, local, *scratch,
):
    f, s = lax.axis_index("fsdp"), lax.axis_index("sp")
    count, lines = fsdp * sp, fsdp // 2
    me = f * sp + s
    rows, cols = o_low.shape[0], D // sp
    height = D // fsdp
    barrier = pltpu.get_barrier_semaphore()
    greet_all(barrier, me, count, sp)
    reads = [
        pltpu.make_async_copy(low_ref, low_in, loads.at[0]),
        pltpu.make_async_copy(w_ref, w_buf, loads.at[1]),
    ]
    for copy in reads:
        copy.start()
    pl.semaphore_wait(barrier, count - 1)
    plane_parts = 6 if sp == 4 else 5
    plane = plane_reduce_of(first, back, scratch[:plane_parts], f, s, sp)
    line = LineReduce(p_ref, scratch[plane_parts:], lines, f, s)
    line.start()

    def first_grads():
        for copy in reads:
            copy.wait()

        def columns(n, carry):
            at = pl.ds(pl.multiple_of(n * 256, 256), 256)
            for d in range(sp):
                rows_at = slice(d * TOK_DEV, (d + 1) * TOK_DEV)
                total = dot_nt(low_in[rows_at, :cols], w_buf[0, at, :])
                total += dot_nt(low_in[rows_at, cols : 2 * cols], w_buf[1, at, :])
                total += dot_nt(low_in[rows_at, 2 * cols :], w_buf[2, at, :])
                first[d, :, at] = total.astype(BF16)
            return carry

        lax.fori_loop(0, D // 256, columns, 0)

    def input_grads():
        gain_sum[...] = jnp.zeros_like(gain_sum)

        def chunk(i, carry):
            at = pl.ds(pl.multiple_of(i * 32, 32), 32)
            x = x_ref[at, :].astype(F32)
            inverse = lax.rsqrt(jnp.mean(x * x, axis=-1, keepdims=True) + EPSILON)
            normed = x * inverse
            grad_y = back[at, :]
            scaled = grad_y * gain[0:1, :]
            mean = jnp.mean(scaled * normed, axis=-1, keepdims=True)
            grad_out[at, :] = mid_ref[at, :] + inverse * (scaled - normed * mean)
            gain_sum[0:1, :] += jnp.sum(grad_y * normed, axis=0, keepdims=True)
            return carry

        lax.fori_loop(0, TOK_DEV // 32, chunk, 0)
        gain_sum[...] += gains_in[...]

        def fill(i, carry):
            at = pl.ds(pl.multiple_of(i * rows // 128 * 128, 128), 128)
            pay[i, 0:8, :] = router_ref[i]
            pay[i, 8:16, :] = gain_sum[:, at]
            return carry

        lax.fori_loop(0, count, fill, 0)

    def m_copy(i):
        other = lax.rem(me + i, count)
        return remote(
            pay.at[other], small.at[me], msend.at[i], mrecv.at[me], (other // sp, lax.rem(other, sp))
        )

    def m_go(i, carry):
        m_copy(i).start()
        return carry

    for t in range(lines - 1):
        line.step(t)
        if t == 0:
            first_grads()
            plane.start()
    plane.forward()
    plane.finish()
    input_grads()
    lax.fori_loop(1, count, m_go, 0)
    line.finish(low)
    for c in range(sp):
        top = 3 * height + c * rows
        o_low[:, c * cols : (c + 1) * cols] = low[top : top + rows, :]

    def q_from(i, place):
        return low.at[pl.ds(pl.multiple_of(i * height + place * rows, rows), rows), :]

    def q_to(i, place):
        return (qkv_0, qkv_1, qkv_2)[i].at[place]

    def q_copy(i, k):
        return remote(q_from(i, s ^ k), q_to(i, s), qsend.at[k, i], qrecv.at[k, i], (f, s ^ k))

    def q_own(i):
        return pltpu.make_async_copy(q_from(i, s), q_to(i, s), local.at[i])

    for k in range(sp - 1, 0, -1):
        for i in range(3):
            q_copy(i, k).start()
    owner = row_owner(f, s, rows, sp)
    target_f, target_s = owner // sp, lax.rem(owner, sp)
    stays = jnp.logical_and(target_s == s, target_f == f)
    o_copy = remote(o_low, o_out, osend, orecv, (target_f, target_s))
    o_own = pltpu.make_async_copy(o_low, o_out, orecv)

    @pl.when(stays)
    def _():
        o_own.start()

    @pl.when(jnp.logical_not(stays))
    def _():
        o_copy.start()

    for i in range(3):
        q_own(i).start()

    def m_end(i, carry):
        m_copy(i).wait_send()
        other = lax.rem(me + i, count)
        landed(small.at[other], mrecv.at[other])
        return carry + small[other]

    small_out[...] = lax.fori_loop(1, count, m_end, pay[me])
    for k in range(1, sp):
        for i in range(3):
            landed(q_to(i, s ^ k), qrecv.at[k, i])
            q_copy(i, k).wait_send()
    landed(o_out, orecv)

    @pl.when(jnp.logical_not(stays))
    def _():
        o_copy.wait_send()

    for i in range(3):
        q_own(i).wait()


def end_exchange(fsdp, sp, partial, low, w, x, grad_mid, gains, gains_in, router, number):
    count = fsdp * sp
    block = partial.shape[1:]
    rows = D // count
    dma = pltpu.SemaphoreType.DMA
    return pl.pallas_call(
        functools.partial(end_kernel, fsdp, sp),
        out_shape=(
            jax.ShapeDtypeStruct((TOK_DEV, D), F32),
            jax.ShapeDtypeStruct((sp, rows, D // sp), BF16),
            jax.ShapeDtypeStruct((sp, rows, D // sp), BF16),
            jax.ShapeDtypeStruct((sp, rows, D // sp), BF16),
            jax.ShapeDtypeStruct((rows, D), BF16),
            jax.ShapeDtypeStruct((16, 128), F32),
        ),
        in_specs=[ANY, ANY, ANY, VMEM, VMEM, VMEM, VMEM, VMEM],
        out_specs=[VMEM, ANY, ANY, ANY, ANY, VMEM],
        scratch_shapes=[
            pltpu.VMEM((sp, TOK_DEV, D), BF16),
            pltpu.VMEM(low.shape, BF16),
            pltpu.VMEM(w.shape, BF16),
            pltpu.VMEM((TOK_DEV, D), F32),
            pltpu.VMEM(block, BF16),
            pltpu.VMEM((rows, D), BF16),
            pltpu.VMEM((8, D), F32),
            pltpu.VMEM((count, 16, 128), F32),
            pltpu.VMEM((count, 16, 128), F32),
            dma((2,)),
            dma((sp, 3)), dma((sp, 3)), dma, dma, dma((count,)), dma((count,)), dma((3,)),
        ]
        + plane_scratch((TOK_DEV, D), sp)
        + LineReduce.scratch(fsdp, block),
        compiler_params=comm_params(number),
        name="end_exchange",
    )(partial, low, w, x, grad_mid, gains, gains_in, router)


def dot_nt(a, b):
    return lax.dot_general(a, b, (((1,), (1,)), ((), ())), preferred_element_type=F32)


def dot_tn(a, b):
    return lax.dot_general(a, b, (((0,), (0,)), ((), ())), preferred_element_type=F32)


def dot_nn(a, b):
    return jnp.dot(a, b, preferred_element_type=F32)


def whole(shape):
    return pl.BlockSpec(shape, lambda *_: (0,) * len(shape))


def lanes(first, second):
    lane = lax.broadcasted_iota(jnp.int32, (first.shape[0], 128), 1)
    return jnp.where(lane == 0, first, jnp.where(lane == 1, second, 0.0))


def inverse_of(sums, lane):
    return lax.rsqrt(sums[:, lane : lane + 1] / D + EPSILON)


def turn(v, table, sign=1.0):
    half = HEAD_DIM // 2
    front = lax.broadcasted_iota(jnp.int32, table.shape, 1) < half
    turned = pltpu.roll(table, half, 1)
    cosine = jnp.where(front, table, turned)
    sine = jnp.where(front, -turned, table)
    return v * cosine + pltpu.roll(v, half, 1) * (sine * sign)


def turn_back(v, table):
    return turn(v, table, -1.0)


def project_kernel(sp, x_ref, gain, w_ref, first_out, q_out, k_out, v_out, sums_out, squares, *scratch):
    step = pl.program_id(0)
    total = PlaneSum(scratch, lax.axis_index("fsdp"), lax.axis_index("sp"), sp)
    barrier = pltpu.get_barrier_semaphore()

    @pl.when(step == 0)
    def _():
        total.greet(barrier)

    x = x_ref[...].astype(F32)
    inverse = lax.rsqrt(jnp.mean(x * x, axis=-1, keepdims=True) + EPSILON)
    first = (x * inverse * gain[0:1, :]).astype(BF16)
    first_out[...] = first
    q = dot_nn(first, w_ref[0])
    q_out[...] = q
    k = dot_nn(first, w_ref[1])
    k_out[...] = k
    at = pl.ds(pl.multiple_of(step * TOK_DEV, TOK_DEV), TOK_DEV)
    squares[at, :] = lanes(
        jnp.sum(q * q, axis=-1, keepdims=True), jnp.sum(k * k, axis=-1, keepdims=True)
    )
    last = step == pl.num_programs(0) - 1

    @pl.when(last)
    def _():
        pl.semaphore_wait(barrier, sp - 1)
        total.start(squares)

    v_out[...] = dot_nn(first, w_ref[2]).astype(BF16)

    @pl.when(last)
    def _():
        total.finish(sums_out)


def project(sp, x, gains, w):
    seq, cols = x.shape[0], w.shape[2]

    def block(width):
        return pl.BlockSpec((TOK_DEV, width), lambda i: (i, 0))

    return pl.pallas_call(
        functools.partial(project_kernel, sp),
        grid=(seq // TOK_DEV,),
        out_shape=(
            jax.ShapeDtypeStruct((seq, D), BF16),
            jax.ShapeDtypeStruct((seq, cols), F32),
            jax.ShapeDtypeStruct((seq, cols), F32),
            jax.ShapeDtypeStruct((seq, cols), BF16),
            jax.ShapeDtypeStruct((seq, 128), F32),
        ),
        in_specs=[block(D), whole(gains.shape), whole(w.shape)],
        out_specs=[block(D), block(cols), block(cols), block(cols), whole((seq, 128))],
        scratch_shapes=[pltpu.VMEM((seq, 128), F32)] + PlaneSum.scratch(seq, sp),
        compiler_params=comm_params(1),
        name="project",
    )(x, gains, w)


def attend_kernel(
    q_raw, k_raw, v_ref, squares, gain, table, o_ref, sum_ref, q_ref, k_ref
):
    head = pl.program_id(0)

    @pl.when(head == 0)
    def _():
        sum_ref[...] = squares[...]

    q_inv, k_inv = inverse_of(squares, 0), inverse_of(squares, 1)
    q_ref[...] = turn(q_raw[...] * q_inv * gain[2:3, :], table[...]).astype(BF16)
    k_ref[...] = turn(k_raw[...] * k_inv * gain[3:4, :], table[...]).astype(BF16)
    for i in range(q_ref.shape[0] // BLK):
        rows, seen = pl.ds(i * BLK, BLK), pl.ds(0, (i + 1) * BLK)
        scores = dot_nt(q_ref[rows, :], k_ref[seen, :]) * SCALE
        row_max = jnp.max(scores, axis=-1, keepdims=True)
        exp_rows = jnp.exp(scores - row_max)
        row_sum = jnp.sum(exp_rows, axis=-1, keepdims=True)
        probs = (exp_rows / row_sum).astype(BF16)
        o_ref[rows, :] = dot_nn(probs, v_ref[seen, :]).astype(BF16)
        lane = lax.broadcasted_iota(jnp.int32, (BLK, 128), 1)
        sum_ref[rows, :] += jnp.where(lane == head + 2, row_max + jnp.log(row_sum), 0.0)


def attend(q_raw, k_raw, v, squares, gains, table):
    seq, width = v.shape
    heads = width // HEAD_DIM
    spec = pl.BlockSpec((seq, HEAD_DIM), lambda h: (0, h))
    return pl.pallas_call(
        attend_kernel,
        grid=(heads,),
        out_shape=(
            jax.ShapeDtypeStruct((seq, width), BF16),
            jax.ShapeDtypeStruct((seq, 128), F32),
            jax.ShapeDtypeStruct((seq, width), BF16),
            jax.ShapeDtypeStruct((seq, width), BF16),
        ),
        in_specs=[
            spec, spec, spec, whole((seq, 128)),
            pl.BlockSpec((4, HEAD_DIM), lambda h: (0, h)),
            whole((seq, HEAD_DIM)),
        ],
        out_specs=[spec, whole((seq, 128)), spec, spec],
        compiler_params=pltpu.CompilerParams(vmem_limit_bytes=VLIM),
        name="attend",
    )(q_raw, k_raw, v, squares, gains, table)


def attend_back_head(
    h, q_ref, k_ref, v_ref, sums, q_raw, k_raw, gain, table,
    q_scaled, k_scaled, dv_out, dots, gains_out, dv_ref,
):
    head = slice(h * HEAD_DIM, (h + 1) * HEAD_DIM)
    k_scaled[:, head] = jnp.zeros(k_raw[:, head].shape, F32)
    dv_ref[...] = jnp.zeros_like(dv_ref)
    gain_q, gain_k = gain[2:3, head], gain[3:4, head]
    gain_sum = jnp.zeros((1, HEAD_DIM), F32)
    size = BLK if q_ref.shape[0] <= 4 * BLK else BLK // 2
    for i in range(q_ref.shape[0] // size):
        rows, seen = pl.ds(i * size, size), pl.ds(0, (i * size // BLK + 1) * BLK)
        q, g, keys = q_ref[rows, head], dv_out[rows, head], k_ref[seen, head]
        scores = dot_nt(q, keys) * SCALE
        probs = jnp.exp(scores - sums[rows, h + 2 : h + 3])
        grad_probs = dot_nt(g, v_ref[seen, head])
        row_dot = jnp.sum(probs * grad_probs, axis=-1, keepdims=True)
        grad_scores = (probs * (grad_probs - row_dot)).astype(BF16)
        k_scaled[seen, head] += dot_tn(grad_scores, q)
        dv_ref[seen, :] += dot_tn(probs.astype(BF16), g)
        grad_y = turn_back(dot_nn(grad_scores, keys) * SCALE, table[rows, :])
        normed = q_raw[rows, head] * inverse_of(sums.at[rows, :], 0)
        scaled = grad_y * gain_q
        q_scaled[rows, head] = scaled
        dots[rows, :] += lanes(jnp.sum(scaled * normed, axis=-1, keepdims=True), 0.0)
        gain_sum += jnp.sum(grad_y * normed, axis=0, keepdims=True)
    grad_y = turn_back(k_scaled[:, head] * SCALE, table[...])
    normed = k_raw[:, head] * inverse_of(sums, 1)
    scaled = grad_y * gain_k
    k_scaled[:, head] = scaled
    k_dots = jnp.sum(scaled * normed, axis=-1, keepdims=True)
    dots[...] += lanes(jnp.zeros_like(k_dots), k_dots)
    gains_out[0:1, head] = gain_sum
    gains_out[1:2, head] = jnp.sum(grad_y * normed, axis=0, keepdims=True)
    dv_out[:, head] = dv_ref[...].astype(BF16)


def branch_back_kernel(
    fsdp, sp, x_ref, p_ref, wo_ref, q_ref, k_ref, v_ref, sums, q_raw, k_raw, gain, table,
    all_ref, out_ref, q_scaled, k_scaled, dv_out, dots, gains_out,
    g_all, dv_ref, xsend, xrecv, own_sem, all_sem, *scratch,
):
    f, s = lax.axis_index("fsdp"), lax.axis_index("sp")
    lines = fsdp // 2
    barrier = pltpu.get_barrier_semaphore()
    sums_over = PlaneSum(scratch[:4], f, s, sp)
    expected = greet_line(barrier, lines, f, s) + sums_over.greet(barrier)
    plane = plane_gather_of(x_ref, g_all, f, s, sp, xsend, xrecv)
    own = pltpu.make_async_copy(x_ref, plane.at(s, 0, x_ref.shape[0]), own_sem)
    own.start()
    pl.semaphore_wait(barrier, expected)
    plane.start()
    line = LineReduce(p_ref, scratch[4:], lines, f, s)
    line.start()
    dots[...] = jnp.zeros_like(dots)
    out_all = pltpu.make_async_copy(g_all, all_ref, all_sem)
    def back_of(place):
        at = pl.ds(pl.multiple_of(place * TOK_DEV, TOK_DEV), TOK_DEV)
        dv_out[at, :] = dot_nt(g_all[at, :], wo_ref[...]).astype(BF16)

    early = (0, 1, 2) if sp == 4 else (0,)
    for t in range(lines - 1):
        line.step(t)
        if t == min(1, lines - 2):
            plane.forward()
            own.wait()
            for k in early:
                back_of(s ^ k)
    plane.finish()
    out_all.start()
    for k in range(len(early), sp):
        back_of(s ^ k)
    for h in range(q_ref.shape[1] // HEAD_DIM):
        attend_back_head(
            h, q_ref, k_ref, v_ref, sums, q_raw, k_raw, gain, table,
            q_scaled, k_scaled, dv_out, dots, gains_out, dv_ref,
        )
    sums_over.start(dots)
    line.finish(out_ref)
    sums_over.finish(dots)
    out_all.wait()


def branch_back(fsdp, sp, x, partial, wo, q, k, v, sums, q_raw, k_raw, gains, table):
    block = partial.shape[1:]
    seq, width = q.shape
    dma = pltpu.SemaphoreType.DMA
    return pl.pallas_call(
        functools.partial(branch_back_kernel, fsdp, sp),
        out_shape=(
            jax.ShapeDtypeStruct((seq, D), BF16),
            jax.ShapeDtypeStruct(block, F32),
            jax.ShapeDtypeStruct((seq, width), F32),
            jax.ShapeDtypeStruct((seq, width), F32),
            jax.ShapeDtypeStruct((seq, width), BF16),
            jax.ShapeDtypeStruct((seq, 128), F32),
            jax.ShapeDtypeStruct((2, width), F32),
        ),
        in_specs=[VMEM, ANY] + [VMEM] * 9,
        out_specs=[ANY] + [VMEM] * 6,
        scratch_shapes=[
            pltpu.VMEM((seq, D), BF16), pltpu.VMEM((seq, HEAD_DIM), F32), dma((sp,)), dma((sp,)), dma, dma,
        ]
        + PlaneSum.scratch(seq, sp)
        + LineReduce.scratch(fsdp, block),
        compiler_params=comm_params(5),
        name="branch_back",
    )(x, partial, wo, q, k, v, sums, q_raw, k_raw, gains, table)


def held(shape):
    return pl.BlockSpec(
        shape, lambda *_: (0,) * len(shape), pipeline_mode=pl.Buffered(buffer_count=1)
    )


def weight_kernel(
    q_scaled, k_scaled, q_raw, k_raw, squares, dots, dv_ref, first, attended, g_ref, out, low, square
):
    f = pl.program_id(0)
    height = first.shape[1]
    rows = out.shape[1] - 3 * height
    cols = out.shape[2]
    sp = D // cols

    @pl.when(f == 0)
    def _():
        for n, scaled, raw in ((0, q_scaled, q_raw), (1, k_scaled, k_raw)):
            inverse = inverse_of(squares, n)
            mean = dots[:, n : n + 1] / D
            low[:, n * cols : (n + 1) * cols] = (
                inverse * (scaled[...] - raw[...] * (inverse * mean))
            ).astype(BF16)
        low[:, 2 * cols :] = dv_ref[...]
        for c in range(sp):
            at = slice(c * cols, (c + 1) * cols)
            square[:, at] = dot_tn(attended[...], g_ref[:, at]).astype(BF16)

    grads = dot_tn(first[...], low[...]).astype(BF16)
    for n in range(3):
        out[0, n * height : (n + 1) * height, :] = grads[:, n * cols : (n + 1) * cols]
    each = rows // sp
    from_rows = pl.ds(pl.multiple_of(f * each, each), each)
    for c in range(sp):
        at = 3 * height + c * each
        out[0, at : at + each, :] = square[from_rows, c * cols : (c + 1) * cols]


def weight_parts(fsdp, q_scaled, k_scaled, q_raw, k_raw, squares, dots, dv, first, attended, g):
    seq, cols = dv.shape
    height = D // fsdp
    each = cols // fsdp
    return pl.pallas_call(
        weight_kernel,
        grid=(fsdp,),
        out_shape=(
            jax.ShapeDtypeStruct((fsdp, 3 * height + D // cols * each, cols), BF16),
            jax.ShapeDtypeStruct((seq, 3 * cols), BF16),
        ),
        in_specs=[held((seq, cols))] * 4
        + [held((seq, 128))] * 2
        + [
            held((seq, cols)),
            pl.BlockSpec((seq, height), lambda f: (0, f)),
            held((seq, cols)),
            held((seq, D)),
        ],
        out_specs=[
            pl.BlockSpec((1, 3 * height + D // cols * each, cols), lambda f: (f, 0, 0)),
            whole((seq, 3 * cols)),
        ],
        scratch_shapes=[pltpu.VMEM((cols, D), BF16)],
        compiler_params=pltpu.CompilerParams(vmem_limit_bytes=VLIM),
        name="weight_parts",
    )(q_scaled, k_scaled, q_raw, k_raw, squares, dots, dv, first, attended, g)


def two_parts(x, axis):
    high = x.astype(BF16)
    return jnp.concatenate([high, (x - high.astype(F32)).astype(BF16)], axis=axis)


def blocks_of(shape):
    return pl.BlockSpec((1,) + shape, lambda b: (b,) + (0,) * len(shape))


def slots_of(slots, width):
    return pl.BlockSpec((EXP_DEV, slots, width), lambda b: (0, b, 0))


def route_kernel(picks, rows_in, router, columns, out, probs_out, gates_out):
    slots = out.shape[1]
    for n in range(D // 512):
        at = pl.ds(n * 512, 512)
        got = dot_nn(picks[0], rows_in[0, :, at]).astype(BF16)
        for e in range(EXP_DEV):
            out[e, :, at] = got[e * slots : (e + 1) * slots]
    logits = dot_nt(rows_in[0], router[...])
    exp_logits = jnp.exp(logits - jnp.max(logits, axis=1, keepdims=True))
    probs = exp_logits / jnp.sum(exp_logits, axis=1, keepdims=True)
    probs_out[0] = probs
    both = two_parts(probs, 1)
    for e in range(EXP_DEV):
        moved = dot_nn(picks[0, e * slots : (e + 1) * slots, :], both)
        mask = columns[e : e + 1, :]
        gates_out[e] = jnp.sum(moved * jnp.concatenate([mask, mask], axis=1), axis=1, keepdims=True)


def route(picks, tokens, router_t, columns):
    blocks = tokens.shape[0]
    slots = picks.shape[1] // EXP_DEV
    total = blocks * slots
    experts = router_t.shape[0]
    return pl.pallas_call(
        route_kernel,
        grid=(blocks,),
        out_shape=(
            jax.ShapeDtypeStruct((EXP_DEV, total, D), BF16),
            jax.ShapeDtypeStruct((blocks, TOK_DEV, experts), F32),
            jax.ShapeDtypeStruct((EXP_DEV, total, 1), F32),
        ),
        in_specs=[
            blocks_of(picks.shape[1:]), blocks_of((TOK_DEV, D)), whole(router_t.shape),
            whole(columns.shape),
        ],
        out_specs=[slots_of(slots, D), blocks_of((TOK_DEV, experts)), slots_of(slots, 1)],
        compiler_params=pltpu.CompilerParams(vmem_limit_bytes=VLIM),
        name="route",
    )(picks, tokens, router_t, columns)


FT = 256


def gate_kernel(x_ref, w_ref, out):
    out[0] = dot_nn(x_ref[0], w_ref[0])


def gate_product(x, w_gate):
    _, total, _ = x.shape
    ff = w_gate.shape[2]
    wide = 2 * FT
    return pl.pallas_call(
        gate_kernel,
        grid=(EXP_DEV, ff // wide),
        out_shape=jax.ShapeDtypeStruct((EXP_DEV, total, ff), F32),
        in_specs=[
            pl.BlockSpec((1, total, D), lambda e, j: (e, 0, 0)),
            pl.BlockSpec((1, D, wide), lambda e, j: (e, 0, j)),
        ],
        out_specs=pl.BlockSpec((1, total, wide), lambda e, j: (e, 0, j)),
        compiler_params=pltpu.CompilerParams(vmem_limit_bytes=VLIM),
        name="gate_product",
    )(x, w_gate)


def active_kernel(x_ref, pre_ref, w_ref, u_ref, gates, gated, grad_gate, grad_up, dots):
    @pl.when(pl.program_id(1) == 0)
    def _():
        dots[...] = jnp.zeros_like(dots)

    total = x_ref.shape[1]
    chunk = total // 4
    for first in range(0, total, chunk):
        at = slice(first, first + chunk)
        gate_pre = pre_ref[0, at, :]
        up_pre = dot_nn(x_ref[0, at, :], w_ref[0])
        sig = jax.nn.sigmoid(gate_pre)
        silu = gate_pre * sig
        hidden = silu * up_pre
        back = u_ref[0, at, :]
        gate = gates[0, at, :]
        dots[0, at, :] += jnp.sum(hidden * back, axis=1, keepdims=True)
        gated[0, at, :] = (hidden * gate).astype(BF16)
        back = back * gate
        grad_gate[0, at, :] = (back * up_pre * (sig * (1.0 + gate_pre * (1.0 - sig)))).astype(BF16)
        grad_up[0, at, :] = (back * silu).astype(BF16)


def active(x, gate_pre, w_up, u, gates):
    _, total, _ = x.shape
    ff = w_up.shape[2]
    wide = 2 * FT
    tile = pl.BlockSpec((1, total, wide), lambda e, j: (e, 0, j))
    weight = pl.BlockSpec((1, D, wide), lambda e, j: (e, 0, j))
    column = pl.BlockSpec((1, total, 1), lambda e, j: (e, 0, 0))
    low = jax.ShapeDtypeStruct((EXP_DEV, total, ff), BF16)
    return pl.pallas_call(
        active_kernel,
        grid=(EXP_DEV, ff // wide),
        out_shape=(low, low, low, jax.ShapeDtypeStruct((EXP_DEV, total, 1), F32)),
        in_specs=[
            pl.BlockSpec((1, total, D), lambda e, j: (e, 0, 0)), tile, weight, tile, column,
        ],
        out_specs=[tile, tile, tile, column],
        compiler_params=pltpu.CompilerParams(vmem_limit_bytes=VLIM),
        name="active",
    )(x, gate_pre, w_up, u, gates)


def weight_grad_kernel(a_ref, b_ref, out):
    out[0] = dot_tn(a_ref[0], b_ref[0]).astype(BF16)


def weight_grad(a, b, name):
    _, total, height = a.shape
    width = b.shape[2]
    size = 1024
    return pl.pallas_call(
        weight_grad_kernel,
        grid=(EXP_DEV, height // size, width // size),
        out_shape=jax.ShapeDtypeStruct((EXP_DEV, height, width), BF16),
        in_specs=[
            pl.BlockSpec((1, total, size), lambda e, i, j: (e, 0, i)),
            pl.BlockSpec((1, total, size), lambda e, i, j: (e, 0, j)),
        ],
        out_specs=pl.BlockSpec((1, size, size), lambda e, i, j: (e, i, j)),
        compiler_params=pltpu.CompilerParams(vmem_limit_bytes=VLIM),
        name=name,
    )(a, b)


def rows_back_kernel(a_ref, b_ref, g_ref, w_ref, out):
    out[0] = (dot_nt(a_ref[0], g_ref[0]) + dot_nt(b_ref[0], w_ref[0])).astype(BF16)


def rows_back(grad_gate_pre, grad_up_pre, w_gate, w_up):
    _, total, ff = grad_up_pre.shape
    size = 512
    row = pl.BlockSpec((1, total, ff), lambda e, j: (e, 0, 0))
    weight = pl.BlockSpec((1, size, ff), lambda e, j: (e, j, 0))
    return pl.pallas_call(
        rows_back_kernel,
        grid=(EXP_DEV, D // size),
        out_shape=jax.ShapeDtypeStruct((EXP_DEV, total, D), BF16),
        in_specs=[row, row, weight, weight],
        out_specs=pl.BlockSpec((1, total, size), lambda e, j: (e, 0, j)),
        compiler_params=pltpu.CompilerParams(vmem_limit_bytes=VLIM),
        name="rows_back",
    )(grad_gate_pre, grad_up_pre, w_gate, w_up)


def combine_kernel(turned, rows_ref, tokens, probs, dots, router, columns, out, router_out):
    @pl.when(pl.program_id(0) == 0)
    def _():
        router_out[...] = jnp.zeros_like(router_out)

    choice = jnp.zeros(probs.shape[1:], F32)
    for e in range(EXP_DEV):
        moved = dot_nn(turned[0, e], dots[e])
        choice += jnp.sum(moved, axis=1, keepdims=True) * columns[e : e + 1, :]
    p = probs[0]
    grad_logits = p * (choice - jnp.sum(p * choice, axis=1, keepdims=True))
    both = two_parts(grad_logits, 1)
    for n in range(D // 512):
        at = pl.ds(n * 512, 512)
        total = dot_nn(both, router[:, at])
        for e in range(EXP_DEV):
            total += dot_nn(turned[0, e], rows_ref[e, :, at])
        out[0, :, at] = total.astype(BF16)
    router_out[...] += dot_tn(both, tokens[0])


def combine(turned, grad_rows, tokens, probs, dots, router_two, columns):
    blocks = tokens.shape[0]
    slots = turned.shape[3]
    return pl.pallas_call(
        combine_kernel,
        grid=(blocks,),
        out_shape=(
            jax.ShapeDtypeStruct((blocks, TOK_DEV, D), BF16),
            jax.ShapeDtypeStruct((router_two.shape[0], D), F32),
        ),
        in_specs=[
            blocks_of(turned.shape[1:]), slots_of(slots, D), blocks_of((TOK_DEV, D)),
            blocks_of(probs.shape[1:]), slots_of(slots, 128), whole(router_two.shape),
            whole(columns.shape),
        ],
        out_specs=[blocks_of((TOK_DEV, D)), whole((router_two.shape[0], D))],
        compiler_params=pltpu.CompilerParams(vmem_limit_bytes=VLIM),
        name="combine",
    )(turned, grad_rows, tokens, probs, dots, router_two, columns)


def widen_kernel(mid, total, *refs):
    *refs, layer_out = refs
    layer_out[...] = (mid[...] + total[...]).astype(BF16)
    count = len(refs) // 2
    for low, out in zip(refs[:count], refs[count:]):
        if len(low.shape) == 2:
            out[...] = low[...].astype(F32)
            continue
        sp, _, cols = low.shape
        for s in range(sp):
            for g in range(cols // HEAD_DIM):
                head = g * sp + s
                out[:, head * HEAD_DIM : (head + 1) * HEAD_DIM] = low[
                    s, :, g * HEAD_DIM : (g + 1) * HEAD_DIM
                ].astype(F32)


def widen(mid, total, by_heads, arrays):
    steps = 4
    flat = [x.reshape(-1, x.shape[-1]) for x in arrays]

    def rows_of(shape, axis):
        tall = shape[axis] // steps if shape[axis] % (16 * steps) == 0 else shape[axis]
        block = shape[:axis] + (tall,) + shape[axis + 1 :]
        moving = tall != shape[axis]
        return pl.BlockSpec(
            block, lambda i: tuple(i if moving and n == axis else 0 for n in range(len(shape)))
        )

    heads_out = [(x.shape[1], x.shape[0] * x.shape[2]) for x in by_heads]
    wide = pl.pallas_call(
        widen_kernel,
        grid=(steps,),
        out_shape=tuple(
            jax.ShapeDtypeStruct(shape, F32) for shape in heads_out + [x.shape for x in flat]
        )
        + (jax.ShapeDtypeStruct(mid.shape, BF16),),
        in_specs=[rows_of(mid.shape, 0)] * 2
        + [rows_of(x.shape, 1) for x in by_heads]
        + [rows_of(x.shape, 0) for x in flat],
        out_specs=[rows_of(shape, 0) for shape in heads_out + [x.shape for x in flat] + [mid.shape]],
        compiler_params=pltpu.CompilerParams(vmem_limit_bytes=VLIM),
        name="widen",
    )(mid, total, *by_heads, *flat)
    split = len(by_heads)
    shaped = [x.reshape(like.shape) for x, like in zip(wide[split:-1], arrays)]
    return list(wide[:split]) + shaped + [wide[-1]]


def angles(seq):
    freqs = np.float32(ROPE_BASE) ** (-2.0 * np.arange(HEAD_DIM // 2, dtype=np.float32) / HEAD_DIM)
    turned = np.arange(seq, dtype=np.float32)[:, None] * freqs[None, :].astype(np.float32)
    return jnp.asarray(np.concatenate([np.cos(turned), np.sin(turned)], axis=1), F32)


def body(
    layer_input, output_grad, w_query, w_key, w_value, w_output, w_router, norm_gains,
    w_gate, w_up, w_down, expert_routes,
):
    fsdp, sp = lax.axis_size("fsdp"), lax.axis_size("sp")
    f, s = lax.axis_index("fsdp"), lax.axis_index("sp")
    count = fsdp * sp
    experts = EXP_DEV * fsdp
    capacity = TOK_DEV * TOP // experts * 17 // 16
    slots = -(-capacity // 16) * 16
    seq = TOK_DEV * sp
    cols = D // sp
    rows = D // count

    down_full = lax.all_gather(w_down, "sp", axis=1, tiled=True)
    gate_full = lax.all_gather(w_gate, "sp", axis=1, tiled=True)
    up_full = lax.all_gather(w_up, "sp", axis=1, tiled=True)

    router_size = rows * experts
    misc = jnp.concatenate([w_router.reshape(router_size), norm_gains.reshape(4 * rows)])
    misc_rows = -(-misc.shape[0] // 2048) * 16
    misc = jnp.pad(misc, (0, misc_rows * 128 - misc.shape[0])).reshape(misc_rows, 128)
    routes = expert_routes.reshape(TOK_DEV * TOP // 128, 128)
    early = TOK_DEV // 8
    x_all, w_all, wo_s, grad_first_half, misc_all, routes_all = gather_start(
        fsdp, sp, layer_input, jnp.stack([w_query, w_key, w_value]), w_output, output_grad[:early],
        misc, routes,
    )
    misc_all = misc_all.reshape(count, misc_rows * 128)
    router_w = misc_all[:, :router_size].reshape(D, experts)
    router_t = router_w.T
    gains_w = misc_all[:, router_size : router_size + 4 * rows].reshape(count, 4, rows)
    gains32 = gains_w.transpose(1, 0, 2).reshape(4, D).astype(F32)
    by_head = gains32.reshape(4, cols // HEAD_DIM, sp, HEAD_DIM)
    gains_own = lax.dynamic_index_in_dim(by_head, s, axis=2, keepdims=False).reshape(4, cols)

    routes_block = routes_all.reshape(fsdp, TOK_DEV, TOP)
    own_ids = f * EXP_DEV + jnp.arange(EXP_DEV, dtype=jnp.int32)
    chosen = jnp.any(routes_block[:, :, :, None] == own_ids, axis=2)
    before = jnp.arange(TOK_DEV)[:, None] > jnp.arange(TOK_DEV)[None, :]
    place = jnp.einsum(
        "ut,fte->feu", before.astype(BF16), chosen.astype(BF16), preferred_element_type=F32
    ).astype(jnp.int32)
    slot_ids = jnp.arange(slots, dtype=jnp.int32)
    picks = (
        (place[:, :, None, :] == slot_ids[:, None]) & chosen.transpose(0, 2, 1)[:, :, None, :]
    ).astype(BF16).reshape(fsdp, EXP_DEV * slots, TOK_DEV)
    turned = (
        (place[:, :, :, None] == slot_ids) & chosen.transpose(0, 2, 1)[:, :, :, None]
    ).astype(BF16)
    columns = (jnp.arange(experts, dtype=jnp.int32)[None, :] == own_ids[:, None]).astype(F32)

    first_in, q_raw, k_raw, values, squares = project(sp, x_all, gains32, w_all)
    table = angles(seq)
    attended, sums, queries, keys = attend(
        q_raw, k_raw, values, squares, gains_own, table
    )
    mid, second_in, grad_second_half = branch_sum(
        fsdp, attended, wo_s, output_grad[early:], layer_input, gains32
    )

    tokens, grad_taken, unscaled = token_gather(
        fsdp, second_in, grad_first_half, grad_second_half, picks, down_full
    )
    received, probs, slot_gates = route(picks, tokens, router_t, columns)
    gate_pre = gate_product(received, gate_full)
    gated, grad_gate_pre, grad_up_pre, slot_dots = active(
        received, gate_pre, up_full, unscaled, slot_gates
    )
    dots_two = jnp.pad(two_parts(slot_dots, 2), ((0, 0), (0, 0), (0, 126)))
    grad_rows = rows_back(grad_gate_pre, grad_up_pre, gate_full, up_full)
    second_part, router_two = combine(
        turned, grad_rows, tokens, probs, dots_two, jnp.concatenate([router_t, router_t], axis=0),
        columns,
    )
    grad_router = (router_two[:experts] + router_two[experts:]).T

    def shed(grad):
        return lax.psum_scatter(grad, "sp", scatter_dimension=1, tiled=True)

    grad_down = shed(weight_grad(gated, grad_taken, "down_grad"))
    grad_gate = shed(weight_grad(received, grad_gate_pre, "gate_grad"))
    grad_mid, grad_mid_low, gain_rows, out_part, up_part = token_back(
        fsdp, second_part, gated, down_full, turned, received, grad_up_pre, mid, output_grad, gains32
    )
    grad_up = shed(up_part)

    grad_branch, out_sum, q_scaled, k_scaled, grad_values, dots, gain_qk = branch_back(
        fsdp, sp, grad_mid_low, out_part, wo_s, queries, keys, values, sums, q_raw, k_raw,
        gains_own, table,
    )
    weight_part, grads_low = weight_parts(
        fsdp, q_scaled, k_scaled, q_raw, k_raw, squares, dots, grad_values, first_in, attended, grad_branch
    )

    gain_rows = lax.dynamic_update_slice(
        gain_rows.reshape(8, cols // HEAD_DIM, sp, HEAD_DIM),
        gain_qk.reshape(2, cols // HEAD_DIM, 1, HEAD_DIM),
        (2, 0, s, 0),
    ).reshape(8, D)
    router_part = grad_router.reshape(count, router_size)
    router_part = jnp.pad(router_part, ((0, 0), (0, 1024 - router_size))).reshape(count, 8, 128)
    input_grad, *weight_grads, small = end_exchange(
        fsdp, sp, weight_part, grads_low, w_all, layer_input, grad_mid, gains32, gain_rows, router_part, 8
    )
    *weight_grads, grad_gate, grad_up, grad_down, layer_out = widen(
        mid, out_sum, weight_grads[:3], [weight_grads[3], grad_gate, grad_up, grad_down]
    )
    grad_router_own = small[:8].reshape(1024)[:router_size].reshape(rows, experts)
    first_lane = (f * sp + s) * rows % 128
    grad_gains = lax.dynamic_slice(small[8:12], (0, first_lane), (4, rows))
    return (
        layer_out, input_grad, *weight_grads,
        grad_router_own, grad_gains, grad_gate, grad_up, grad_down,
    )


def solution(mesh):
    both, split = P(("fsdp", "sp"), None), P("fsdp", "sp", None)
    gains = P(None, ("fsdp", "sp"))
    return jax.shard_map(
        body,
        mesh=mesh,
        in_specs=(both,) * 7 + (gains,) + (split,) * 3 + (both,),
        out_specs=(both,) * 7 + (gains,) + (split,) * 3,
        check_vma=False,
    )
```

```python
import functools

import jax
import jax.numpy as jnp
import numpy as np
from jax import lax
from jax.experimental import pallas as pl
from jax.experimental.pallas import tpu as pltpu
from jax.sharding import PartitionSpec as P

D = 2048
HEADS = 16
HEAD_DIM = 128
TOP = 8
EXP_DEV = 2
BLK = 256
TOK_DEV = 256
EPSILON = 1e-05
ROPE_BASE = 10000.0
MASKED = -1000000000.0
SCALE = HEAD_DIM ** (-0.5)
MESH = pl.DeviceIdType.MESH
ANY = pl.BlockSpec(memory_space=pl.ANY)
VMEM = pl.BlockSpec(memory_space=pltpu.VMEM)
VLIM = 60 * 1024 * 1024
F32 = jnp.float32
BF16 = jnp.bfloat16


def remote(src, dst, send_sem, recv_sem, device):
    return pltpu.make_async_remote_copy(
        src_ref=src,
        dst_ref=dst,
        send_sem=send_sem,
        recv_sem=recv_sem,
        device_id=device,
        device_id_type=MESH,
    )


def landed(ref, sem):
    pltpu.make_async_copy(ref, ref, sem).wait()


def signal(sem, device):
    pl.semaphore_signal(sem, inc=1, device_id=device, device_id_type=MESH)


def greet_line(barrier, lines, f, s):
    place, core = f // 2, f % 2
    signal(barrier, (f + 1 - 2 * core, s))

    @pl.when(place > 0)
    def _():
        signal(barrier, (f - 2, s))

    @pl.when(place < lines - 1)
    def _():
        signal(barrier, (f + 2, s))

    return 1 + jnp.where(place > 0, 1, 0) + jnp.where(place < lines - 1, 1, 0)


class LineGather:
    def __init__(self, views, owns, lines, f, s, send, recv):
        self.views, self.owns, self.lines, self.f, self.s = views, owns, lines, f, s
        self.send, self.recv = send, recv
        self.place, self.core = f // 2, f % 2

    def copy(self, v, block, slot, way):
        device = {
            "right": (self.f + 2, self.s),
            "left": (self.f - 2, self.s),
            "partner": (self.f + 1 - 2 * self.core, self.s),
        }[way]
        index = {"right": 0, "left": 1, "partner": 2}[way]
        ref = self.views[v](block)
        own = self.owns[v] if slot == 0 and self.owns[v] is not None else ref
        return remote(own, ref, self.send.at[v, slot, index], self.recv.at[v, block], device)

    def start_own(self, v):
        @pl.when(self.place < self.lines - 1)
        def _():
            self.copy(v, self.f, 0, "right").start()

        @pl.when(self.place > 0)
        def _():
            self.copy(v, self.f, 0, "left").start()

        self.copy(v, self.f, 0, "partner").start()

    def forward(self, v, k):
        place, lines = self.place, self.lines

        @pl.when(place >= k)
        def _():
            block = self.f - 2 * k
            landed(self.views[v](block), self.recv.at[v, block])

            @pl.when(place < lines - 1)
            def _():
                self.copy(v, block, k, "right").start()

            self.copy(v, block, k, "partner").start()

        @pl.when(place + k < lines)
        def _():
            block = self.f + 2 * k
            landed(self.views[v](block), self.recv.at[v, block])

            @pl.when(place > 0)
            def _():
                self.copy(v, block, lines - 1 + k, "left").start()

            self.copy(v, block, lines - 1 + k, "partner").start()

    def finish(self, v):
        place, lines = self.place, self.lines
        for line in range(lines):
            block = 2 * line + 1 - self.core
            landed(self.views[v](block), self.recv.at[v, block])
        self.copy(v, self.f, 0, "partner").wait_send()

        @pl.when(place < lines - 1)
        def _():
            self.copy(v, self.f, 0, "right").wait_send()

        @pl.when(place > 0)
        def _():
            self.copy(v, self.f, 0, "left").wait_send()

        for k in range(1, lines):

            @pl.when(place >= k)
            def _():
                block = self.f - 2 * k

                @pl.when(place < lines - 1)
                def _():
                    self.copy(v, block, k, "right").wait_send()

                self.copy(v, block, k, "partner").wait_send()

            @pl.when(place + k < lines)
            def _():
                block = self.f + 2 * k

                @pl.when(place > 0)
                def _():
                    self.copy(v, block, lines - 1 + k, "left").wait_send()

                self.copy(v, block, lines - 1 + k, "partner").wait_send()


def line_sems(arrays, fsdp):
    lines = fsdp // 2
    return [
        pltpu.SemaphoreType.DMA((arrays, 2 * lines, 3)),
        pltpu.SemaphoreType.DMA((arrays, fsdp)),
    ]


def add_rows(dst, a, b, rows):
    def step(i, carry):
        at = pl.ds(pl.multiple_of(i * 32, 32), 32)
        dst[at, :] = a[at, :].astype(dst.dtype) + b[at, :].astype(dst.dtype)
        return carry

    lax.fori_loop(0, rows // 32, step, 0)


class LineReduce:
    def __init__(self, p_ref, scratch, lines, f, s):
        self.p_ref, self.lines, self.f, self.s = p_ref, lines, f, s
        self.own, self.paired, self.got, self.last = scratch[:4]
        self.psend, self.precv, self.send, self.recv, self.final, self.local = scratch[4:]
        self.place, self.core = f // 2, f % 2
        self.rows = p_ref.shape[1]
        self.order = []
        for n in range(lines):
            for d in (lines - 1 - n, n):
                if d not in self.order:
                    self.order.append(d)

    @staticmethod
    def scratch(fsdp, block):
        lines = fsdp // 2
        dma = pltpu.SemaphoreType.DMA
        return [
            pltpu.VMEM((lines,) + block, BF16),
            pltpu.VMEM((lines,) + block, BF16),
            pltpu.VMEM((lines,) + block, BF16),
            pltpu.VMEM(block, BF16),
            dma((lines,)), dma((lines,)), dma((lines,)), dma((lines,)), dma, dma((lines,)),
        ]

    def load(self, i):
        return pltpu.make_async_copy(self.p_ref.at[2 * i + self.core], self.own.at[i], self.local.at[i])

    def swap(self, i):
        return remote(
            self.p_ref.at[2 * i + 1 - self.core], self.paired.at[i], self.psend.at[i],
            self.precv.at[i], (self.f + 1 - 2 * self.core, self.s),
        )

    def right(self, d, last):
        dst = self.last if last else self.got.at[d]
        sem = self.final if last else self.recv.at[d]
        return remote(self.own.at[d], dst, self.send.at[d], sem, (self.f + 2, self.s))

    def left(self, d):
        return remote(
            self.own.at[d], self.got.at[d], self.send.at[d], self.recv.at[d], (self.f - 2, self.s)
        )

    def start(self):
        for i in self.order[:2]:
            self.swap(i).start()
        for i in self.order:
            self.load(i).start()
        self.added = 0
        self.add_pairs(2)

    def add_pairs(self, until):
        for i in self.order[self.added : until]:
            self.load(i).wait()
            landed(self.paired.at[i], self.precv.at[i])
            add_rows(self.own.at[i], self.own.at[i], self.paired.at[i], self.rows)
        self.added = max(self.added, until)

    def step(self, t):
        place, lines = self.place, self.lines
        d = lines - 1 - t + place

        @pl.when(t >= place)
        def _():
            @pl.when(place > 0)
            def _():
                landed(self.got.at[d], self.recv.at[d])
                add_rows(self.own.at[d], self.own.at[d], self.got.at[d], self.rows)

            @pl.when(d == place + 1)
            def _():
                self.right(d, True).start()

            @pl.when(d != place + 1)
            def _():
                self.right(d, False).start()

        e = t - (lines - 1 - place)

        @pl.when(e >= 0)
        def _():
            @pl.when(place < lines - 1)
            def _():
                landed(self.got.at[e], self.recv.at[e])
                add_rows(self.own.at[e], self.own.at[e], self.got.at[e], self.rows)

            self.left(e).start()

        if t == 0:
            for i in self.order[2:]:
                self.swap(i).start()
        self.add_pairs(2 * t + 4)

    def finish(self, out_ref):
        place, lines, rows = self.place, self.lines, self.rows

        def total(*extra):
            def step(i, carry):
                at = pl.ds(pl.multiple_of(i * 32, 32), 32)
                value = self.own[place, at, :].astype(F32)
                for ref in extra:
                    value += ref[at, :].astype(F32)
                out_ref[at, :] = value.astype(out_ref.dtype)
                return carry

            lax.fori_loop(0, rows // 32, step, 0)

        @pl.when(place > 0)
        def _():
            landed(self.last, self.final)

        @pl.when(place < lines - 1)
        def _():
            landed(self.got.at[place], self.recv.at[place])

        @pl.when(place == 0)
        def _():
            total(self.got.at[place])

        @pl.when(place == lines - 1)
        def _():
            total(self.last)

        @pl.when(jnp.logical_and(place > 0, place < lines - 1))
        def _():
            total(self.last, self.got.at[place])

        for i in range(lines):
            self.swap(i).wait_send()

            @pl.when(place < i)
            def _():
                self.right(i, False).wait_send()

            @pl.when(place > i)
            def _():
                self.left(i).wait_send()


class PlaneGather:
    def __init__(self, own, out, f, s, send, recv):
        self.own, self.out, self.f, self.s, self.send, self.recv = own, out, f, s, send, recv
        self.rows = own.shape[0]
        self.half = self.rows // 2

    def at(self, place, first, size):
        return self.out.at[pl.ds(pl.multiple_of(place * self.rows + first, self.half), size), :]

    def near(self, k):
        return remote(
            self.own, self.at(self.s, 0, self.rows), self.send.at[k - 1], self.recv.at[k - 1],
            (self.f, self.s ^ k),
        )

    def on(self, k):
        ref = self.at(self.s ^ k, (k - 1) * self.half, self.half)
        return remote(ref, ref, self.send.at[k + 1], self.recv.at[k + 1], (self.f, self.s ^ (3 - k)))

    def start(self):
        self.near(1).start()
        self.near(2).start()

    def forward(self):
        for k in (1, 2):
            landed(self.at(self.s ^ k, 0, self.rows), self.recv.at[k - 1])
            self.on(k).start()

    def finish(self):
        landed(self.at(self.s ^ 3, 0, self.half), self.recv.at[2])
        landed(self.at(self.s ^ 3, self.half, self.half), self.recv.at[3])
        for k in (1, 2):
            self.near(k).wait_send()
            self.on(k).wait_send()


class AnyGather:
    def __init__(self, own, out, f, s, sp, send, recv):
        self.own, self.out, self.f, self.s, self.sp = own, out, f, s, sp
        self.send, self.recv = send, recv
        self.rows = own.shape[0]

    def at(self, place, first, size):
        return self.out.at[pl.ds(pl.multiple_of(place * self.rows + first, size), size), :]

    def copy(self, k):
        dst = self.at(self.s, 0, self.rows)
        return remote(self.own, dst, self.send.at[k], self.recv.at[k], (self.f, self.s ^ k))

    def start(self):
        for k in range(1, self.sp):
            self.copy(k).start()

    def forward(self):
        pass

    def finish(self):
        for k in range(1, self.sp):
            landed(self.at(self.s ^ k, 0, self.rows), self.recv.at[k])
            self.copy(k).wait_send()


class AnyReduce:
    def __init__(self, p_ref, out_ref, scratch, f, s, sp):
        self.p_ref, self.out_ref, self.f, self.s, self.sp = p_ref, out_ref, f, s, sp
        self.own, self.got, self.send, self.recv, self.local = scratch

    @staticmethod
    def scratch(block, sp):
        dma = pltpu.SemaphoreType.DMA
        return [
            pltpu.VMEM(block, BF16), pltpu.VMEM((sp,) + block, BF16), dma((sp,)), dma((sp,)), dma,
        ]

    def copy(self, k):
        d = self.s ^ k
        return remote(
            self.p_ref.at[d], self.got.at[k], self.send.at[k], self.recv.at[k], (self.f, d)
        )

    def load(self):
        return pltpu.make_async_copy(self.p_ref.at[self.s], self.own, self.local)

    def start(self, make=lambda d: None):
        for k in range(self.sp - 1, 0, -1):
            make(self.s ^ k)
            self.copy(k).start()
        make(self.s)
        self.load().start()

    def forward(self):
        self.load().wait()

    def finish(self):
        rows = self.own.shape[0]
        for k in range(1, self.sp):
            landed(self.got.at[k], self.recv.at[k])
            add_rows(self.out_ref, self.own if k == 1 else self.out_ref, self.got.at[k], rows)
        for k in range(1, self.sp):
            self.copy(k).wait_send()


def plane_gather_of(own, out, f, s, sp, send, recv):
    if sp == 4:
        return PlaneGather(own, out, f, s, send, recv)
    return AnyGather(own, out, f, s, sp, send, recv)


def plane_reduce_of(p_ref, out_ref, scratch, f, s, sp):
    if sp == 4:
        return PlaneReduce(p_ref, out_ref, scratch, f, s)
    return AnyReduce(p_ref, out_ref, scratch, f, s, sp)


def plane_scratch(block, sp):
    return PlaneReduce.scratch(block) if sp == 4 else AnyReduce.scratch(block, sp)


class PlaneReduce:
    WAYS = ((0, 1, 1), (1, 2, 2))

    def __init__(self, p_ref, out_ref, scratch, f, s):
        self.p_ref, self.out_ref, self.f, self.s = p_ref, out_ref, f, s
        self.own, self.got, self.got_on, self.send, self.recv, self.local = scratch
        self.half = p_ref.shape[1] // 2

    @staticmethod
    def scratch(block):
        dma = pltpu.SemaphoreType.DMA
        return [
            pltpu.VMEM((3,) + block, BF16), pltpu.VMEM((2,) + block, BF16),
            pltpu.VMEM(block, BF16), dma((2, 3)), dma((2, 3)), dma((3,)),
        ]

    def part(self, ref, h):
        return ref.at[pl.ds(h * self.half, self.half), :]

    def load(self, n):
        d = (self.s, self.s ^ 2, self.s ^ 1)[n]
        return pltpu.make_async_copy(self.p_ref.at[d], self.own.at[n], self.local.at[n])

    def hop(self, h, k, far):
        d = self.s ^ 3 if far else self.s ^ k
        n = 0 if far else 1
        return remote(
            self.part(self.p_ref.at[d], h), self.part(self.got.at[1 - n], h), self.send.at[h, n],
            self.recv.at[h, n], (self.f, self.s ^ k),
        )

    def on(self, h, k, n):
        return remote(
            self.part(self.own.at[n], h), self.part(self.got_on, h), self.send.at[h, 2],
            self.recv.at[h, 2], (self.f, self.s ^ (3 - k)),
        )

    def start(self, make=lambda d: None):
        make(self.s ^ 3)
        for h, k, _ in self.WAYS:
            self.hop(h, k, True).start()
        make(self.s ^ 1)
        make(self.s ^ 2)
        for h, k, _ in self.WAYS:
            self.hop(h, k, False).start()
        make(self.s)
        for n in range(3):
            self.load(n).start()

    def forward(self):
        for n in range(3):
            self.load(n).wait()
        for h, k, n in self.WAYS:
            mine = self.part(self.own.at[n], h)
            landed(self.part(self.got.at[1], h), self.recv.at[h, 0])
            add_rows(mine, mine, self.part(self.got.at[1], h), self.half)
            self.on(h, k, n).start()

    def finish(self):
        for h in (0, 1):
            landed(self.part(self.got.at[0], h), self.recv.at[h, 1])
            add_rows(
                self.part(self.out_ref, h), self.part(self.own.at[0], h), self.part(self.got.at[0], h),
                self.half,
            )
        for h in (0, 1):
            landed(self.part(self.got_on, h), self.recv.at[h, 2])
            out = self.part(self.out_ref, h)
            add_rows(out, out, self.part(self.got_on, h), self.half)
        for h, k, n in self.WAYS:
            self.hop(h, k, True).wait_send()
            self.hop(h, k, False).wait_send()
            self.on(h, k, n).wait_send()


def greet_plane(barrier, f, s, sp):
    ways = (1, 2) if sp == 4 else range(1, sp)
    for k in ways:
        signal(barrier, (f, s ^ k))
    return len(ways)


def greet_all(barrier, me, count, sp):
    def greet(i, carry):
        other = lax.rem(me + i, count)
        signal(barrier, (other // sp, lax.rem(other, sp)))
        return carry

    lax.fori_loop(1, count, greet, 0)


def rows_view(ref, rows):
    return lambda b: ref.at[pl.ds(pl.multiple_of(b * rows, rows), rows), :]


def block_view(ref):
    return lambda b: ref.at[b]


def comm_params(number):
    return pltpu.CompilerParams(
        collective_id=number, has_side_effects=True, vmem_limit_bytes=VLIM
    )


def row_target(i, rows, sp):
    parts = HEAD_DIM // rows
    head, part = i // parts, lax.rem(i, parts)
    return head // sp * parts + part, lax.rem(head, sp)


def row_owner(f, s, rows, sp):
    parts = HEAD_DIM // rows
    return (f // parts * sp + s) * parts + lax.rem(f, parts)


def start_kernel(
    fsdp, sp, x_ref, w_ref, wo_ref, g_ref, misc_ref, routes_ref,
    x_all, w_all, wo_all, g_all, misc_all, routes_all,
    send, recv, xsend, xrecv, psend, precv, wsend, wrecv, msend, mrecv, rsend, rrecv, local, wlocal,
):
    f, s = lax.axis_index("fsdp"), lax.axis_index("sp")
    count, lines = fsdp * sp, fsdp // 2
    me = f * sp + s
    rows = w_ref.shape[1]
    heads = D // sp // HEAD_DIM
    barrier = pltpu.get_barrier_semaphore()

    def w_block(s_to, g):
        at = pl.multiple_of((g * sp + s_to) * HEAD_DIM, HEAD_DIM)
        return w_ref.at[:, :, pl.ds(at, HEAD_DIM)]

    def w_rows(i, g):
        at = pl.ds(pl.multiple_of(i * rows, rows), rows)
        return w_all.at[:, at, pl.ds(g * HEAD_DIM, HEAD_DIM)]

    def w_view(b):
        size = rows * sp
        return w_all.at[:, pl.ds(pl.multiple_of(b * size, size), size), :]

    wo_view = rows_view(wo_all, rows)
    x_view = rows_view(x_all, TOK_DEV)
    w_owns = [
        pltpu.make_async_copy(w_block(s, g), w_rows(me, g), wlocal.at[g]) for g in range(heads)
    ]
    owns = [
        pltpu.make_async_copy(x_ref, x_view(s), local.at[0]),
        pltpu.make_async_copy(misc_ref, misc_all.at[me], local.at[1]),
        pltpu.make_async_copy(routes_ref, routes_all.at[f], local.at[2]),
        pltpu.make_async_copy(g_ref, g_all.at[f], local.at[3]),
    ]
    for copy in w_owns + owns:
        copy.start()
    greet_all(barrier, me, count, sp)
    pl.semaphore_wait(barrier, count - 1)

    line = LineGather([w_view, wo_view, block_view(g_all)], [None, None, g_ref], lines, f, s, send, recv)
    line.start_own(2)
    w_copies = []
    for k in range(sp - 1, 0, -1):
        s_to = s ^ k
        for g in range(heads):
            copy = remote(
                w_block(s_to, g), w_rows(me, g), psend.at[k, g], precv.at[k, g], (f, s_to)
            )
            copy.start()
            w_copies.append(copy)
    target_f, target_s = row_target(me, rows, sp)
    stays = jnp.logical_and(target_s == s, target_f == f)
    wo_copy = remote(wo_ref, wo_view(target_f), wsend, wrecv, (target_f, target_s))
    wo_own = pltpu.make_async_copy(wo_ref, wo_view(f), wrecv)

    @pl.when(stays)
    def _():
        wo_own.start()

    @pl.when(jnp.logical_not(stays))
    def _():
        wo_copy.start()

    def misc_copy(i):
        other = lax.rem(me + i, count)
        return remote(
            misc_ref, misc_all.at[me], msend.at[i], mrecv.at[me], (other // sp, lax.rem(other, sp))
        )

    def misc_go(i, carry):
        misc_copy(i).start()
        return carry

    lax.fori_loop(1, count, misc_go, 0)

    def routes_copy(i):
        other = lax.rem(f + i, fsdp)
        return remote(routes_ref, routes_all.at[f], rsend.at[i], rrecv.at[f], (other, s))

    def routes_go(i, carry):
        routes_copy(i).start()
        return carry

    lax.fori_loop(1, fsdp, routes_go, 0)

    for copy in w_owns:
        copy.wait()
    for k in range(1, sp):
        for g in range(heads):
            landed(w_rows(f * sp + (s ^ k), g), precv.at[k, g])
    line.start_own(0)
    tokens = plane_gather_of(x_ref, x_all, f, s, sp, xsend, xrecv)
    tokens.start()
    landed(wo_view(f), wrecv)
    line.start_own(1)
    for k in range(1, lines):
        for v in (2, 0, 1):
            line.forward(v, k)
        if k == min(2, lines - 1):
            tokens.forward()
    for v in range(3):
        line.finish(v)
    tokens.finish()

    def misc_end(i, carry):
        misc_copy(i).wait_send()
        other = lax.rem(me + i, count)
        landed(misc_all.at[other], mrecv.at[other])
        return carry

    lax.fori_loop(1, count, misc_end, 0)

    def routes_end(i, carry):
        routes_copy(i).wait_send()
        other = lax.rem(f + i, fsdp)
        landed(routes_all.at[other], rrecv.at[other])
        return carry

    lax.fori_loop(1, fsdp, routes_end, 0)
    for copy in w_copies:
        copy.wait_send()

    @pl.when(jnp.logical_not(stays))
    def _():
        wo_copy.wait_send()

    for copy in owns:
        copy.wait()


def gather_start(fsdp, sp, x, w, wo, g, misc, routes):
    count = fsdp * sp
    heads = D // sp // HEAD_DIM
    dma = pltpu.SemaphoreType.DMA
    return pl.pallas_call(
        functools.partial(start_kernel, fsdp, sp),
        out_shape=(
            jax.ShapeDtypeStruct((sp * TOK_DEV, D), BF16),
            jax.ShapeDtypeStruct((3, D, D // sp), BF16),
            jax.ShapeDtypeStruct((D // sp, D), BF16),
            jax.ShapeDtypeStruct((fsdp,) + g.shape, BF16),
            jax.ShapeDtypeStruct((count,) + misc.shape, BF16),
            jax.ShapeDtypeStruct((fsdp,) + routes.shape, jnp.int32),
        ),
        in_specs=[VMEM] * 6,
        out_specs=[ANY] * 6,
        scratch_shapes=line_sems(3, fsdp)
        + [
            dma((sp,)), dma((sp,)), dma((sp, heads)), dma((sp, heads)), dma, dma,
            dma((count,)), dma((count,)), dma((fsdp,)), dma((fsdp,)), dma((4,)), dma((heads,)),
        ],
        compiler_params=comm_params(0),
        name="gather_start",
    )(x, w, wo, g, misc, routes)


def branch_kernel(
    fsdp, sp, a_ref, w_ref, g_ref, x_ref, gain, out_ref, second_ref, g_all, terms, *scratch
):
    f, s = lax.axis_index("fsdp"), lax.axis_index("sp")
    lines = fsdp // 2
    barrier = pltpu.get_barrier_semaphore()
    expected = greet_line(barrier, lines, f, s) + greet_plane(barrier, f, s, sp)
    send, recv, own_sem = scratch[-3:]
    own = pltpu.make_async_copy(g_ref, g_all.at[f], own_sem)
    own.start()
    pl.semaphore_wait(barrier, expected)
    plane = plane_reduce_of(terms, out_ref, scratch[:-3], f, s, sp)
    line = LineGather([block_view(g_all)], [g_ref], lines, f, s, send, recv)
    line.start_own(0)

    def branch_of(d):
        rows = pl.ds(pl.multiple_of(d * TOK_DEV, TOK_DEV), TOK_DEV)
        for n in range(D // 512):
            at = pl.ds(n * 512, 512)
            terms[d, :, at] = dot_nn(a_ref[rows, :], w_ref[:, at]).astype(BF16)

    plane.start(branch_of)
    for k in range(1, lines):
        line.forward(0, k)
        if k == min(2, lines - 1):
            plane.forward()
    plane.finish()

    def norm(i, carry):
        at = pl.ds(pl.multiple_of(i * 32, 32), 32)
        mid = x_ref[at, :].astype(F32) + out_ref[at, :]
        out_ref[at, :] = mid
        inverse = lax.rsqrt(jnp.mean(mid * mid, axis=-1, keepdims=True) + EPSILON)
        second_ref[at, :] = (mid * inverse * gain[1:2, :]).astype(BF16)
        return carry

    lax.fori_loop(0, TOK_DEV // 32, norm, 0)
    line.finish(0)
    own.wait()


def branch_sum(fsdp, attended, w, g, x, gains):
    sp, block = attended.shape[0] // TOK_DEV, x.shape
    return pl.pallas_call(
        functools.partial(branch_kernel, fsdp, sp),
        out_shape=(
            jax.ShapeDtypeStruct(block, F32),
            jax.ShapeDtypeStruct(block, BF16),
            jax.ShapeDtypeStruct((fsdp,) + g.shape, BF16),
        ),
        in_specs=[VMEM] * 5,
        out_specs=[VMEM, VMEM, ANY],
        scratch_shapes=[pltpu.VMEM((sp,) + block, BF16)]
        + plane_scratch(block, sp) + line_sems(1, fsdp) + [pltpu.SemaphoreType.DMA],
        compiler_params=comm_params(2),
        name="branch_sum",
    )(attended, w, g, x, gains)


def token_kernel(
    fsdp, sp, x_ref, g_first, g_second, picks, w_ref, up_ref, out_ref, taken_ref, back_ref, up_all,
    g_buf, w_buf, taken, back, send, recv, local, loads, stores, back_sem, usend, urecv, ulocal,
):
    f, s = lax.axis_index("fsdp"), lax.axis_index("sp")
    lines = fsdp // 2
    parts = 2
    size = TOK_DEV // parts
    early, later = g_first.shape[1], g_second.shape[1]
    slots = picks.shape[1] // EXP_DEV
    ff = w_ref.shape[1]
    barrier = pltpu.get_barrier_semaphore()
    expected = greet_line(barrier, lines, f, s) + greet_plane(barrier, f, s, sp)
    plane = plane_gather_of(up_ref, up_all, f, s, sp, usend, urecv)
    up_own = pltpu.make_async_copy(up_ref, plane.at(s, 0, up_ref.shape[0]), ulocal)
    up_own.start()
    own = pltpu.make_async_copy(x_ref, out_ref.at[f], local)
    own.start()
    reads = [
        pltpu.make_async_copy(g_first, g_buf.at[:, pl.ds(0, early), :], loads.at[0]),
        pltpu.make_async_copy(g_second, g_buf.at[:, pl.ds(early, later), :], loads.at[1]),
        pltpu.make_async_copy(w_ref, w_buf, loads.at[2]),
    ]
    for copy in reads:
        copy.start()
    pl.semaphore_wait(barrier, expected)

    def view(part):
        return lambda b: out_ref.at[b, pl.ds(part * size, size), :]

    owns = [x_ref.at[pl.ds(p * size, size), :] for p in range(parts)]
    line = LineGather([view(p) for p in range(parts)], owns, lines, f, s, send, recv)
    for p in range(parts):
        line.start_own(p)
    plane.start()

    def take_all():
        reads[0].wait()
        reads[1].wait()

        def block(b, carry):
            for n in range(D // 512):
                at = pl.ds(n * 512, 512)
                got = dot_nn(picks[b], g_buf[b, :, at]).astype(BF16)
                for e in range(EXP_DEV):
                    to = pl.ds(pl.multiple_of(b * slots, 16), slots)
                    taken[e, to, at] = got[e * slots : (e + 1) * slots]
            return carry

        lax.fori_loop(0, fsdp, block, 0)
        for e in range(EXP_DEV):
            pltpu.make_async_copy(taken.at[e], taken_ref.at[e], stores.at[e]).start()

    def back_copy(e, j, slot):
        at = pl.ds(pl.multiple_of(j * FT, FT), FT)
        return pltpu.make_async_copy(back.at[slot], back_ref.at[e, :, at], back_sem.at[slot])

    def back_of(e):
        if e == 0:
            reads[2].wait()
        for j in range(ff // FT):
            slot = j % 2
            if e > 0 or j > 1:
                back_copy(e, j, slot).wait()
            back[slot] = dot_nt(taken[e], w_buf[e, pl.ds(j * FT, FT), :])
            back_copy(e, j, slot).start()

    work = [take_all] + [functools.partial(back_of, e) for e in range(EXP_DEV)]
    for k in range(1, lines):
        if k - 1 < len(work):
            work[k - 1]()
        for p in range(parts):
            line.forward(p, k)
        if k == min(2, lines - 1):
            plane.forward()
    for unit in work[lines - 1 :]:
        unit()
    for p in range(parts):
        line.finish(p)
    plane.finish()
    up_own.wait()
    own.wait()
    for slot in range(2):
        back_copy(0, slot, slot).wait()
    for e in range(EXP_DEV):
        pltpu.make_async_copy(taken.at[e], taken_ref.at[e], stores.at[e]).wait()


def token_gather(fsdp, sp, x, g_first, g_second, picks, w_down, up):
    slots = picks.shape[1] // EXP_DEV
    total = fsdp * slots
    ff = w_down.shape[1]
    dma = pltpu.SemaphoreType.DMA
    return pl.pallas_call(
        functools.partial(token_kernel, fsdp, sp),
        out_shape=(
            jax.ShapeDtypeStruct((fsdp, TOK_DEV, D), BF16),
            jax.ShapeDtypeStruct((EXP_DEV, total, D), BF16),
            jax.ShapeDtypeStruct((EXP_DEV, total, ff), F32),
            jax.ShapeDtypeStruct((sp * up.shape[0], up.shape[1]), BF16),
        ),
        in_specs=[VMEM, ANY, ANY, VMEM, ANY, VMEM],
        out_specs=[ANY, ANY, ANY, ANY],
        scratch_shapes=[
            pltpu.VMEM((fsdp, TOK_DEV, D), BF16),
            pltpu.VMEM((EXP_DEV, ff, D), BF16),
            pltpu.VMEM((EXP_DEV, total, D), BF16),
            pltpu.VMEM((2, total, FT), F32),
        ]
        + line_sems(2, fsdp)
        + [dma, dma((3,)), dma((EXP_DEV,)), dma((2,)), dma((sp,)), dma((sp,)), dma],
        compiler_params=comm_params(3),
        name="token_gather",
    )(x, g_first, g_second, picks, w_down, up)


def token_back_kernel(
    fsdp, p_ref, gated_ref, w_ref, turned, x_ref, gu_ref, mid_ref, g_ref, gain,
    out_ref, low_ref, gain_out, part_ref, wu_ref, wide, narrow, w_buf, tile, grad_tile, loads, tile_sem, grad_sem, *scratch,
):
    f, s = lax.axis_index("fsdp"), lax.axis_index("sp")
    lines = fsdp // 2
    slots = turned.shape[3]
    height = grad_tile.shape[1]
    barrier = pltpu.get_barrier_semaphore()
    expected = greet_line(barrier, lines, f, s)
    reads = [
        pltpu.make_async_copy(gated_ref, narrow, loads.at[0]),
        pltpu.make_async_copy(w_ref.at[0], w_buf, loads.at[1]),
        pltpu.make_async_copy(x_ref, wide, loads.at[2]),
        pltpu.make_async_copy(gu_ref, narrow, loads.at[3]),
        pltpu.make_async_copy(w_ref.at[1], w_buf, loads.at[1]),
    ]
    reads[0].start()
    reads[1].start()
    pl.semaphore_wait(barrier, expected)
    line = LineReduce(p_ref, scratch, lines, f, s)
    line.start()

    def down_of(e):
        if e == 0:
            reads[0].wait()
            reads[1].wait()
        else:
            reads[4].wait()

        def columns(n, carry):
            at = pl.ds(pl.multiple_of(n * 512, 512), 512)
            wide[e, :, at] = dot_nn(narrow[e], w_buf[:, at]).astype(BF16)
            return carry

        lax.fori_loop(0, D // 512, columns, 0)
        if e == 0:
            reads[4].start()

    def tile_copy(b, slot):
        return pltpu.make_async_copy(tile.at[slot], part_ref.at[b], tile_sem.at[slot])

    def sum_all():
        reads[3].start()

        def pair(i, carry):
            for slot in range(2):
                b = 2 * i + slot

                @pl.when(i > 0)
                def _():
                    tile_copy(b, slot).wait()

                for n in range(D // 512):
                    at = pl.ds(n * 512, 512)
                    summed = jnp.zeros((TOK_DEV, 512), F32)
                    for e in range(EXP_DEV):
                        rows = wide[e, pl.ds(pl.multiple_of(b * slots, 16), slots), at]
                        summed += dot_nn(turned[b, e], rows)
                    tile[slot, :, at] = summed.astype(BF16)
                tile_copy(b, slot).start()
            return carry

        lax.fori_loop(0, fsdp // 2, pair, 0)
        reads[2].start()

    def grad_copy(e, i, slot):
        at = pl.ds(pl.multiple_of(i * height, height), height)
        return pltpu.make_async_copy(grad_tile.at[slot], wu_ref.at[e, at, :], grad_sem.at[slot])

    def grad_of(e):
        if e == 0:
            reads[2].wait()
            reads[3].wait()

        def pair(i, carry):
            for slot in range(2):
                part = 2 * i + slot

                def before():
                    grad_copy(e, part, slot).wait()

                if e == 0:
                    pl.when(i > 0)(before)
                else:
                    before()
                at = pl.ds(pl.multiple_of(part * height, height), height)
                grad_tile[slot] = dot_tn(wide[e, :, at], narrow[e]).astype(BF16)
                grad_copy(e, part, slot).start()
            return carry

        lax.fori_loop(0, D // height // 2, pair, 0)

    work = [functools.partial(down_of, e) for e in range(EXP_DEV)] + [sum_all]
    work += [functools.partial(grad_of, e) for e in range(EXP_DEV)]
    done = 0
    for t in range(lines - 1):
        line.step(t)
        until = (t + 1) * len(work) // (lines - 1)
        for unit in work[done:until]:
            unit()
        done = until
    line.finish(out_ref)
    gain_out[...] = jnp.zeros_like(gain_out)

    def norm_back(i, carry):
        at = pl.ds(pl.multiple_of(i * 32, 32), 32)
        mid = mid_ref[at, :]
        inverse = lax.rsqrt(jnp.mean(mid * mid, axis=-1, keepdims=True) + EPSILON)
        normed = mid * inverse
        grad_y = out_ref[at, :]
        scaled = grad_y * gain[1:2, :]
        mean = jnp.mean(scaled * normed, axis=-1, keepdims=True)
        grad = g_ref[at, :].astype(F32) + inverse * (scaled - normed * mean)
        out_ref[at, :] = grad
        low_ref[at, :] = grad.astype(BF16)
        gain_out[1:2, :] += jnp.sum(grad_y * normed, axis=0, keepdims=True)
        return carry

    lax.fori_loop(0, TOK_DEV // 32, norm_back, 0)
    for slot in range(2):
        tile_copy(slot, slot).wait()
        grad_copy(0, slot, slot).wait()


def token_back(fsdp, partial, gated, w_down, turned, received, grad_up_pre, mid, g, gains):
    block = partial.shape[1:]
    total, ff = gated.shape[1:]
    height = 256
    dma = pltpu.SemaphoreType.DMA
    return pl.pallas_call(
        functools.partial(token_back_kernel, fsdp),
        out_shape=(
            jax.ShapeDtypeStruct(block, F32),
            jax.ShapeDtypeStruct(block, BF16),
            jax.ShapeDtypeStruct((8, D), F32),
            jax.ShapeDtypeStruct(partial.shape, BF16),
            jax.ShapeDtypeStruct((EXP_DEV, D, ff), BF16),
        ),
        in_specs=[ANY, ANY, ANY, VMEM, ANY, ANY, VMEM, VMEM, VMEM],
        out_specs=[VMEM, VMEM, VMEM, ANY, ANY],
        scratch_shapes=[
            pltpu.VMEM((EXP_DEV, total, D), BF16),
            pltpu.VMEM((EXP_DEV, total, ff), BF16),
            pltpu.VMEM((ff, D), BF16),
            pltpu.VMEM((2,) + block, BF16),
            pltpu.VMEM((2, height, ff), BF16),
            dma((4,)),
            dma((2,)),
            dma((2,)),
        ]
        + LineReduce.scratch(fsdp, block),
        compiler_params=comm_params(4),
        name="token_back",
    )(partial, gated, w_down, turned, received, grad_up_pre, mid, g, gains)


class PlaneSum:
    def __init__(self, scratch, f, s, sp):
        self.own, self.got, self.send, self.recv = scratch
        self.f, self.s, self.sp = f, s, sp

    @staticmethod
    def scratch(seq, sp):
        dma = pltpu.SemaphoreType.DMA
        return [
            pltpu.VMEM((8, seq), F32), pltpu.VMEM((sp, 8, seq), F32), dma((sp,)), dma((sp,)),
        ]

    def greet(self, barrier):
        for k in range(1, self.sp):
            signal(barrier, (self.f, self.s ^ k))
        return self.sp - 1

    def copy(self, k):
        return remote(
            self.own, self.got.at[k], self.send.at[k], self.recv.at[k], (self.f, self.s ^ k)
        )

    def start(self, x_ref):
        self.own[...] = x_ref[...].T[:8]
        for k in range(1, self.sp):
            self.copy(k).start()

    def finish(self, out_ref):
        for k in range(1, self.sp):
            self.copy(k).wait()
        terms = [self.own[...]] + [self.got[k] for k in range(1, self.sp)]
        while len(terms) > 1:
            terms = [terms[i] + terms[i + 1] for i in range(0, len(terms), 2)]
        seq = out_ref.shape[0]
        out_ref[...] = jnp.concatenate([terms[0], jnp.zeros((120, seq), F32)], axis=0).T


def end_kernel(
    fsdp, sp, p_ref, low_ref, w_ref, x_ref, mid_ref, gain, gains_in, router_ref,
    grad_out, qkv_0, qkv_1, qkv_2, o_out, small_out,
    first, low_in, w_buf, back, low, o_low, gain_sum, pay, small, loads,
    qsend, qrecv, osend, orecv, msend, mrecv, local, *scratch,
):
    f, s = lax.axis_index("fsdp"), lax.axis_index("sp")
    count, lines = fsdp * sp, fsdp // 2
    me = f * sp + s
    rows, cols = o_low.shape[0], D // sp
    height = D // fsdp
    barrier = pltpu.get_barrier_semaphore()
    greet_all(barrier, me, count, sp)
    reads = [
        pltpu.make_async_copy(low_ref, low_in, loads.at[0]),
        pltpu.make_async_copy(w_ref, w_buf, loads.at[1]),
    ]
    for copy in reads:
        copy.start()
    pl.semaphore_wait(barrier, count - 1)
    plane_parts = 6 if sp == 4 else 5
    plane = plane_reduce_of(first, back, scratch[:plane_parts], f, s, sp)
    line = LineReduce(p_ref, scratch[plane_parts:], lines, f, s)
    line.start()

    def first_grads():
        for copy in reads:
            copy.wait()

        def columns(n, carry):
            at = pl.ds(pl.multiple_of(n * 256, 256), 256)
            for d in range(sp):
                rows_at = slice(d * TOK_DEV, (d + 1) * TOK_DEV)
                total = dot_nt(low_in[rows_at, :cols], w_buf[0, at, :])
                total += dot_nt(low_in[rows_at, cols : 2 * cols], w_buf[1, at, :])
                total += dot_nt(low_in[rows_at, 2 * cols :], w_buf[2, at, :])
                first[d, :, at] = total.astype(BF16)
            return carry

        lax.fori_loop(0, D // 256, columns, 0)

    def input_grads():
        gain_sum[...] = jnp.zeros_like(gain_sum)

        def chunk(i, carry):
            at = pl.ds(pl.multiple_of(i * 32, 32), 32)
            x = x_ref[at, :].astype(F32)
            inverse = lax.rsqrt(jnp.mean(x * x, axis=-1, keepdims=True) + EPSILON)
            normed = x * inverse
            grad_y = back[at, :]
            scaled = grad_y * gain[0:1, :]
            mean = jnp.mean(scaled * normed, axis=-1, keepdims=True)
            grad_out[at, :] = mid_ref[at, :] + inverse * (scaled - normed * mean)
            gain_sum[0:1, :] += jnp.sum(grad_y * normed, axis=0, keepdims=True)
            return carry

        lax.fori_loop(0, TOK_DEV // 32, chunk, 0)
        gain_sum[...] += gains_in[...]

        def fill(i, carry):
            at = pl.ds(pl.multiple_of(i * rows // 128 * 128, 128), 128)
            pay[i, 0:8, :] = router_ref[i]
            pay[i, 8:16, :] = gain_sum[:, at]
            return carry

        lax.fori_loop(0, count, fill, 0)

    def m_copy(i):
        other = lax.rem(me + i, count)
        return remote(
            pay.at[other], small.at[me], msend.at[i], mrecv.at[me], (other // sp, lax.rem(other, sp))
        )

    def m_go(i, carry):
        m_copy(i).start()
        return carry

    for t in range(lines - 1):
        line.step(t)
        if t == 0:
            first_grads()
            plane.start()
    plane.forward()
    plane.finish()
    input_grads()
    lax.fori_loop(1, count, m_go, 0)
    line.finish(low)
    for c in range(sp):
        top = 3 * height + c * rows
        o_low[:, c * cols : (c + 1) * cols] = low[top : top + rows, :]

    def q_from(i, place):
        return low.at[pl.ds(pl.multiple_of(i * height + place * rows, rows), rows), :]

    def q_to(i, place):
        return (qkv_0, qkv_1, qkv_2)[i].at[place]

    def q_copy(i, k):
        return remote(q_from(i, s ^ k), q_to(i, s), qsend.at[k, i], qrecv.at[k, i], (f, s ^ k))

    def q_own(i):
        return pltpu.make_async_copy(q_from(i, s), q_to(i, s), local.at[i])

    for k in range(sp - 1, 0, -1):
        for i in range(3):
            q_copy(i, k).start()
    owner = row_owner(f, s, rows, sp)
    target_f, target_s = owner // sp, lax.rem(owner, sp)
    stays = jnp.logical_and(target_s == s, target_f == f)
    o_copy = remote(o_low, o_out, osend, orecv, (target_f, target_s))
    o_own = pltpu.make_async_copy(o_low, o_out, orecv)

    @pl.when(stays)
    def _():
        o_own.start()

    @pl.when(jnp.logical_not(stays))
    def _():
        o_copy.start()

    for i in range(3):
        q_own(i).start()

    def m_end(i, carry):
        m_copy(i).wait_send()
        other = lax.rem(me + i, count)
        landed(small.at[other], mrecv.at[other])
        return carry + small[other]

    small_out[...] = lax.fori_loop(1, count, m_end, pay[me])
    for k in range(1, sp):
        for i in range(3):
            landed(q_to(i, s ^ k), qrecv.at[k, i])
            q_copy(i, k).wait_send()
    landed(o_out, orecv)

    @pl.when(jnp.logical_not(stays))
    def _():
        o_copy.wait_send()

    for i in range(3):
        q_own(i).wait()


def end_exchange(fsdp, sp, partial, low, w, x, grad_mid, gains, gains_in, router, number):
    count = fsdp * sp
    block = partial.shape[1:]
    rows = D // count
    dma = pltpu.SemaphoreType.DMA
    return pl.pallas_call(
        functools.partial(end_kernel, fsdp, sp),
        out_shape=(
            jax.ShapeDtypeStruct((TOK_DEV, D), F32),
            jax.ShapeDtypeStruct((sp, rows, D // sp), BF16),
            jax.ShapeDtypeStruct((sp, rows, D // sp), BF16),
            jax.ShapeDtypeStruct((sp, rows, D // sp), BF16),
            jax.ShapeDtypeStruct((rows, D), BF16),
            jax.ShapeDtypeStruct((16, 128), F32),
        ),
        in_specs=[ANY, ANY, ANY, VMEM, VMEM, VMEM, VMEM, VMEM],
        out_specs=[VMEM, ANY, ANY, ANY, ANY, VMEM],
        scratch_shapes=[
            pltpu.VMEM((sp, TOK_DEV, D), BF16),
            pltpu.VMEM(low.shape, BF16),
            pltpu.VMEM(w.shape, BF16),
            pltpu.VMEM((TOK_DEV, D), F32),
            pltpu.VMEM(block, BF16),
            pltpu.VMEM((rows, D), BF16),
            pltpu.VMEM((8, D), F32),
            pltpu.VMEM((count, 16, 128), F32),
            pltpu.VMEM((count, 16, 128), F32),
            dma((2,)),
            dma((sp, 3)), dma((sp, 3)), dma, dma, dma((count,)), dma((count,)), dma((3,)),
        ]
        + plane_scratch((TOK_DEV, D), sp)
        + LineReduce.scratch(fsdp, block),
        compiler_params=comm_params(number),
        name="end_exchange",
    )(partial, low, w, x, grad_mid, gains, gains_in, router)


def dot_nt(a, b):
    return lax.dot_general(a, b, (((1,), (1,)), ((), ())), preferred_element_type=F32)


def dot_tn(a, b):
    return lax.dot_general(a, b, (((0,), (0,)), ((), ())), preferred_element_type=F32)


def dot_nn(a, b):
    return jnp.dot(a, b, preferred_element_type=F32)


def whole(shape):
    return pl.BlockSpec(shape, lambda *_: (0,) * len(shape))


def lanes(first, second):
    lane = lax.broadcasted_iota(jnp.int32, (first.shape[0], 128), 1)
    return jnp.where(lane == 0, first, jnp.where(lane == 1, second, 0.0))


def inverse_of(sums, lane):
    return lax.rsqrt(sums[:, lane : lane + 1] / D + EPSILON)


def turn(v, table, sign=1.0):
    half = HEAD_DIM // 2
    front = lax.broadcasted_iota(jnp.int32, table.shape, 1) < half
    turned = pltpu.roll(table, half, 1)
    cosine = jnp.where(front, table, turned)
    sine = jnp.where(front, -turned, table)
    return v * cosine + pltpu.roll(v, half, 1) * (sine * sign)


def turn_back(v, table):
    return turn(v, table, -1.0)


def project_kernel(sp, x_ref, gain, w_ref, first_out, q_out, k_out, v_out, sums_out, squares, *scratch):
    step = pl.program_id(0)
    total = PlaneSum(scratch, lax.axis_index("fsdp"), lax.axis_index("sp"), sp)
    barrier = pltpu.get_barrier_semaphore()

    @pl.when(step == 0)
    def _():
        total.greet(barrier)

    x = x_ref[...].astype(F32)
    inverse = lax.rsqrt(jnp.mean(x * x, axis=-1, keepdims=True) + EPSILON)
    first = (x * inverse * gain[0:1, :]).astype(BF16)
    first_out[...] = first
    q = dot_nn(first, w_ref[0])
    q_out[...] = q
    k = dot_nn(first, w_ref[1])
    k_out[...] = k
    at = pl.ds(pl.multiple_of(step * TOK_DEV, TOK_DEV), TOK_DEV)
    squares[at, :] = lanes(
        jnp.sum(q * q, axis=-1, keepdims=True), jnp.sum(k * k, axis=-1, keepdims=True)
    )
    last = step == pl.num_programs(0) - 1

    @pl.when(last)
    def _():
        pl.semaphore_wait(barrier, sp - 1)
        total.start(squares)

    v_out[...] = dot_nn(first, w_ref[2]).astype(BF16)

    @pl.when(last)
    def _():
        total.finish(sums_out)


def project(sp, x, gains, w):
    seq, cols = x.shape[0], w.shape[2]

    def block(width):
        return pl.BlockSpec((TOK_DEV, width), lambda i: (i, 0))

    return pl.pallas_call(
        functools.partial(project_kernel, sp),
        grid=(seq // TOK_DEV,),
        out_shape=(
            jax.ShapeDtypeStruct((seq, D), BF16),
            jax.ShapeDtypeStruct((seq, cols), F32),
            jax.ShapeDtypeStruct((seq, cols), F32),
            jax.ShapeDtypeStruct((seq, cols), BF16),
            jax.ShapeDtypeStruct((seq, 128), F32),
        ),
        in_specs=[block(D), whole(gains.shape), whole(w.shape)],
        out_specs=[block(D), block(cols), block(cols), block(cols), whole((seq, 128))],
        scratch_shapes=[pltpu.VMEM((seq, 128), F32)] + PlaneSum.scratch(seq, sp),
        compiler_params=comm_params(1),
        name="project",
    )(x, gains, w)


def attend_kernel(
    q_raw, k_raw, v_ref, squares, gain, table, o_ref, sum_ref, q_ref, k_ref
):
    head = pl.program_id(0)

    @pl.when(head == 0)
    def _():
        sum_ref[...] = squares[...]

    q_inv, k_inv = inverse_of(squares, 0), inverse_of(squares, 1)
    q_ref[...] = turn(q_raw[...] * q_inv * gain[2:3, :], table[...]).astype(BF16)
    k_ref[...] = turn(k_raw[...] * k_inv * gain[3:4, :], table[...]).astype(BF16)
    for i in range(q_ref.shape[0] // BLK):
        rows, seen = pl.ds(i * BLK, BLK), pl.ds(0, (i + 1) * BLK)
        scores = dot_nt(q_ref[rows, :], k_ref[seen, :]) * SCALE
        row_max = jnp.max(scores, axis=-1, keepdims=True)
        exp_rows = jnp.exp(scores - row_max)
        row_sum = jnp.sum(exp_rows, axis=-1, keepdims=True)
        probs = (exp_rows / row_sum).astype(BF16)
        o_ref[rows, :] = dot_nn(probs, v_ref[seen, :]).astype(BF16)
        lane = lax.broadcasted_iota(jnp.int32, (BLK, 128), 1)
        sum_ref[rows, :] += jnp.where(lane == head + 2, row_max + jnp.log(row_sum), 0.0)


def attend(q_raw, k_raw, v, squares, gains, table):
    seq, width = v.shape
    heads = width // HEAD_DIM
    spec = pl.BlockSpec((seq, HEAD_DIM), lambda h: (0, h))
    return pl.pallas_call(
        attend_kernel,
        grid=(heads,),
        out_shape=(
            jax.ShapeDtypeStruct((seq, width), BF16),
            jax.ShapeDtypeStruct((seq, 128), F32),
            jax.ShapeDtypeStruct((seq, width), BF16),
            jax.ShapeDtypeStruct((seq, width), BF16),
        ),
        in_specs=[
            spec, spec, spec, whole((seq, 128)),
            pl.BlockSpec((4, HEAD_DIM), lambda h: (0, h)),
            whole((seq, HEAD_DIM)),
        ],
        out_specs=[spec, whole((seq, 128)), spec, spec],
        compiler_params=pltpu.CompilerParams(vmem_limit_bytes=VLIM),
        name="attend",
    )(q_raw, k_raw, v, squares, gains, table)


def attend_back_head(
    h, q_ref, k_ref, v_ref, sums, q_raw, k_raw, gain, table,
    q_scaled, k_scaled, dv_out, dots, gains_out, dv_ref,
):
    head = slice(h * HEAD_DIM, (h + 1) * HEAD_DIM)
    k_scaled[:, head] = jnp.zeros(k_raw[:, head].shape, F32)
    dv_ref[...] = jnp.zeros_like(dv_ref)
    gain_q, gain_k = gain[2:3, head], gain[3:4, head]
    gain_sum = jnp.zeros((1, HEAD_DIM), F32)
    size = BLK if q_ref.shape[0] <= 4 * BLK else BLK // 2
    for i in range(q_ref.shape[0] // size):
        rows, seen = pl.ds(i * size, size), pl.ds(0, (i * size // BLK + 1) * BLK)
        q, g, keys = q_ref[rows, head], dv_out[rows, head], k_ref[seen, head]
        scores = dot_nt(q, keys) * SCALE
        probs = jnp.exp(scores - sums[rows, h + 2 : h + 3])
        grad_probs = dot_nt(g, v_ref[seen, head])
        row_dot = jnp.sum(probs * grad_probs, axis=-1, keepdims=True)
        grad_scores = (probs * (grad_probs - row_dot)).astype(BF16)
        k_scaled[seen, head] += dot_tn(grad_scores, q)
        dv_ref[seen, :] += dot_tn(probs.astype(BF16), g)
        grad_y = turn_back(dot_nn(grad_scores, keys) * SCALE, table[rows, :])
        normed = q_raw[rows, head] * inverse_of(sums.at[rows, :], 0)
        scaled = grad_y * gain_q
        q_scaled[rows, head] = scaled
        dots[rows, :] += lanes(jnp.sum(scaled * normed, axis=-1, keepdims=True), 0.0)
        gain_sum += jnp.sum(grad_y * normed, axis=0, keepdims=True)
    grad_y = turn_back(k_scaled[:, head] * SCALE, table[...])
    normed = k_raw[:, head] * inverse_of(sums, 1)
    scaled = grad_y * gain_k
    k_scaled[:, head] = scaled
    k_dots = jnp.sum(scaled * normed, axis=-1, keepdims=True)
    dots[...] += lanes(jnp.zeros_like(k_dots), k_dots)
    gains_out[0:1, head] = gain_sum
    gains_out[1:2, head] = jnp.sum(grad_y * normed, axis=0, keepdims=True)
    dv_out[:, head] = dv_ref[...].astype(BF16)


def branch_back_kernel(
    fsdp, sp, x_ref, p_ref, wo_ref, q_ref, k_ref, v_ref, sums, q_raw, k_raw, gain, table,
    all_ref, out_ref, q_scaled, k_scaled, dv_out, dots, gains_out,
    g_all, dv_ref, xsend, xrecv, own_sem, all_sem, *scratch,
):
    f, s = lax.axis_index("fsdp"), lax.axis_index("sp")
    lines = fsdp // 2
    barrier = pltpu.get_barrier_semaphore()
    sums_over = PlaneSum(scratch[:4], f, s, sp)
    expected = greet_line(barrier, lines, f, s) + sums_over.greet(barrier)
    plane = plane_gather_of(x_ref, g_all, f, s, sp, xsend, xrecv)
    own = pltpu.make_async_copy(x_ref, plane.at(s, 0, x_ref.shape[0]), own_sem)
    own.start()
    pl.semaphore_wait(barrier, expected)
    plane.start()
    line = LineReduce(p_ref, scratch[4:], lines, f, s)
    line.start()
    dots[...] = jnp.zeros_like(dots)
    out_all = pltpu.make_async_copy(g_all, all_ref, all_sem)
    def back_of(place):
        at = pl.ds(pl.multiple_of(place * TOK_DEV, TOK_DEV), TOK_DEV)
        dv_out[at, :] = dot_nt(g_all[at, :], wo_ref[...]).astype(BF16)

    early = (0, 1, 2) if sp == 4 else (0,)
    for t in range(lines - 1):
        line.step(t)
        if t == min(1, lines - 2):
            plane.forward()
            own.wait()
            for k in early:
                back_of(s ^ k)
    plane.finish()
    out_all.start()
    for k in range(len(early), sp):
        back_of(s ^ k)
    for h in range(q_ref.shape[1] // HEAD_DIM):
        attend_back_head(
            h, q_ref, k_ref, v_ref, sums, q_raw, k_raw, gain, table,
            q_scaled, k_scaled, dv_out, dots, gains_out, dv_ref,
        )
    sums_over.start(dots)
    line.finish(out_ref)
    sums_over.finish(dots)
    out_all.wait()


def branch_back(fsdp, sp, x, partial, wo, q, k, v, sums, q_raw, k_raw, gains, table):
    block = partial.shape[1:]
    seq, width = q.shape
    dma = pltpu.SemaphoreType.DMA
    return pl.pallas_call(
        functools.partial(branch_back_kernel, fsdp, sp),
        out_shape=(
            jax.ShapeDtypeStruct((seq, D), BF16),
            jax.ShapeDtypeStruct(block, F32),
            jax.ShapeDtypeStruct((seq, width), F32),
            jax.ShapeDtypeStruct((seq, width), F32),
            jax.ShapeDtypeStruct((seq, width), BF16),
            jax.ShapeDtypeStruct((seq, 128), F32),
            jax.ShapeDtypeStruct((2, width), F32),
        ),
        in_specs=[VMEM, ANY] + [VMEM] * 9,
        out_specs=[ANY] + [VMEM] * 6,
        scratch_shapes=[
            pltpu.VMEM((seq, D), BF16), pltpu.VMEM((seq, HEAD_DIM), F32), dma((sp,)), dma((sp,)), dma, dma,
        ]
        + PlaneSum.scratch(seq, sp)
        + LineReduce.scratch(fsdp, block),
        compiler_params=comm_params(5),
        name="branch_back",
    )(x, partial, wo, q, k, v, sums, q_raw, k_raw, gains, table)


def held(shape):
    return pl.BlockSpec(
        shape, lambda *_: (0,) * len(shape), pipeline_mode=pl.Buffered(buffer_count=1)
    )


def weight_kernel(
    q_scaled, k_scaled, q_raw, k_raw, squares, dots, dv_ref, first, attended, g_ref, out, low, square
):
    f = pl.program_id(0)
    height = first.shape[1]
    rows = out.shape[1] - 3 * height
    cols = out.shape[2]
    sp = D // cols

    @pl.when(f == 0)
    def _():
        for n, scaled, raw in ((0, q_scaled, q_raw), (1, k_scaled, k_raw)):
            inverse = inverse_of(squares, n)
            mean = dots[:, n : n + 1] / D
            low[:, n * cols : (n + 1) * cols] = (
                inverse * (scaled[...] - raw[...] * (inverse * mean))
            ).astype(BF16)
        low[:, 2 * cols :] = dv_ref[...]
        for c in range(sp):
            at = slice(c * cols, (c + 1) * cols)
            square[:, at] = dot_tn(attended[...], g_ref[:, at]).astype(BF16)

    grads = dot_tn(first[...], low[...]).astype(BF16)
    for n in range(3):
        out[0, n * height : (n + 1) * height, :] = grads[:, n * cols : (n + 1) * cols]
    each = rows // sp
    from_rows = pl.ds(pl.multiple_of(f * each, each), each)
    for c in range(sp):
        at = 3 * height + c * each
        out[0, at : at + each, :] = square[from_rows, c * cols : (c + 1) * cols]


def weight_parts(fsdp, q_scaled, k_scaled, q_raw, k_raw, squares, dots, dv, first, attended, g):
    seq, cols = dv.shape
    height = D // fsdp
    each = cols // fsdp
    return pl.pallas_call(
        weight_kernel,
        grid=(fsdp,),
        out_shape=(
            jax.ShapeDtypeStruct((fsdp, 3 * height + D // cols * each, cols), BF16),
            jax.ShapeDtypeStruct((seq, 3 * cols), BF16),
        ),
        in_specs=[held((seq, cols))] * 4
        + [held((seq, 128))] * 2
        + [
            held((seq, cols)),
            pl.BlockSpec((seq, height), lambda f: (0, f)),
            held((seq, cols)),
            held((seq, D)),
        ],
        out_specs=[
            pl.BlockSpec((1, 3 * height + D // cols * each, cols), lambda f: (f, 0, 0)),
            whole((seq, 3 * cols)),
        ],
        scratch_shapes=[pltpu.VMEM((cols, D), BF16)],
        compiler_params=pltpu.CompilerParams(vmem_limit_bytes=VLIM),
        name="weight_parts",
    )(q_scaled, k_scaled, q_raw, k_raw, squares, dots, dv, first, attended, g)


def two_parts(x, axis):
    high = x.astype(BF16)
    return jnp.concatenate([high, (x - high.astype(F32)).astype(BF16)], axis=axis)


def blocks_of(shape):
    return pl.BlockSpec((1,) + shape, lambda b: (b,) + (0,) * len(shape))


def slots_of(slots, width):
    return pl.BlockSpec((EXP_DEV, slots, width), lambda b: (0, b, 0))


def route_kernel(picks, rows_in, router, columns, out, probs_out, gates_out):
    slots = out.shape[1]
    for n in range(D // 512):
        at = pl.ds(n * 512, 512)
        got = dot_nn(picks[0], rows_in[0, :, at]).astype(BF16)
        for e in range(EXP_DEV):
            out[e, :, at] = got[e * slots : (e + 1) * slots]
    logits = dot_nt(rows_in[0], router[...])
    exp_logits = jnp.exp(logits - jnp.max(logits, axis=1, keepdims=True))
    probs = exp_logits / jnp.sum(exp_logits, axis=1, keepdims=True)
    probs_out[0] = probs
    both = two_parts(probs, 1)
    for e in range(EXP_DEV):
        moved = dot_nn(picks[0, e * slots : (e + 1) * slots, :], both)
        mask = columns[e : e + 1, :]
        gates_out[e] = jnp.sum(moved * jnp.concatenate([mask, mask], axis=1), axis=1, keepdims=True)


def route(picks, tokens, router_t, columns):
    blocks = tokens.shape[0]
    slots = picks.shape[1] // EXP_DEV
    total = blocks * slots
    experts = router_t.shape[0]
    return pl.pallas_call(
        route_kernel,
        grid=(blocks,),
        out_shape=(
            jax.ShapeDtypeStruct((EXP_DEV, total, D), BF16),
            jax.ShapeDtypeStruct((blocks, TOK_DEV, experts), F32),
            jax.ShapeDtypeStruct((EXP_DEV, total, 1), F32),
        ),
        in_specs=[
            blocks_of(picks.shape[1:]), blocks_of((TOK_DEV, D)), whole(router_t.shape),
            whole(columns.shape),
        ],
        out_specs=[slots_of(slots, D), blocks_of((TOK_DEV, experts)), slots_of(slots, 1)],
        compiler_params=pltpu.CompilerParams(vmem_limit_bytes=VLIM),
        name="route",
    )(picks, tokens, router_t, columns)


FT = 256


def active_tile(x_ref, g_ref, up, u_ref, gates, gated, grad_gate, grad_up, dots):
    total = x_ref.shape[1]
    chunk = total // 4
    for first in range(0, total, chunk):
        at = slice(first, first + chunk)
        gate_pre = dot_nn(x_ref[0, at, :], g_ref[0])
        up_pre = dot_nn(x_ref[0, at, :], up)
        sig = jax.nn.sigmoid(gate_pre)
        silu = gate_pre * sig
        hidden = silu * up_pre
        back = u_ref[0, at, :]
        gate = gates[0, at, :]
        dots[0, at, :] += jnp.sum(hidden * back, axis=1, keepdims=True)
        gated[0, at, :] = (hidden * gate).astype(BF16)
        back = back * gate
        grad_gate[0, at, :] = (back * up_pre * (sig * (1.0 + gate_pre * (1.0 - sig)))).astype(BF16)
        grad_up[0, at, :] = (back * silu).astype(BF16)


def active_kernel(x_ref, g_ref, first_ref, second_ref, u_ref, gates, gated, grad_gate, grad_up, dots):
    rest = (u_ref, gates, gated, grad_gate, grad_up, dots)

    @pl.when(pl.program_id(1) == 0)
    def _():
        dots[...] = jnp.zeros_like(dots)
        active_tile(x_ref, g_ref, first_ref[0], *rest)

    @pl.when(pl.program_id(1) == 1)
    def _():
        active_tile(x_ref, g_ref, second_ref[...].reshape(first_ref.shape[1:]), *rest)


def active(x, w_gate, up_first, up_second, u, gates):
    _, total, _ = x.shape
    wide = up_first.shape[2]
    sp, _, height, _ = up_second.shape
    tile = pl.BlockSpec((1, total, wide), lambda e, j: (e, 0, j))
    column = pl.BlockSpec((1, total, 1), lambda e, j: (e, 0, 0))
    low = jax.ShapeDtypeStruct((EXP_DEV, total, 2 * wide), BF16)
    return pl.pallas_call(
        active_kernel,
        grid=(EXP_DEV, 2),
        out_shape=(low, low, low, jax.ShapeDtypeStruct((EXP_DEV, total, 1), F32)),
        in_specs=[
            pl.BlockSpec((1, total, D), lambda e, j: (e, 0, 0)),
            pl.BlockSpec((1, D, wide), lambda e, j: (e, 0, j)),
            pl.BlockSpec((1, D, wide), lambda e, j: (e, 0, 0)),
            pl.BlockSpec((sp, 1, height, wide), lambda e, j: (0, e, 0, 0)),
            tile,
            column,
        ],
        out_specs=[tile, tile, tile, column],
        compiler_params=pltpu.CompilerParams(vmem_limit_bytes=VLIM),
        name="active",
    )(x, w_gate, up_first, up_second, u, gates)


def weight_grad_kernel(a_ref, b_ref, out):
    out[0] = dot_tn(a_ref[0], b_ref[0]).astype(BF16)


def weight_grad(a, b, name):
    _, total, height = a.shape
    width = b.shape[2]
    size = 1024
    return pl.pallas_call(
        weight_grad_kernel,
        grid=(EXP_DEV, height // size, width // size),
        out_shape=jax.ShapeDtypeStruct((EXP_DEV, height, width), BF16),
        in_specs=[
            pl.BlockSpec((1, total, size), lambda e, i, j: (e, 0, i)),
            pl.BlockSpec((1, total, size), lambda e, i, j: (e, 0, j)),
        ],
        out_specs=pl.BlockSpec((1, size, size), lambda e, i, j: (e, i, j)),
        compiler_params=pltpu.CompilerParams(vmem_limit_bytes=VLIM),
        name=name,
    )(a, b)


def rows_back_kernel(a_ref, b_ref, g_ref, first_ref, second_ref, out):
    wide = first_ref.shape[2]
    total = dot_nt(a_ref[0], g_ref[0]) + dot_nt(b_ref[0, :, :wide], first_ref[0])
    second = second_ref[...].reshape(first_ref.shape[1:])
    out[0] = (total + dot_nt(b_ref[0, :, wide:], second)).astype(BF16)


def rows_back(grad_gate_pre, grad_up_pre, w_gate, up_first, up_second):
    _, total, ff = grad_up_pre.shape
    size = 512
    wide = up_first.shape[2]
    height = up_second.shape[2]
    row = pl.BlockSpec((1, total, ff), lambda e, j: (e, 0, 0))
    return pl.pallas_call(
        rows_back_kernel,
        grid=(EXP_DEV, D // size),
        out_shape=jax.ShapeDtypeStruct((EXP_DEV, total, D), BF16),
        in_specs=[
            row,
            row,
            pl.BlockSpec((1, size, ff), lambda e, j: (e, j, 0)),
            pl.BlockSpec((1, size, wide), lambda e, j: (e, j, 0)),
            pl.BlockSpec((size // height, 1, height, wide), lambda e, j: (j, e, 0, 0)),
        ],
        out_specs=pl.BlockSpec((1, total, size), lambda e, j: (e, 0, j)),
        compiler_params=pltpu.CompilerParams(vmem_limit_bytes=VLIM),
        name="rows_back",
    )(grad_gate_pre, grad_up_pre, w_gate, up_first, up_second)


def combine_kernel(turned, rows_ref, tokens, probs, dots, router, columns, out, router_out):
    @pl.when(pl.program_id(0) == 0)
    def _():
        router_out[...] = jnp.zeros_like(router_out)

    choice = jnp.zeros(probs.shape[1:], F32)
    for e in range(EXP_DEV):
        moved = dot_nn(turned[0, e], dots[e])
        choice += jnp.sum(moved, axis=1, keepdims=True) * columns[e : e + 1, :]
    p = probs[0]
    grad_logits = p * (choice - jnp.sum(p * choice, axis=1, keepdims=True))
    both = two_parts(grad_logits, 1)
    for n in range(D // 512):
        at = pl.ds(n * 512, 512)
        total = dot_nn(both, router[:, at])
        for e in range(EXP_DEV):
            total += dot_nn(turned[0, e], rows_ref[e, :, at])
        out[0, :, at] = total.astype(BF16)
    router_out[...] += dot_tn(both, tokens[0])


def combine(turned, grad_rows, tokens, probs, dots, router_two, columns):
    blocks = tokens.shape[0]
    slots = turned.shape[3]
    return pl.pallas_call(
        combine_kernel,
        grid=(blocks,),
        out_shape=(
            jax.ShapeDtypeStruct((blocks, TOK_DEV, D), BF16),
            jax.ShapeDtypeStruct((router_two.shape[0], D), F32),
        ),
        in_specs=[
            blocks_of(turned.shape[1:]), slots_of(slots, D), blocks_of((TOK_DEV, D)),
            blocks_of(probs.shape[1:]), slots_of(slots, 128), whole(router_two.shape),
            whole(columns.shape),
        ],
        out_specs=[blocks_of((TOK_DEV, D)), whole((router_two.shape[0], D))],
        compiler_params=pltpu.CompilerParams(vmem_limit_bytes=VLIM),
        name="combine",
    )(turned, grad_rows, tokens, probs, dots, router_two, columns)


def widen_kernel(mid, total, *refs):
    *refs, layer_out = refs
    layer_out[...] = (mid[...] + total[...]).astype(BF16)
    count = len(refs) // 2
    for low, out in zip(refs[:count], refs[count:]):
        if len(low.shape) == 2:
            out[...] = low[...].astype(F32)
            continue
        sp, _, cols = low.shape
        for s in range(sp):
            for g in range(cols // HEAD_DIM):
                head = g * sp + s
                out[:, head * HEAD_DIM : (head + 1) * HEAD_DIM] = low[
                    s, :, g * HEAD_DIM : (g + 1) * HEAD_DIM
                ].astype(F32)


def widen(mid, total, by_heads, arrays):
    steps = 4
    flat = [x.reshape(-1, x.shape[-1]) for x in arrays]

    def rows_of(shape, axis):
        tall = shape[axis] // steps if shape[axis] % (16 * steps) == 0 else shape[axis]
        block = shape[:axis] + (tall,) + shape[axis + 1 :]
        moving = tall != shape[axis]
        return pl.BlockSpec(
            block, lambda i: tuple(i if moving and n == axis else 0 for n in range(len(shape)))
        )

    heads_out = [(x.shape[1], x.shape[0] * x.shape[2]) for x in by_heads]
    wide = pl.pallas_call(
        widen_kernel,
        grid=(steps,),
        out_shape=tuple(
            jax.ShapeDtypeStruct(shape, F32) for shape in heads_out + [x.shape for x in flat]
        )
        + (jax.ShapeDtypeStruct(mid.shape, BF16),),
        in_specs=[rows_of(mid.shape, 0)] * 2
        + [rows_of(x.shape, 1) for x in by_heads]
        + [rows_of(x.shape, 0) for x in flat],
        out_specs=[rows_of(shape, 0) for shape in heads_out + [x.shape for x in flat] + [mid.shape]],
        compiler_params=pltpu.CompilerParams(vmem_limit_bytes=VLIM),
        name="widen",
    )(mid, total, *by_heads, *flat)
    split = len(by_heads)
    shaped = [x.reshape(like.shape) for x, like in zip(wide[split:-1], arrays)]
    return list(wide[:split]) + shaped + [wide[-1]]


def angles(seq):
    freqs = np.float32(ROPE_BASE) ** (-2.0 * np.arange(HEAD_DIM // 2, dtype=np.float32) / HEAD_DIM)
    turned = np.arange(seq, dtype=np.float32)[:, None] * freqs[None, :].astype(np.float32)
    return jnp.asarray(np.concatenate([np.cos(turned), np.sin(turned)], axis=1), F32)


def body(
    layer_input, output_grad, w_query, w_key, w_value, w_output, w_router, norm_gains,
    w_gate, w_up, w_down, expert_routes,
):
    fsdp, sp = lax.axis_size("fsdp"), lax.axis_size("sp")
    f, s = lax.axis_index("fsdp"), lax.axis_index("sp")
    count = fsdp * sp
    experts = EXP_DEV * fsdp
    capacity = TOK_DEV * TOP // experts * 17 // 16
    slots = -(-capacity // 16) * 16
    seq = TOK_DEV * sp
    cols = D // sp
    rows = D // count

    down_full = lax.all_gather(w_down, "sp", axis=1, tiled=True)
    gate_full = lax.all_gather(w_gate, "sp", axis=1, tiled=True)
    wide = w_up.shape[2] // 2
    up_first = lax.all_gather(w_up[:, :, :wide], "sp", axis=1, tiled=True)

    router_size = rows * experts
    misc = jnp.concatenate([w_router.reshape(router_size), norm_gains.reshape(4 * rows)])
    misc_rows = -(-misc.shape[0] // 2048) * 16
    misc = jnp.pad(misc, (0, misc_rows * 128 - misc.shape[0])).reshape(misc_rows, 128)
    routes = expert_routes.reshape(TOK_DEV * TOP // 128, 128)
    early = TOK_DEV // 8
    x_all, w_all, wo_s, grad_first_half, misc_all, routes_all = gather_start(
        fsdp, sp, layer_input, jnp.stack([w_query, w_key, w_value]), w_output, output_grad[:early],
        misc, routes,
    )
    misc_all = misc_all.reshape(count, misc_rows * 128)
    router_w = misc_all[:, :router_size].reshape(D, experts)
    router_t = router_w.T
    gains_w = misc_all[:, router_size : router_size + 4 * rows].reshape(count, 4, rows)
    gains32 = gains_w.transpose(1, 0, 2).reshape(4, D).astype(F32)
    by_head = gains32.reshape(4, cols // HEAD_DIM, sp, HEAD_DIM)
    gains_own = lax.dynamic_index_in_dim(by_head, s, axis=2, keepdims=False).reshape(4, cols)

    routes_block = routes_all.reshape(fsdp, TOK_DEV, TOP)
    own_ids = f * EXP_DEV + jnp.arange(EXP_DEV, dtype=jnp.int32)
    chosen = jnp.any(routes_block[:, :, :, None] == own_ids, axis=2)
    before = jnp.arange(TOK_DEV)[:, None] > jnp.arange(TOK_DEV)[None, :]
    place = jnp.einsum(
        "ut,fte->feu", before.astype(BF16), chosen.astype(BF16), preferred_element_type=F32
    ).astype(jnp.int32)
    slot_ids = jnp.arange(slots, dtype=jnp.int32)
    picks = (
        (place[:, :, None, :] == slot_ids[:, None]) & chosen.transpose(0, 2, 1)[:, :, None, :]
    ).astype(BF16).reshape(fsdp, EXP_DEV * slots, TOK_DEV)
    turned = (
        (place[:, :, :, None] == slot_ids) & chosen.transpose(0, 2, 1)[:, :, :, None]
    ).astype(BF16)
    columns = (jnp.arange(experts, dtype=jnp.int32)[None, :] == own_ids[:, None]).astype(F32)

    first_in, q_raw, k_raw, values, squares = project(sp, x_all, gains32, w_all)
    table = angles(seq)
    attended, sums, queries, keys = attend(
        q_raw, k_raw, values, squares, gains_own, table
    )
    mid, second_in, grad_second_half = branch_sum(
        fsdp, attended, wo_s, output_grad[early:], layer_input, gains32
    )

    tokens, grad_taken, unscaled, up_second = token_gather(
        fsdp, sp, second_in, grad_first_half, grad_second_half, picks, down_full,
        w_up[:, :, wide:].reshape(-1, wide),
    )
    up_second = up_second.reshape(sp, EXP_DEV, D // sp, wide)
    received, probs, slot_gates = route(picks, tokens, router_t, columns)
    gated, grad_gate_pre, grad_up_pre, slot_dots = active(
        received, gate_full, up_first, up_second, unscaled, slot_gates
    )
    dots_two = jnp.pad(two_parts(slot_dots, 2), ((0, 0), (0, 0), (0, 126)))
    grad_rows = rows_back(grad_gate_pre, grad_up_pre, gate_full, up_first, up_second)
    second_part, router_two = combine(
        turned, grad_rows, tokens, probs, dots_two, jnp.concatenate([router_t, router_t], axis=0),
        columns,
    )
    grad_router = (router_two[:experts] + router_two[experts:]).T

    def shed(grad):
        return lax.psum_scatter(grad, "sp", scatter_dimension=1, tiled=True)

    grad_down = shed(weight_grad(gated, grad_taken, "down_grad"))
    grad_gate = shed(weight_grad(received, grad_gate_pre, "gate_grad"))
    grad_mid, grad_mid_low, gain_rows, out_part, up_part = token_back(
        fsdp, second_part, gated, down_full, turned, received, grad_up_pre, mid, output_grad, gains32
    )
    grad_up = shed(up_part)

    grad_branch, out_sum, q_scaled, k_scaled, grad_values, dots, gain_qk = branch_back(
        fsdp, sp, grad_mid_low, out_part, wo_s, queries, keys, values, sums, q_raw, k_raw,
        gains_own, table,
    )
    weight_part, grads_low = weight_parts(
        fsdp, q_scaled, k_scaled, q_raw, k_raw, squares, dots, grad_values, first_in, attended, grad_branch
    )

    gain_rows = lax.dynamic_update_slice(
        gain_rows.reshape(8, cols // HEAD_DIM, sp, HEAD_DIM),
        gain_qk.reshape(2, cols // HEAD_DIM, 1, HEAD_DIM),
        (2, 0, s, 0),
    ).reshape(8, D)
    router_part = grad_router.reshape(count, router_size)
    router_part = jnp.pad(router_part, ((0, 0), (0, 1024 - router_size))).reshape(count, 8, 128)
    input_grad, *weight_grads, small = end_exchange(
        fsdp, sp, weight_part, grads_low, w_all, layer_input, grad_mid, gains32, gain_rows, router_part, 8
    )
    *weight_grads, grad_gate, grad_up, grad_down, layer_out = widen(
        mid, out_sum, weight_grads[:3], [weight_grads[3], grad_gate, grad_up, grad_down]
    )
    grad_router_own = small[:8].reshape(1024)[:router_size].reshape(rows, experts)
    first_lane = (f * sp + s) * rows % 128
    grad_gains = lax.dynamic_slice(small[8:12], (0, first_lane), (4, rows))
    return (
        layer_out, input_grad, *weight_grads,
        grad_router_own, grad_gains, grad_gate, grad_up, grad_down,
    )


def solution(mesh):
    both, split = P(("fsdp", "sp"), None), P("fsdp", "sp", None)
    gains = P(None, ("fsdp", "sp"))
    return jax.shard_map(
        body,
        mesh=mesh,
        in_specs=(both,) * 7 + (gains,) + (split,) * 3 + (both,),
        out_specs=(both,) * 7 + (gains,) + (split,) * 3,
        check_vma=False,
    )
```

```python
import functools

import jax
import jax.numpy as jnp
import numpy as np
from jax import lax
from jax.experimental import pallas as pl
from jax.experimental.pallas import tpu as pltpu
from jax.sharding import PartitionSpec as P

D = 2048
HEADS = 16
HEAD_DIM = 128
TOP = 8
EXP_DEV = 2
BLK = 256
TOK_DEV = 256
EPSILON = 1e-05
ROPE_BASE = 10000.0
MASKED = -1000000000.0
SCALE = HEAD_DIM ** (-0.5)
MESH = pl.DeviceIdType.MESH
ANY = pl.BlockSpec(memory_space=pl.ANY)
VMEM = pl.BlockSpec(memory_space=pltpu.VMEM)
VLIM = 60 * 1024 * 1024
F32 = jnp.float32
BF16 = jnp.bfloat16


def remote(src, dst, send_sem, recv_sem, device):
    return pltpu.make_async_remote_copy(
        src_ref=src,
        dst_ref=dst,
        send_sem=send_sem,
        recv_sem=recv_sem,
        device_id=device,
        device_id_type=MESH,
    )


def landed(ref, sem):
    pltpu.make_async_copy(ref, ref, sem).wait()


def signal(sem, device):
    pl.semaphore_signal(sem, inc=1, device_id=device, device_id_type=MESH)


def greet_line(barrier, lines, f, s):
    place, core = f // 2, f % 2
    signal(barrier, (f + 1 - 2 * core, s))

    @pl.when(place > 0)
    def _():
        signal(barrier, (f - 2, s))

    @pl.when(place < lines - 1)
    def _():
        signal(barrier, (f + 2, s))

    return 1 + jnp.where(place > 0, 1, 0) + jnp.where(place < lines - 1, 1, 0)


class LineGather:
    def __init__(self, views, owns, lines, f, s, send, recv):
        self.views, self.owns, self.lines, self.f, self.s = views, owns, lines, f, s
        self.send, self.recv = send, recv
        self.place, self.core = f // 2, f % 2

    def copy(self, v, block, slot, way):
        device = {
            "right": (self.f + 2, self.s),
            "left": (self.f - 2, self.s),
            "partner": (self.f + 1 - 2 * self.core, self.s),
        }[way]
        index = {"right": 0, "left": 1, "partner": 2}[way]
        ref = self.views[v](block)
        own = self.owns[v] if slot == 0 and self.owns[v] is not None else ref
        return remote(own, ref, self.send.at[v, slot, index], self.recv.at[v, block], device)

    def start_own(self, v):
        @pl.when(self.place < self.lines - 1)
        def _():
            self.copy(v, self.f, 0, "right").start()

        @pl.when(self.place > 0)
        def _():
            self.copy(v, self.f, 0, "left").start()

        self.copy(v, self.f, 0, "partner").start()

    def forward(self, v, k):
        place, lines = self.place, self.lines

        @pl.when(place >= k)
        def _():
            block = self.f - 2 * k
            landed(self.views[v](block), self.recv.at[v, block])

            @pl.when(place < lines - 1)
            def _():
                self.copy(v, block, k, "right").start()

            self.copy(v, block, k, "partner").start()

        @pl.when(place + k < lines)
        def _():
            block = self.f + 2 * k
            landed(self.views[v](block), self.recv.at[v, block])

            @pl.when(place > 0)
            def _():
                self.copy(v, block, lines - 1 + k, "left").start()

            self.copy(v, block, lines - 1 + k, "partner").start()

    def finish(self, v):
        place, lines = self.place, self.lines
        for line in range(lines):
            block = 2 * line + 1 - self.core
            landed(self.views[v](block), self.recv.at[v, block])
        self.copy(v, self.f, 0, "partner").wait_send()

        @pl.when(place < lines - 1)
        def _():
            self.copy(v, self.f, 0, "right").wait_send()

        @pl.when(place > 0)
        def _():
            self.copy(v, self.f, 0, "left").wait_send()

        for k in range(1, lines):

            @pl.when(place >= k)
            def _():
                block = self.f - 2 * k

                @pl.when(place < lines - 1)
                def _():
                    self.copy(v, block, k, "right").wait_send()

                self.copy(v, block, k, "partner").wait_send()

            @pl.when(place + k < lines)
            def _():
                block = self.f + 2 * k

                @pl.when(place > 0)
                def _():
                    self.copy(v, block, lines - 1 + k, "left").wait_send()

                self.copy(v, block, lines - 1 + k, "partner").wait_send()


def line_sems(arrays, fsdp):
    lines = fsdp // 2
    return [
        pltpu.SemaphoreType.DMA((arrays, 2 * lines, 3)),
        pltpu.SemaphoreType.DMA((arrays, fsdp)),
    ]


def add_rows(dst, a, b, rows):
    def step(i, carry):
        at = pl.ds(pl.multiple_of(i * 32, 32), 32)
        dst[at, :] = a[at, :].astype(dst.dtype) + b[at, :].astype(dst.dtype)
        return carry

    lax.fori_loop(0, rows // 32, step, 0)


class LineReduce:
    def __init__(self, p_ref, scratch, lines, f, s):
        self.p_ref, self.lines, self.f, self.s = p_ref, lines, f, s
        self.own, self.paired, self.got, self.last = scratch[:4]
        self.psend, self.precv, self.send, self.recv, self.final, self.local = scratch[4:]
        self.place, self.core = f // 2, f % 2
        self.rows = p_ref.shape[1]
        self.order = []
        for n in range(lines):
            for d in (lines - 1 - n, n):
                if d not in self.order:
                    self.order.append(d)

    @staticmethod
    def scratch(fsdp, block):
        lines = fsdp // 2
        dma = pltpu.SemaphoreType.DMA
        return [
            pltpu.VMEM((lines,) + block, BF16),
            pltpu.VMEM((lines,) + block, BF16),
            pltpu.VMEM((lines,) + block, BF16),
            pltpu.VMEM(block, BF16),
            dma((lines,)), dma((lines,)), dma((lines, 2)), dma((lines, 2)), dma((2,)), dma((lines,)),
        ]

    def load(self, i):
        return pltpu.make_async_copy(self.p_ref.at[2 * i + self.core], self.own.at[i], self.local.at[i])

    def swap(self, i):
        return remote(
            self.p_ref.at[2 * i + 1 - self.core], self.paired.at[i], self.psend.at[i],
            self.precv.at[i], (self.f + 1 - 2 * self.core, self.s),
        )

    def half(self, ref, h):
        return ref.at[pl.ds(h * (self.rows // 2), self.rows // 2), :]

    def right(self, d, last, h):
        dst = self.last if last else self.got.at[d]
        sem = self.final.at[h] if last else self.recv.at[d, h]
        own = self.half(self.own.at[d], h)
        return remote(own, self.half(dst, h), self.send.at[d, h], sem, (self.f + 2, self.s))

    def left(self, d, h):
        own, dst = self.half(self.own.at[d], h), self.half(self.got.at[d], h)
        return remote(own, dst, self.send.at[d, h], self.recv.at[d, h], (self.f - 2, self.s))

    def add_got(self, d, h):
        own, got = self.half(self.own.at[d], h), self.half(self.got.at[d], h)
        landed(got, self.recv.at[d, h])
        add_rows(own, own, got, self.rows // 2)

    def start(self):
        for i in self.order[:2]:
            self.swap(i).start()
        for i in self.order:
            self.load(i).start()
        self.added = 0
        self.add_pairs(2)

    def add_pairs(self, until):
        for i in self.order[self.added : until]:
            self.load(i).wait()
            landed(self.paired.at[i], self.precv.at[i])
            add_rows(self.own.at[i], self.own.at[i], self.paired.at[i], self.rows)
        self.added = max(self.added, until)

    def step(self, t):
        place, lines = self.place, self.lines
        d = lines - 1 - t + place
        e = t - (lines - 1 - place)
        for h in range(2):

            @pl.when(t >= place)
            def _():
                @pl.when(place > 0)
                def _():
                    self.add_got(d, h)

                @pl.when(d == place + 1)
                def _():
                    self.right(d, True, h).start()

                @pl.when(d != place + 1)
                def _():
                    self.right(d, False, h).start()

            @pl.when(e >= 0)
            def _():
                @pl.when(place < lines - 1)
                def _():
                    self.add_got(e, h)

                self.left(e, h).start()

        if t == 0:
            for i in self.order[2:]:
                self.swap(i).start()
        self.add_pairs(2 * t + 4)

    def finish(self, out_ref):
        place, lines, rows = self.place, self.lines, self.rows

        def total(*extra):
            def step(i, carry):
                at = pl.ds(pl.multiple_of(i * 32, 32), 32)
                value = self.own[place, at, :].astype(F32)
                for ref in extra:
                    value += ref[at, :].astype(F32)
                out_ref[at, :] = value.astype(out_ref.dtype)
                return carry

            lax.fori_loop(0, rows // 32, step, 0)

        @pl.when(place > 0)
        def _():
            for h in range(2):
                landed(self.half(self.last, h), self.final.at[h])

        @pl.when(place < lines - 1)
        def _():
            for h in range(2):
                landed(self.half(self.got.at[place], h), self.recv.at[place, h])

        @pl.when(place == 0)
        def _():
            total(self.got.at[place])

        @pl.when(place == lines - 1)
        def _():
            total(self.last)

        @pl.when(jnp.logical_and(place > 0, place < lines - 1))
        def _():
            total(self.last, self.got.at[place])

        for i in range(lines):
            self.swap(i).wait_send()

            @pl.when(place < i)
            def _():
                for h in range(2):
                    self.right(i, False, h).wait_send()

            @pl.when(place > i)
            def _():
                for h in range(2):
                    self.left(i, h).wait_send()


class PlaneGather:
    def __init__(self, own, out, f, s, send, recv):
        self.own, self.out, self.f, self.s, self.send, self.recv = own, out, f, s, send, recv
        self.rows = own.shape[0]
        self.half = self.rows // 2

    def at(self, place, first, size):
        return self.out.at[pl.ds(pl.multiple_of(place * self.rows + first, self.half), size), :]

    def near(self, k):
        return remote(
            self.own, self.at(self.s, 0, self.rows), self.send.at[k - 1], self.recv.at[k - 1],
            (self.f, self.s ^ k),
        )

    def on(self, k):
        ref = self.at(self.s ^ k, (k - 1) * self.half, self.half)
        return remote(ref, ref, self.send.at[k + 1], self.recv.at[k + 1], (self.f, self.s ^ (3 - k)))

    def start(self):
        self.near(1).start()
        self.near(2).start()

    def forward(self):
        for k in (1, 2):
            landed(self.at(self.s ^ k, 0, self.rows), self.recv.at[k - 1])
            self.on(k).start()

    def finish(self):
        landed(self.at(self.s ^ 3, 0, self.half), self.recv.at[2])
        landed(self.at(self.s ^ 3, self.half, self.half), self.recv.at[3])
        for k in (1, 2):
            self.near(k).wait_send()
            self.on(k).wait_send()


class AnyGather:
    def __init__(self, own, out, f, s, sp, send, recv):
        self.own, self.out, self.f, self.s, self.sp = own, out, f, s, sp
        self.send, self.recv = send, recv
        self.rows = own.shape[0]

    def at(self, place, first, size):
        return self.out.at[pl.ds(pl.multiple_of(place * self.rows + first, size), size), :]

    def copy(self, k):
        dst = self.at(self.s, 0, self.rows)
        return remote(self.own, dst, self.send.at[k], self.recv.at[k], (self.f, self.s ^ k))

    def start(self):
        for k in range(1, self.sp):
            self.copy(k).start()

    def forward(self):
        pass

    def finish(self):
        for k in range(1, self.sp):
            landed(self.at(self.s ^ k, 0, self.rows), self.recv.at[k])
            self.copy(k).wait_send()


class AnyReduce:
    def __init__(self, p_ref, out_ref, scratch, f, s, sp):
        self.p_ref, self.out_ref, self.f, self.s, self.sp = p_ref, out_ref, f, s, sp
        self.own, self.got, self.send, self.recv, self.local = scratch

    @staticmethod
    def scratch(block, sp):
        dma = pltpu.SemaphoreType.DMA
        return [
            pltpu.VMEM(block, BF16), pltpu.VMEM((sp,) + block, BF16), dma((sp,)), dma((sp,)), dma,
        ]

    def copy(self, k):
        d = self.s ^ k
        return remote(
            self.p_ref.at[d], self.got.at[k], self.send.at[k], self.recv.at[k], (self.f, d)
        )

    def load(self):
        return pltpu.make_async_copy(self.p_ref.at[self.s], self.own, self.local)

    def start(self, make=lambda d: None):
        for k in range(self.sp - 1, 0, -1):
            make(self.s ^ k)
            self.copy(k).start()
        make(self.s)
        self.load().start()

    def forward(self):
        self.load().wait()

    def finish(self):
        rows = self.own.shape[0]
        for k in range(1, self.sp):
            landed(self.got.at[k], self.recv.at[k])
            add_rows(self.out_ref, self.own if k == 1 else self.out_ref, self.got.at[k], rows)
        for k in range(1, self.sp):
            self.copy(k).wait_send()


def plane_gather_of(own, out, f, s, sp, send, recv):
    if sp == 4:
        return PlaneGather(own, out, f, s, send, recv)
    return AnyGather(own, out, f, s, sp, send, recv)


def plane_reduce_of(p_ref, out_ref, scratch, f, s, sp):
    if sp == 4:
        return PlaneReduce(p_ref, out_ref, scratch, f, s)
    return AnyReduce(p_ref, out_ref, scratch, f, s, sp)


def plane_scratch(block, sp):
    return PlaneReduce.scratch(block) if sp == 4 else AnyReduce.scratch(block, sp)


class PlaneReduce:
    WAYS = ((0, 1, 1), (1, 2, 2))

    def __init__(self, p_ref, out_ref, scratch, f, s):
        self.p_ref, self.out_ref, self.f, self.s = p_ref, out_ref, f, s
        self.own, self.got, self.got_on, self.send, self.recv, self.local = scratch
        self.half = p_ref.shape[1] // 2

    @staticmethod
    def scratch(block):
        dma = pltpu.SemaphoreType.DMA
        return [
            pltpu.VMEM((3,) + block, BF16), pltpu.VMEM((2,) + block, BF16),
            pltpu.VMEM(block, BF16), dma((2, 3)), dma((2, 3)), dma((3,)),
        ]

    def part(self, ref, h):
        return ref.at[pl.ds(h * self.half, self.half), :]

    def load(self, n):
        d = (self.s, self.s ^ 2, self.s ^ 1)[n]
        return pltpu.make_async_copy(self.p_ref.at[d], self.own.at[n], self.local.at[n])

    def hop(self, h, k, far):
        d = self.s ^ 3 if far else self.s ^ k
        n = 0 if far else 1
        return remote(
            self.part(self.p_ref.at[d], h), self.part(self.got.at[1 - n], h), self.send.at[h, n],
            self.recv.at[h, n], (self.f, self.s ^ k),
        )

    def on(self, h, k, n):
        return remote(
            self.part(self.own.at[n], h), self.part(self.got_on, h), self.send.at[h, 2],
            self.recv.at[h, 2], (self.f, self.s ^ (3 - k)),
        )

    def start(self, make=lambda d: None):
        make(self.s ^ 3)
        for h, k, _ in self.WAYS:
            self.hop(h, k, True).start()
        make(self.s ^ 1)
        make(self.s ^ 2)
        for h, k, _ in self.WAYS:
            self.hop(h, k, False).start()
        make(self.s)
        for n in range(3):
            self.load(n).start()

    def forward(self):
        for n in range(3):
            self.load(n).wait()
        for h, k, n in self.WAYS:
            mine = self.part(self.own.at[n], h)
            landed(self.part(self.got.at[1], h), self.recv.at[h, 0])
            add_rows(mine, mine, self.part(self.got.at[1], h), self.half)
            self.on(h, k, n).start()

    def finish(self):
        for h in (0, 1):
            landed(self.part(self.got.at[0], h), self.recv.at[h, 1])
            add_rows(
                self.part(self.out_ref, h), self.part(self.own.at[0], h), self.part(self.got.at[0], h),
                self.half,
            )
        for h in (0, 1):
            landed(self.part(self.got_on, h), self.recv.at[h, 2])
            out = self.part(self.out_ref, h)
            add_rows(out, out, self.part(self.got_on, h), self.half)
        for h, k, n in self.WAYS:
            self.hop(h, k, True).wait_send()
            self.hop(h, k, False).wait_send()
            self.on(h, k, n).wait_send()


def greet_plane(barrier, f, s, sp):
    ways = (1, 2) if sp == 4 else range(1, sp)
    for k in ways:
        signal(barrier, (f, s ^ k))
    return len(ways)


def greet_all(barrier, me, count, sp):
    def greet(i, carry):
        other = lax.rem(me + i, count)
        signal(barrier, (other // sp, lax.rem(other, sp)))
        return carry

    lax.fori_loop(1, count, greet, 0)


def rows_view(ref, rows):
    return lambda b: ref.at[pl.ds(pl.multiple_of(b * rows, rows), rows), :]


def block_view(ref):
    return lambda b: ref.at[b]


def comm_params(number):
    return pltpu.CompilerParams(
        collective_id=number, has_side_effects=True, vmem_limit_bytes=VLIM
    )


def row_target(i, rows, sp):
    parts = HEAD_DIM // rows
    head, part = i // parts, lax.rem(i, parts)
    return head // sp * parts + part, lax.rem(head, sp)


def row_owner(f, s, rows, sp):
    parts = HEAD_DIM // rows
    return (f // parts * sp + s) * parts + lax.rem(f, parts)


def start_kernel(
    fsdp, sp, x_ref, w_ref, wo_ref, g_ref, misc_ref, routes_ref,
    x_all, w_all, wo_all, g_all, misc_all, routes_all,
    send, recv, xsend, xrecv, psend, precv, wsend, wrecv, msend, mrecv, rsend, rrecv, local, wlocal,
):
    f, s = lax.axis_index("fsdp"), lax.axis_index("sp")
    count, lines = fsdp * sp, fsdp // 2
    me = f * sp + s
    rows = w_ref.shape[1]
    heads = D // sp // HEAD_DIM
    barrier = pltpu.get_barrier_semaphore()

    def w_block(s_to, g):
        at = pl.multiple_of((g * sp + s_to) * HEAD_DIM, HEAD_DIM)
        return w_ref.at[:, :, pl.ds(at, HEAD_DIM)]

    def w_rows(i, g):
        at = pl.ds(pl.multiple_of(i * rows, rows), rows)
        return w_all.at[:, at, pl.ds(g * HEAD_DIM, HEAD_DIM)]

    def w_view(b):
        size = rows * sp
        return w_all.at[:, pl.ds(pl.multiple_of(b * size, size), size), :]

    wo_view = rows_view(wo_all, rows)
    x_view = rows_view(x_all, TOK_DEV)
    w_owns = [
        pltpu.make_async_copy(w_block(s, g), w_rows(me, g), wlocal.at[g]) for g in range(heads)
    ]
    owns = [
        pltpu.make_async_copy(x_ref, x_view(s), local.at[0]),
        pltpu.make_async_copy(misc_ref, misc_all.at[me], local.at[1]),
        pltpu.make_async_copy(routes_ref, routes_all.at[f], local.at[2]),
        pltpu.make_async_copy(g_ref, g_all.at[f], local.at[3]),
    ]
    for copy in w_owns + owns:
        copy.start()
    greet_all(barrier, me, count, sp)
    pl.semaphore_wait(barrier, count - 1)

    line = LineGather([w_view, wo_view, block_view(g_all)], [None, None, g_ref], lines, f, s, send, recv)
    line.start_own(2)
    w_copies = []
    for k in range(sp - 1, 0, -1):
        s_to = s ^ k
        for g in range(heads):
            copy = remote(
                w_block(s_to, g), w_rows(me, g), psend.at[k, g], precv.at[k, g], (f, s_to)
            )
            copy.start()
            w_copies.append(copy)
    target_f, target_s = row_target(me, rows, sp)
    stays = jnp.logical_and(target_s == s, target_f == f)
    wo_copy = remote(wo_ref, wo_view(target_f), wsend, wrecv, (target_f, target_s))
    wo_own = pltpu.make_async_copy(wo_ref, wo_view(f), wrecv)

    @pl.when(stays)
    def _():
        wo_own.start()

    @pl.when(jnp.logical_not(stays))
    def _():
        wo_copy.start()

    def misc_copy(i):
        other = lax.rem(me + i, count)
        return remote(
            misc_ref, misc_all.at[me], msend.at[i], mrecv.at[me], (other // sp, lax.rem(other, sp))
        )

    def misc_go(i, carry):
        misc_copy(i).start()
        return carry

    lax.fori_loop(1, count, misc_go, 0)

    def routes_copy(i):
        other = lax.rem(f + i, fsdp)
        return remote(routes_ref, routes_all.at[f], rsend.at[i], rrecv.at[f], (other, s))

    def routes_go(i, carry):
        routes_copy(i).start()
        return carry

    lax.fori_loop(1, fsdp, routes_go, 0)

    for copy in w_owns:
        copy.wait()
    for k in range(1, sp):
        for g in range(heads):
            landed(w_rows(f * sp + (s ^ k), g), precv.at[k, g])
    line.start_own(0)
    tokens = plane_gather_of(x_ref, x_all, f, s, sp, xsend, xrecv)
    tokens.start()
    landed(wo_view(f), wrecv)
    line.start_own(1)
    for k in range(1, lines):
        for v in (2, 0, 1):
            line.forward(v, k)
        if k == min(2, lines - 1):
            tokens.forward()
    for v in range(3):
        line.finish(v)
    tokens.finish()

    def misc_end(i, carry):
        misc_copy(i).wait_send()
        other = lax.rem(me + i, count)
        landed(misc_all.at[other], mrecv.at[other])
        return carry

    lax.fori_loop(1, count, misc_end, 0)

    def routes_end(i, carry):
        routes_copy(i).wait_send()
        other = lax.rem(f + i, fsdp)
        landed(routes_all.at[other], rrecv.at[other])
        return carry

    lax.fori_loop(1, fsdp, routes_end, 0)
    for copy in w_copies:
        copy.wait_send()

    @pl.when(jnp.logical_not(stays))
    def _():
        wo_copy.wait_send()

    for copy in owns:
        copy.wait()


def gather_start(fsdp, sp, x, w, wo, g, misc, routes):
    count = fsdp * sp
    heads = D // sp // HEAD_DIM
    dma = pltpu.SemaphoreType.DMA
    return pl.pallas_call(
        functools.partial(start_kernel, fsdp, sp),
        out_shape=(
            jax.ShapeDtypeStruct((sp * TOK_DEV, D), BF16),
            jax.ShapeDtypeStruct((3, D, D // sp), BF16),
            jax.ShapeDtypeStruct((D // sp, D), BF16),
            jax.ShapeDtypeStruct((fsdp,) + g.shape, BF16),
            jax.ShapeDtypeStruct((count,) + misc.shape, BF16),
            jax.ShapeDtypeStruct((fsdp,) + routes.shape, jnp.int32),
        ),
        in_specs=[VMEM] * 6,
        out_specs=[ANY] * 6,
        scratch_shapes=line_sems(3, fsdp)
        + [
            dma((sp,)), dma((sp,)), dma((sp, heads)), dma((sp, heads)), dma, dma,
            dma((count,)), dma((count,)), dma((fsdp,)), dma((fsdp,)), dma((4,)), dma((heads,)),
        ],
        compiler_params=comm_params(0),
        name="gather_start",
    )(x, w, wo, g, misc, routes)


def branch_kernel(
    fsdp, sp, a_ref, w_ref, g_ref, x_ref, gain, out_ref, second_ref, g_all, terms, *scratch
):
    f, s = lax.axis_index("fsdp"), lax.axis_index("sp")
    lines = fsdp // 2
    barrier = pltpu.get_barrier_semaphore()
    expected = greet_line(barrier, lines, f, s) + greet_plane(barrier, f, s, sp)
    send, recv, own_sem = scratch[-3:]
    own = pltpu.make_async_copy(g_ref, g_all.at[f], own_sem)
    own.start()
    pl.semaphore_wait(barrier, expected)
    plane = plane_reduce_of(terms, out_ref, scratch[:-3], f, s, sp)
    line = LineGather([block_view(g_all)], [g_ref], lines, f, s, send, recv)
    line.start_own(0)

    def branch_of(d):
        rows = pl.ds(pl.multiple_of(d * TOK_DEV, TOK_DEV), TOK_DEV)
        for n in range(D // 512):
            at = pl.ds(n * 512, 512)
            terms[d, :, at] = dot_nn(a_ref[rows, :], w_ref[:, at]).astype(BF16)

    plane.start(branch_of)
    for k in range(1, lines):
        line.forward(0, k)
        if k == min(2, lines - 1):
            plane.forward()
    plane.finish()

    def norm(i, carry):
        at = pl.ds(pl.multiple_of(i * 32, 32), 32)
        mid = x_ref[at, :].astype(F32) + out_ref[at, :]
        out_ref[at, :] = mid
        inverse = lax.rsqrt(jnp.mean(mid * mid, axis=-1, keepdims=True) + EPSILON)
        second_ref[at, :] = (mid * inverse * gain[1:2, :]).astype(BF16)
        return carry

    lax.fori_loop(0, TOK_DEV // 32, norm, 0)
    line.finish(0)
    own.wait()


def branch_sum(fsdp, attended, w, g, x, gains):
    sp, block = attended.shape[0] // TOK_DEV, x.shape
    return pl.pallas_call(
        functools.partial(branch_kernel, fsdp, sp),
        out_shape=(
            jax.ShapeDtypeStruct(block, F32),
            jax.ShapeDtypeStruct(block, BF16),
            jax.ShapeDtypeStruct((fsdp,) + g.shape, BF16),
        ),
        in_specs=[VMEM] * 5,
        out_specs=[VMEM, VMEM, ANY],
        scratch_shapes=[pltpu.VMEM((sp,) + block, BF16)]
        + plane_scratch(block, sp) + line_sems(1, fsdp) + [pltpu.SemaphoreType.DMA],
        compiler_params=comm_params(2),
        name="branch_sum",
    )(attended, w, g, x, gains)


def token_kernel(
    fsdp, sp, x_ref, g_first, g_second, picks, w_ref, up_ref, out_ref, taken_ref, back_ref, up_all,
    g_buf, w_buf, taken, back, send, recv, local, loads, stores, back_sem, usend, urecv, ulocal,
):
    f, s = lax.axis_index("fsdp"), lax.axis_index("sp")
    lines = fsdp // 2
    parts = 2
    size = TOK_DEV // parts
    early, later = g_first.shape[1], g_second.shape[1]
    slots = picks.shape[1] // EXP_DEV
    ff = w_ref.shape[1]
    barrier = pltpu.get_barrier_semaphore()
    expected = greet_line(barrier, lines, f, s) + greet_plane(barrier, f, s, sp)
    plane = plane_gather_of(up_ref, up_all, f, s, sp, usend, urecv)
    up_own = pltpu.make_async_copy(up_ref, plane.at(s, 0, up_ref.shape[0]), ulocal)
    up_own.start()
    own = pltpu.make_async_copy(x_ref, out_ref.at[f], local)
    own.start()
    reads = [
        pltpu.make_async_copy(g_first, g_buf.at[:, pl.ds(0, early), :], loads.at[0]),
        pltpu.make_async_copy(g_second, g_buf.at[:, pl.ds(early, later), :], loads.at[1]),
        pltpu.make_async_copy(w_ref, w_buf, loads.at[2]),
    ]
    for copy in reads:
        copy.start()
    pl.semaphore_wait(barrier, expected)

    def view(part):
        return lambda b: out_ref.at[b, pl.ds(part * size, size), :]

    owns = [x_ref.at[pl.ds(p * size, size), :] for p in range(parts)]
    line = LineGather([view(p) for p in range(parts)], owns, lines, f, s, send, recv)
    for p in range(parts):
        line.start_own(p)
    plane.start()

    def take_all():
        reads[0].wait()
        reads[1].wait()

        def block(b, carry):
            for n in range(D // 512):
                at = pl.ds(n * 512, 512)
                got = dot_nn(picks[b], g_buf[b, :, at]).astype(BF16)
                for e in range(EXP_DEV):
                    to = pl.ds(pl.multiple_of(b * slots, 16), slots)
                    taken[e, to, at] = got[e * slots : (e + 1) * slots]
            return carry

        lax.fori_loop(0, fsdp, block, 0)
        for e in range(EXP_DEV):
            pltpu.make_async_copy(taken.at[e], taken_ref.at[e], stores.at[e]).start()

    def back_copy(e, j, slot):
        at = pl.ds(pl.multiple_of(j * FT, FT), FT)
        return pltpu.make_async_copy(back.at[slot], back_ref.at[e, :, at], back_sem.at[slot])

    def back_of(e):
        if e == 0:
            reads[2].wait()
        for j in range(ff // FT):
            slot = j % 2
            if e > 0 or j > 1:
                back_copy(e, j, slot).wait()
            back[slot] = dot_nt(taken[e], w_buf[e, pl.ds(j * FT, FT), :])
            back_copy(e, j, slot).start()

    work = [take_all] + [functools.partial(back_of, e) for e in range(EXP_DEV)]
    for k in range(1, lines):
        if k - 1 < len(work):
            work[k - 1]()
        for p in range(parts):
            line.forward(p, k)
        if k == min(2, lines - 1):
            plane.forward()
    for unit in work[lines - 1 :]:
        unit()
    for p in range(parts):
        line.finish(p)
    plane.finish()
    up_own.wait()
    own.wait()
    for slot in range(2):
        back_copy(0, slot, slot).wait()
    for e in range(EXP_DEV):
        pltpu.make_async_copy(taken.at[e], taken_ref.at[e], stores.at[e]).wait()


def token_gather(fsdp, sp, x, g_first, g_second, picks, w_down, up):
    slots = picks.shape[1] // EXP_DEV
    total = fsdp * slots
    ff = w_down.shape[1]
    dma = pltpu.SemaphoreType.DMA
    return pl.pallas_call(
        functools.partial(token_kernel, fsdp, sp),
        out_shape=(
            jax.ShapeDtypeStruct((fsdp, TOK_DEV, D), BF16),
            jax.ShapeDtypeStruct((EXP_DEV, total, D), BF16),
            jax.ShapeDtypeStruct((EXP_DEV, total, ff), F32),
            jax.ShapeDtypeStruct((sp * up.shape[0], up.shape[1]), BF16),
        ),
        in_specs=[VMEM, ANY, ANY, VMEM, ANY, VMEM],
        out_specs=[ANY, ANY, ANY, ANY],
        scratch_shapes=[
            pltpu.VMEM((fsdp, TOK_DEV, D), BF16),
            pltpu.VMEM((EXP_DEV, ff, D), BF16),
            pltpu.VMEM((EXP_DEV, total, D), BF16),
            pltpu.VMEM((2, total, FT), F32),
        ]
        + line_sems(2, fsdp)
        + [dma, dma((3,)), dma((EXP_DEV,)), dma((2,)), dma((sp,)), dma((sp,)), dma],
        compiler_params=comm_params(3),
        name="token_gather",
    )(x, g_first, g_second, picks, w_down, up)


def token_back_kernel(
    fsdp, p_ref, gated_ref, w_ref, turned, x_ref, gu_ref, mid_ref, g_ref, gain,
    out_ref, low_ref, gain_out, part_ref, wu_ref, wide, narrow, w_buf, tile, grad_tile, loads, tile_sem, grad_sem, *scratch,
):
    f, s = lax.axis_index("fsdp"), lax.axis_index("sp")
    lines = fsdp // 2
    slots = turned.shape[3]
    height = grad_tile.shape[1]
    barrier = pltpu.get_barrier_semaphore()
    expected = greet_line(barrier, lines, f, s)
    reads = [
        pltpu.make_async_copy(gated_ref, narrow, loads.at[0]),
        pltpu.make_async_copy(w_ref.at[0], w_buf, loads.at[1]),
        pltpu.make_async_copy(x_ref, wide, loads.at[2]),
        pltpu.make_async_copy(gu_ref, narrow, loads.at[3]),
        pltpu.make_async_copy(w_ref.at[1], w_buf, loads.at[1]),
    ]
    reads[0].start()
    reads[1].start()
    pl.semaphore_wait(barrier, expected)
    line = LineReduce(p_ref, scratch, lines, f, s)
    line.start()

    def down_of(e):
        if e == 0:
            reads[0].wait()
            reads[1].wait()
        else:
            reads[4].wait()

        def columns(n, carry):
            at = pl.ds(pl.multiple_of(n * 512, 512), 512)
            wide[e, :, at] = dot_nn(narrow[e], w_buf[:, at]).astype(BF16)
            return carry

        lax.fori_loop(0, D // 512, columns, 0)
        if e == 0:
            reads[4].start()

    def tile_copy(b, slot):
        return pltpu.make_async_copy(tile.at[slot], part_ref.at[b], tile_sem.at[slot])

    def sum_all():
        reads[3].start()

        def pair(i, carry):
            for slot in range(2):
                b = 2 * i + slot

                @pl.when(i > 0)
                def _():
                    tile_copy(b, slot).wait()

                for n in range(D // 512):
                    at = pl.ds(n * 512, 512)
                    summed = jnp.zeros((TOK_DEV, 512), F32)
                    for e in range(EXP_DEV):
                        rows = wide[e, pl.ds(pl.multiple_of(b * slots, 16), slots), at]
                        summed += dot_nn(turned[b, e], rows)
                    tile[slot, :, at] = summed.astype(BF16)
                tile_copy(b, slot).start()
            return carry

        lax.fori_loop(0, fsdp // 2, pair, 0)
        reads[2].start()

    def grad_copy(e, i, slot):
        at = pl.ds(pl.multiple_of(i * height, height), height)
        return pltpu.make_async_copy(grad_tile.at[slot], wu_ref.at[e, at, :], grad_sem.at[slot])

    def grad_of(e):
        if e == 0:
            reads[2].wait()
            reads[3].wait()

        def pair(i, carry):
            for slot in range(2):
                part = 2 * i + slot

                def before():
                    grad_copy(e, part, slot).wait()

                if e == 0:
                    pl.when(i > 0)(before)
                else:
                    before()
                at = pl.ds(pl.multiple_of(part * height, height), height)
                grad_tile[slot] = dot_tn(wide[e, :, at], narrow[e]).astype(BF16)
                grad_copy(e, part, slot).start()
            return carry

        lax.fori_loop(0, D // height // 2, pair, 0)

    work = [functools.partial(down_of, e) for e in range(EXP_DEV)] + [sum_all]
    work += [functools.partial(grad_of, e) for e in range(EXP_DEV)]
    done = 0
    for t in range(lines - 1):
        line.step(t)
        until = (t + 1) * len(work) // (lines - 1)
        for unit in work[done:until]:
            unit()
        done = until
    line.finish(out_ref)
    gain_out[...] = jnp.zeros_like(gain_out)

    def norm_back(i, carry):
        at = pl.ds(pl.multiple_of(i * 32, 32), 32)
        mid = mid_ref[at, :]
        inverse = lax.rsqrt(jnp.mean(mid * mid, axis=-1, keepdims=True) + EPSILON)
        normed = mid * inverse
        grad_y = out_ref[at, :]
        scaled = grad_y * gain[1:2, :]
        mean = jnp.mean(scaled * normed, axis=-1, keepdims=True)
        grad = g_ref[at, :].astype(F32) + inverse * (scaled - normed * mean)
        out_ref[at, :] = grad
        low_ref[at, :] = grad.astype(BF16)
        gain_out[1:2, :] += jnp.sum(grad_y * normed, axis=0, keepdims=True)
        return carry

    lax.fori_loop(0, TOK_DEV // 32, norm_back, 0)
    for slot in range(2):
        tile_copy(slot, slot).wait()
        grad_copy(0, slot, slot).wait()


def token_back(fsdp, partial, gated, w_down, turned, received, grad_up_pre, mid, g, gains):
    block = partial.shape[1:]
    total, ff = gated.shape[1:]
    height = 256
    dma = pltpu.SemaphoreType.DMA
    return pl.pallas_call(
        functools.partial(token_back_kernel, fsdp),
        out_shape=(
            jax.ShapeDtypeStruct(block, F32),
            jax.ShapeDtypeStruct(block, BF16),
            jax.ShapeDtypeStruct((8, D), F32),
            jax.ShapeDtypeStruct(partial.shape, BF16),
            jax.ShapeDtypeStruct((EXP_DEV, D, ff), BF16),
        ),
        in_specs=[ANY, ANY, ANY, VMEM, ANY, ANY, VMEM, VMEM, VMEM],
        out_specs=[VMEM, VMEM, VMEM, ANY, ANY],
        scratch_shapes=[
            pltpu.VMEM((EXP_DEV, total, D), BF16),
            pltpu.VMEM((EXP_DEV, total, ff), BF16),
            pltpu.VMEM((ff, D), BF16),
            pltpu.VMEM((2,) + block, BF16),
            pltpu.VMEM((2, height, ff), BF16),
            dma((4,)),
            dma((2,)),
            dma((2,)),
        ]
        + LineReduce.scratch(fsdp, block),
        compiler_params=comm_params(4),
        name="token_back",
    )(partial, gated, w_down, turned, received, grad_up_pre, mid, g, gains)


class PlaneSum:
    def __init__(self, scratch, f, s, sp):
        self.own, self.got, self.send, self.recv = scratch
        self.f, self.s, self.sp = f, s, sp

    @staticmethod
    def scratch(seq, sp):
        dma = pltpu.SemaphoreType.DMA
        return [
            pltpu.VMEM((8, seq), F32), pltpu.VMEM((sp, 8, seq), F32), dma((sp,)), dma((sp,)),
        ]

    def greet(self, barrier):
        for k in range(1, self.sp):
            signal(barrier, (self.f, self.s ^ k))
        return self.sp - 1

    def copy(self, k):
        return remote(
            self.own, self.got.at[k], self.send.at[k], self.recv.at[k], (self.f, self.s ^ k)
        )

    def start(self, x_ref):
        self.own[...] = x_ref[...].T[:8]
        for k in range(1, self.sp):
            self.copy(k).start()

    def finish(self, out_ref):
        for k in range(1, self.sp):
            self.copy(k).wait()
        terms = [self.own[...]] + [self.got[k] for k in range(1, self.sp)]
        while len(terms) > 1:
            terms = [terms[i] + terms[i + 1] for i in range(0, len(terms), 2)]
        seq = out_ref.shape[0]
        out_ref[...] = jnp.concatenate([terms[0], jnp.zeros((120, seq), F32)], axis=0).T


def end_kernel(
    fsdp, sp, p_ref, low_ref, w_ref, x_ref, mid_ref, gain, gains_in, router_ref,
    grad_out, qkv_0, qkv_1, qkv_2, o_out, small_out,
    first, low_in, w_buf, back, low, o_low, gain_sum, pay, small, loads,
    qsend, qrecv, osend, orecv, msend, mrecv, local, *scratch,
):
    f, s = lax.axis_index("fsdp"), lax.axis_index("sp")
    count, lines = fsdp * sp, fsdp // 2
    me = f * sp + s
    rows, cols = o_low.shape[0], D // sp
    height = D // fsdp
    barrier = pltpu.get_barrier_semaphore()
    greet_all(barrier, me, count, sp)
    reads = [
        pltpu.make_async_copy(low_ref, low_in, loads.at[0]),
        pltpu.make_async_copy(w_ref, w_buf, loads.at[1]),
    ]
    for copy in reads:
        copy.start()
    pl.semaphore_wait(barrier, count - 1)
    plane_parts = 6 if sp == 4 else 5
    plane = plane_reduce_of(first, back, scratch[:plane_parts], f, s, sp)
    line = LineReduce(p_ref, scratch[plane_parts:], lines, f, s)
    line.start()

    def first_grads():
        for copy in reads:
            copy.wait()

        def columns(n, carry):
            at = pl.ds(pl.multiple_of(n * 256, 256), 256)
            for d in range(sp):
                rows_at = slice(d * TOK_DEV, (d + 1) * TOK_DEV)
                total = dot_nt(low_in[rows_at, :cols], w_buf[0, at, :])
                total += dot_nt(low_in[rows_at, cols : 2 * cols], w_buf[1, at, :])
                total += dot_nt(low_in[rows_at, 2 * cols :], w_buf[2, at, :])
                first[d, :, at] = total.astype(BF16)
            return carry

        lax.fori_loop(0, D // 256, columns, 0)

    def input_grads():
        gain_sum[...] = jnp.zeros_like(gain_sum)

        def chunk(i, carry):
            at = pl.ds(pl.multiple_of(i * 32, 32), 32)
            x = x_ref[at, :].astype(F32)
            inverse = lax.rsqrt(jnp.mean(x * x, axis=-1, keepdims=True) + EPSILON)
            normed = x * inverse
            grad_y = back[at, :]
            scaled = grad_y * gain[0:1, :]
            mean = jnp.mean(scaled * normed, axis=-1, keepdims=True)
            grad_out[at, :] = mid_ref[at, :] + inverse * (scaled - normed * mean)
            gain_sum[0:1, :] += jnp.sum(grad_y * normed, axis=0, keepdims=True)
            return carry

        lax.fori_loop(0, TOK_DEV // 32, chunk, 0)
        gain_sum[...] += gains_in[...]

        def fill(i, carry):
            at = pl.ds(pl.multiple_of(i * rows // 128 * 128, 128), 128)
            pay[i, 0:8, :] = router_ref[i]
            pay[i, 8:16, :] = gain_sum[:, at]
            return carry

        lax.fori_loop(0, count, fill, 0)

    def m_copy(i):
        other = lax.rem(me + i, count)
        return remote(
            pay.at[other], small.at[me], msend.at[i], mrecv.at[me], (other // sp, lax.rem(other, sp))
        )

    def m_go(i, carry):
        m_copy(i).start()
        return carry

    for t in range(lines - 1):
        line.step(t)
        if t == 0:
            first_grads()
            plane.start()
    plane.forward()
    plane.finish()
    input_grads()
    lax.fori_loop(1, count, m_go, 0)
    line.finish(low)
    for c in range(sp):
        top = 3 * height + c * rows
        o_low[:, c * cols : (c + 1) * cols] = low[top : top + rows, :]

    def q_from(i, place):
        return low.at[pl.ds(pl.multiple_of(i * height + place * rows, rows), rows), :]

    def q_to(i, place):
        return (qkv_0, qkv_1, qkv_2)[i].at[place]

    def q_copy(i, k):
        return remote(q_from(i, s ^ k), q_to(i, s), qsend.at[k, i], qrecv.at[k, i], (f, s ^ k))

    def q_own(i):
        return pltpu.make_async_copy(q_from(i, s), q_to(i, s), local.at[i])

    for k in range(sp - 1, 0, -1):
        for i in range(3):
            q_copy(i, k).start()
    owner = row_owner(f, s, rows, sp)
    target_f, target_s = owner // sp, lax.rem(owner, sp)
    stays = jnp.logical_and(target_s == s, target_f == f)
    o_copy = remote(o_low, o_out, osend, orecv, (target_f, target_s))
    o_own = pltpu.make_async_copy(o_low, o_out, orecv)

    @pl.when(stays)
    def _():
        o_own.start()

    @pl.when(jnp.logical_not(stays))
    def _():
        o_copy.start()

    for i in range(3):
        q_own(i).start()

    def m_end(i, carry):
        m_copy(i).wait_send()
        other = lax.rem(me + i, count)
        landed(small.at[other], mrecv.at[other])
        return carry + small[other]

    small_out[...] = lax.fori_loop(1, count, m_end, pay[me])
    for k in range(1, sp):
        for i in range(3):
            landed(q_to(i, s ^ k), qrecv.at[k, i])
            q_copy(i, k).wait_send()
    landed(o_out, orecv)

    @pl.when(jnp.logical_not(stays))
    def _():
        o_copy.wait_send()

    for i in range(3):
        q_own(i).wait()


def end_exchange(fsdp, sp, partial, low, w, x, grad_mid, gains, gains_in, router, number):
    count = fsdp * sp
    block = partial.shape[1:]
    rows = D // count
    dma = pltpu.SemaphoreType.DMA
    return pl.pallas_call(
        functools.partial(end_kernel, fsdp, sp),
        out_shape=(
            jax.ShapeDtypeStruct((TOK_DEV, D), F32),
            jax.ShapeDtypeStruct((sp, rows, D // sp), BF16),
            jax.ShapeDtypeStruct((sp, rows, D // sp), BF16),
            jax.ShapeDtypeStruct((sp, rows, D // sp), BF16),
            jax.ShapeDtypeStruct((rows, D), BF16),
            jax.ShapeDtypeStruct((16, 128), F32),
        ),
        in_specs=[ANY, ANY, ANY, VMEM, VMEM, VMEM, VMEM, VMEM],
        out_specs=[VMEM, ANY, ANY, ANY, ANY, VMEM],
        scratch_shapes=[
            pltpu.VMEM((sp, TOK_DEV, D), BF16),
            pltpu.VMEM(low.shape, BF16),
            pltpu.VMEM(w.shape, BF16),
            pltpu.VMEM((TOK_DEV, D), F32),
            pltpu.VMEM(block, BF16),
            pltpu.VMEM((rows, D), BF16),
            pltpu.VMEM((8, D), F32),
            pltpu.VMEM((count, 16, 128), F32),
            pltpu.VMEM((count, 16, 128), F32),
            dma((2,)),
            dma((sp, 3)), dma((sp, 3)), dma, dma, dma((count,)), dma((count,)), dma((3,)),
        ]
        + plane_scratch((TOK_DEV, D), sp)
        + LineReduce.scratch(fsdp, block),
        compiler_params=comm_params(number),
        name="end_exchange",
    )(partial, low, w, x, grad_mid, gains, gains_in, router)


def dot_nt(a, b):
    return lax.dot_general(a, b, (((1,), (1,)), ((), ())), preferred_element_type=F32)


def dot_tn(a, b):
    return lax.dot_general(a, b, (((0,), (0,)), ((), ())), preferred_element_type=F32)


def dot_nn(a, b):
    return jnp.dot(a, b, preferred_element_type=F32)


def whole(shape):
    return pl.BlockSpec(shape, lambda *_: (0,) * len(shape))


def lanes(first, second):
    lane = lax.broadcasted_iota(jnp.int32, (first.shape[0], 128), 1)
    return jnp.where(lane == 0, first, jnp.where(lane == 1, second, 0.0))


def inverse_of(sums, lane):
    return lax.rsqrt(sums[:, lane : lane + 1] / D + EPSILON)


def turn(v, table, sign=1.0):
    half = HEAD_DIM // 2
    front = lax.broadcasted_iota(jnp.int32, table.shape, 1) < half
    turned = pltpu.roll(table, half, 1)
    cosine = jnp.where(front, table, turned)
    sine = jnp.where(front, -turned, table)
    return v * cosine + pltpu.roll(v, half, 1) * (sine * sign)


def turn_back(v, table):
    return turn(v, table, -1.0)


def project_kernel(sp, x_ref, gain, w_ref, first_out, q_out, k_out, v_out, sums_out, squares, *scratch):
    step = pl.program_id(0)
    total = PlaneSum(scratch, lax.axis_index("fsdp"), lax.axis_index("sp"), sp)
    barrier = pltpu.get_barrier_semaphore()

    @pl.when(step == 0)
    def _():
        total.greet(barrier)

    x = x_ref[...].astype(F32)
    inverse = lax.rsqrt(jnp.mean(x * x, axis=-1, keepdims=True) + EPSILON)
    first = (x * inverse * gain[0:1, :]).astype(BF16)
    first_out[...] = first
    q = dot_nn(first, w_ref[0])
    q_out[...] = q
    k = dot_nn(first, w_ref[1])
    k_out[...] = k
    at = pl.ds(pl.multiple_of(step * TOK_DEV, TOK_DEV), TOK_DEV)
    squares[at, :] = lanes(
        jnp.sum(q * q, axis=-1, keepdims=True), jnp.sum(k * k, axis=-1, keepdims=True)
    )
    last = step == pl.num_programs(0) - 1

    @pl.when(last)
    def _():
        pl.semaphore_wait(barrier, sp - 1)
        total.start(squares)

    v_out[...] = dot_nn(first, w_ref[2]).astype(BF16)

    @pl.when(last)
    def _():
        total.finish(sums_out)


def project(sp, x, gains, w):
    seq, cols = x.shape[0], w.shape[2]

    def block(width):
        return pl.BlockSpec((TOK_DEV, width), lambda i: (i, 0))

    return pl.pallas_call(
        functools.partial(project_kernel, sp),
        grid=(seq // TOK_DEV,),
        out_shape=(
            jax.ShapeDtypeStruct((seq, D), BF16),
            jax.ShapeDtypeStruct((seq, cols), F32),
            jax.ShapeDtypeStruct((seq, cols), F32),
            jax.ShapeDtypeStruct((seq, cols), BF16),
            jax.ShapeDtypeStruct((seq, 128), F32),
        ),
        in_specs=[block(D), whole(gains.shape), whole(w.shape)],
        out_specs=[block(D), block(cols), block(cols), block(cols), whole((seq, 128))],
        scratch_shapes=[pltpu.VMEM((seq, 128), F32)] + PlaneSum.scratch(seq, sp),
        compiler_params=comm_params(1),
        name="project",
    )(x, gains, w)


def attend_kernel(
    q_raw, k_raw, v_ref, squares, gain, table, o_ref, sum_ref, q_ref, k_ref
):
    head = pl.program_id(0)

    @pl.when(head == 0)
    def _():
        sum_ref[...] = squares[...]

    q_inv, k_inv = inverse_of(squares, 0), inverse_of(squares, 1)
    q_ref[...] = turn(q_raw[...] * q_inv * gain[2:3, :], table[...]).astype(BF16)
    k_ref[...] = turn(k_raw[...] * k_inv * gain[3:4, :], table[...]).astype(BF16)
    for i in range(q_ref.shape[0] // BLK):
        rows, seen = pl.ds(i * BLK, BLK), pl.ds(0, (i + 1) * BLK)
        scores = dot_nt(q_ref[rows, :], k_ref[seen, :]) * SCALE
        row_max = jnp.max(scores, axis=-1, keepdims=True)
        exp_rows = jnp.exp(scores - row_max)
        row_sum = jnp.sum(exp_rows, axis=-1, keepdims=True)
        probs = (exp_rows / row_sum).astype(BF16)
        o_ref[rows, :] = dot_nn(probs, v_ref[seen, :]).astype(BF16)
        lane = lax.broadcasted_iota(jnp.int32, (BLK, 128), 1)
        sum_ref[rows, :] += jnp.where(lane == head + 2, row_max + jnp.log(row_sum), 0.0)


def attend(q_raw, k_raw, v, squares, gains, table):
    seq, width = v.shape
    heads = width // HEAD_DIM
    spec = pl.BlockSpec((seq, HEAD_DIM), lambda h: (0, h))
    return pl.pallas_call(
        attend_kernel,
        grid=(heads,),
        out_shape=(
            jax.ShapeDtypeStruct((seq, width), BF16),
            jax.ShapeDtypeStruct((seq, 128), F32),
            jax.ShapeDtypeStruct((seq, width), BF16),
            jax.ShapeDtypeStruct((seq, width), BF16),
        ),
        in_specs=[
            spec, spec, spec, whole((seq, 128)),
            pl.BlockSpec((4, HEAD_DIM), lambda h: (0, h)),
            whole((seq, HEAD_DIM)),
        ],
        out_specs=[spec, whole((seq, 128)), spec, spec],
        compiler_params=pltpu.CompilerParams(vmem_limit_bytes=VLIM),
        name="attend",
    )(q_raw, k_raw, v, squares, gains, table)


def attend_back_head(
    h, q_ref, k_ref, v_ref, sums, q_raw, k_raw, gain, table,
    q_scaled, k_scaled, dv_out, dots, gains_out, dv_ref,
):
    head = slice(h * HEAD_DIM, (h + 1) * HEAD_DIM)
    k_scaled[:, head] = jnp.zeros(k_raw[:, head].shape, F32)
    dv_ref[...] = jnp.zeros_like(dv_ref)
    gain_q, gain_k = gain[2:3, head], gain[3:4, head]
    gain_sum = jnp.zeros((1, HEAD_DIM), F32)
    size = BLK if q_ref.shape[0] <= 4 * BLK else BLK // 2
    for i in range(q_ref.shape[0] // size):
        rows, seen = pl.ds(i * size, size), pl.ds(0, (i * size // BLK + 1) * BLK)
        q, g, keys = q_ref[rows, head], dv_out[rows, head], k_ref[seen, head]
        scores = dot_nt(q, keys) * SCALE
        probs = jnp.exp(scores - sums[rows, h + 2 : h + 3])
        grad_probs = dot_nt(g, v_ref[seen, head])
        row_dot = jnp.sum(probs * grad_probs, axis=-1, keepdims=True)
        grad_scores = (probs * (grad_probs - row_dot)).astype(BF16)
        k_scaled[seen, head] += dot_tn(grad_scores, q)
        dv_ref[seen, :] += dot_tn(probs.astype(BF16), g)
        grad_y = turn_back(dot_nn(grad_scores, keys) * SCALE, table[rows, :])
        normed = q_raw[rows, head] * inverse_of(sums.at[rows, :], 0)
        scaled = grad_y * gain_q
        q_scaled[rows, head] = scaled
        dots[rows, :] += lanes(jnp.sum(scaled * normed, axis=-1, keepdims=True), 0.0)
        gain_sum += jnp.sum(grad_y * normed, axis=0, keepdims=True)
    grad_y = turn_back(k_scaled[:, head] * SCALE, table[...])
    normed = k_raw[:, head] * inverse_of(sums, 1)
    scaled = grad_y * gain_k
    k_scaled[:, head] = scaled
    k_dots = jnp.sum(scaled * normed, axis=-1, keepdims=True)
    dots[...] += lanes(jnp.zeros_like(k_dots), k_dots)
    gains_out[0:1, head] = gain_sum
    gains_out[1:2, head] = jnp.sum(grad_y * normed, axis=0, keepdims=True)
    dv_out[:, head] = dv_ref[...].astype(BF16)


def branch_back_kernel(
    fsdp, sp, x_ref, p_ref, wo_ref, q_ref, k_ref, v_ref, sums, q_raw, k_raw, gain, table,
    all_ref, out_ref, q_scaled, k_scaled, dv_out, dots, gains_out,
    g_all, dv_ref, xsend, xrecv, own_sem, all_sem, *scratch,
):
    f, s = lax.axis_index("fsdp"), lax.axis_index("sp")
    lines = fsdp // 2
    barrier = pltpu.get_barrier_semaphore()
    sums_over = PlaneSum(scratch[:4], f, s, sp)
    expected = greet_line(barrier, lines, f, s) + sums_over.greet(barrier)
    plane = plane_gather_of(x_ref, g_all, f, s, sp, xsend, xrecv)
    own = pltpu.make_async_copy(x_ref, plane.at(s, 0, x_ref.shape[0]), own_sem)
    own.start()
    pl.semaphore_wait(barrier, expected)
    plane.start()
    line = LineReduce(p_ref, scratch[4:], lines, f, s)
    line.start()
    dots[...] = jnp.zeros_like(dots)
    out_all = pltpu.make_async_copy(g_all, all_ref, all_sem)
    def back_of(place):
        at = pl.ds(pl.multiple_of(place * TOK_DEV, TOK_DEV), TOK_DEV)
        dv_out[at, :] = dot_nt(g_all[at, :], wo_ref[...]).astype(BF16)

    early = (0, 1, 2) if sp == 4 else (0,)
    for t in range(lines - 1):
        line.step(t)
        if t == min(1, lines - 2):
            plane.forward()
            own.wait()
            for k in early:
                back_of(s ^ k)
    plane.finish()
    out_all.start()
    for k in range(len(early), sp):
        back_of(s ^ k)
    for h in range(q_ref.shape[1] // HEAD_DIM):
        attend_back_head(
            h, q_ref, k_ref, v_ref, sums, q_raw, k_raw, gain, table,
            q_scaled, k_scaled, dv_out, dots, gains_out, dv_ref,
        )
    sums_over.start(dots)
    line.finish(out_ref)
    sums_over.finish(dots)
    out_all.wait()


def branch_back(fsdp, sp, x, partial, wo, q, k, v, sums, q_raw, k_raw, gains, table):
    block = partial.shape[1:]
    seq, width = q.shape
    dma = pltpu.SemaphoreType.DMA
    return pl.pallas_call(
        functools.partial(branch_back_kernel, fsdp, sp),
        out_shape=(
            jax.ShapeDtypeStruct((seq, D), BF16),
            jax.ShapeDtypeStruct(block, F32),
            jax.ShapeDtypeStruct((seq, width), F32),
            jax.ShapeDtypeStruct((seq, width), F32),
            jax.ShapeDtypeStruct((seq, width), BF16),
            jax.ShapeDtypeStruct((seq, 128), F32),
            jax.ShapeDtypeStruct((2, width), F32),
        ),
        in_specs=[VMEM, ANY] + [VMEM] * 9,
        out_specs=[ANY] + [VMEM] * 6,
        scratch_shapes=[
            pltpu.VMEM((seq, D), BF16), pltpu.VMEM((seq, HEAD_DIM), F32), dma((sp,)), dma((sp,)), dma, dma,
        ]
        + PlaneSum.scratch(seq, sp)
        + LineReduce.scratch(fsdp, block),
        compiler_params=comm_params(5),
        name="branch_back",
    )(x, partial, wo, q, k, v, sums, q_raw, k_raw, gains, table)


def held(shape):
    return pl.BlockSpec(
        shape, lambda *_: (0,) * len(shape), pipeline_mode=pl.Buffered(buffer_count=1)
    )


def weight_kernel(
    q_scaled, k_scaled, q_raw, k_raw, squares, dots, dv_ref, first, attended, g_ref, out, low, square
):
    f = pl.program_id(0)
    height = first.shape[1]
    rows = out.shape[1] - 3 * height
    cols = out.shape[2]
    sp = D // cols

    @pl.when(f == 0)
    def _():
        for n, scaled, raw in ((0, q_scaled, q_raw), (1, k_scaled, k_raw)):
            inverse = inverse_of(squares, n)
            mean = dots[:, n : n + 1] / D
            low[:, n * cols : (n + 1) * cols] = (
                inverse * (scaled[...] - raw[...] * (inverse * mean))
            ).astype(BF16)
        low[:, 2 * cols :] = dv_ref[...]
        for c in range(sp):
            at = slice(c * cols, (c + 1) * cols)
            square[:, at] = dot_tn(attended[...], g_ref[:, at]).astype(BF16)

    grads = dot_tn(first[...], low[...]).astype(BF16)
    for n in range(3):
        out[0, n * height : (n + 1) * height, :] = grads[:, n * cols : (n + 1) * cols]
    each = rows // sp
    from_rows = pl.ds(pl.multiple_of(f * each, each), each)
    for c in range(sp):
        at = 3 * height + c * each
        out[0, at : at + each, :] = square[from_rows, c * cols : (c + 1) * cols]


def weight_parts(fsdp, q_scaled, k_scaled, q_raw, k_raw, squares, dots, dv, first, attended, g):
    seq, cols = dv.shape
    height = D // fsdp
    each = cols // fsdp
    return pl.pallas_call(
        weight_kernel,
        grid=(fsdp,),
        out_shape=(
            jax.ShapeDtypeStruct((fsdp, 3 * height + D // cols * each, cols), BF16),
            jax.ShapeDtypeStruct((seq, 3 * cols), BF16),
        ),
        in_specs=[held((seq, cols))] * 4
        + [held((seq, 128))] * 2
        + [
            held((seq, cols)),
            pl.BlockSpec((seq, height), lambda f: (0, f)),
            held((seq, cols)),
            held((seq, D)),
        ],
        out_specs=[
            pl.BlockSpec((1, 3 * height + D // cols * each, cols), lambda f: (f, 0, 0)),
            whole((seq, 3 * cols)),
        ],
        scratch_shapes=[pltpu.VMEM((cols, D), BF16)],
        compiler_params=pltpu.CompilerParams(vmem_limit_bytes=VLIM),
        name="weight_parts",
    )(q_scaled, k_scaled, q_raw, k_raw, squares, dots, dv, first, attended, g)


def two_parts(x, axis):
    high = x.astype(BF16)
    return jnp.concatenate([high, (x - high.astype(F32)).astype(BF16)], axis=axis)


def blocks_of(shape):
    return pl.BlockSpec((1,) + shape, lambda b: (b,) + (0,) * len(shape))


def slots_of(slots, width):
    return pl.BlockSpec((EXP_DEV, slots, width), lambda b: (0, b, 0))


def route_kernel(picks, rows_in, router, columns, out, probs_out, gates_out):
    slots = out.shape[1]
    for n in range(D // 512):
        at = pl.ds(n * 512, 512)
        got = dot_nn(picks[0], rows_in[0, :, at]).astype(BF16)
        for e in range(EXP_DEV):
            out[e, :, at] = got[e * slots : (e + 1) * slots]
    logits = dot_nt(rows_in[0], router[...])
    exp_logits = jnp.exp(logits - jnp.max(logits, axis=1, keepdims=True))
    probs = exp_logits / jnp.sum(exp_logits, axis=1, keepdims=True)
    probs_out[0] = probs
    both = two_parts(probs, 1)
    for e in range(EXP_DEV):
        moved = dot_nn(picks[0, e * slots : (e + 1) * slots, :], both)
        mask = columns[e : e + 1, :]
        gates_out[e] = jnp.sum(moved * jnp.concatenate([mask, mask], axis=1), axis=1, keepdims=True)


def route(picks, tokens, router_t, columns):
    blocks = tokens.shape[0]
    slots = picks.shape[1] // EXP_DEV
    total = blocks * slots
    experts = router_t.shape[0]
    return pl.pallas_call(
        route_kernel,
        grid=(blocks,),
        out_shape=(
            jax.ShapeDtypeStruct((EXP_DEV, total, D), BF16),
            jax.ShapeDtypeStruct((blocks, TOK_DEV, experts), F32),
            jax.ShapeDtypeStruct((EXP_DEV, total, 1), F32),
        ),
        in_specs=[
            blocks_of(picks.shape[1:]), blocks_of((TOK_DEV, D)), whole(router_t.shape),
            whole(columns.shape),
        ],
        out_specs=[slots_of(slots, D), blocks_of((TOK_DEV, experts)), slots_of(slots, 1)],
        compiler_params=pltpu.CompilerParams(vmem_limit_bytes=VLIM),
        name="route",
    )(picks, tokens, router_t, columns)


FT = 256


def active_tile(x_ref, g_ref, up, u_ref, gates, gated, grad_gate, grad_up, dots):
    total = x_ref.shape[1]
    chunk = total // 4
    for first in range(0, total, chunk):
        at = slice(first, first + chunk)
        gate_pre = dot_nn(x_ref[0, at, :], g_ref[0])
        up_pre = dot_nn(x_ref[0, at, :], up)
        sig = jax.nn.sigmoid(gate_pre)
        silu = gate_pre * sig
        hidden = silu * up_pre
        back = u_ref[0, at, :]
        gate = gates[0, at, :]
        dots[0, at, :] += jnp.sum(hidden * back, axis=1, keepdims=True)
        gated[0, at, :] = (hidden * gate).astype(BF16)
        back = back * gate
        grad_gate[0, at, :] = (back * up_pre * (sig * (1.0 + gate_pre * (1.0 - sig)))).astype(BF16)
        grad_up[0, at, :] = (back * silu).astype(BF16)


def active_kernel(x_ref, g_ref, first_ref, second_ref, u_ref, gates, gated, grad_gate, grad_up, dots):
    rest = (u_ref, gates, gated, grad_gate, grad_up, dots)

    @pl.when(pl.program_id(1) == 0)
    def _():
        dots[...] = jnp.zeros_like(dots)
        active_tile(x_ref, g_ref, first_ref[0], *rest)

    @pl.when(pl.program_id(1) == 1)
    def _():
        active_tile(x_ref, g_ref, second_ref[...].reshape(first_ref.shape[1:]), *rest)


def active(x, w_gate, up_first, up_second, u, gates):
    _, total, _ = x.shape
    wide = up_first.shape[2]
    sp, _, height, _ = up_second.shape
    tile = pl.BlockSpec((1, total, wide), lambda e, j: (e, 0, j))
    column = pl.BlockSpec((1, total, 1), lambda e, j: (e, 0, 0))
    low = jax.ShapeDtypeStruct((EXP_DEV, total, 2 * wide), BF16)
    return pl.pallas_call(
        active_kernel,
        grid=(EXP_DEV, 2),
        out_shape=(low, low, low, jax.ShapeDtypeStruct((EXP_DEV, total, 1), F32)),
        in_specs=[
            pl.BlockSpec((1, total, D), lambda e, j: (e, 0, 0)),
            pl.BlockSpec((1, D, wide), lambda e, j: (e, 0, j)),
            pl.BlockSpec((1, D, wide), lambda e, j: (e, 0, 0)),
            pl.BlockSpec((sp, 1, height, wide), lambda e, j: (0, e, 0, 0)),
            tile,
            column,
        ],
        out_specs=[tile, tile, tile, column],
        compiler_params=pltpu.CompilerParams(vmem_limit_bytes=VLIM),
        name="active",
    )(x, w_gate, up_first, up_second, u, gates)


def weight_grad_kernel(a_ref, b_ref, out):
    out[0] = dot_tn(a_ref[0], b_ref[0]).astype(BF16)


def weight_grad(a, b, name):
    _, total, height = a.shape
    width = b.shape[2]
    size = 1024
    return pl.pallas_call(
        weight_grad_kernel,
        grid=(EXP_DEV, height // size, width // size),
        out_shape=jax.ShapeDtypeStruct((EXP_DEV, height, width), BF16),
        in_specs=[
            pl.BlockSpec((1, total, size), lambda e, i, j: (e, 0, i)),
            pl.BlockSpec((1, total, size), lambda e, i, j: (e, 0, j)),
        ],
        out_specs=pl.BlockSpec((1, size, size), lambda e, i, j: (e, i, j)),
        compiler_params=pltpu.CompilerParams(vmem_limit_bytes=VLIM),
        name=name,
    )(a, b)


def rows_back_kernel(a_ref, b_ref, g_ref, first_ref, second_ref, out):
    wide = first_ref.shape[2]
    total = dot_nt(a_ref[0], g_ref[0]) + dot_nt(b_ref[0, :, :wide], first_ref[0])
    second = second_ref[...].reshape(first_ref.shape[1:])
    out[0] = (total + dot_nt(b_ref[0, :, wide:], second)).astype(BF16)


def rows_back(grad_gate_pre, grad_up_pre, w_gate, up_first, up_second):
    _, total, ff = grad_up_pre.shape
    size = 512
    wide = up_first.shape[2]
    height = up_second.shape[2]
    row = pl.BlockSpec((1, total, ff), lambda e, j: (e, 0, 0))
    return pl.pallas_call(
        rows_back_kernel,
        grid=(EXP_DEV, D // size),
        out_shape=jax.ShapeDtypeStruct((EXP_DEV, total, D), BF16),
        in_specs=[
            row,
            row,
            pl.BlockSpec((1, size, ff), lambda e, j: (e, j, 0)),
            pl.BlockSpec((1, size, wide), lambda e, j: (e, j, 0)),
            pl.BlockSpec((size // height, 1, height, wide), lambda e, j: (j, e, 0, 0)),
        ],
        out_specs=pl.BlockSpec((1, total, size), lambda e, j: (e, 0, j)),
        compiler_params=pltpu.CompilerParams(vmem_limit_bytes=VLIM),
        name="rows_back",
    )(grad_gate_pre, grad_up_pre, w_gate, up_first, up_second)


def combine_kernel(turned, rows_ref, tokens, probs, dots, router, columns, out, router_out):
    @pl.when(pl.program_id(0) == 0)
    def _():
        router_out[...] = jnp.zeros_like(router_out)

    choice = jnp.zeros(probs.shape[1:], F32)
    for e in range(EXP_DEV):
        moved = dot_nn(turned[0, e], dots[e])
        choice += jnp.sum(moved, axis=1, keepdims=True) * columns[e : e + 1, :]
    p = probs[0]
    grad_logits = p * (choice - jnp.sum(p * choice, axis=1, keepdims=True))
    both = two_parts(grad_logits, 1)
    for n in range(D // 512):
        at = pl.ds(n * 512, 512)
        total = dot_nn(both, router[:, at])
        for e in range(EXP_DEV):
            total += dot_nn(turned[0, e], rows_ref[e, :, at])
        out[0, :, at] = total.astype(BF16)
    router_out[...] += dot_tn(both, tokens[0])


def combine(turned, grad_rows, tokens, probs, dots, router_two, columns):
    blocks = tokens.shape[0]
    slots = turned.shape[3]
    return pl.pallas_call(
        combine_kernel,
        grid=(blocks,),
        out_shape=(
            jax.ShapeDtypeStruct((blocks, TOK_DEV, D), BF16),
            jax.ShapeDtypeStruct((router_two.shape[0], D), F32),
        ),
        in_specs=[
            blocks_of(turned.shape[1:]), slots_of(slots, D), blocks_of((TOK_DEV, D)),
            blocks_of(probs.shape[1:]), slots_of(slots, 128), whole(router_two.shape),
            whole(columns.shape),
        ],
        out_specs=[blocks_of((TOK_DEV, D)), whole((router_two.shape[0], D))],
        compiler_params=pltpu.CompilerParams(vmem_limit_bytes=VLIM),
        name="combine",
    )(turned, grad_rows, tokens, probs, dots, router_two, columns)


def widen_kernel(mid, total, *refs):
    *refs, layer_out = refs
    layer_out[...] = (mid[...] + total[...]).astype(BF16)
    count = len(refs) // 2
    for low, out in zip(refs[:count], refs[count:]):
        if len(low.shape) == 2:
            out[...] = low[...].astype(F32)
            continue
        sp, _, cols = low.shape
        for s in range(sp):
            for g in range(cols // HEAD_DIM):
                head = g * sp + s
                out[:, head * HEAD_DIM : (head + 1) * HEAD_DIM] = low[
                    s, :, g * HEAD_DIM : (g + 1) * HEAD_DIM
                ].astype(F32)


def widen(mid, total, by_heads, arrays):
    steps = 4
    flat = [x.reshape(-1, x.shape[-1]) for x in arrays]

    def rows_of(shape, axis):
        tall = shape[axis] // steps if shape[axis] % (16 * steps) == 0 else shape[axis]
        block = shape[:axis] + (tall,) + shape[axis + 1 :]
        moving = tall != shape[axis]
        return pl.BlockSpec(
            block, lambda i: tuple(i if moving and n == axis else 0 for n in range(len(shape)))
        )

    heads_out = [(x.shape[1], x.shape[0] * x.shape[2]) for x in by_heads]
    wide = pl.pallas_call(
        widen_kernel,
        grid=(steps,),
        out_shape=tuple(
            jax.ShapeDtypeStruct(shape, F32) for shape in heads_out + [x.shape for x in flat]
        )
        + (jax.ShapeDtypeStruct(mid.shape, BF16),),
        in_specs=[rows_of(mid.shape, 0)] * 2
        + [rows_of(x.shape, 1) for x in by_heads]
        + [rows_of(x.shape, 0) for x in flat],
        out_specs=[rows_of(shape, 0) for shape in heads_out + [x.shape for x in flat] + [mid.shape]],
        compiler_params=pltpu.CompilerParams(vmem_limit_bytes=VLIM),
        name="widen",
    )(mid, total, *by_heads, *flat)
    split = len(by_heads)
    shaped = [x.reshape(like.shape) for x, like in zip(wide[split:-1], arrays)]
    return list(wide[:split]) + shaped + [wide[-1]]


def angles(seq):
    freqs = np.float32(ROPE_BASE) ** (-2.0 * np.arange(HEAD_DIM // 2, dtype=np.float32) / HEAD_DIM)
    turned = np.arange(seq, dtype=np.float32)[:, None] * freqs[None, :].astype(np.float32)
    return jnp.asarray(np.concatenate([np.cos(turned), np.sin(turned)], axis=1), F32)


def body(
    layer_input, output_grad, w_query, w_key, w_value, w_output, w_router, norm_gains,
    w_gate, w_up, w_down, expert_routes,
):
    fsdp, sp = lax.axis_size("fsdp"), lax.axis_size("sp")
    f, s = lax.axis_index("fsdp"), lax.axis_index("sp")
    count = fsdp * sp
    experts = EXP_DEV * fsdp
    capacity = TOK_DEV * TOP // experts * 17 // 16
    slots = -(-capacity // 16) * 16
    seq = TOK_DEV * sp
    cols = D // sp
    rows = D // count

    down_full = lax.all_gather(w_down, "sp", axis=1, tiled=True)
    gate_full = lax.all_gather(w_gate, "sp", axis=1, tiled=True)
    wide = w_up.shape[2] // 2
    up_first = lax.all_gather(w_up[:, :, :wide], "sp", axis=1, tiled=True)

    router_size = rows * experts
    misc = jnp.concatenate([w_router.reshape(router_size), norm_gains.reshape(4 * rows)])
    misc_rows = -(-misc.shape[0] // 2048) * 16
    misc = jnp.pad(misc, (0, misc_rows * 128 - misc.shape[0])).reshape(misc_rows, 128)
    routes = expert_routes.reshape(TOK_DEV * TOP // 128, 128)
    early = TOK_DEV // 8
    x_all, w_all, wo_s, grad_first_half, misc_all, routes_all = gather_start(
        fsdp, sp, layer_input, jnp.stack([w_query, w_key, w_value]), w_output, output_grad[:early],
        misc, routes,
    )
    misc_all = misc_all.reshape(count, misc_rows * 128)
    router_w = misc_all[:, :router_size].reshape(D, experts)
    router_t = router_w.T
    gains_w = misc_all[:, router_size : router_size + 4 * rows].reshape(count, 4, rows)
    gains32 = gains_w.transpose(1, 0, 2).reshape(4, D).astype(F32)
    by_head = gains32.reshape(4, cols // HEAD_DIM, sp, HEAD_DIM)
    gains_own = lax.dynamic_index_in_dim(by_head, s, axis=2, keepdims=False).reshape(4, cols)

    routes_block = routes_all.reshape(fsdp, TOK_DEV, TOP)
    own_ids = f * EXP_DEV + jnp.arange(EXP_DEV, dtype=jnp.int32)
    chosen = jnp.any(routes_block[:, :, :, None] == own_ids, axis=2)
    before = jnp.arange(TOK_DEV)[:, None] > jnp.arange(TOK_DEV)[None, :]
    place = jnp.einsum(
        "ut,fte->feu", before.astype(BF16), chosen.astype(BF16), preferred_element_type=F32
    ).astype(jnp.int32)
    slot_ids = jnp.arange(slots, dtype=jnp.int32)
    picks = (
        (place[:, :, None, :] == slot_ids[:, None]) & chosen.transpose(0, 2, 1)[:, :, None, :]
    ).astype(BF16).reshape(fsdp, EXP_DEV * slots, TOK_DEV)
    turned = (
        (place[:, :, :, None] == slot_ids) & chosen.transpose(0, 2, 1)[:, :, :, None]
    ).astype(BF16)
    columns = (jnp.arange(experts, dtype=jnp.int32)[None, :] == own_ids[:, None]).astype(F32)

    first_in, q_raw, k_raw, values, squares = project(sp, x_all, gains32, w_all)
    table = angles(seq)
    attended, sums, queries, keys = attend(
        q_raw, k_raw, values, squares, gains_own, table
    )
    mid, second_in, grad_second_half = branch_sum(
        fsdp, attended, wo_s, output_grad[early:], layer_input, gains32
    )

    tokens, grad_taken, unscaled, up_second = token_gather(
        fsdp, sp, second_in, grad_first_half, grad_second_half, picks, down_full,
        w_up[:, :, wide:].reshape(-1, wide),
    )
    up_second = up_second.reshape(sp, EXP_DEV, D // sp, wide)
    received, probs, slot_gates = route(picks, tokens, router_t, columns)
    gated, grad_gate_pre, grad_up_pre, slot_dots = active(
        received, gate_full, up_first, up_second, unscaled, slot_gates
    )
    dots_two = jnp.pad(two_parts(slot_dots, 2), ((0, 0), (0, 0), (0, 126)))
    grad_rows = rows_back(grad_gate_pre, grad_up_pre, gate_full, up_first, up_second)
    second_part, router_two = combine(
        turned, grad_rows, tokens, probs, dots_two, jnp.concatenate([router_t, router_t], axis=0),
        columns,
    )
    grad_router = (router_two[:experts] + router_two[experts:]).T

    def shed(grad):
        return lax.psum_scatter(grad, "sp", scatter_dimension=1, tiled=True)

    grad_down = shed(weight_grad(gated, grad_taken, "down_grad"))
    grad_gate = shed(weight_grad(received, grad_gate_pre, "gate_grad"))
    grad_mid, grad_mid_low, gain_rows, out_part, up_part = token_back(
        fsdp, second_part, gated, down_full, turned, received, grad_up_pre, mid, output_grad, gains32
    )
    grad_up = shed(up_part)

    grad_branch, out_sum, q_scaled, k_scaled, grad_values, dots, gain_qk = branch_back(
        fsdp, sp, grad_mid_low, out_part, wo_s, queries, keys, values, sums, q_raw, k_raw,
        gains_own, table,
    )
    weight_part, grads_low = weight_parts(
        fsdp, q_scaled, k_scaled, q_raw, k_raw, squares, dots, grad_values, first_in, attended, grad_branch
    )

    gain_rows = lax.dynamic_update_slice(
        gain_rows.reshape(8, cols // HEAD_DIM, sp, HEAD_DIM),
        gain_qk.reshape(2, cols // HEAD_DIM, 1, HEAD_DIM),
        (2, 0, s, 0),
    ).reshape(8, D)
    router_part = grad_router.reshape(count, router_size)
    router_part = jnp.pad(router_part, ((0, 0), (0, 1024 - router_size))).reshape(count, 8, 128)
    input_grad, *weight_grads, small = end_exchange(
        fsdp, sp, weight_part, grads_low, w_all, layer_input, grad_mid, gains32, gain_rows, router_part, 8
    )
    *weight_grads, grad_gate, grad_up, grad_down, layer_out = widen(
        mid, out_sum, weight_grads[:3], [weight_grads[3], grad_gate, grad_up, grad_down]
    )
    grad_router_own = small[:8].reshape(1024)[:router_size].reshape(rows, experts)
    first_lane = (f * sp + s) * rows % 128
    grad_gains = lax.dynamic_slice(small[8:12], (0, first_lane), (4, rows))
    return (
        layer_out, input_grad, *weight_grads,
        grad_router_own, grad_gains, grad_gate, grad_up, grad_down,
    )


def solution(mesh):
    both, split = P(("fsdp", "sp"), None), P("fsdp", "sp", None)
    gains = P(None, ("fsdp", "sp"))
    return jax.shard_map(
        body,
        mesh=mesh,
        in_specs=(both,) * 7 + (gains,) + (split,) * 3 + (both,),
        out_specs=(both,) * 7 + (gains,) + (split,) * 3,
        check_vma=False,
    )
```

```python
import functools

import jax
import jax.numpy as jnp
import numpy as np
from jax import lax
from jax.experimental import pallas as pl
from jax.experimental.pallas import tpu as pltpu
from jax.sharding import PartitionSpec as P

D = 2048
HEADS = 16
HEAD_DIM = 128
TOP = 8
EXP_DEV = 2
BLK = 256
TOK_DEV = 256
EPSILON = 1e-05
ROPE_BASE = 10000.0
MASKED = -1000000000.0
SCALE = HEAD_DIM ** (-0.5)
MESH = pl.DeviceIdType.MESH
ANY = pl.BlockSpec(memory_space=pl.ANY)
VMEM = pl.BlockSpec(memory_space=pltpu.VMEM)
VLIM = 60 * 1024 * 1024
F32 = jnp.float32
BF16 = jnp.bfloat16


def remote(src, dst, send_sem, recv_sem, device):
    return pltpu.make_async_remote_copy(
        src_ref=src,
        dst_ref=dst,
        send_sem=send_sem,
        recv_sem=recv_sem,
        device_id=device,
        device_id_type=MESH,
    )


def landed(ref, sem):
    pltpu.make_async_copy(ref, ref, sem).wait()


def signal(sem, device):
    pl.semaphore_signal(sem, inc=1, device_id=device, device_id_type=MESH)


def greet_line(barrier, lines, f, s):
    place, core = f // 2, f % 2
    signal(barrier, (f + 1 - 2 * core, s))

    @pl.when(place > 0)
    def _():
        signal(barrier, (f - 2, s))

    @pl.when(place < lines - 1)
    def _():
        signal(barrier, (f + 2, s))

    return 1 + jnp.where(place > 0, 1, 0) + jnp.where(place < lines - 1, 1, 0)


class LineGather:
    def __init__(self, views, owns, lines, f, s, send, recv):
        self.views, self.owns, self.lines, self.f, self.s = views, owns, lines, f, s
        self.send, self.recv = send, recv
        self.place, self.core = f // 2, f % 2

    def copy(self, v, block, slot, way):
        device = {
            "right": (self.f + 2, self.s),
            "left": (self.f - 2, self.s),
            "partner": (self.f + 1 - 2 * self.core, self.s),
        }[way]
        index = {"right": 0, "left": 1, "partner": 2}[way]
        ref = self.views[v](block)
        own = self.owns[v] if slot == 0 and self.owns[v] is not None else ref
        return remote(own, ref, self.send.at[v, slot, index], self.recv.at[v, block], device)

    def start_own(self, v):
        @pl.when(self.place < self.lines - 1)
        def _():
            self.copy(v, self.f, 0, "right").start()

        @pl.when(self.place > 0)
        def _():
            self.copy(v, self.f, 0, "left").start()

        self.copy(v, self.f, 0, "partner").start()

    def forward(self, v, k):
        place, lines = self.place, self.lines

        @pl.when(place >= k)
        def _():
            block = self.f - 2 * k
            landed(self.views[v](block), self.recv.at[v, block])

            @pl.when(place < lines - 1)
            def _():
                self.copy(v, block, k, "right").start()

            self.copy(v, block, k, "partner").start()

        @pl.when(place + k < lines)
        def _():
            block = self.f + 2 * k
            landed(self.views[v](block), self.recv.at[v, block])

            @pl.when(place > 0)
            def _():
                self.copy(v, block, lines - 1 + k, "left").start()

            self.copy(v, block, lines - 1 + k, "partner").start()

    def finish(self, v):
        place, lines = self.place, self.lines
        for line in range(lines):
            block = 2 * line + 1 - self.core
            landed(self.views[v](block), self.recv.at[v, block])
        self.copy(v, self.f, 0, "partner").wait_send()

        @pl.when(place < lines - 1)
        def _():
            self.copy(v, self.f, 0, "right").wait_send()

        @pl.when(place > 0)
        def _():
            self.copy(v, self.f, 0, "left").wait_send()

        for k in range(1, lines):

            @pl.when(place >= k)
            def _():
                block = self.f - 2 * k

                @pl.when(place < lines - 1)
                def _():
                    self.copy(v, block, k, "right").wait_send()

                self.copy(v, block, k, "partner").wait_send()

            @pl.when(place + k < lines)
            def _():
                block = self.f + 2 * k

                @pl.when(place > 0)
                def _():
                    self.copy(v, block, lines - 1 + k, "left").wait_send()

                self.copy(v, block, lines - 1 + k, "partner").wait_send()


def line_sems(arrays, fsdp):
    lines = fsdp // 2
    return [
        pltpu.SemaphoreType.DMA((arrays, 2 * lines, 3)),
        pltpu.SemaphoreType.DMA((arrays, fsdp)),
    ]


def add_rows(dst, a, b, rows):
    def step(i, carry):
        at = pl.ds(pl.multiple_of(i * 32, 32), 32)
        dst[at, :] = a[at, :].astype(dst.dtype) + b[at, :].astype(dst.dtype)
        return carry

    lax.fori_loop(0, rows // 32, step, 0)


class LineReduce:
    def __init__(self, p_ref, scratch, lines, f, s):
        self.p_ref, self.lines, self.f, self.s = p_ref, lines, f, s
        self.own, self.paired, self.got, self.last = scratch[:4]
        self.psend, self.precv, self.send, self.recv, self.final, self.local = scratch[4:]
        self.place, self.core = f // 2, f % 2
        self.rows = p_ref.shape[1]
        self.order = []
        for n in range(lines):
            for d in (lines - 1 - n, n):
                if d not in self.order:
                    self.order.append(d)

    @staticmethod
    def scratch(fsdp, block):
        lines = fsdp // 2
        dma = pltpu.SemaphoreType.DMA
        return [
            pltpu.VMEM((lines,) + block, BF16),
            pltpu.VMEM((lines,) + block, BF16),
            pltpu.VMEM((lines,) + block, BF16),
            pltpu.VMEM(block, BF16),
            dma((lines,)), dma((lines,)), dma((lines, 4)), dma((lines, 4)), dma((4,)), dma((lines,)),
        ]

    def load(self, i):
        return pltpu.make_async_copy(self.p_ref.at[2 * i + self.core], self.own.at[i], self.local.at[i])

    def swap(self, i):
        return remote(
            self.p_ref.at[2 * i + 1 - self.core], self.paired.at[i], self.psend.at[i],
            self.precv.at[i], (self.f + 1 - 2 * self.core, self.s),
        )

    def part(self, ref, h):
        return ref.at[pl.ds(h * (self.rows // 4), self.rows // 4), :]

    def right(self, d, last, h):
        dst = self.last if last else self.got.at[d]
        sem = self.final.at[h] if last else self.recv.at[d, h]
        own = self.part(self.own.at[d], h)
        return remote(own, self.part(dst, h), self.send.at[d, h], sem, (self.f + 2, self.s))

    def left(self, d, h):
        own, dst = self.part(self.own.at[d], h), self.part(self.got.at[d], h)
        return remote(own, dst, self.send.at[d, h], self.recv.at[d, h], (self.f - 2, self.s))

    def add_got(self, d, h):
        own, got = self.part(self.own.at[d], h), self.part(self.got.at[d], h)
        landed(got, self.recv.at[d, h])
        add_rows(own, own, got, self.rows // 4)

    def start(self):
        for i in self.order[:2]:
            self.swap(i).start()
        for i in self.order:
            self.load(i).start()
        self.added = 0
        self.add_pairs(2)

    def add_pairs(self, until):
        for i in self.order[self.added : until]:
            self.load(i).wait()
            landed(self.paired.at[i], self.precv.at[i])
            add_rows(self.own.at[i], self.own.at[i], self.paired.at[i], self.rows)
        self.added = max(self.added, until)

    def step(self, t):
        place, lines = self.place, self.lines
        d = lines - 1 - t + place
        e = t - (lines - 1 - place)
        for h in range(4):

            @pl.when(t >= place)
            def _():
                @pl.when(place > 0)
                def _():
                    self.add_got(d, h)

                @pl.when(d == place + 1)
                def _():
                    self.right(d, True, h).start()

                @pl.when(d != place + 1)
                def _():
                    self.right(d, False, h).start()

            @pl.when(e >= 0)
            def _():
                @pl.when(place < lines - 1)
                def _():
                    self.add_got(e, h)

                self.left(e, h).start()

        if t == 0:
            for i in self.order[2:]:
                self.swap(i).start()
        self.add_pairs(2 * t + 4)

    def finish(self, out_ref):
        place, lines, rows = self.place, self.lines, self.rows

        def total(*extra):
            def step(i, carry):
                at = pl.ds(pl.multiple_of(i * 32, 32), 32)
                value = self.own[place, at, :].astype(F32)
                for ref in extra:
                    value += ref[at, :].astype(F32)
                out_ref[at, :] = value.astype(out_ref.dtype)
                return carry

            lax.fori_loop(0, rows // 32, step, 0)

        @pl.when(place > 0)
        def _():
            for h in range(4):
                landed(self.part(self.last, h), self.final.at[h])

        @pl.when(place < lines - 1)
        def _():
            for h in range(4):
                landed(self.part(self.got.at[place], h), self.recv.at[place, h])

        @pl.when(place == 0)
        def _():
            total(self.got.at[place])

        @pl.when(place == lines - 1)
        def _():
            total(self.last)

        @pl.when(jnp.logical_and(place > 0, place < lines - 1))
        def _():
            total(self.last, self.got.at[place])

        for i in range(lines):
            self.swap(i).wait_send()

            @pl.when(place < i)
            def _():
                for h in range(4):
                    self.right(i, False, h).wait_send()

            @pl.when(place > i)
            def _():
                for h in range(4):
                    self.left(i, h).wait_send()


class PlaneGather:
    def __init__(self, own, out, f, s, send, recv):
        self.own, self.out, self.f, self.s, self.send, self.recv = own, out, f, s, send, recv
        self.rows = own.shape[0]
        self.half = self.rows // 2

    def at(self, place, first, size):
        return self.out.at[pl.ds(pl.multiple_of(place * self.rows + first, self.half), size), :]

    def near(self, k):
        return remote(
            self.own, self.at(self.s, 0, self.rows), self.send.at[k - 1], self.recv.at[k - 1],
            (self.f, self.s ^ k),
        )

    def on(self, k):
        ref = self.at(self.s ^ k, (k - 1) * self.half, self.half)
        return remote(ref, ref, self.send.at[k + 1], self.recv.at[k + 1], (self.f, self.s ^ (3 - k)))

    def start(self):
        self.near(1).start()
        self.near(2).start()

    def forward(self):
        for k in (1, 2):
            landed(self.at(self.s ^ k, 0, self.rows), self.recv.at[k - 1])
            self.on(k).start()

    def finish(self):
        landed(self.at(self.s ^ 3, 0, self.half), self.recv.at[2])
        landed(self.at(self.s ^ 3, self.half, self.half), self.recv.at[3])
        for k in (1, 2):
            self.near(k).wait_send()
            self.on(k).wait_send()


class AnyGather:
    def __init__(self, own, out, f, s, sp, send, recv):
        self.own, self.out, self.f, self.s, self.sp = own, out, f, s, sp
        self.send, self.recv = send, recv
        self.rows = own.shape[0]

    def at(self, place, first, size):
        return self.out.at[pl.ds(pl.multiple_of(place * self.rows + first, size), size), :]

    def copy(self, k):
        dst = self.at(self.s, 0, self.rows)
        return remote(self.own, dst, self.send.at[k], self.recv.at[k], (self.f, self.s ^ k))

    def start(self):
        for k in range(1, self.sp):
            self.copy(k).start()

    def forward(self):
        pass

    def finish(self):
        for k in range(1, self.sp):
            landed(self.at(self.s ^ k, 0, self.rows), self.recv.at[k])
            self.copy(k).wait_send()


class AnyReduce:
    def __init__(self, p_ref, out_ref, scratch, f, s, sp):
        self.p_ref, self.out_ref, self.f, self.s, self.sp = p_ref, out_ref, f, s, sp
        self.own, self.got, self.send, self.recv, self.local = scratch

    @staticmethod
    def scratch(block, sp):
        dma = pltpu.SemaphoreType.DMA
        return [
            pltpu.VMEM(block, BF16), pltpu.VMEM((sp,) + block, BF16), dma((sp,)), dma((sp,)), dma,
        ]

    def copy(self, k):
        d = self.s ^ k
        return remote(
            self.p_ref.at[d], self.got.at[k], self.send.at[k], self.recv.at[k], (self.f, d)
        )

    def load(self):
        return pltpu.make_async_copy(self.p_ref.at[self.s], self.own, self.local)

    def start(self, make=lambda d: None):
        for k in range(self.sp - 1, 0, -1):
            make(self.s ^ k)
            self.copy(k).start()
        make(self.s)
        self.load().start()

    def forward(self):
        self.load().wait()

    def finish(self):
        rows = self.own.shape[0]
        for k in range(1, self.sp):
            landed(self.got.at[k], self.recv.at[k])
            add_rows(self.out_ref, self.own if k == 1 else self.out_ref, self.got.at[k], rows)
        for k in range(1, self.sp):
            self.copy(k).wait_send()


def plane_gather_of(own, out, f, s, sp, send, recv):
    if sp == 4:
        return PlaneGather(own, out, f, s, send, recv)
    return AnyGather(own, out, f, s, sp, send, recv)


def plane_reduce_of(p_ref, out_ref, scratch, f, s, sp):
    if sp == 4:
        return PlaneReduce(p_ref, out_ref, scratch, f, s)
    return AnyReduce(p_ref, out_ref, scratch, f, s, sp)


def plane_scratch(block, sp):
    return PlaneReduce.scratch(block) if sp == 4 else AnyReduce.scratch(block, sp)


class PlaneReduce:
    WAYS = ((0, 1, 1), (1, 2, 2))

    def __init__(self, p_ref, out_ref, scratch, f, s):
        self.p_ref, self.out_ref, self.f, self.s = p_ref, out_ref, f, s
        self.own, self.got, self.got_on, self.send, self.recv, self.local = scratch
        self.half = p_ref.shape[1] // 2

    @staticmethod
    def scratch(block):
        dma = pltpu.SemaphoreType.DMA
        return [
            pltpu.VMEM((3,) + block, BF16), pltpu.VMEM((2,) + block, BF16),
            pltpu.VMEM(block, BF16), dma((2, 3)), dma((2, 3)), dma((3,)),
        ]

    def part(self, ref, h):
        return ref.at[pl.ds(h * self.half, self.half), :]

    def load(self, n):
        d = (self.s, self.s ^ 2, self.s ^ 1)[n]
        return pltpu.make_async_copy(self.p_ref.at[d], self.own.at[n], self.local.at[n])

    def hop(self, h, k, far):
        d = self.s ^ 3 if far else self.s ^ k
        n = 0 if far else 1
        return remote(
            self.part(self.p_ref.at[d], h), self.part(self.got.at[1 - n], h), self.send.at[h, n],
            self.recv.at[h, n], (self.f, self.s ^ k),
        )

    def on(self, h, k, n):
        return remote(
            self.part(self.own.at[n], h), self.part(self.got_on, h), self.send.at[h, 2],
            self.recv.at[h, 2], (self.f, self.s ^ (3 - k)),
        )

    def start(self, make=lambda d: None):
        make(self.s ^ 3)
        for h, k, _ in self.WAYS:
            self.hop(h, k, True).start()
        make(self.s ^ 1)
        make(self.s ^ 2)
        for h, k, _ in self.WAYS:
            self.hop(h, k, False).start()
        make(self.s)
        for n in range(3):
            self.load(n).start()

    def forward(self):
        for n in range(3):
            self.load(n).wait()
        for h, k, n in self.WAYS:
            mine = self.part(self.own.at[n], h)
            landed(self.part(self.got.at[1], h), self.recv.at[h, 0])
            add_rows(mine, mine, self.part(self.got.at[1], h), self.half)
            self.on(h, k, n).start()

    def finish(self):
        for h in (0, 1):
            landed(self.part(self.got.at[0], h), self.recv.at[h, 1])
            add_rows(
                self.part(self.out_ref, h), self.part(self.own.at[0], h), self.part(self.got.at[0], h),
                self.half,
            )
        for h in (0, 1):
            landed(self.part(self.got_on, h), self.recv.at[h, 2])
            out = self.part(self.out_ref, h)
            add_rows(out, out, self.part(self.got_on, h), self.half)
        for h, k, n in self.WAYS:
            self.hop(h, k, True).wait_send()
            self.hop(h, k, False).wait_send()
            self.on(h, k, n).wait_send()


def greet_plane(barrier, f, s, sp):
    ways = (1, 2) if sp == 4 else range(1, sp)
    for k in ways:
        signal(barrier, (f, s ^ k))
    return len(ways)


def greet_all(barrier, me, count, sp):
    def greet(i, carry):
        other = lax.rem(me + i, count)
        signal(barrier, (other // sp, lax.rem(other, sp)))
        return carry

    lax.fori_loop(1, count, greet, 0)


def rows_view(ref, rows):
    return lambda b: ref.at[pl.ds(pl.multiple_of(b * rows, rows), rows), :]


def block_view(ref):
    return lambda b: ref.at[b]


def comm_params(number):
    return pltpu.CompilerParams(
        collective_id=number, has_side_effects=True, vmem_limit_bytes=VLIM
    )


def row_target(i, rows, sp):
    parts = HEAD_DIM // rows
    head, part = i // parts, lax.rem(i, parts)
    return head // sp * parts + part, lax.rem(head, sp)


def row_owner(f, s, rows, sp):
    parts = HEAD_DIM // rows
    return (f // parts * sp + s) * parts + lax.rem(f, parts)


def start_kernel(
    fsdp, sp, x_ref, w_ref, wo_ref, g_ref, misc_ref, routes_ref,
    x_all, w_all, wo_all, g_all, misc_all, routes_all,
    send, recv, xsend, xrecv, psend, precv, wsend, wrecv, msend, mrecv, rsend, rrecv, local, wlocal,
):
    f, s = lax.axis_index("fsdp"), lax.axis_index("sp")
    count, lines = fsdp * sp, fsdp // 2
    me = f * sp + s
    rows = w_ref.shape[1]
    heads = D // sp // HEAD_DIM
    barrier = pltpu.get_barrier_semaphore()

    def w_block(s_to, g):
        at = pl.multiple_of((g * sp + s_to) * HEAD_DIM, HEAD_DIM)
        return w_ref.at[:, :, pl.ds(at, HEAD_DIM)]

    def w_rows(i, g):
        at = pl.ds(pl.multiple_of(i * rows, rows), rows)
        return w_all.at[:, at, pl.ds(g * HEAD_DIM, HEAD_DIM)]

    def w_view(b):
        size = rows * sp
        return w_all.at[:, pl.ds(pl.multiple_of(b * size, size), size), :]

    wo_view = rows_view(wo_all, rows)
    x_view = rows_view(x_all, TOK_DEV)
    w_owns = [
        pltpu.make_async_copy(w_block(s, g), w_rows(me, g), wlocal.at[g]) for g in range(heads)
    ]
    owns = [
        pltpu.make_async_copy(x_ref, x_view(s), local.at[0]),
        pltpu.make_async_copy(misc_ref, misc_all.at[me], local.at[1]),
        pltpu.make_async_copy(routes_ref, routes_all.at[f], local.at[2]),
        pltpu.make_async_copy(g_ref, g_all.at[f], local.at[3]),
    ]
    for copy in w_owns + owns:
        copy.start()
    greet_all(barrier, me, count, sp)
    pl.semaphore_wait(barrier, count - 1)

    line = LineGather([w_view, wo_view, block_view(g_all)], [None, None, g_ref], lines, f, s, send, recv)
    line.start_own(2)
    w_copies = []
    for k in range(sp - 1, 0, -1):
        s_to = s ^ k
        for g in range(heads):
            copy = remote(
                w_block(s_to, g), w_rows(me, g), psend.at[k, g], precv.at[k, g], (f, s_to)
            )
            copy.start()
            w_copies.append(copy)
    target_f, target_s = row_target(me, rows, sp)
    stays = jnp.logical_and(target_s == s, target_f == f)
    wo_copy = remote(wo_ref, wo_view(target_f), wsend, wrecv, (target_f, target_s))
    wo_own = pltpu.make_async_copy(wo_ref, wo_view(f), wrecv)

    @pl.when(stays)
    def _():
        wo_own.start()

    @pl.when(jnp.logical_not(stays))
    def _():
        wo_copy.start()

    def misc_copy(i):
        other = lax.rem(me + i, count)
        return remote(
            misc_ref, misc_all.at[me], msend.at[i], mrecv.at[me], (other // sp, lax.rem(other, sp))
        )

    def misc_go(i, carry):
        misc_copy(i).start()
        return carry

    lax.fori_loop(1, count, misc_go, 0)

    def routes_copy(i):
        other = lax.rem(f + i, fsdp)
        return remote(routes_ref, routes_all.at[f], rsend.at[i], rrecv.at[f], (other, s))

    def routes_go(i, carry):
        routes_copy(i).start()
        return carry

    lax.fori_loop(1, fsdp, routes_go, 0)

    for copy in w_owns:
        copy.wait()
    for k in range(1, sp):
        for g in range(heads):
            landed(w_rows(f * sp + (s ^ k), g), precv.at[k, g])
    line.start_own(0)
    tokens = plane_gather_of(x_ref, x_all, f, s, sp, xsend, xrecv)
    tokens.start()
    landed(wo_view(f), wrecv)
    line.start_own(1)
    for k in range(1, lines):
        for v in (2, 0, 1):
            line.forward(v, k)
        if k == min(2, lines - 1):
            tokens.forward()
    for v in range(3):
        line.finish(v)
    tokens.finish()

    def misc_end(i, carry):
        misc_copy(i).wait_send()
        other = lax.rem(me + i, count)
        landed(misc_all.at[other], mrecv.at[other])
        return carry

    lax.fori_loop(1, count, misc_end, 0)

    def routes_end(i, carry):
        routes_copy(i).wait_send()
        other = lax.rem(f + i, fsdp)
        landed(routes_all.at[other], rrecv.at[other])
        return carry

    lax.fori_loop(1, fsdp, routes_end, 0)
    for copy in w_copies:
        copy.wait_send()

    @pl.when(jnp.logical_not(stays))
    def _():
        wo_copy.wait_send()

    for copy in owns:
        copy.wait()


def gather_start(fsdp, sp, x, w, wo, g, misc, routes):
    count = fsdp * sp
    heads = D // sp // HEAD_DIM
    dma = pltpu.SemaphoreType.DMA
    return pl.pallas_call(
        functools.partial(start_kernel, fsdp, sp),
        out_shape=(
            jax.ShapeDtypeStruct((sp * TOK_DEV, D), BF16),
            jax.ShapeDtypeStruct((3, D, D // sp), BF16),
            jax.ShapeDtypeStruct((D // sp, D), BF16),
            jax.ShapeDtypeStruct((fsdp,) + g.shape, BF16),
            jax.ShapeDtypeStruct((count,) + misc.shape, BF16),
            jax.ShapeDtypeStruct((fsdp,) + routes.shape, jnp.int32),
        ),
        in_specs=[VMEM] * 6,
        out_specs=[ANY] * 6,
        scratch_shapes=line_sems(3, fsdp)
        + [
            dma((sp,)), dma((sp,)), dma((sp, heads)), dma((sp, heads)), dma, dma,
            dma((count,)), dma((count,)), dma((fsdp,)), dma((fsdp,)), dma((4,)), dma((heads,)),
        ],
        compiler_params=comm_params(0),
        name="gather_start",
    )(x, w, wo, g, misc, routes)


def branch_kernel(
    fsdp, sp, a_ref, w_ref, g_ref, x_ref, gain, out_ref, second_ref, g_all, terms, *scratch
):
    f, s = lax.axis_index("fsdp"), lax.axis_index("sp")
    lines = fsdp // 2
    barrier = pltpu.get_barrier_semaphore()
    expected = greet_line(barrier, lines, f, s) + greet_plane(barrier, f, s, sp)
    send, recv, own_sem = scratch[-3:]
    own = pltpu.make_async_copy(g_ref, g_all.at[f], own_sem)
    own.start()
    pl.semaphore_wait(barrier, expected)
    plane = plane_reduce_of(terms, out_ref, scratch[:-3], f, s, sp)
    line = LineGather([block_view(g_all)], [g_ref], lines, f, s, send, recv)
    line.start_own(0)

    def branch_of(d):
        rows = pl.ds(pl.multiple_of(d * TOK_DEV, TOK_DEV), TOK_DEV)
        for n in range(D // 512):
            at = pl.ds(n * 512, 512)
            terms[d, :, at] = dot_nn(a_ref[rows, :], w_ref[:, at]).astype(BF16)

    plane.start(branch_of)
    for k in range(1, lines):
        line.forward(0, k)
        if k == min(2, lines - 1):
            plane.forward()
    plane.finish()

    def norm(i, carry):
        at = pl.ds(pl.multiple_of(i * 32, 32), 32)
        mid = x_ref[at, :].astype(F32) + out_ref[at, :]
        out_ref[at, :] = mid
        inverse = lax.rsqrt(jnp.mean(mid * mid, axis=-1, keepdims=True) + EPSILON)
        second_ref[at, :] = (mid * inverse * gain[1:2, :]).astype(BF16)
        return carry

    lax.fori_loop(0, TOK_DEV // 32, norm, 0)
    line.finish(0)
    own.wait()


def branch_sum(fsdp, attended, w, g, x, gains):
    sp, block = attended.shape[0] // TOK_DEV, x.shape
    return pl.pallas_call(
        functools.partial(branch_kernel, fsdp, sp),
        out_shape=(
            jax.ShapeDtypeStruct(block, F32),
            jax.ShapeDtypeStruct(block, BF16),
            jax.ShapeDtypeStruct((fsdp,) + g.shape, BF16),
        ),
        in_specs=[VMEM] * 5,
        out_specs=[VMEM, VMEM, ANY],
        scratch_shapes=[pltpu.VMEM((sp,) + block, BF16)]
        + plane_scratch(block, sp) + line_sems(1, fsdp) + [pltpu.SemaphoreType.DMA],
        compiler_params=comm_params(2),
        name="branch_sum",
    )(attended, w, g, x, gains)


def token_kernel(
    fsdp, sp, x_ref, g_first, g_second, picks, w_ref, up_ref, out_ref, taken_ref, back_ref, up_all,
    g_buf, w_buf, taken, back, send, recv, local, loads, stores, back_sem, usend, urecv, ulocal,
):
    f, s = lax.axis_index("fsdp"), lax.axis_index("sp")
    lines = fsdp // 2
    parts = 2
    size = TOK_DEV // parts
    early, later = g_first.shape[1], g_second.shape[1]
    slots = picks.shape[1] // EXP_DEV
    ff = w_ref.shape[1]
    barrier = pltpu.get_barrier_semaphore()
    expected = greet_line(barrier, lines, f, s) + greet_plane(barrier, f, s, sp)
    plane = plane_gather_of(up_ref, up_all, f, s, sp, usend, urecv)
    up_own = pltpu.make_async_copy(up_ref, plane.at(s, 0, up_ref.shape[0]), ulocal)
    up_own.start()
    own = pltpu.make_async_copy(x_ref, out_ref.at[f], local)
    own.start()
    reads = [
        pltpu.make_async_copy(g_first, g_buf.at[:, pl.ds(0, early), :], loads.at[0]),
        pltpu.make_async_copy(g_second, g_buf.at[:, pl.ds(early, later), :], loads.at[1]),
        pltpu.make_async_copy(w_ref, w_buf, loads.at[2]),
    ]
    for copy in reads:
        copy.start()
    pl.semaphore_wait(barrier, expected)

    def view(part):
        return lambda b: out_ref.at[b, pl.ds(part * size, size), :]

    owns = [x_ref.at[pl.ds(p * size, size), :] for p in range(parts)]
    line = LineGather([view(p) for p in range(parts)], owns, lines, f, s, send, recv)
    for p in range(parts):
        line.start_own(p)
    plane.start()

    def take_all():
        reads[0].wait()
        reads[1].wait()

        def block(b, carry):
            for n in range(D // 512):
                at = pl.ds(n * 512, 512)
                got = dot_nn(picks[b], g_buf[b, :, at]).astype(BF16)
                for e in range(EXP_DEV):
                    to = pl.ds(pl.multiple_of(b * slots, 16), slots)
                    taken[e, to, at] = got[e * slots : (e + 1) * slots]
            return carry

        lax.fori_loop(0, fsdp, block, 0)
        for e in range(EXP_DEV):
            pltpu.make_async_copy(taken.at[e], taken_ref.at[e], stores.at[e]).start()

    def back_copy(e, j, slot):
        at = pl.ds(pl.multiple_of(j * FT, FT), FT)
        return pltpu.make_async_copy(back.at[slot], back_ref.at[e, :, at], back_sem.at[slot])

    def back_of(e):
        if e == 0:
            reads[2].wait()
        for j in range(ff // FT):
            slot = j % 2
            if e > 0 or j > 1:
                back_copy(e, j, slot).wait()
            back[slot] = dot_nt(taken[e], w_buf[e, pl.ds(j * FT, FT), :])
            back_copy(e, j, slot).start()

    work = [take_all] + [functools.partial(back_of, e) for e in range(EXP_DEV)]
    for k in range(1, lines):
        if k - 1 < len(work):
            work[k - 1]()
        for p in range(parts):
            line.forward(p, k)
        if k == min(2, lines - 1):
            plane.forward()
    for unit in work[lines - 1 :]:
        unit()
    for p in range(parts):
        line.finish(p)
    plane.finish()
    up_own.wait()
    own.wait()
    for slot in range(2):
        back_copy(0, slot, slot).wait()
    for e in range(EXP_DEV):
        pltpu.make_async_copy(taken.at[e], taken_ref.at[e], stores.at[e]).wait()


def token_gather(fsdp, sp, x, g_first, g_second, picks, w_down, up):
    slots = picks.shape[1] // EXP_DEV
    total = fsdp * slots
    ff = w_down.shape[1]
    dma = pltpu.SemaphoreType.DMA
    return pl.pallas_call(
        functools.partial(token_kernel, fsdp, sp),
        out_shape=(
            jax.ShapeDtypeStruct((fsdp, TOK_DEV, D), BF16),
            jax.ShapeDtypeStruct((EXP_DEV, total, D), BF16),
            jax.ShapeDtypeStruct((EXP_DEV, total, ff), F32),
            jax.ShapeDtypeStruct((sp * up.shape[0], up.shape[1]), BF16),
        ),
        in_specs=[VMEM, ANY, ANY, VMEM, ANY, VMEM],
        out_specs=[ANY, ANY, ANY, ANY],
        scratch_shapes=[
            pltpu.VMEM((fsdp, TOK_DEV, D), BF16),
            pltpu.VMEM((EXP_DEV, ff, D), BF16),
            pltpu.VMEM((EXP_DEV, total, D), BF16),
            pltpu.VMEM((2, total, FT), F32),
        ]
        + line_sems(2, fsdp)
        + [dma, dma((3,)), dma((EXP_DEV,)), dma((2,)), dma((sp,)), dma((sp,)), dma],
        compiler_params=comm_params(3),
        name="token_gather",
    )(x, g_first, g_second, picks, w_down, up)


def token_back_kernel(
    fsdp, p_ref, gated_ref, w_ref, turned, x_ref, gu_ref, mid_ref, g_ref, gain,
    out_ref, low_ref, gain_out, part_ref, wu_ref, wide, narrow, w_buf, tile, grad_tile, loads, tile_sem, grad_sem, *scratch,
):
    f, s = lax.axis_index("fsdp"), lax.axis_index("sp")
    lines = fsdp // 2
    slots = turned.shape[3]
    height = grad_tile.shape[1]
    barrier = pltpu.get_barrier_semaphore()
    expected = greet_line(barrier, lines, f, s)
    reads = [
        pltpu.make_async_copy(gated_ref, narrow, loads.at[0]),
        pltpu.make_async_copy(w_ref.at[0], w_buf, loads.at[1]),
        pltpu.make_async_copy(x_ref, wide, loads.at[2]),
        pltpu.make_async_copy(gu_ref, narrow, loads.at[3]),
        pltpu.make_async_copy(w_ref.at[1], w_buf, loads.at[1]),
    ]
    reads[0].start()
    reads[1].start()
    pl.semaphore_wait(barrier, expected)
    line = LineReduce(p_ref, scratch, lines, f, s)
    line.start()

    def down_of(e):
        if e == 0:
            reads[0].wait()
            reads[1].wait()
        else:
            reads[4].wait()

        def columns(n, carry):
            at = pl.ds(pl.multiple_of(n * 512, 512), 512)
            wide[e, :, at] = dot_nn(narrow[e], w_buf[:, at]).astype(BF16)
            return carry

        lax.fori_loop(0, D // 512, columns, 0)
        if e == 0:
            reads[4].start()

    def tile_copy(b, slot):
        return pltpu.make_async_copy(tile.at[slot], part_ref.at[b], tile_sem.at[slot])

    def sum_all():
        reads[3].start()

        def pair(i, carry):
            for slot in range(2):
                b = 2 * i + slot

                @pl.when(i > 0)
                def _():
                    tile_copy(b, slot).wait()

                for n in range(D // 512):
                    at = pl.ds(n * 512, 512)
                    summed = jnp.zeros((TOK_DEV, 512), F32)
                    for e in range(EXP_DEV):
                        rows = wide[e, pl.ds(pl.multiple_of(b * slots, 16), slots), at]
                        summed += dot_nn(turned[b, e], rows)
                    tile[slot, :, at] = summed.astype(BF16)
                tile_copy(b, slot).start()
            return carry

        lax.fori_loop(0, fsdp // 2, pair, 0)
        reads[2].start()

    def grad_copy(e, i, slot):
        at = pl.ds(pl.multiple_of(i * height, height), height)
        return pltpu.make_async_copy(grad_tile.at[slot], wu_ref.at[e, at, :], grad_sem.at[slot])

    def grad_of(e):
        if e == 0:
            reads[2].wait()
            reads[3].wait()

        def pair(i, carry):
            for slot in range(2):
                part = 2 * i + slot

                def before():
                    grad_copy(e, part, slot).wait()

                if e == 0:
                    pl.when(i > 0)(before)
                else:
                    before()
                at = pl.ds(pl.multiple_of(part * height, height), height)
                grad_tile[slot] = dot_tn(wide[e, :, at], narrow[e]).astype(BF16)
                grad_copy(e, part, slot).start()
            return carry

        lax.fori_loop(0, D // height // 2, pair, 0)

    work = [functools.partial(down_of, e) for e in range(EXP_DEV)] + [sum_all]
    work += [functools.partial(grad_of, e) for e in range(EXP_DEV)]
    done = 0
    for t in range(lines - 1):
        line.step(t)
        until = (t + 1) * len(work) // (lines - 1)
        for unit in work[done:until]:
            unit()
        done = until
    line.finish(out_ref)
    gain_out[...] = jnp.zeros_like(gain_out)

    def norm_back(i, carry):
        at = pl.ds(pl.multiple_of(i * 32, 32), 32)
        mid = mid_ref[at, :]
        inverse = lax.rsqrt(jnp.mean(mid * mid, axis=-1, keepdims=True) + EPSILON)
        normed = mid * inverse
        grad_y = out_ref[at, :]
        scaled = grad_y * gain[1:2, :]
        mean = jnp.mean(scaled * normed, axis=-1, keepdims=True)
        grad = g_ref[at, :].astype(F32) + inverse * (scaled - normed * mean)
        out_ref[at, :] = grad
        low_ref[at, :] = grad.astype(BF16)
        gain_out[1:2, :] += jnp.sum(grad_y * normed, axis=0, keepdims=True)
        return carry

    lax.fori_loop(0, TOK_DEV // 32, norm_back, 0)
    for slot in range(2):
        tile_copy(slot, slot).wait()
        grad_copy(0, slot, slot).wait()


def token_back(fsdp, partial, gated, w_down, turned, received, grad_up_pre, mid, g, gains):
    block = partial.shape[1:]
    total, ff = gated.shape[1:]
    height = 256
    dma = pltpu.SemaphoreType.DMA
    return pl.pallas_call(
        functools.partial(token_back_kernel, fsdp),
        out_shape=(
            jax.ShapeDtypeStruct(block, F32),
            jax.ShapeDtypeStruct(block, BF16),
            jax.ShapeDtypeStruct((8, D), F32),
            jax.ShapeDtypeStruct(partial.shape, BF16),
            jax.ShapeDtypeStruct((EXP_DEV, D, ff), BF16),
        ),
        in_specs=[ANY, ANY, ANY, VMEM, ANY, ANY, VMEM, VMEM, VMEM],
        out_specs=[VMEM, VMEM, VMEM, ANY, ANY],
        scratch_shapes=[
            pltpu.VMEM((EXP_DEV, total, D), BF16),
            pltpu.VMEM((EXP_DEV, total, ff), BF16),
            pltpu.VMEM((ff, D), BF16),
            pltpu.VMEM((2,) + block, BF16),
            pltpu.VMEM((2, height, ff), BF16),
            dma((4,)),
            dma((2,)),
            dma((2,)),
        ]
        + LineReduce.scratch(fsdp, block),
        compiler_params=comm_params(4),
        name="token_back",
    )(partial, gated, w_down, turned, received, grad_up_pre, mid, g, gains)


class PlaneSum:
    def __init__(self, scratch, f, s, sp):
        self.own, self.got, self.send, self.recv = scratch
        self.f, self.s, self.sp = f, s, sp

    @staticmethod
    def scratch(seq, sp):
        dma = pltpu.SemaphoreType.DMA
        return [
            pltpu.VMEM((8, seq), F32), pltpu.VMEM((sp, 8, seq), F32), dma((sp,)), dma((sp,)),
        ]

    def greet(self, barrier):
        for k in range(1, self.sp):
            signal(barrier, (self.f, self.s ^ k))
        return self.sp - 1

    def copy(self, k):
        return remote(
            self.own, self.got.at[k], self.send.at[k], self.recv.at[k], (self.f, self.s ^ k)
        )

    def start(self, x_ref):
        self.own[...] = x_ref[...].T[:8]
        for k in range(1, self.sp):
            self.copy(k).start()

    def finish(self, out_ref):
        for k in range(1, self.sp):
            self.copy(k).wait()
        terms = [self.own[...]] + [self.got[k] for k in range(1, self.sp)]
        while len(terms) > 1:
            terms = [terms[i] + terms[i + 1] for i in range(0, len(terms), 2)]
        seq = out_ref.shape[0]
        out_ref[...] = jnp.concatenate([terms[0], jnp.zeros((120, seq), F32)], axis=0).T


def end_kernel(
    fsdp, sp, p_ref, low_ref, w_ref, x_ref, mid_ref, gain, gains_in, router_ref,
    grad_out, qkv_0, qkv_1, qkv_2, o_out, small_out,
    first, low_in, w_buf, back, low, o_low, gain_sum, pay, small, loads,
    qsend, qrecv, osend, orecv, msend, mrecv, local, *scratch,
):
    f, s = lax.axis_index("fsdp"), lax.axis_index("sp")
    count, lines = fsdp * sp, fsdp // 2
    me = f * sp + s
    rows, cols = o_low.shape[0], D // sp
    height = D // fsdp
    barrier = pltpu.get_barrier_semaphore()
    greet_all(barrier, me, count, sp)
    reads = [
        pltpu.make_async_copy(low_ref, low_in, loads.at[0]),
        pltpu.make_async_copy(w_ref, w_buf, loads.at[1]),
    ]
    for copy in reads:
        copy.start()
    pl.semaphore_wait(barrier, count - 1)
    plane_parts = 6 if sp == 4 else 5
    plane = plane_reduce_of(first, back, scratch[:plane_parts], f, s, sp)
    line = LineReduce(p_ref, scratch[plane_parts:], lines, f, s)
    line.start()

    def first_grads():
        for copy in reads:
            copy.wait()

        def columns(n, carry):
            at = pl.ds(pl.multiple_of(n * 256, 256), 256)
            for d in range(sp):
                rows_at = slice(d * TOK_DEV, (d + 1) * TOK_DEV)
                total = dot_nt(low_in[rows_at, :cols], w_buf[0, at, :])
                total += dot_nt(low_in[rows_at, cols : 2 * cols], w_buf[1, at, :])
                total += dot_nt(low_in[rows_at, 2 * cols :], w_buf[2, at, :])
                first[d, :, at] = total.astype(BF16)
            return carry

        lax.fori_loop(0, D // 256, columns, 0)

    def input_grads():
        gain_sum[...] = jnp.zeros_like(gain_sum)

        def chunk(i, carry):
            at = pl.ds(pl.multiple_of(i * 32, 32), 32)
            x = x_ref[at, :].astype(F32)
            inverse = lax.rsqrt(jnp.mean(x * x, axis=-1, keepdims=True) + EPSILON)
            normed = x * inverse
            grad_y = back[at, :]
            scaled = grad_y * gain[0:1, :]
            mean = jnp.mean(scaled * normed, axis=-1, keepdims=True)
            grad_out[at, :] = mid_ref[at, :] + inverse * (scaled - normed * mean)
            gain_sum[0:1, :] += jnp.sum(grad_y * normed, axis=0, keepdims=True)
            return carry

        lax.fori_loop(0, TOK_DEV // 32, chunk, 0)
        gain_sum[...] += gains_in[...]

        def fill(i, carry):
            at = pl.ds(pl.multiple_of(i * rows // 128 * 128, 128), 128)
            pay[i, 0:8, :] = router_ref[i]
            pay[i, 8:16, :] = gain_sum[:, at]
            return carry

        lax.fori_loop(0, count, fill, 0)

    def m_copy(i):
        other = lax.rem(me + i, count)
        return remote(
            pay.at[other], small.at[me], msend.at[i], mrecv.at[me], (other // sp, lax.rem(other, sp))
        )

    def m_go(i, carry):
        m_copy(i).start()
        return carry

    for t in range(lines - 1):
        line.step(t)
        if t == 0:
            first_grads()
            plane.start()
    plane.forward()
    plane.finish()
    input_grads()
    lax.fori_loop(1, count, m_go, 0)
    line.finish(low)
    for c in range(sp):
        top = 3 * height + c * rows
        o_low[:, c * cols : (c + 1) * cols] = low[top : top + rows, :]

    def q_from(i, place):
        return low.at[pl.ds(pl.multiple_of(i * height + place * rows, rows), rows), :]

    def q_to(i, place):
        return (qkv_0, qkv_1, qkv_2)[i].at[place]

    def q_copy(i, k):
        return remote(q_from(i, s ^ k), q_to(i, s), qsend.at[k, i], qrecv.at[k, i], (f, s ^ k))

    def q_own(i):
        return pltpu.make_async_copy(q_from(i, s), q_to(i, s), local.at[i])

    for k in range(sp - 1, 0, -1):
        for i in range(3):
            q_copy(i, k).start()
    owner = row_owner(f, s, rows, sp)
    target_f, target_s = owner // sp, lax.rem(owner, sp)
    stays = jnp.logical_and(target_s == s, target_f == f)
    o_copy = remote(o_low, o_out, osend, orecv, (target_f, target_s))
    o_own = pltpu.make_async_copy(o_low, o_out, orecv)

    @pl.when(stays)
    def _():
        o_own.start()

    @pl.when(jnp.logical_not(stays))
    def _():
        o_copy.start()

    for i in range(3):
        q_own(i).start()

    def m_end(i, carry):
        m_copy(i).wait_send()
        other = lax.rem(me + i, count)
        landed(small.at[other], mrecv.at[other])
        return carry + small[other]

    small_out[...] = lax.fori_loop(1, count, m_end, pay[me])
    for k in range(1, sp):
        for i in range(3):
            landed(q_to(i, s ^ k), qrecv.at[k, i])
            q_copy(i, k).wait_send()
    landed(o_out, orecv)

    @pl.when(jnp.logical_not(stays))
    def _():
        o_copy.wait_send()

    for i in range(3):
        q_own(i).wait()


def end_exchange(fsdp, sp, partial, low, w, x, grad_mid, gains, gains_in, router, number):
    count = fsdp * sp
    block = partial.shape[1:]
    rows = D // count
    dma = pltpu.SemaphoreType.DMA
    return pl.pallas_call(
        functools.partial(end_kernel, fsdp, sp),
        out_shape=(
            jax.ShapeDtypeStruct((TOK_DEV, D), F32),
            jax.ShapeDtypeStruct((sp, rows, D // sp), BF16),
            jax.ShapeDtypeStruct((sp, rows, D // sp), BF16),
            jax.ShapeDtypeStruct((sp, rows, D // sp), BF16),
            jax.ShapeDtypeStruct((rows, D), BF16),
            jax.ShapeDtypeStruct((16, 128), F32),
        ),
        in_specs=[ANY, ANY, ANY, VMEM, VMEM, VMEM, VMEM, VMEM],
        out_specs=[VMEM, ANY, ANY, ANY, ANY, VMEM],
        scratch_shapes=[
            pltpu.VMEM((sp, TOK_DEV, D), BF16),
            pltpu.VMEM(low.shape, BF16),
            pltpu.VMEM(w.shape, BF16),
            pltpu.VMEM((TOK_DEV, D), F32),
            pltpu.VMEM(block, BF16),
            pltpu.VMEM((rows, D), BF16),
            pltpu.VMEM((8, D), F32),
            pltpu.VMEM((count, 16, 128), F32),
            pltpu.VMEM((count, 16, 128), F32),
            dma((2,)),
            dma((sp, 3)), dma((sp, 3)), dma, dma, dma((count,)), dma((count,)), dma((3,)),
        ]
        + plane_scratch((TOK_DEV, D), sp)
        + LineReduce.scratch(fsdp, block),
        compiler_params=comm_params(number),
        name="end_exchange",
    )(partial, low, w, x, grad_mid, gains, gains_in, router)


def dot_nt(a, b):
    return lax.dot_general(a, b, (((1,), (1,)), ((), ())), preferred_element_type=F32)


def dot_tn(a, b):
    return lax.dot_general(a, b, (((0,), (0,)), ((), ())), preferred_element_type=F32)


def dot_nn(a, b):
    return jnp.dot(a, b, preferred_element_type=F32)


def whole(shape):
    return pl.BlockSpec(shape, lambda *_: (0,) * len(shape))


def lanes(first, second):
    lane = lax.broadcasted_iota(jnp.int32, (first.shape[0], 128), 1)
    return jnp.where(lane == 0, first, jnp.where(lane == 1, second, 0.0))


def inverse_of(sums, lane):
    return lax.rsqrt(sums[:, lane : lane + 1] / D + EPSILON)


def turn(v, table, sign=1.0):
    half = HEAD_DIM // 2
    front = lax.broadcasted_iota(jnp.int32, table.shape, 1) < half
    turned = pltpu.roll(table, half, 1)
    cosine = jnp.where(front, table, turned)
    sine = jnp.where(front, -turned, table)
    return v * cosine + pltpu.roll(v, half, 1) * (sine * sign)


def turn_back(v, table):
    return turn(v, table, -1.0)


def project_kernel(sp, x_ref, gain, w_ref, first_out, q_out, k_out, v_out, sums_out, squares, *scratch):
    step = pl.program_id(0)
    total = PlaneSum(scratch, lax.axis_index("fsdp"), lax.axis_index("sp"), sp)
    barrier = pltpu.get_barrier_semaphore()

    @pl.when(step == 0)
    def _():
        total.greet(barrier)

    x = x_ref[...].astype(F32)
    inverse = lax.rsqrt(jnp.mean(x * x, axis=-1, keepdims=True) + EPSILON)
    first = (x * inverse * gain[0:1, :]).astype(BF16)
    first_out[...] = first
    q = dot_nn(first, w_ref[0])
    q_out[...] = q
    k = dot_nn(first, w_ref[1])
    k_out[...] = k
    at = pl.ds(pl.multiple_of(step * TOK_DEV, TOK_DEV), TOK_DEV)
    squares[at, :] = lanes(
        jnp.sum(q * q, axis=-1, keepdims=True), jnp.sum(k * k, axis=-1, keepdims=True)
    )
    last = step == pl.num_programs(0) - 1

    @pl.when(last)
    def _():
        pl.semaphore_wait(barrier, sp - 1)
        total.start(squares)

    v_out[...] = dot_nn(first, w_ref[2]).astype(BF16)

    @pl.when(last)
    def _():
        total.finish(sums_out)


def project(sp, x, gains, w):
    seq, cols = x.shape[0], w.shape[2]

    def block(width):
        return pl.BlockSpec((TOK_DEV, width), lambda i: (i, 0))

    return pl.pallas_call(
        functools.partial(project_kernel, sp),
        grid=(seq // TOK_DEV,),
        out_shape=(
            jax.ShapeDtypeStruct((seq, D), BF16),
            jax.ShapeDtypeStruct((seq, cols), F32),
            jax.ShapeDtypeStruct((seq, cols), F32),
            jax.ShapeDtypeStruct((seq, cols), BF16),
            jax.ShapeDtypeStruct((seq, 128), F32),
        ),
        in_specs=[block(D), whole(gains.shape), whole(w.shape)],
        out_specs=[block(D), block(cols), block(cols), block(cols), whole((seq, 128))],
        scratch_shapes=[pltpu.VMEM((seq, 128), F32)] + PlaneSum.scratch(seq, sp),
        compiler_params=comm_params(1),
        name="project",
    )(x, gains, w)


def attend_kernel(
    q_raw, k_raw, v_ref, squares, gain, table, o_ref, sum_ref, q_ref, k_ref
):
    head = pl.program_id(0)

    @pl.when(head == 0)
    def _():
        sum_ref[...] = squares[...]

    q_inv, k_inv = inverse_of(squares, 0), inverse_of(squares, 1)
    q_ref[...] = turn(q_raw[...] * q_inv * gain[2:3, :], table[...]).astype(BF16)
    k_ref[...] = turn(k_raw[...] * k_inv * gain[3:4, :], table[...]).astype(BF16)
    for i in range(q_ref.shape[0] // BLK):
        rows, seen = pl.ds(i * BLK, BLK), pl.ds(0, (i + 1) * BLK)
        scores = dot_nt(q_ref[rows, :], k_ref[seen, :]) * SCALE
        row_max = jnp.max(scores, axis=-1, keepdims=True)
        exp_rows = jnp.exp(scores - row_max)
        row_sum = jnp.sum(exp_rows, axis=-1, keepdims=True)
        probs = (exp_rows / row_sum).astype(BF16)
        o_ref[rows, :] = dot_nn(probs, v_ref[seen, :]).astype(BF16)
        lane = lax.broadcasted_iota(jnp.int32, (BLK, 128), 1)
        sum_ref[rows, :] += jnp.where(lane == head + 2, row_max + jnp.log(row_sum), 0.0)


def attend(q_raw, k_raw, v, squares, gains, table):
    seq, width = v.shape
    heads = width // HEAD_DIM
    spec = pl.BlockSpec((seq, HEAD_DIM), lambda h: (0, h))
    return pl.pallas_call(
        attend_kernel,
        grid=(heads,),
        out_shape=(
            jax.ShapeDtypeStruct((seq, width), BF16),
            jax.ShapeDtypeStruct((seq, 128), F32),
            jax.ShapeDtypeStruct((seq, width), BF16),
            jax.ShapeDtypeStruct((seq, width), BF16),
        ),
        in_specs=[
            spec, spec, spec, whole((seq, 128)),
            pl.BlockSpec((4, HEAD_DIM), lambda h: (0, h)),
            whole((seq, HEAD_DIM)),
        ],
        out_specs=[spec, whole((seq, 128)), spec, spec],
        compiler_params=pltpu.CompilerParams(vmem_limit_bytes=VLIM),
        name="attend",
    )(q_raw, k_raw, v, squares, gains, table)


def attend_back_head(
    h, q_ref, k_ref, v_ref, sums, q_raw, k_raw, gain, table,
    q_scaled, k_scaled, dv_out, dots, gains_out, dv_ref,
):
    head = slice(h * HEAD_DIM, (h + 1) * HEAD_DIM)
    k_scaled[:, head] = jnp.zeros(k_raw[:, head].shape, F32)
    dv_ref[...] = jnp.zeros_like(dv_ref)
    gain_q, gain_k = gain[2:3, head], gain[3:4, head]
    gain_sum = jnp.zeros((1, HEAD_DIM), F32)
    size = BLK if q_ref.shape[0] <= 4 * BLK else BLK // 2
    for i in range(q_ref.shape[0] // size):
        rows, seen = pl.ds(i * size, size), pl.ds(0, (i * size // BLK + 1) * BLK)
        q, g, keys = q_ref[rows, head], dv_out[rows, head], k_ref[seen, head]
        scores = dot_nt(q, keys) * SCALE
        probs = jnp.exp(scores - sums[rows, h + 2 : h + 3])
        grad_probs = dot_nt(g, v_ref[seen, head])
        row_dot = jnp.sum(probs * grad_probs, axis=-1, keepdims=True)
        grad_scores = (probs * (grad_probs - row_dot)).astype(BF16)
        k_scaled[seen, head] += dot_tn(grad_scores, q)
        dv_ref[seen, :] += dot_tn(probs.astype(BF16), g)
        grad_y = turn_back(dot_nn(grad_scores, keys) * SCALE, table[rows, :])
        normed = q_raw[rows, head] * inverse_of(sums.at[rows, :], 0)
        scaled = grad_y * gain_q
        q_scaled[rows, head] = scaled
        dots[rows, :] += lanes(jnp.sum(scaled * normed, axis=-1, keepdims=True), 0.0)
        gain_sum += jnp.sum(grad_y * normed, axis=0, keepdims=True)
    grad_y = turn_back(k_scaled[:, head] * SCALE, table[...])
    normed = k_raw[:, head] * inverse_of(sums, 1)
    scaled = grad_y * gain_k
    k_scaled[:, head] = scaled
    k_dots = jnp.sum(scaled * normed, axis=-1, keepdims=True)
    dots[...] += lanes(jnp.zeros_like(k_dots), k_dots)
    gains_out[0:1, head] = gain_sum
    gains_out[1:2, head] = jnp.sum(grad_y * normed, axis=0, keepdims=True)
    dv_out[:, head] = dv_ref[...].astype(BF16)


def branch_back_kernel(
    fsdp, sp, x_ref, p_ref, wo_ref, q_ref, k_ref, v_ref, sums, q_raw, k_raw, gain, table,
    all_ref, out_ref, q_scaled, k_scaled, dv_out, dots, gains_out,
    g_all, dv_ref, xsend, xrecv, own_sem, all_sem, *scratch,
):
    f, s = lax.axis_index("fsdp"), lax.axis_index("sp")
    lines = fsdp // 2
    barrier = pltpu.get_barrier_semaphore()
    sums_over = PlaneSum(scratch[:4], f, s, sp)
    expected = greet_line(barrier, lines, f, s) + sums_over.greet(barrier)
    plane = plane_gather_of(x_ref, g_all, f, s, sp, xsend, xrecv)
    own = pltpu.make_async_copy(x_ref, plane.at(s, 0, x_ref.shape[0]), own_sem)
    own.start()
    pl.semaphore_wait(barrier, expected)
    plane.start()
    line = LineReduce(p_ref, scratch[4:], lines, f, s)
    line.start()
    dots[...] = jnp.zeros_like(dots)
    out_all = pltpu.make_async_copy(g_all, all_ref, all_sem)
    def back_of(place):
        at = pl.ds(pl.multiple_of(place * TOK_DEV, TOK_DEV), TOK_DEV)
        dv_out[at, :] = dot_nt(g_all[at, :], wo_ref[...]).astype(BF16)

    early = (0, 1, 2) if sp == 4 else (0,)
    for t in range(lines - 1):
        line.step(t)
        if t == min(1, lines - 2):
            plane.forward()
            own.wait()
            for k in early:
                back_of(s ^ k)
    plane.finish()
    out_all.start()
    for k in range(len(early), sp):
        back_of(s ^ k)
    for h in range(q_ref.shape[1] // HEAD_DIM):
        attend_back_head(
            h, q_ref, k_ref, v_ref, sums, q_raw, k_raw, gain, table,
            q_scaled, k_scaled, dv_out, dots, gains_out, dv_ref,
        )
    sums_over.start(dots)
    line.finish(out_ref)
    sums_over.finish(dots)
    out_all.wait()


def branch_back(fsdp, sp, x, partial, wo, q, k, v, sums, q_raw, k_raw, gains, table):
    block = partial.shape[1:]
    seq, width = q.shape
    dma = pltpu.SemaphoreType.DMA
    return pl.pallas_call(
        functools.partial(branch_back_kernel, fsdp, sp),
        out_shape=(
            jax.ShapeDtypeStruct((seq, D), BF16),
            jax.ShapeDtypeStruct(block, F32),
            jax.ShapeDtypeStruct((seq, width), F32),
            jax.ShapeDtypeStruct((seq, width), F32),
            jax.ShapeDtypeStruct((seq, width), BF16),
            jax.ShapeDtypeStruct((seq, 128), F32),
            jax.ShapeDtypeStruct((2, width), F32),
        ),
        in_specs=[VMEM, ANY] + [VMEM] * 9,
        out_specs=[ANY] + [VMEM] * 6,
        scratch_shapes=[
            pltpu.VMEM((seq, D), BF16), pltpu.VMEM((seq, HEAD_DIM), F32), dma((sp,)), dma((sp,)), dma, dma,
        ]
        + PlaneSum.scratch(seq, sp)
        + LineReduce.scratch(fsdp, block),
        compiler_params=comm_params(5),
        name="branch_back",
    )(x, partial, wo, q, k, v, sums, q_raw, k_raw, gains, table)


def held(shape):
    return pl.BlockSpec(
        shape, lambda *_: (0,) * len(shape), pipeline_mode=pl.Buffered(buffer_count=1)
    )


def weight_kernel(
    q_scaled, k_scaled, q_raw, k_raw, squares, dots, dv_ref, first, attended, g_ref, out, low, square
):
    f = pl.program_id(0)
    height = first.shape[1]
    rows = out.shape[1] - 3 * height
    cols = out.shape[2]
    sp = D // cols

    @pl.when(f == 0)
    def _():
        for n, scaled, raw in ((0, q_scaled, q_raw), (1, k_scaled, k_raw)):
            inverse = inverse_of(squares, n)
            mean = dots[:, n : n + 1] / D
            low[:, n * cols : (n + 1) * cols] = (
                inverse * (scaled[...] - raw[...] * (inverse * mean))
            ).astype(BF16)
        low[:, 2 * cols :] = dv_ref[...]
        for c in range(sp):
            at = slice(c * cols, (c + 1) * cols)
            square[:, at] = dot_tn(attended[...], g_ref[:, at]).astype(BF16)

    grads = dot_tn(first[...], low[...]).astype(BF16)
    for n in range(3):
        out[0, n * height : (n + 1) * height, :] = grads[:, n * cols : (n + 1) * cols]
    each = rows // sp
    from_rows = pl.ds(pl.multiple_of(f * each, each), each)
    for c in range(sp):
        at = 3 * height + c * each
        out[0, at : at + each, :] = square[from_rows, c * cols : (c + 1) * cols]


def weight_parts(fsdp, q_scaled, k_scaled, q_raw, k_raw, squares, dots, dv, first, attended, g):
    seq, cols = dv.shape
    height = D // fsdp
    each = cols // fsdp
    return pl.pallas_call(
        weight_kernel,
        grid=(fsdp,),
        out_shape=(
            jax.ShapeDtypeStruct((fsdp, 3 * height + D // cols * each, cols), BF16),
            jax.ShapeDtypeStruct((seq, 3 * cols), BF16),
        ),
        in_specs=[held((seq, cols))] * 4
        + [held((seq, 128))] * 2
        + [
            held((seq, cols)),
            pl.BlockSpec((seq, height), lambda f: (0, f)),
            held((seq, cols)),
            held((seq, D)),
        ],
        out_specs=[
            pl.BlockSpec((1, 3 * height + D // cols * each, cols), lambda f: (f, 0, 0)),
            whole((seq, 3 * cols)),
        ],
        scratch_shapes=[pltpu.VMEM((cols, D), BF16)],
        compiler_params=pltpu.CompilerParams(vmem_limit_bytes=VLIM),
        name="weight_parts",
    )(q_scaled, k_scaled, q_raw, k_raw, squares, dots, dv, first, attended, g)


def two_parts(x, axis):
    high = x.astype(BF16)
    return jnp.concatenate([high, (x - high.astype(F32)).astype(BF16)], axis=axis)


def blocks_of(shape):
    return pl.BlockSpec((1,) + shape, lambda b: (b,) + (0,) * len(shape))


def slots_of(slots, width):
    return pl.BlockSpec((EXP_DEV, slots, width), lambda b: (0, b, 0))


def route_kernel(picks, rows_in, router, columns, out, probs_out, gates_out):
    slots = out.shape[1]
    for n in range(D // 512):
        at = pl.ds(n * 512, 512)
        got = dot_nn(picks[0], rows_in[0, :, at]).astype(BF16)
        for e in range(EXP_DEV):
            out[e, :, at] = got[e * slots : (e + 1) * slots]
    logits = dot_nt(rows_in[0], router[...])
    exp_logits = jnp.exp(logits - jnp.max(logits, axis=1, keepdims=True))
    probs = exp_logits / jnp.sum(exp_logits, axis=1, keepdims=True)
    probs_out[0] = probs
    both = two_parts(probs, 1)
    for e in range(EXP_DEV):
        moved = dot_nn(picks[0, e * slots : (e + 1) * slots, :], both)
        mask = columns[e : e + 1, :]
        gates_out[e] = jnp.sum(moved * jnp.concatenate([mask, mask], axis=1), axis=1, keepdims=True)


def route(picks, tokens, router_t, columns):
    blocks = tokens.shape[0]
    slots = picks.shape[1] // EXP_DEV
    total = blocks * slots
    experts = router_t.shape[0]
    return pl.pallas_call(
        route_kernel,
        grid=(blocks,),
        out_shape=(
            jax.ShapeDtypeStruct((EXP_DEV, total, D), BF16),
            jax.ShapeDtypeStruct((blocks, TOK_DEV, experts), F32),
            jax.ShapeDtypeStruct((EXP_DEV, total, 1), F32),
        ),
        in_specs=[
            blocks_of(picks.shape[1:]), blocks_of((TOK_DEV, D)), whole(router_t.shape),
            whole(columns.shape),
        ],
        out_specs=[slots_of(slots, D), blocks_of((TOK_DEV, experts)), slots_of(slots, 1)],
        compiler_params=pltpu.CompilerParams(vmem_limit_bytes=VLIM),
        name="route",
    )(picks, tokens, router_t, columns)


FT = 256


def active_tile(x_ref, g_ref, up, u_ref, gates, gated, grad_gate, grad_up, dots):
    total = x_ref.shape[1]
    chunk = total // 4
    for first in range(0, total, chunk):
        at = slice(first, first + chunk)
        gate_pre = dot_nn(x_ref[0, at, :], g_ref[0])
        up_pre = dot_nn(x_ref[0, at, :], up)
        sig = jax.nn.sigmoid(gate_pre)
        silu = gate_pre * sig
        hidden = silu * up_pre
        back = u_ref[0, at, :]
        gate = gates[0, at, :]
        dots[0, at, :] += jnp.sum(hidden * back, axis=1, keepdims=True)
        gated[0, at, :] = (hidden * gate).astype(BF16)
        back = back * gate
        grad_gate[0, at, :] = (back * up_pre * (sig * (1.0 + gate_pre * (1.0 - sig)))).astype(BF16)
        grad_up[0, at, :] = (back * silu).astype(BF16)


def active_kernel(x_ref, g_ref, first_ref, second_ref, u_ref, gates, gated, grad_gate, grad_up, dots):
    rest = (u_ref, gates, gated, grad_gate, grad_up, dots)

    @pl.when(pl.program_id(1) == 0)
    def _():
        dots[...] = jnp.zeros_like(dots)
        active_tile(x_ref, g_ref, first_ref[0], *rest)

    @pl.when(pl.program_id(1) == 1)
    def _():
        active_tile(x_ref, g_ref, second_ref[...].reshape(first_ref.shape[1:]), *rest)


def active(x, w_gate, up_first, up_second, u, gates):
    _, total, _ = x.shape
    wide = up_first.shape[2]
    sp, _, height, _ = up_second.shape
    tile = pl.BlockSpec((1, total, wide), lambda e, j: (e, 0, j))
    column = pl.BlockSpec((1, total, 1), lambda e, j: (e, 0, 0))
    low = jax.ShapeDtypeStruct((EXP_DEV, total, 2 * wide), BF16)
    return pl.pallas_call(
        active_kernel,
        grid=(EXP_DEV, 2),
        out_shape=(low, low, low, jax.ShapeDtypeStruct((EXP_DEV, total, 1), F32)),
        in_specs=[
            pl.BlockSpec((1, total, D), lambda e, j: (e, 0, 0)),
            pl.BlockSpec((1, D, wide), lambda e, j: (e, 0, j)),
            pl.BlockSpec((1, D, wide), lambda e, j: (e, 0, 0)),
            pl.BlockSpec((sp, 1, height, wide), lambda e, j: (0, e, 0, 0)),
            tile,
            column,
        ],
        out_specs=[tile, tile, tile, column],
        compiler_params=pltpu.CompilerParams(vmem_limit_bytes=VLIM),
        name="active",
    )(x, w_gate, up_first, up_second, u, gates)


def weight_grad_kernel(a_ref, b_ref, out):
    out[0] = dot_tn(a_ref[0], b_ref[0]).astype(BF16)


def weight_grad(a, b, name):
    _, total, height = a.shape
    width = b.shape[2]
    size = 1024
    return pl.pallas_call(
        weight_grad_kernel,
        grid=(EXP_DEV, height // size, width // size),
        out_shape=jax.ShapeDtypeStruct((EXP_DEV, height, width), BF16),
        in_specs=[
            pl.BlockSpec((1, total, size), lambda e, i, j: (e, 0, i)),
            pl.BlockSpec((1, total, size), lambda e, i, j: (e, 0, j)),
        ],
        out_specs=pl.BlockSpec((1, size, size), lambda e, i, j: (e, i, j)),
        compiler_params=pltpu.CompilerParams(vmem_limit_bytes=VLIM),
        name=name,
    )(a, b)


def rows_back_kernel(a_ref, b_ref, g_ref, first_ref, second_ref, out):
    wide = first_ref.shape[2]
    total = dot_nt(a_ref[0], g_ref[0]) + dot_nt(b_ref[0, :, :wide], first_ref[0])
    second = second_ref[...].reshape(first_ref.shape[1:])
    out[0] = (total + dot_nt(b_ref[0, :, wide:], second)).astype(BF16)


def rows_back(grad_gate_pre, grad_up_pre, w_gate, up_first, up_second):
    _, total, ff = grad_up_pre.shape
    size = 512
    wide = up_first.shape[2]
    height = up_second.shape[2]
    row = pl.BlockSpec((1, total, ff), lambda e, j: (e, 0, 0))
    return pl.pallas_call(
        rows_back_kernel,
        grid=(EXP_DEV, D // size),
        out_shape=jax.ShapeDtypeStruct((EXP_DEV, total, D), BF16),
        in_specs=[
            row,
            row,
            pl.BlockSpec((1, size, ff), lambda e, j: (e, j, 0)),
            pl.BlockSpec((1, size, wide), lambda e, j: (e, j, 0)),
            pl.BlockSpec((size // height, 1, height, wide), lambda e, j: (j, e, 0, 0)),
        ],
        out_specs=pl.BlockSpec((1, total, size), lambda e, j: (e, 0, j)),
        compiler_params=pltpu.CompilerParams(vmem_limit_bytes=VLIM),
        name="rows_back",
    )(grad_gate_pre, grad_up_pre, w_gate, up_first, up_second)


def combine_kernel(turned, rows_ref, tokens, probs, dots, router, columns, out, router_out):
    @pl.when(pl.program_id(0) == 0)
    def _():
        router_out[...] = jnp.zeros_like(router_out)

    choice = jnp.zeros(probs.shape[1:], F32)
    for e in range(EXP_DEV):
        moved = dot_nn(turned[0, e], dots[e])
        choice += jnp.sum(moved, axis=1, keepdims=True) * columns[e : e + 1, :]
    p = probs[0]
    grad_logits = p * (choice - jnp.sum(p * choice, axis=1, keepdims=True))
    both = two_parts(grad_logits, 1)
    for n in range(D // 512):
        at = pl.ds(n * 512, 512)
        total = dot_nn(both, router[:, at])
        for e in range(EXP_DEV):
            total += dot_nn(turned[0, e], rows_ref[e, :, at])
        out[0, :, at] = total.astype(BF16)
    router_out[...] += dot_tn(both, tokens[0])


def combine(turned, grad_rows, tokens, probs, dots, router_two, columns):
    blocks = tokens.shape[0]
    slots = turned.shape[3]
    return pl.pallas_call(
        combine_kernel,
        grid=(blocks,),
        out_shape=(
            jax.ShapeDtypeStruct((blocks, TOK_DEV, D), BF16),
            jax.ShapeDtypeStruct((router_two.shape[0], D), F32),
        ),
        in_specs=[
            blocks_of(turned.shape[1:]), slots_of(slots, D), blocks_of((TOK_DEV, D)),
            blocks_of(probs.shape[1:]), slots_of(slots, 128), whole(router_two.shape),
            whole(columns.shape),
        ],
        out_specs=[blocks_of((TOK_DEV, D)), whole((router_two.shape[0], D))],
        compiler_params=pltpu.CompilerParams(vmem_limit_bytes=VLIM),
        name="combine",
    )(turned, grad_rows, tokens, probs, dots, router_two, columns)


def widen_kernel(mid, total, *refs):
    *refs, layer_out = refs
    layer_out[...] = (mid[...] + total[...]).astype(BF16)
    count = len(refs) // 2
    for low, out in zip(refs[:count], refs[count:]):
        if len(low.shape) == 2:
            out[...] = low[...].astype(F32)
            continue
        sp, _, cols = low.shape
        for s in range(sp):
            for g in range(cols // HEAD_DIM):
                head = g * sp + s
                out[:, head * HEAD_DIM : (head + 1) * HEAD_DIM] = low[
                    s, :, g * HEAD_DIM : (g + 1) * HEAD_DIM
                ].astype(F32)


def widen(mid, total, by_heads, arrays):
    steps = 4
    flat = [x.reshape(-1, x.shape[-1]) for x in arrays]

    def rows_of(shape, axis):
        tall = shape[axis] // steps if shape[axis] % (16 * steps) == 0 else shape[axis]
        block = shape[:axis] + (tall,) + shape[axis + 1 :]
        moving = tall != shape[axis]
        return pl.BlockSpec(
            block, lambda i: tuple(i if moving and n == axis else 0 for n in range(len(shape)))
        )

    heads_out = [(x.shape[1], x.shape[0] * x.shape[2]) for x in by_heads]
    wide = pl.pallas_call(
        widen_kernel,
        grid=(steps,),
        out_shape=tuple(
            jax.ShapeDtypeStruct(shape, F32) for shape in heads_out + [x.shape for x in flat]
        )
        + (jax.ShapeDtypeStruct(mid.shape, BF16),),
        in_specs=[rows_of(mid.shape, 0)] * 2
        + [rows_of(x.shape, 1) for x in by_heads]
        + [rows_of(x.shape, 0) for x in flat],
        out_specs=[rows_of(shape, 0) for shape in heads_out + [x.shape for x in flat] + [mid.shape]],
        compiler_params=pltpu.CompilerParams(vmem_limit_bytes=VLIM),
        name="widen",
    )(mid, total, *by_heads, *flat)
    split = len(by_heads)
    shaped = [x.reshape(like.shape) for x, like in zip(wide[split:-1], arrays)]
    return list(wide[:split]) + shaped + [wide[-1]]


def angles(seq):
    freqs = np.float32(ROPE_BASE) ** (-2.0 * np.arange(HEAD_DIM // 2, dtype=np.float32) / HEAD_DIM)
    turned = np.arange(seq, dtype=np.float32)[:, None] * freqs[None, :].astype(np.float32)
    return jnp.asarray(np.concatenate([np.cos(turned), np.sin(turned)], axis=1), F32)


def body(
    layer_input, output_grad, w_query, w_key, w_value, w_output, w_router, norm_gains,
    w_gate, w_up, w_down, expert_routes,
):
    fsdp, sp = lax.axis_size("fsdp"), lax.axis_size("sp")
    f, s = lax.axis_index("fsdp"), lax.axis_index("sp")
    count = fsdp * sp
    experts = EXP_DEV * fsdp
    capacity = TOK_DEV * TOP // experts * 17 // 16
    slots = -(-capacity // 16) * 16
    seq = TOK_DEV * sp
    cols = D // sp
    rows = D // count

    down_full = lax.all_gather(w_down, "sp", axis=1, tiled=True)
    gate_full = lax.all_gather(w_gate, "sp", axis=1, tiled=True)
    wide = w_up.shape[2] // 2
    up_first = lax.all_gather(w_up[:, :, :wide], "sp", axis=1, tiled=True)

    router_size = rows * experts
    misc = jnp.concatenate([w_router.reshape(router_size), norm_gains.reshape(4 * rows)])
    misc_rows = -(-misc.shape[0] // 2048) * 16
    misc = jnp.pad(misc, (0, misc_rows * 128 - misc.shape[0])).reshape(misc_rows, 128)
    routes = expert_routes.reshape(TOK_DEV * TOP // 128, 128)
    early = TOK_DEV // 8
    x_all, w_all, wo_s, grad_first_half, misc_all, routes_all = gather_start(
        fsdp, sp, layer_input, jnp.stack([w_query, w_key, w_value]), w_output, output_grad[:early],
        misc, routes,
    )
    misc_all = misc_all.reshape(count, misc_rows * 128)
    router_w = misc_all[:, :router_size].reshape(D, experts)
    router_t = router_w.T
    gains_w = misc_all[:, router_size : router_size + 4 * rows].reshape(count, 4, rows)
    gains32 = gains_w.transpose(1, 0, 2).reshape(4, D).astype(F32)
    by_head = gains32.reshape(4, cols // HEAD_DIM, sp, HEAD_DIM)
    gains_own = lax.dynamic_index_in_dim(by_head, s, axis=2, keepdims=False).reshape(4, cols)

    routes_block = routes_all.reshape(fsdp, TOK_DEV, TOP)
    own_ids = f * EXP_DEV + jnp.arange(EXP_DEV, dtype=jnp.int32)
    chosen = jnp.any(routes_block[:, :, :, None] == own_ids, axis=2)
    before = jnp.arange(TOK_DEV)[:, None] > jnp.arange(TOK_DEV)[None, :]
    place = jnp.einsum(
        "ut,fte->feu", before.astype(BF16), chosen.astype(BF16), preferred_element_type=F32
    ).astype(jnp.int32)
    slot_ids = jnp.arange(slots, dtype=jnp.int32)
    picks = (
        (place[:, :, None, :] == slot_ids[:, None]) & chosen.transpose(0, 2, 1)[:, :, None, :]
    ).astype(BF16).reshape(fsdp, EXP_DEV * slots, TOK_DEV)
    turned = (
        (place[:, :, :, None] == slot_ids) & chosen.transpose(0, 2, 1)[:, :, :, None]
    ).astype(BF16)
    columns = (jnp.arange(experts, dtype=jnp.int32)[None, :] == own_ids[:, None]).astype(F32)

    first_in, q_raw, k_raw, values, squares = project(sp, x_all, gains32, w_all)
    table = angles(seq)
    attended, sums, queries, keys = attend(
        q_raw, k_raw, values, squares, gains_own, table
    )
    mid, second_in, grad_second_half = branch_sum(
        fsdp, attended, wo_s, output_grad[early:], layer_input, gains32
    )

    tokens, grad_taken, unscaled, up_second = token_gather(
        fsdp, sp, second_in, grad_first_half, grad_second_half, picks, down_full,
        w_up[:, :, wide:].reshape(-1, wide),
    )
    up_second = up_second.reshape(sp, EXP_DEV, D // sp, wide)
    received, probs, slot_gates = route(picks, tokens, router_t, columns)
    gated, grad_gate_pre, grad_up_pre, slot_dots = active(
        received, gate_full, up_first, up_second, unscaled, slot_gates
    )
    dots_two = jnp.pad(two_parts(slot_dots, 2), ((0, 0), (0, 0), (0, 126)))
    grad_rows = rows_back(grad_gate_pre, grad_up_pre, gate_full, up_first, up_second)
    second_part, router_two = combine(
        turned, grad_rows, tokens, probs, dots_two, jnp.concatenate([router_t, router_t], axis=0),
        columns,
    )
    grad_router = (router_two[:experts] + router_two[experts:]).T

    def shed(grad):
        return lax.psum_scatter(grad, "sp", scatter_dimension=1, tiled=True)

    grad_down = shed(weight_grad(gated, grad_taken, "down_grad"))
    grad_gate = shed(weight_grad(received, grad_gate_pre, "gate_grad"))
    grad_mid, grad_mid_low, gain_rows, out_part, up_part = token_back(
        fsdp, second_part, gated, down_full, turned, received, grad_up_pre, mid, output_grad, gains32
    )
    grad_up = shed(up_part)

    grad_branch, out_sum, q_scaled, k_scaled, grad_values, dots, gain_qk = branch_back(
        fsdp, sp, grad_mid_low, out_part, wo_s, queries, keys, values, sums, q_raw, k_raw,
        gains_own, table,
    )
    weight_part, grads_low = weight_parts(
        fsdp, q_scaled, k_scaled, q_raw, k_raw, squares, dots, grad_values, first_in, attended, grad_branch
    )

    gain_rows = lax.dynamic_update_slice(
        gain_rows.reshape(8, cols // HEAD_DIM, sp, HEAD_DIM),
        gain_qk.reshape(2, cols // HEAD_DIM, 1, HEAD_DIM),
        (2, 0, s, 0),
    ).reshape(8, D)
    router_part = grad_router.reshape(count, router_size)
    router_part = jnp.pad(router_part, ((0, 0), (0, 1024 - router_size))).reshape(count, 8, 128)
    input_grad, *weight_grads, small = end_exchange(
        fsdp, sp, weight_part, grads_low, w_all, layer_input, grad_mid, gains32, gain_rows, router_part, 8
    )
    *weight_grads, grad_gate, grad_up, grad_down, layer_out = widen(
        mid, out_sum, weight_grads[:3], [weight_grads[3], grad_gate, grad_up, grad_down]
    )
    grad_router_own = small[:8].reshape(1024)[:router_size].reshape(rows, experts)
    first_lane = (f * sp + s) * rows % 128
    grad_gains = lax.dynamic_slice(small[8:12], (0, first_lane), (4, rows))
    return (
        layer_out, input_grad, *weight_grads,
        grad_router_own, grad_gains, grad_gate, grad_up, grad_down,
    )


def solution(mesh):
    both, split = P(("fsdp", "sp"), None), P("fsdp", "sp", None)
    gains = P(None, ("fsdp", "sp"))
    return jax.shard_map(
        body,
        mesh=mesh,
        in_specs=(both,) * 7 + (gains,) + (split,) * 3 + (both,),
        out_specs=(both,) * 7 + (gains,) + (split,) * 3,
        check_vma=False,
    )
```
